32 devices in a mesh: dp: 2 (over x), context: 4 (over z), tensor: 4 (over y, core).
Axes of the slice: x: 2, y: 2, z: 4, core: 2. Of those that a mesh axis runs over, the one named last changes fastest.
Arguments:
- tokens: bfloat16 [2, 2048, 2560], P('dp', 'context'), may hold values from -6 to 6
- cotangent: bfloat16 [2, 2048, 2560], P('dp', 'context'), may hold values from -6 to 6
- group_order: int32 [8], replicated, may hold values from 0 to 7, each once
- attn_gain: float32 [2560], replicated, may hold values from 0.25 to 1.75
- query_down: bfloat16 [2560, 768], replicated, may hold values from -0.125 to 0.125
- query_gain: float32 [768], replicated, may hold values from 0.25 to 1.75
- latent_down: bfloat16 [2560, 288], replicated, may hold values from -0.125 to 0.125
- latent_gain: float32 [256], replicated, may hold values from 0.25 to 1.75
- query_up: bfloat16 [768, 3840], P(None, 'tensor'), may hold values from -0.4375 to 0.4375
- latent_up: bfloat16 [256, 5120], P(None, 'tensor'), may hold values from -0.375 to 0.375
- attn_out: bfloat16 [2560, 2560], P('tensor'), may hold values from -4 to 4
- mlp_gain: float32 [2560], replicated, may hold values from 0.25 to 1.75
- gate_proj: bfloat16 [2560, 6400], P(None, 'tensor'), may hold values from -0.125 to 0.125
- up_proj: bfloat16 [2560, 6400], P(None, 'tensor'), may hold values from -0.125 to 0.125
- down_proj: bfloat16 [6400, 2560], P('tensor'), may hold values from -0.875 to 0.875
Outputs:
- layer_out: bfloat16 [2, 2048, 2560], P('dp', 'context')
- token_grad: float32 [2, 2048, 2560], P('dp', 'context')
- attn_gain_grad: float32 [2560], P(('dp', 'context'))
- query_down_grad: float32 [2560, 768], P(('dp', 'context'))
- query_gain_grad: float32 [768], P(('dp', 'context'))
- latent_down_grad: float32 [2560, 288], P(('dp', 'context'))
- latent_gain_grad: float32 [256], P(('dp', 'context'))
- query_up_grad: float32 [768, 3840], P(('dp', 'context'), 'tensor')
- latent_up_grad: float32 [256, 5120], P(('dp', 'context'), 'tensor')
- attn_out_grad: float32 [2560, 2560], P('tensor', ('dp', 'context'))
- mlp_gain_grad: float32 [2560], P(('dp', 'context'))
- gate_proj_grad: float32 [2560, 6400], P(('dp', 'context'), 'tensor')
- up_proj_grad: float32 [2560, 6400], P(('dp', 'context'), 'tensor')
- down_proj_grad: float32 [6400, 2560], P('tensor', ('dp', 'context'))
The draws below stay inside these ranges and needn't reach their ends.
Inputs may be any that keep to these rules, and one draw needn't show every extreme that they name: group_order is a permutation; the shard of context index c holds, in this order, the blocks group_order[2 c] and group_order[2 c + 1] of 256 consecutive positions of each of its sequences.
All inputs are finite; a program needn't handle non-finite values.
Results may differ from the reference program's by a relative error of at most 0.025.
Values may be sent and summed in bfloat16 or wider, within the bound.
A program may use at most 192 MiB of HBM per device.

```python
import math
import jax
import jax.numpy as jnp
from jax import lax

D = 2560
HEADS = 40
NOPE = 64
ROPE = 32
V_DIM = 64
Q_RANK = 768
KV_RANK = 256
FF = 6400
HALF = 256
SEQ_LEN = 2048
SEQS = 2
N_CONTEXT = 4


def shard_levels(stream_key, dims, cuts, low, top_value):
    level = 1.0
    for position, shards_of in cuts:
        steps = jax.random.uniform(jax.random.fold_in(jax.random.fold_in(stream_key, 6), position), (shards_of,), jnp.float32, low / len(cuts), top_value / len(cuts))
        level = level * jnp.repeat(jnp.exp(steps), dims[position] // shards_of).reshape((-1,) + (1,) * (len(dims) - 1 - position))
    return level


def normal_values(stream_key, shape, deviation, limit, shards=(), kind=jnp.bfloat16):
    entries = jax.random.normal(stream_key, shape, jnp.float32) * deviation
    if len(shards) > 0:
        entries = shard_levels(stream_key, shape, shards, -0.22, 0.18) * entries
    return jnp.clip(entries, min=-limit, max=limit).astype(kind)


def setup_inputs(seed: int = 0) -> dict:
    key_list = jax.random.split(jax.random.key(seed), 16)
    tokens = normal_values(key_list[0], (SEQS, SEQ_LEN, D), 1.0, 6.0, ((0, 2), (1, 4)))
    cotangent = normal_values(key_list[1], (SEQS, SEQ_LEN, D), 1.0, 6.0, ((0, 2), (1, 4)))
    group_order = jax.random.permutation(key_list[2], 2 * N_CONTEXT).astype(jnp.int32)
    attn_gain = jnp.clip(1.0 + 0.15 * jax.random.normal(key_list[3], (D,), jnp.float32), 0.25, 1.75)
    query_down = normal_values(key_list[4], (D, Q_RANK), D ** -0.5, 0.125)
    query_gain = jnp.clip(1.0 + 0.15 * jax.random.normal(key_list[5], (Q_RANK,), jnp.float32), 0.25, 1.75)
    latent_down = normal_values(key_list[6], (D, KV_RANK + ROPE), D ** -0.5, 0.125)
    latent_gain = jnp.clip(1.0 + 0.15 * jax.random.normal(key_list[7], (KV_RANK,), jnp.float32), 0.25, 1.75)
    query_up = normal_values(key_list[8], (Q_RANK, HEADS * (NOPE + ROPE)), (Q_RANK // 4) ** -0.5, 0.4375, ((1, 4),))
    latent_up = normal_values(key_list[9], (KV_RANK, HEADS * (NOPE + V_DIM)), KV_RANK ** -0.5, 0.375, ((1, 4),))
    attn_out = normal_values(key_list[10], (HEADS * V_DIM, D), (max(1, HEADS * V_DIM // 1024)) ** -0.5, 4.0, ((0, 4),))
    mlp_gain = jnp.clip(1.0 + 0.15 * jax.random.normal(key_list[11], (D,), jnp.float32), 0.25, 1.75)
    gate_proj = normal_values(key_list[12], (D, FF), D ** -0.5, 0.125, ((1, 4),))
    up_proj = normal_values(key_list[13], (D, FF), D ** -0.5, 0.125, ((1, 4),))
    down_proj = normal_values(key_list[14], (FF, D), (max(1, FF // 128)) ** -0.5, 0.875, ((0, 4),))
    return {"tokens": tokens, "cotangent": cotangent, "group_order": group_order, "attn_gain": attn_gain, "query_down": query_down, "query_gain": query_gain, "latent_down": latent_down, "latent_gain": latent_gain, "query_up": query_up, "latent_up": latent_up, "attn_out": attn_out, "mlp_gain": mlp_gain, "gate_proj": gate_proj, "up_proj": up_proj, "down_proj": down_proj}


EPS = 1e-05
RESIDUAL = 1.4 / math.sqrt(62.0)
PRECISE = lax.Precision.HIGHEST

@jax.custom_vjp
def low(v):
    return lax.optimization_barrier(v.astype(jnp.bfloat16)).astype(jnp.float32)

@jax.custom_vjp
def low_back(v):
    return v

def low_keep(v):
    return (low(v), None)

def low_pass(kept, grad):
    return (grad,)

def back_keep(v):
    return (v, None)

def back_low(kept, grad):
    return (low(grad),)
low.defvjp(low_keep, low_pass)
low_back.defvjp(back_keep, back_low)

def matmul(left, right):
    return jnp.dot(left, right, precision=PRECISE, preferred_element_type=jnp.float32)

def norm(value, gain):
    return value * lax.rsqrt(lax.optimization_barrier(jnp.mean(value * value, axis=-1, keepdims=True)) + EPS) * gain

def rope_tables(positions):
    count = ROPE // 2
    freq = 10000.0 ** (-2.0 * jnp.arange(count, dtype=jnp.float32) / ROPE)
    angle = positions.astype(jnp.float32)[:, None] * freq[None, :]
    return (jnp.cos(angle), jnp.sin(angle))

def rotate(value, cosine, sine):
    count = value.shape[-1] // 2
    first = value[..., :count]
    second = value[..., count:]
    return jnp.concatenate([first * cosine - second * sine, second * cosine + first * sine], axis=-1)

def attend(q_nope, q_rope, k_nope, k_rope, values, positions):
    size = min(512, SEQ_LEN)
    count = SEQ_LEN // size
    scale = 1.0 / math.sqrt(NOPE + ROPE)

    def block(piece):
        part_nope, part_rope, part_pos = piece
        raw = jnp.einsum('qhd,khd->hqk', part_nope, k_nope, precision=PRECISE)
        raw = (raw + jnp.einsum('qhd,kd->hqk', part_rope, k_rope, precision=PRECISE)) * scale
        allowed = positions[None, None, :] <= part_pos[None, :, None]
        score = jnp.where(allowed, low_back(raw), -1e+30)
        top = lax.optimization_barrier(jnp.max(score, axis=-1, keepdims=True))
        weight = jnp.exp(score - top)
        prob = weight / lax.optimization_barrier(jnp.sum(weight, axis=-1, keepdims=True))
        return jnp.einsum('hqk,khd->qhd', low(prob), values, precision=PRECISE)
    pieces = (q_nope.reshape(count, size, HEADS, NOPE), q_rope.reshape(count, size, HEADS, ROPE), positions.reshape(count, size))
    mixed = lax.map(jax.checkpoint(block), pieces)
    return mixed.reshape(SEQ_LEN, HEADS, V_DIM)

def layer(params, inputs, positions):
    attn_gain, query_down, query_gain, latent_down, latent_gain, query_up, latent_up, attn_out, mlp_gain, gate_proj, up_proj, down_proj = params
    cosine, sine = rope_tables(positions)
    hidden_one = low(norm(inputs, attn_gain))
    query_low = low_back(matmul(hidden_one, query_down))
    latent_raw = low_back(matmul(hidden_one, latent_down))
    query_latent = low(norm(query_low, query_gain))
    latent = low(norm(latent_raw[:, :KV_RANK], latent_gain))
    key_rope = low(rotate(latent_raw[:, KV_RANK:], cosine, sine))
    query_full = low_back(matmul(query_latent, query_up)).reshape(SEQ_LEN, HEADS, NOPE + ROPE)
    query_nope = low(query_full[:, :, :NOPE])
    query_rope = low(rotate(query_full[:, :, NOPE:], cosine[:, None, :], sine[:, None, :]))
    key_values = low(matmul(latent, latent_up)).reshape(SEQ_LEN, HEADS, NOPE + V_DIM)
    mixed = attend(query_nope, query_rope, key_values[:, :, :NOPE], key_rope, key_values[:, :, NOPE:], positions)
    joined = low(low_back(mixed)).reshape(SEQ_LEN, HEADS * V_DIM)
    branch = low_back(matmul(joined, attn_out))
    middle = inputs + RESIDUAL * branch
    hidden_two = low(norm(middle, mlp_gain))
    gate = low_back(matmul(hidden_two, gate_proj))
    upper = low_back(matmul(hidden_two, up_proj))
    hidden_mid = low(jax.nn.silu(gate) * upper)
    feed = low_back(matmul(hidden_mid, down_proj))
    return middle + RESIDUAL * feed

def reference(tokens, cotangent, group_order, attn_gain, query_down, query_gain, latent_down, latent_gain, query_up, latent_up, attn_out, mlp_gain, gate_proj, up_proj, down_proj):
    offsets = jnp.arange(HALF, dtype=jnp.int32)
    positions = (group_order.astype(jnp.int32)[:, None] * HALF + offsets[None, :]).reshape(SEQ_LEN)
    params = tuple((p.astype(jnp.float32) for p in (attn_gain, query_down, query_gain, latent_down, latent_gain, query_up, latent_up, attn_out, mlp_gain, gate_proj, up_proj, down_proj)))

    def one(total, pair):
        inputs, upstream = pair
        result, pull = jax.vjp(lambda p, v: layer(p, v, positions), params, inputs.astype(jnp.float32))
        grad_params, grad_inputs = pull(upstream.astype(jnp.float32))
        total = jax.tree.map(lambda a, b: a + b, total, grad_params)
        return (total, (result.astype(jnp.bfloat16), grad_inputs))
    zeros = tuple((jnp.zeros(p.shape, jnp.float32) for p in params))
    total, (outputs, grads) = lax.scan(one, zeros, (tokens, cotangent))
    return (outputs, grads, total[0], total[1], total[2], total[3], total[4], total[5], total[6], total[7], total[8], total[9], total[10], total[11])
```

```python
import functools
import math

import jax
import jax.numpy as jnp
from jax import lax
from jax.experimental import pallas as pl
from jax.experimental.pallas import tpu as pltpu
from jax.sharding import PartitionSpec as P

NOPE = 64
ROPE = 32
V_DIM = 64
KV_RANK = 256
HALF = 256
GROUP = 5

EPS = 1e-05
RESIDUAL = 1.4 / math.sqrt(62.0)
SCALE = 1.0 / math.sqrt(NOPE + ROPE)
LOG2E = 1.0 / math.log(2.0)
F32 = jnp.float32
BF16 = jnp.bfloat16


def matmul(left, right):
    return jnp.dot(left, right, preferred_element_type=F32)


def times_transposed(left, right):
    return lax.dot_general(left, right, (((1,), (1,)), ((), ())), preferred_element_type=F32)


def transposed_times(left, right):
    return lax.dot_general(left, right, (((0,), (0,)), ((), ())), preferred_element_type=F32)


def scaled(value):
    inverse = lax.rsqrt(jnp.mean(value * value, axis=-1, keepdims=True) + EPS)
    return (value * inverse, inverse)


def norm_back(incoming, normed, inverse, gain):
    weighted = incoming * gain
    grad_gain = jnp.sum(incoming * normed, axis=0)
    grad_value = inverse * (weighted - normed * jnp.mean(weighted * normed, axis=-1, keepdims=True))
    return (grad_value, grad_gain)


def rotate(value, cosine, sine):
    count = value.shape[-1] // 2
    first = value[..., :count]
    second = value[..., count:]
    return jnp.concatenate(
        [first * cosine - second * sine, second * cosine + first * sine], axis=-1
    )


def unrotate(value, cosine, sine):
    count = value.shape[-1] // 2
    first = value[..., :count]
    second = value[..., count:]
    return jnp.concatenate(
        [first * cosine + second * sine, second * cosine - first * sine], axis=-1
    )


def load_heads(heads, latent, rope_keys, latent_up, q_t, kcat, q_wide):
    for h in range(heads):
        kcat[h, :, :128] = matmul(latent[...], latent_up[:, h * 128 : (h + 1) * 128]).astype(BF16)
        kcat[h, :, 128:] = rope_keys[...]
        q_wide[h, 0:64, :] = q_t[h, 0:64, :]
        q_wide[h, 64:128, :] = jnp.zeros((64, q_wide.shape[2]), BF16)
        q_wide[h, 128:160, :] = q_t[h, 64:96, :]
        q_wide[h, 160:256, :] = jnp.zeros((96, q_wide.shape[2]), BF16)


def causal():
    key_row = lax.broadcasted_iota(jnp.int32, (HALF, HALF), 0)
    query_col = lax.broadcasted_iota(jnp.int32, (HALF, HALF), 1)
    return key_row <= query_col


def fold(value, op):
    return op(value.reshape(HALF // 8, 8, value.shape[-1]), axis=0)


def forward_kernel(
    heads,
    place,
    q_t,
    latent,
    latent_t,
    rope_keys,
    latent_up,
    latent_up_t,
    joined_t,
    exact_t,
    lse,
    kcat,
    v_t,
    q_wide,
    scores,
    top,
    total,
    acc,
):
    load_heads(heads, latent, rope_keys, latent_up, q_t, kcat, q_wide)
    for h in range(heads):
        v_t[h] = matmul(latent_up_t[h * 128 + 64 : (h + 1) * 128, :], latent_t[...]).astype(BF16)
    factor = SCALE * LOG2E
    for block in range(2):
        cols = slice(block * HALF, (block + 1) * HALF)
        position = place[block]

        def score(j, masked):
            rows = pl.ds(pl.multiple_of(place[2 + j], HALF), HALF)
            spot = pl.ds(pl.multiple_of(j * HALF, HALF), HALF)
            for h in range(heads):
                s = matmul(kcat[h, rows, :], q_wide[h, :, cols])
                if masked:
                    s = jnp.where(causal(), s, -1e30)
                scores[h, spot, :] = s
                peak = fold(s, jnp.max)
                top[h] = peak if masked else jnp.maximum(top[h], peak)

        score(position, True)

        @pl.loop(0, position)
        def _(j):
            score(j, False)

        for h in range(heads):
            peak = jnp.max(top[h], axis=0, keepdims=True) * factor
            top[h] = jnp.broadcast_to(peak, (8, HALF))
            total[h] = jnp.zeros((8, HALF), F32)
            acc[h] = jnp.zeros((V_DIM, HALF), F32)

        @pl.loop(0, position + 1)
        def _(j):
            rows = pl.ds(pl.multiple_of(place[2 + j], HALF), HALF)
            spot = pl.ds(pl.multiple_of(j * HALF, HALF), HALF)
            for h in range(heads):
                p = jnp.exp2(scores[h, spot, :] * factor - top[h, 0:1, :])
                total[h] += fold(p, jnp.sum)
                acc[h] += matmul(v_t[h, :, rows], p.astype(BF16))

        for h in range(heads):
            summed = jnp.sum(total[h], axis=0, keepdims=True)
            out = acc[h] / summed
            joined_t[h * V_DIM : (h + 1) * V_DIM, cols] = out.astype(BF16)
            exact_t[h, :, cols] = out
            lse[h, :, cols] = top[h, 0:1, :] + jnp.log2(summed)


def backward_kernel(
    heads,
    place,
    q_t,
    latent,
    latent_t,
    rope_keys,
    rope_keys_t,
    latent_up,
    latent_up_t,
    exact_t,
    lse,
    dmix_t,
    cos_t,
    sin_t,
    dq_t,
    grad_up,
    dlat_t,
    kcat,
    k_t,
    q_wide,
    dmix_wide,
    delta,
    dk,
    dq,
    lat_acc,
    rope_acc,
):
    factor = SCALE * LOG2E
    step = pl.program_id(0)
    load_heads(heads, latent, rope_keys, latent_up, q_t, kcat, q_wide)
    for h in range(heads):
        k_t[h, 0:64, :] = matmul(latent_up_t[h * 128 : h * 128 + 64, :], latent_t[...]).astype(BF16)
        k_t[h, 64:96, :] = rope_keys_t[...]
        piece = dmix_t[h * V_DIM : (h + 1) * V_DIM, :]
        dmix_wide[h, 0:64, :] = jnp.zeros_like(piece)
        dmix_wide[h, 64:128, :] = piece
        delta[h] = jnp.sum(piece.astype(F32) * exact_t[h], axis=0, keepdims=True)
        dk[h] = jnp.zeros(dk.shape[1:], F32)

    for block in range(2):
        cols = slice(block * HALF, (block + 1) * HALF)
        position = place[block]

        def tile(j, masked):
            rows = pl.ds(pl.multiple_of(place[2 + j], HALF), HALF)
            for h in range(heads):
                s = matmul(kcat[h, rows, :], q_wide[h, :, cols])
                p = jnp.exp2(s * factor - lse[h, :, cols])
                if masked:
                    p = jnp.where(causal(), p, 0.0)
                dp = matmul(kcat[h, rows, :128], dmix_wide[h, :, cols])
                ds = (p * (dp - delta[h, :, cols])).astype(BF16)
                change = matmul(k_t[h, :, rows], ds)
                dq[h] = change if masked else dq[h] + change
                dk[h, rows, :] += times_transposed(ds, q_wide[h, :, cols])
                dk[h, rows, :128] += times_transposed(p.astype(BF16), dmix_wide[h, :, cols])

        tile(position, True)

        @pl.loop(0, position)
        def _(j):
            tile(j, False)

        cosine = cos_t[:, cols]
        sine = sin_t[:, cols]
        for h in range(heads):
            value = dq[h] * SCALE
            first = value[64:80]
            second = value[80:96]
            dq_t[h, 0:64, cols] = value[0:64].astype(BF16)
            dq_t[h, 64:80, cols] = (first * cosine + second * sine).astype(BF16)
            dq_t[h, 80:96, cols] = (second * cosine - first * sine).astype(BF16)

    @pl.when(step == 0)
    def _():
        lat_acc[...] = jnp.zeros_like(lat_acc)
        rope_acc[...] = jnp.zeros_like(rope_acc)

    lane = lax.broadcasted_iota(jnp.int32, (1, 128), 1)
    weight = jnp.where(lane < NOPE, SCALE, 1.0).astype(F32)
    for h in range(heads):
        pair = (dk[h, :, :128] * weight).astype(BF16)
        grad_up[:, h * 128 : (h + 1) * 128] = matmul(latent_t[...], pair).astype(BF16)
        lat_acc[...] += times_transposed(latent_up[:, h * 128 : (h + 1) * 128], pair)
        rope_acc[...] += dk[h, :, 128:]

    @pl.when(step == pl.num_programs(0) - 1)
    def _():
        dlat_t[0:KV_RANK, :] = lat_acc[...].astype(BF16)
        dlat_t[KV_RANK:, :] = (rope_acc[...] * SCALE).T[:ROPE].astype(BF16)


def whole_spec(shape):
    return pl.BlockSpec(shape, lambda g: (0,) * len(shape))


def attention_forward(place, q_t, latent, latent_t, rope_keys, latent_up, latent_up_t):
    count, _, rows = q_t.shape
    keys = latent.shape[0]
    heads = GROUP
    flops = 2 * count * rows * keys * 384
    return pl.pallas_call(
        functools.partial(forward_kernel, heads),
        grid=(count // heads,),
        in_specs=[
            pl.BlockSpec(memory_space=pltpu.SMEM),
            pl.BlockSpec((heads, 96, rows), lambda g: (g, 0, 0)),
            whole_spec((keys, KV_RANK)),
            whole_spec((KV_RANK, keys)),
            whole_spec((keys, 128)),
            pl.BlockSpec((KV_RANK, heads * 128), lambda g: (0, g)),
            pl.BlockSpec((heads * 128, KV_RANK), lambda g: (g, 0)),
        ],
        out_specs=[
            pl.BlockSpec((heads * V_DIM, rows), lambda g: (g, 0)),
            pl.BlockSpec((heads, V_DIM, rows), lambda g: (g, 0, 0)),
            pl.BlockSpec((heads, 1, rows), lambda g: (g, 0, 0)),
        ],
        out_shape=[
            jax.ShapeDtypeStruct((count * V_DIM, rows), BF16),
            jax.ShapeDtypeStruct((count, V_DIM, rows), F32),
            jax.ShapeDtypeStruct((count, 1, rows), F32),
        ],
        scratch_shapes=[
            pltpu.VMEM((heads, keys, 256), BF16),
            pltpu.VMEM((heads, V_DIM, keys), BF16),
            pltpu.VMEM((heads, 256, rows), BF16),
            pltpu.VMEM((heads, keys, HALF), F32),
            pltpu.VMEM((heads, 8, HALF), F32),
            pltpu.VMEM((heads, 8, HALF), F32),
            pltpu.VMEM((heads, V_DIM, HALF), F32),
        ],
        compiler_params=pltpu.CompilerParams(vmem_limit_bytes=56 * 1024 * 1024),
        cost_estimate=pl.CostEstimate(
            flops=flops, bytes_accessed=12 * 1024 * 1024, transcendentals=count * rows * keys
        ),
        name="attention_forward",
    )(place, q_t, latent, latent_t, rope_keys, latent_up, latent_up_t)


def attention_backward(
    place,
    q_t,
    latent,
    latent_t,
    rope_keys,
    rope_keys_t,
    latent_up,
    latent_up_t,
    exact_t,
    lse,
    dmix_t,
    cos_t,
    sin_t,
):
    count, _, rows = q_t.shape
    keys = latent.shape[0]
    heads = GROUP
    flops = 2 * count * rows * keys * 1000
    return pl.pallas_call(
        functools.partial(backward_kernel, heads),
        grid=(count // heads,),
        in_specs=[
            pl.BlockSpec(memory_space=pltpu.SMEM),
            pl.BlockSpec((heads, 96, rows), lambda g: (g, 0, 0)),
            whole_spec((keys, KV_RANK)),
            whole_spec((KV_RANK, keys)),
            whole_spec((keys, 128)),
            whole_spec((ROPE, keys)),
            pl.BlockSpec((KV_RANK, heads * 128), lambda g: (0, g)),
            pl.BlockSpec((heads * 128, KV_RANK), lambda g: (g, 0)),
            pl.BlockSpec((heads, V_DIM, rows), lambda g: (g, 0, 0)),
            pl.BlockSpec((heads, 1, rows), lambda g: (g, 0, 0)),
            pl.BlockSpec((heads * V_DIM, rows), lambda g: (g, 0)),
            whole_spec((ROPE // 2, rows)),
            whole_spec((ROPE // 2, rows)),
        ],
        out_specs=[
            pl.BlockSpec((heads, 96, rows), lambda g: (g, 0, 0)),
            pl.BlockSpec((KV_RANK, heads * 128), lambda g: (0, g)),
            whole_spec((KV_RANK + ROPE, keys)),
        ],
        out_shape=[
            jax.ShapeDtypeStruct((count, 96, rows), BF16),
            jax.ShapeDtypeStruct((KV_RANK, count * 128), BF16),
            jax.ShapeDtypeStruct((KV_RANK + ROPE, keys), BF16),
        ],
        scratch_shapes=[
            pltpu.VMEM((heads, keys, 256), BF16),
            pltpu.VMEM((heads, 96, keys), BF16),
            pltpu.VMEM((heads, 256, rows), BF16),
            pltpu.VMEM((heads, 128, rows), BF16),
            pltpu.VMEM((heads, 1, rows), F32),
            pltpu.VMEM((heads, keys, 256), F32),
            pltpu.VMEM((heads, 96, HALF), F32),
            pltpu.VMEM((KV_RANK, keys), F32),
            pltpu.VMEM((keys, 128), F32),
        ],
        compiler_params=pltpu.CompilerParams(vmem_limit_bytes=60 * 1024 * 1024),
        cost_estimate=pl.CostEstimate(
            flops=flops, bytes_accessed=16 * 1024 * 1024, transcendentals=count * rows * keys
        ),
        name="attention_backward",
    )(
        place,
        q_t,
        latent,
        latent_t,
        rope_keys,
        rope_keys_t,
        latent_up,
        latent_up_t,
        exact_t,
        lse,
        dmix_t,
        cos_t,
        sin_t,
    )


def swap(value, axis, size, bit):
    return lax.ppermute(value, axis, [(i, i ^ bit) for i in range(size)])


def shift(value, axis, size, by):
    return lax.ppermute(value, axis, [(i, (i + by) % size) for i in range(size)])


def tensor_sum(value, size):
    low = value.astype(BF16)
    bit = lax.axis_index("tensor") % 2
    half = low.shape[0] // 2
    keep = lax.dynamic_slice_in_dim(low, bit * half, half, 0)
    give = lax.dynamic_slice_in_dim(low, (1 - bit) * half, half, 0)
    mine = (keep.astype(F32) + swap(give, "tensor", size, 1).astype(F32)).astype(BF16)
    step = 2
    while step < size:
        mine = (mine.astype(F32) + swap(mine, "tensor", size, step).astype(F32)).astype(BF16)
        step *= 2
    other = swap(mine, "tensor", size, 1)
    first = jnp.where(bit == 0, mine, other)
    second = jnp.where(bit == 0, other, mine)
    return jnp.concatenate([first, second], axis=0).astype(F32)


def line_scatter(pieces, size):
    z = lax.axis_index("context")
    last = size - 1

    def take(index):
        return lax.dynamic_index_in_dim(pieces, index, 0, keepdims=False)

    right = left = None
    for step in range(1, size):
        up = take(jnp.clip(size + z - step, 0, last))
        down = take(jnp.clip(last - (size + (last - z) - step), 0, last))
        if right is not None:
            up = (up.astype(F32) + right.astype(F32)).astype(BF16)
            down = (down.astype(F32) + left.astype(F32)).astype(BF16)
        right = lax.ppermute(up, "context", [(i, i + 1) for i in range(step)])
        left = lax.ppermute(down, "context", [(last - i, last - i - 1) for i in range(step)])
    return take(z).astype(F32) + right.astype(F32) + left.astype(F32)


def direct_scatter(pieces, size):
    z = lax.axis_index("context")
    total = lax.dynamic_index_in_dim(pieces, z, 0, keepdims=False).astype(F32)
    for by in range(1, size):
        piece = lax.dynamic_index_in_dim(pieces, (z + by) % size, 0, keepdims=False)
        total = total + shift(piece, "context", size, by).astype(F32)
    return total


def pair_scatter(value):
    d = lax.axis_index("dp")
    keep = lax.dynamic_index_in_dim(value, d, 0, keepdims=False)
    give = lax.dynamic_index_in_dim(value, 1 - d, 0, keepdims=False)
    return (keep.astype(F32) + swap(give, "dp", 2, 1).astype(F32)).astype(BF16)


def tensor_gather(value, size):
    t = lax.axis_index("tensor")
    out = jnp.zeros((size,) + value.shape, value.dtype)
    out = lax.dynamic_update_index_in_dim(out, value, t, 0)
    for by in range(1, size):
        got = shift(value, "tensor", size, by)
        out = lax.dynamic_update_index_in_dim(out, got, (t - by) % size, 0)
    return out


def per_device(
    sizes,
    tokens,
    cotangent,
    group_order,
    attn_gain,
    query_down,
    query_gain,
    latent_down,
    latent_gain,
    query_up,
    latent_up,
    attn_out,
    mlp_gain,
    gate_proj,
    up_proj,
    down_proj,
):
    contexts, tensors = sizes
    rows, width = tokens.shape[1:]
    blocks = group_order.shape[0]
    heads = query_up.shape[1] // (NOPE + ROPE)
    z = lax.axis_index("context")
    d = lax.axis_index("dp")
    t = lax.axis_index("tensor")
    half_width = width // 2

    mine = lax.dynamic_slice_in_dim(group_order, 2 * z, 2)
    offsets = jnp.arange(HALF, dtype=jnp.int32)
    query_pos = (mine[:, None] * HALF + offsets[None, :]).reshape(rows)
    index = jnp.arange(blocks, dtype=jnp.int32)
    spot = ((z - index // 2) % contexts) * 2 * HALF + (index % 2) * HALF
    where = jnp.sum(
        jnp.where(group_order[None, :] == index[:, None], spot[None, :], 0), axis=1
    ).astype(jnp.int32)
    place = jnp.concatenate([mine, where])

    freq = 10000.0 ** (-2.0 * jnp.arange(ROPE // 2, dtype=F32) / ROPE)
    angle = query_pos.astype(F32)[:, None] * freq[None, :]
    cosine, sine = jnp.cos(angle), jnp.sin(angle)
    angle_t = freq[:, None] * query_pos.astype(F32)[None, :]
    cos_t, sin_t = jnp.cos(angle_t), jnp.sin(angle_t)

    inputs = tokens[0].astype(F32)
    upstream = cotangent[0].astype(F32)
    grad_feed = (RESIDUAL * upstream).astype(BF16)

    def own_half(value):
        return lax.dynamic_slice_in_dim(value, d * half_width, half_width, 1)

    def other_half(value):
        return lax.dynamic_slice_in_dim(value, (1 - d) * half_width, half_width, 1)

    grad_feed_both = jnp.concatenate(
        [own_half(grad_feed), swap(other_half(grad_feed), "dp", 2, 1)], axis=0
    )

    first_normed, first_inverse = scaled(inputs)
    hidden_one = (first_normed * attn_gain).astype(BF16)
    latent_raw = matmul(hidden_one, latent_down)
    cache_normed, cache_inverse = scaled(latent_raw[:, :KV_RANK])
    latent = (cache_normed * latent_gain).astype(BF16)
    key_rope = rotate(latent_raw[:, KV_RANK:], cosine, sine).astype(BF16)
    keys_own = jnp.concatenate([latent, key_rope], axis=1)
    bit = t % 2
    part = lax.dynamic_slice_in_dim(keys_own, bit * (rows // 2), rows // 2, 0)
    far = jnp.stack([shift(part, "context", contexts, by) for by in range(1, contexts)])
    far_other = swap(far, "tensor", tensors, 1)
    far_all = jnp.concatenate(
        [jnp.where(bit == 0, far, far_other), jnp.where(bit == 0, far_other, far)], axis=1
    )
    keys_all = jnp.concatenate([keys_own[None], far_all], axis=0).reshape(
        contexts * rows, KV_RANK + ROPE
    )
    latent_all = keys_all[:, :KV_RANK]
    rope_all = jnp.pad(keys_all[:, KV_RANK:], ((0, 0), (0, 128 - ROPE)))
    keys_all_t = keys_all.T
    latent_all_t = keys_all_t[:KV_RANK]
    rope_all_t = keys_all_t[KV_RANK:]
    latent_up_t = latent_up.T

    query_low = matmul(hidden_one, query_down)
    query_normed, query_inverse = scaled(query_low)
    query_latent = (query_normed * query_gain).astype(BF16)
    query_full_t = lax.dot_general(
        query_up, query_latent, (((0,), (1,)), ((), ())), preferred_element_type=F32
    ).reshape(heads, NOPE + ROPE, rows)
    first = query_full_t[:, 64:80]
    second = query_full_t[:, 80:96]
    q_t = jnp.concatenate(
        [
            query_full_t[:, :64],
            first * cos_t - second * sin_t,
            second * cos_t + first * sin_t,
        ],
        axis=1,
    ).astype(BF16)

    joined_t, exact_t, lse = attention_forward(
        place, q_t, latent_all, latent_all_t, rope_all, latent_up, latent_up_t
    )

    branch = tensor_sum(transposed_times(joined_t, attn_out), tensors)
    middle = inputs + RESIDUAL * branch
    second_normed, second_inverse = scaled(middle)
    hidden_two = (second_normed * mlp_gain).astype(BF16)
    hidden_two_both = jnp.concatenate(
        [own_half(hidden_two), swap(other_half(hidden_two), "dp", 2, 1)], axis=0
    )
    grad_hidden = times_transposed(grad_feed, down_proj)
    gate = matmul(hidden_two, gate_proj)
    upper = matmul(hidden_two, up_proj)
    sigma = jax.nn.sigmoid(gate)
    hidden_mid = (gate * sigma * upper).astype(BF16)
    grad_gate = (grad_hidden * upper * sigma * (1.0 + gate * (1.0 - sigma))).astype(BF16)
    grad_upper = (grad_hidden * gate * sigma).astype(BF16)

    def both(value):
        return jnp.concatenate([value, swap(value, "dp", 2, 1)], axis=0)

    def weight_pieces(left, right):
        full = transposed_times(left, right).astype(BF16)
        return full.reshape(contexts, half_width // contexts, right.shape[1])

    grad_hidden_two = tensor_sum(
        times_transposed(grad_gate, gate_proj) + times_transposed(grad_upper, up_proj), tensors
    )
    feed = tensor_sum(matmul(hidden_mid, down_proj), tensors)
    layer_out = (middle + RESIDUAL * feed).astype(BF16)

    grad_down = line_scatter(weight_pieces(grad_feed_both, both(hidden_mid)), contexts).T
    grad_gate_proj = line_scatter(weight_pieces(hidden_two_both, both(grad_gate)), contexts)
    grad_up_proj = line_scatter(weight_pieces(hidden_two_both, both(grad_upper)), contexts)

    grad_norm_two, grad_mlp_gain = norm_back(
        grad_hidden_two, second_normed, second_inverse, mlp_gain
    )
    grad_middle = upstream + grad_norm_two
    grad_branch = (RESIDUAL * grad_middle).astype(BF16)
    grad_attn_out_t = lax.dot_general(
        grad_branch, joined_t, (((0,), (1,)), ((), ())), preferred_element_type=F32
    ).astype(BF16)
    grad_attn_out = line_scatter(
        pair_scatter(
            grad_attn_out_t.reshape(2, contexts, half_width // contexts, joined_t.shape[0])
        ),
        contexts,
    ).T
    dmix_t = times_transposed(attn_out, grad_branch).astype(BF16)

    dq_t, grad_latent_up, dlat_t = attention_backward(
        place,
        q_t,
        latent_all,
        latent_all_t,
        rope_all,
        rope_all_t,
        latent_up,
        latent_up_t,
        exact_t,
        lse,
        dmix_t,
        cos_t,
        sin_t,
    )
    grad_query_full_t = dq_t.reshape(heads * (NOPE + ROPE), rows)
    grad_query_latent = tensor_sum(
        lax.dot_general(
            grad_query_full_t, query_up, (((0,), (1,)), ((), ())), preferred_element_type=F32
        ),
        tensors,
    )
    grad_query_up = lax.dot_general(
        query_latent, grad_query_full_t, (((0,), (1,)), ((), ())), preferred_element_type=F32
    ).astype(BF16)

    dlat = tensor_sum(dlat_t, tensors).astype(BF16)
    total = dlat[:, :rows].astype(F32)
    for by in range(1, contexts):
        total = total + shift(dlat[:, by * rows : (by + 1) * rows], "context", contexts, -by).astype(
            F32
        )
    grad_keys = total.T
    grad_query_low, grad_query_gain = norm_back(
        grad_query_latent, query_normed, query_inverse, query_gain
    )
    grad_cache, grad_latent_gain = norm_back(
        grad_keys[:, :KV_RANK], cache_normed, cache_inverse, latent_gain
    )
    grad_low = jnp.concatenate(
        [grad_query_low, grad_cache, unrotate(grad_keys[:, KV_RANK:], cosine, sine)], axis=1
    ).astype(BF16)
    rank = query_down.shape[1]
    grad_hidden_one = times_transposed(grad_low[:, :rank], query_down) + times_transposed(
        grad_low[:, rank:], latent_down
    )
    grad_norm_one, grad_attn_gain = norm_back(
        grad_hidden_one, first_normed, first_inverse, attn_gain
    )
    token_grad = grad_middle + grad_norm_one

    grad_query_up = direct_scatter(
        pair_scatter(grad_query_up.reshape(2, contexts, -1, grad_query_up.shape[1])), contexts
    )
    grad_latent_up = direct_scatter(
        pair_scatter(grad_latent_up.reshape(2, contexts, -1, grad_latent_up.shape[1])), contexts
    )
    grad_down_low = transposed_times(hidden_one, grad_low).astype(BF16)
    grad_down_low = grad_down_low.reshape(2, contexts, tensors, -1, grad_low.shape[1])
    grad_down_low = lax.dynamic_index_in_dim(grad_down_low, t, 2, keepdims=False)
    grad_down_low = direct_scatter(pair_scatter(grad_down_low), contexts).astype(BF16)
    grad_down_low = (
        tensor_gather(grad_down_low, tensors).reshape(-1, grad_low.shape[1]).astype(F32)
    )

    def pieces(value):
        return value.reshape(2 * contexts, -1)

    gains = jnp.concatenate(
        [
            pieces(grad_attn_gain),
            pieces(grad_query_gain),
            pieces(grad_latent_gain),
            pieces(grad_mlp_gain),
        ],
        axis=1,
    )
    gains = lax.dynamic_index_in_dim(
        lax.psum(gains, ("dp", "context")), d * contexts + z, 0, keepdims=False
    )
    sizes = [v.shape[0] // (2 * contexts) for v in (attn_gain, query_gain, latent_gain, mlp_gain)]
    edges = [0]
    for size in sizes:
        edges.append(edges[-1] + size)
    gain_grads = [gains[a:b] for a, b in zip(edges[:-1], edges[1:])]

    return (
        layer_out[None],
        token_grad[None],
        gain_grads[0],
        grad_down_low[:, :rank],
        gain_grads[1],
        grad_down_low[:, rank:],
        gain_grads[2],
        grad_query_up,
        grad_latent_up,
        grad_attn_out,
        gain_grads[3],
        grad_gate_proj,
        grad_up_proj,
        grad_down,
    )


def solution(mesh):
    in_specs = (
        P("dp", "context", None),
        P("dp", "context", None),
        P(),
        P(),
        P(),
        P(),
        P(),
        P(),
        P(None, "tensor"),
        P(None, "tensor"),
        P("tensor", None),
        P(),
        P(None, "tensor"),
        P(None, "tensor"),
        P("tensor", None),
    )
    out_specs = (
        P("dp", "context", None),
        P("dp", "context", None),
        P(("dp", "context")),
        P(("dp", "context"), None),
        P(("dp", "context")),
        P(("dp", "context"), None),
        P(("dp", "context")),
        P(("dp", "context"), "tensor"),
        P(("dp", "context"), "tensor"),
        P("tensor", ("dp", "context")),
        P(("dp", "context")),
        P(("dp", "context"), "tensor"),
        P(("dp", "context"), "tensor"),
        P("tensor", ("dp", "context")),
    )
    sizes = (mesh.shape["context"], mesh.shape["tensor"])
    return jax.shard_map(
        functools.partial(per_device, sizes),
        mesh=mesh,
        in_specs=in_specs,
        out_specs=out_specs,
        check_vma=False,
    )
```

```python
import functools
import math

import jax
import jax.numpy as jnp
from jax import lax
from jax.experimental import pallas as pl
from jax.experimental.pallas import tpu as pltpu
from jax.sharding import PartitionSpec as P

NOPE = 64
ROPE = 32
V_DIM = 64
KV_RANK = 256
HALF = 256
GROUP = 5
CHUNK = 256

EPS = 1e-05
RESIDUAL = 1.4 / math.sqrt(62.0)
SCALE = 1.0 / math.sqrt(NOPE + ROPE)
LOG2E = 1.0 / math.log(2.0)
F32 = jnp.float32
BF16 = jnp.bfloat16


def matmul(left, right):
    return jnp.dot(left, right, preferred_element_type=F32)


def times_transposed(left, right):
    return lax.dot_general(left, right, (((1,), (1,)), ((), ())), preferred_element_type=F32)


def transposed_times(left, right):
    return lax.dot_general(left, right, (((0,), (0,)), ((), ())), preferred_element_type=F32)


def scaled(value):
    inverse = lax.rsqrt(jnp.mean(value * value, axis=-1, keepdims=True) + EPS)
    return (value * inverse, inverse)


def norm_back(incoming, normed, inverse, gain):
    weighted = incoming * gain
    grad_gain = jnp.sum(incoming * normed, axis=0)
    grad_value = inverse * (weighted - normed * jnp.mean(weighted * normed, axis=-1, keepdims=True))
    return (grad_value, grad_gain)


def rotate(value, cosine, sine):
    count = value.shape[-1] // 2
    first = value[..., :count]
    second = value[..., count:]
    return jnp.concatenate(
        [first * cosine - second * sine, second * cosine + first * sine], axis=-1
    )


def unrotate(value, cosine, sine):
    count = value.shape[-1] // 2
    first = value[..., :count]
    second = value[..., count:]
    return jnp.concatenate(
        [first * cosine + second * sine, second * cosine - first * sine], axis=-1
    )


def load_heads(heads, latent, rope_keys, latent_up, q_t, kcat, q_wide):
    for h in range(heads):
        kcat[h, :, :128] = matmul(latent[...], latent_up[:, h * 128 : (h + 1) * 128]).astype(BF16)
        kcat[h, :, 128:] = rope_keys[...]
        q_wide[h, 0:64, :] = q_t[h, 0:64, :]
        q_wide[h, 64:128, :] = jnp.zeros((64, q_wide.shape[2]), BF16)
        q_wide[h, 128:160, :] = q_t[h, 64:96, :]
        q_wide[h, 160:256, :] = jnp.zeros((96, q_wide.shape[2]), BF16)


def causal():
    key_row = lax.broadcasted_iota(jnp.int32, (HALF, HALF), 0)
    query_col = lax.broadcasted_iota(jnp.int32, (HALF, HALF), 1)
    return key_row <= query_col


def fold(value, op):
    return op(value.reshape(HALF // 8, 8, value.shape[-1]), axis=0)


def forward_kernel(
    heads,
    place,
    q_t,
    latent,
    latent_t,
    rope_keys,
    latent_up,
    latent_up_t,
    joined_t,
    exact_t,
    lse,
    kcat,
    v_t,
    q_wide,
    scores,
    top,
    total,
    acc,
):
    load_heads(heads, latent, rope_keys, latent_up, q_t, kcat, q_wide)
    for h in range(heads):
        v_t[h] = matmul(latent_up_t[h * 128 + 64 : (h + 1) * 128, :], latent_t[...]).astype(BF16)
    factor = SCALE * LOG2E
    for block in range(2):
        cols = slice(block * HALF, (block + 1) * HALF)
        position = place[block]

        def score(j, masked):
            rows = pl.ds(pl.multiple_of(place[2 + j], HALF), HALF)
            spot = pl.ds(pl.multiple_of(j * HALF, HALF), HALF)
            for h in range(heads):
                s = matmul(kcat[h, rows, :], q_wide[h, :, cols])
                if masked:
                    s = jnp.where(causal(), s, -1e30)
                scores[h, spot, :] = s
                peak = fold(s, jnp.max)
                top[h] = peak if masked else jnp.maximum(top[h], peak)

        score(position, True)

        @pl.loop(0, position)
        def _(j):
            score(j, False)

        for h in range(heads):
            peak = jnp.max(top[h], axis=0, keepdims=True) * factor
            top[h] = jnp.broadcast_to(peak, (8, HALF))
            total[h] = jnp.zeros((8, HALF), F32)
            acc[h] = jnp.zeros((V_DIM, HALF), F32)

        @pl.loop(0, position + 1)
        def _(j):
            rows = pl.ds(pl.multiple_of(place[2 + j], HALF), HALF)
            spot = pl.ds(pl.multiple_of(j * HALF, HALF), HALF)
            for h in range(heads):
                p = jnp.exp2(scores[h, spot, :] * factor - top[h, 0:1, :])
                total[h] += fold(p, jnp.sum)
                acc[h] += matmul(v_t[h, :, rows], p.astype(BF16))

        for h in range(heads):
            summed = jnp.sum(total[h], axis=0, keepdims=True)
            out = acc[h] / summed
            joined_t[h * V_DIM : (h + 1) * V_DIM, cols] = out.astype(BF16)
            exact_t[h, :, cols] = out
            lse[h, :, cols] = top[h, 0:1, :] + jnp.log2(summed)


def backward_kernel(
    heads,
    place,
    q_t,
    latent,
    latent_t,
    rope_keys,
    rope_keys_t,
    latent_up,
    latent_up_t,
    exact_t,
    lse,
    dmix_t,
    cos_t,
    sin_t,
    dq_t,
    grad_up,
    dlat_t,
    kcat,
    k_t,
    q_wide,
    dmix_wide,
    delta,
    dk,
    dq,
    lat_acc,
    rope_acc,
):
    factor = SCALE * LOG2E
    step = pl.program_id(0)
    load_heads(heads, latent, rope_keys, latent_up, q_t, kcat, q_wide)
    for h in range(heads):
        k_t[h, 0:64, :] = matmul(latent_up_t[h * 128 : h * 128 + 64, :], latent_t[...]).astype(BF16)
        k_t[h, 64:96, :] = rope_keys_t[...]
        piece = dmix_t[h * V_DIM : (h + 1) * V_DIM, :]
        dmix_wide[h, 0:64, :] = jnp.zeros_like(piece)
        dmix_wide[h, 64:128, :] = piece
        delta[h] = jnp.sum(piece.astype(F32) * exact_t[h], axis=0, keepdims=True)
        dk[h] = jnp.zeros(dk.shape[1:], F32)

    for block in range(2):
        cols = slice(block * HALF, (block + 1) * HALF)
        position = place[block]

        def tile(j, masked):
            rows = pl.ds(pl.multiple_of(place[2 + j], HALF), HALF)
            for h in range(heads):
                s = matmul(kcat[h, rows, :], q_wide[h, :, cols])
                p = jnp.exp2(s * factor - lse[h, :, cols])
                if masked:
                    p = jnp.where(causal(), p, 0.0)
                dp = matmul(kcat[h, rows, :128], dmix_wide[h, :, cols])
                ds = (p * (dp - delta[h, :, cols])).astype(BF16)
                change = matmul(k_t[h, :, rows], ds)
                dq[h] = change if masked else dq[h] + change
                dk[h, rows, :] += times_transposed(ds, q_wide[h, :, cols])
                dk[h, rows, :128] += times_transposed(p.astype(BF16), dmix_wide[h, :, cols])

        tile(position, True)

        @pl.loop(0, position)
        def _(j):
            tile(j, False)

        cosine = cos_t[:, cols]
        sine = sin_t[:, cols]
        for h in range(heads):
            value = dq[h] * SCALE
            first = value[64:80]
            second = value[80:96]
            dq_t[h, 0:64, cols] = value[0:64].astype(BF16)
            dq_t[h, 64:80, cols] = (first * cosine + second * sine).astype(BF16)
            dq_t[h, 80:96, cols] = (second * cosine - first * sine).astype(BF16)

    @pl.when(step == 0)
    def _():
        lat_acc[...] = jnp.zeros_like(lat_acc)
        rope_acc[...] = jnp.zeros_like(rope_acc)

    lane = lax.broadcasted_iota(jnp.int32, (1, 128), 1)
    weight = jnp.where(lane < NOPE, SCALE, 1.0).astype(F32)
    for h in range(heads):
        pair = (dk[h, :, :128] * weight).astype(BF16)
        grad_up[:, h * 128 : (h + 1) * 128] = matmul(latent_t[...], pair).astype(BF16)
        lat_acc[...] += times_transposed(latent_up[:, h * 128 : (h + 1) * 128], pair)
        rope_acc[...] += dk[h, :, 128:]

    @pl.when(step == pl.num_programs(0) - 1)
    def _():
        dlat_t[0:KV_RANK, :] = lat_acc[...].astype(BF16)
        dlat_t[KV_RANK:, :] = (rope_acc[...] * SCALE).T[:ROPE].astype(BF16)


def whole_spec(shape):
    return pl.BlockSpec(shape, lambda g: (0,) * len(shape))


def attention_forward(place, q_t, latent, latent_t, rope_keys, latent_up, latent_up_t):
    count, _, rows = q_t.shape
    keys = latent.shape[0]
    heads = GROUP
    flops = 2 * count * rows * keys * 384
    return pl.pallas_call(
        functools.partial(forward_kernel, heads),
        grid=(count // heads,),
        in_specs=[
            pl.BlockSpec(memory_space=pltpu.SMEM),
            pl.BlockSpec((heads, 96, rows), lambda g: (g, 0, 0)),
            whole_spec((keys, KV_RANK)),
            whole_spec((KV_RANK, keys)),
            whole_spec((keys, 128)),
            pl.BlockSpec((KV_RANK, heads * 128), lambda g: (0, g)),
            pl.BlockSpec((heads * 128, KV_RANK), lambda g: (g, 0)),
        ],
        out_specs=[
            pl.BlockSpec((heads * V_DIM, rows), lambda g: (g, 0)),
            pl.BlockSpec((heads, V_DIM, rows), lambda g: (g, 0, 0)),
            pl.BlockSpec((heads, 1, rows), lambda g: (g, 0, 0)),
        ],
        out_shape=[
            jax.ShapeDtypeStruct((count * V_DIM, rows), BF16),
            jax.ShapeDtypeStruct((count, V_DIM, rows), F32),
            jax.ShapeDtypeStruct((count, 1, rows), F32),
        ],
        scratch_shapes=[
            pltpu.VMEM((heads, keys, 256), BF16),
            pltpu.VMEM((heads, V_DIM, keys), BF16),
            pltpu.VMEM((heads, 256, rows), BF16),
            pltpu.VMEM((heads, keys, HALF), F32),
            pltpu.VMEM((heads, 8, HALF), F32),
            pltpu.VMEM((heads, 8, HALF), F32),
            pltpu.VMEM((heads, V_DIM, HALF), F32),
        ],
        compiler_params=pltpu.CompilerParams(vmem_limit_bytes=56 * 1024 * 1024),
        cost_estimate=pl.CostEstimate(
            flops=flops, bytes_accessed=12 * 1024 * 1024, transcendentals=count * rows * keys
        ),
        name="attention_forward",
    )(place, q_t, latent, latent_t, rope_keys, latent_up, latent_up_t)


def attention_backward(
    place,
    q_t,
    latent,
    latent_t,
    rope_keys,
    rope_keys_t,
    latent_up,
    latent_up_t,
    exact_t,
    lse,
    dmix_t,
    cos_t,
    sin_t,
):
    count, _, rows = q_t.shape
    keys = latent.shape[0]
    heads = GROUP
    flops = 2 * count * rows * keys * 1000
    return pl.pallas_call(
        functools.partial(backward_kernel, heads),
        grid=(count // heads,),
        in_specs=[
            pl.BlockSpec(memory_space=pltpu.SMEM),
            pl.BlockSpec((heads, 96, rows), lambda g: (g, 0, 0)),
            whole_spec((keys, KV_RANK)),
            whole_spec((KV_RANK, keys)),
            whole_spec((keys, 128)),
            whole_spec((ROPE, keys)),
            pl.BlockSpec((KV_RANK, heads * 128), lambda g: (0, g)),
            pl.BlockSpec((heads * 128, KV_RANK), lambda g: (g, 0)),
            pl.BlockSpec((heads, V_DIM, rows), lambda g: (g, 0, 0)),
            pl.BlockSpec((heads, 1, rows), lambda g: (g, 0, 0)),
            pl.BlockSpec((heads * V_DIM, rows), lambda g: (g, 0)),
            whole_spec((ROPE // 2, rows)),
            whole_spec((ROPE // 2, rows)),
        ],
        out_specs=[
            pl.BlockSpec((heads, 96, rows), lambda g: (g, 0, 0)),
            pl.BlockSpec((KV_RANK, heads * 128), lambda g: (0, g)),
            whole_spec((KV_RANK + ROPE, keys)),
        ],
        out_shape=[
            jax.ShapeDtypeStruct((count, 96, rows), BF16),
            jax.ShapeDtypeStruct((KV_RANK, count * 128), BF16),
            jax.ShapeDtypeStruct((KV_RANK + ROPE, keys), BF16),
        ],
        scratch_shapes=[
            pltpu.VMEM((heads, keys, 256), BF16),
            pltpu.VMEM((heads, 96, keys), BF16),
            pltpu.VMEM((heads, 256, rows), BF16),
            pltpu.VMEM((heads, 128, rows), BF16),
            pltpu.VMEM((heads, 1, rows), F32),
            pltpu.VMEM((heads, keys, 256), F32),
            pltpu.VMEM((heads, 96, HALF), F32),
            pltpu.VMEM((KV_RANK, keys), F32),
            pltpu.VMEM((keys, 128), F32),
        ],
        compiler_params=pltpu.CompilerParams(vmem_limit_bytes=60 * 1024 * 1024),
        cost_estimate=pl.CostEstimate(
            flops=flops, bytes_accessed=16 * 1024 * 1024, transcendentals=count * rows * keys
        ),
        name="attention_backward",
    )(
        place,
        q_t,
        latent,
        latent_t,
        rope_keys,
        rope_keys_t,
        latent_up,
        latent_up_t,
        exact_t,
        lse,
        dmix_t,
        cos_t,
        sin_t,
    )


MESH = pl.DeviceIdType.MESH


def cuts(size, step=512):
    count = max(1, size // step)
    edges = [i * step for i in range(count)] + [size]
    return list(zip(edges[:-1], edges[1:]))


def feed_forward_kernel(
    tensors,
    joined_t,
    tokens,
    cotangent,
    gain,
    attn_out_h,
    down_h,
    gate_h,
    up_h,
    branch_o,
    two_o,
    hidden_o,
    dgate_o,
    dup_o,
    feed_o,
    dmiddle_o,
    dmix_t,
    gain_o,
    attn_out,
    down,
    gate_w,
    up_w,
    part,
    final,
    near,
    across,
    dhid,
    two,
    trio,
    feed,
    dmiddle,
    load_sem,
    save_sem,
    send_sem,
    recv_sem,
):
    rows, width = tokens.shape
    half = width // 2
    t = lax.axis_index("tensor")
    bit = lax.rem(t, 2)
    pair = t + 1 - 2 * bit
    others = [pair]
    step = 2
    while step < tensors:
        others.append(t + step - 2 * step * lax.rem(t // step, 2))
        step *= 2

    loads = [
        pltpu.make_async_copy(src, dst, load_sem.at[i])
        for i, (src, dst) in enumerate(
            [(attn_out_h, attn_out), (down_h, down), (gate_h, gate_w), (up_h, up_w)]
        )
    ]
    for load in loads:
        load.start()

    barrier = pltpu.get_barrier_semaphore()
    for other in others:
        pl.semaphore_signal(barrier, inc=1, device_id={"tensor": other}, device_id_type=MESH)
    pl.semaphore_wait(barrier, len(others))

    def send(src, dst, job, kind, c, device):
        return pltpu.make_async_remote_copy(
            src_ref=src,
            dst_ref=dst,
            send_sem=send_sem.at[job, kind, c],
            recv_sem=recv_sem.at[job, kind, c],
            device_id={"tensor": device},
            device_id_type=MESH,
        )

    def span(c):
        return pl.ds(c * CHUNK, CHUNK)

    last = len(others)

    def hop(job, c, kind):
        if kind == 0:
            return send(
                part.at[1 - bit, span(c)], near.at[job, span(c)], job, 0, c, pair
            )
        if kind == last:
            here = final.at[job, bit, span(c)]
            return send(here, here, job, last, c, pair)
        src = near if kind == 1 else across.at[kind - 2]
        return send(
            src.at[job, span(c)], across.at[kind - 1, job, span(c)], job, kind, c, others[kind]
        )

    def reduce_pair(job, c):
        hop(job, c, 0).wait_recv()

        @pl.loop(0, CHUNK // 32)
        def _(i):
            r = pl.ds(pl.multiple_of(c * CHUNK + i * 32, 32), 32)
            near[job, r, :] = (
                near[job, r, :].astype(F32) + part[bit, r, :].astype(F32)
            ).astype(BF16)

        hop(job, c, 1).start()

    def reduce_across(job, c):
        for kind in range(1, last):
            hop(job, c, kind).wait_recv()
            src = near if kind == 1 else across.at[kind - 2]
            ending = kind == last - 1

            @pl.loop(0, CHUNK // 32)
            def _(i):
                r = pl.ds(pl.multiple_of(c * CHUNK + i * 32, 32), 32)
                value = (
                    src[job, r, :].astype(F32) + across[kind - 1, job, r, :].astype(F32)
                ).astype(BF16)
                if ending:
                    final[job, bit, r, :] = value
                else:
                    across[kind - 1, job, r, :] = value

            hop(job, c, kind + 1).start()
        hop(job, c, last).wait_recv()

    def middle_rows(r):
        parts = []
        for h in range(2):
            cols = slice(h * half, (h + 1) * half)
            parts.append(
                tokens[r, cols].astype(F32) + RESIDUAL * final[0, h, r, :].astype(F32)
            )
        square = sum(jnp.sum(p * p, axis=-1, keepdims=True) for p in parts)
        inverse = lax.rsqrt(square * (1.0 / width) + EPS)
        return parts, inverse

    chunks = rows // CHUNK
    loads[0].wait()
    for c in range(chunks):
        left = joined_t[:, c * CHUNK : (c + 1) * CHUNK]

        @pl.loop(0, width // 256)
        def _(n):
            cols = pl.ds(pl.multiple_of(n * 256, 256), 256)
            side = n // (half // 256)
            place = pl.ds(pl.multiple_of(lax.rem(n, half // 256) * 256, 256), 256)
            part[side, span(c), place] = transposed_times(left, attn_out[:, cols]).astype(BF16)

        hop(0, c, 0).start()
    for c in range(chunks):
        reduce_pair(0, c)

    loads[1].wait()
    for c in range(chunks):

        @pl.loop(0, CHUNK // 32)
        def _(i):
            r = pl.ds(pl.multiple_of(c * CHUNK + i * 32, 32), 32)
            o = pl.ds(pl.multiple_of(i * 32, 32), 32)
            two[o, :] = (RESIDUAL * cotangent[r, :].astype(F32)).astype(BF16)

        for a, b in cuts(down.shape[0]):
            dhid[span(c), a:b] = times_transposed(two[...], down[a:b, :]).astype(BF16)

    loads[2].wait()
    loads[3].wait()
    saves = []

    def save(src, dst):
        copy = pltpu.make_async_copy(src, dst, save_sem.at[len(saves)])
        copy.start()
        saves.append(copy)
        return copy

    two_saved = None
    for c in range(chunks):
        reduce_across(0, c)
        if two_saved is not None:
            two_saved.wait()

        @pl.loop(0, CHUNK // 32)
        def _(i):
            r = pl.ds(pl.multiple_of(c * CHUNK + i * 32, 32), 32)
            o = pl.ds(pl.multiple_of(i * 32, 32), 32)
            parts, inverse = middle_rows(r)
            for h in range(2):
                cols = slice(h * half, (h + 1) * half)
                two[o, cols] = (parts[h] * inverse * gain[:, cols]).astype(BF16)

        two_saved = save(two, two_o.at[span(c)])
        for a, b in cuts(gate_w.shape[0]):
            gate = times_transposed(two[...], gate_w[a:b, :])
            upper = times_transposed(two[...], up_w[a:b, :])
            grad = dhid[span(c), a:b].astype(F32)
            sigma = 1.0 / (1.0 + jnp.exp(-gate))
            act = gate * sigma
            trio[0, span(c), a:b] = (act * upper).astype(BF16)
            trio[1, span(c), a:b] = (
                grad * upper * sigma * (1.0 + gate * (1.0 - sigma))
            ).astype(BF16)
            trio[2, span(c), a:b] = (grad * act).astype(BF16)
        for k, out in enumerate((hidden_o, dgate_o, dup_o)):
            save(trio.at[k, span(c)], out.at[span(c)])
        hop(0, c, 0).wait_send()

        @pl.loop(0, width // 256)
        def _(n):
            cols = pl.ds(pl.multiple_of(n * 256, 256), 256)
            side = n // (half // 256)
            place = pl.ds(pl.multiple_of(lax.rem(n, half // 256) * 256, 256), 256)
            value = matmul(trio[1, span(c), :], gate_w[:, cols])
            value += matmul(trio[2, span(c), :], up_w[:, cols])
            part[side, span(c), place] = value.astype(BF16)

        hop(1, c, 0).start()
        if c > 0:
            reduce_pair(1, c - 1)
    reduce_pair(1, chunks - 1)
    two_saved.wait()

    gain_o[...] = jnp.zeros_like(gain_o)
    feed_saved = dmiddle_saved = None
    for c in range(chunks):
        if feed_saved is not None:
            feed_saved.wait()

        @pl.loop(0, width // 256)
        def _(n):
            cols = pl.ds(pl.multiple_of(n * 256, 256), 256)
            feed[:, cols] = matmul(trio[0, span(c), :], down[:, cols]).astype(BF16)

        feed_saved = save(feed, feed_o.at[span(c)])
        reduce_across(1, c)
        if dmiddle_saved is not None:
            dmiddle_saved.wait()

        @pl.loop(0, CHUNK // 32)
        def _(i):
            r = pl.ds(pl.multiple_of(c * CHUNK + i * 32, 32), 32)
            o = pl.ds(pl.multiple_of(i * 32, 32), 32)
            parts, inverse = middle_rows(r)
            dot = jnp.zeros((32, 1), F32)
            for h in range(2):
                cols = slice(h * half, (h + 1) * half)
                product = final[1, h, r, :].astype(F32) * (parts[h] * inverse)
                gain_o[:, cols] += jnp.sum(product.reshape(4, 8, half), axis=0)
                dot += jnp.sum(product * gain[:, cols], axis=-1, keepdims=True)
            dot = dot * (1.0 / width)
            for h in range(2):
                cols = slice(h * half, (h + 1) * half)
                weighted = final[1, h, r, :].astype(F32) * gain[:, cols]
                value = cotangent[r, cols].astype(F32) + inverse * (
                    weighted - parts[h] * inverse * dot
                )
                dmiddle[o, cols] = value
                two[o, cols] = (RESIDUAL * value).astype(BF16)

        dmiddle_saved = save(dmiddle, dmiddle_o.at[span(c)])
        dmix_t[:, c * CHUNK : (c + 1) * CHUNK] = times_transposed(attn_out[...], two[...]).astype(
            BF16
        )
    for h in range(2):
        save(final.at[0, h], branch_o.at[h])
    for copy in saves[-2:] + [feed_saved, dmiddle_saved]:
        copy.wait()
    for c in range(chunks):
        for k in range(3):
            saves[c * 4 + 1 + k].wait()
    for job in range(2):
        for c in range(chunks):
            for kind in range(1 - job, last + 1):
                hop(job, c, kind).wait_send()


def feed_forward(tensors, joined_t, tokens, cotangent, gain, attn_out, down, gate_w, up_w):
    rows, width = tokens.shape
    units = down.shape[0]
    chunks = rows // CHUNK
    hops = tensors.bit_length() - 1
    anywhere = pl.BlockSpec(memory_space=pl.ANY)
    inside = pl.BlockSpec(memory_space=pltpu.VMEM)
    return pl.pallas_call(
        functools.partial(feed_forward_kernel, tensors),
        in_specs=[inside] * 4 + [anywhere] * 4,
        out_specs=[anywhere] * 7 + [inside] * 2,
        out_shape=[
            jax.ShapeDtypeStruct((2, rows, width // 2), BF16),
            jax.ShapeDtypeStruct((rows, width), BF16),
            jax.ShapeDtypeStruct((rows, units), BF16),
            jax.ShapeDtypeStruct((rows, units), BF16),
            jax.ShapeDtypeStruct((rows, units), BF16),
            jax.ShapeDtypeStruct((rows, width), BF16),
            jax.ShapeDtypeStruct((rows, width), F32),
            jax.ShapeDtypeStruct((joined_t.shape[0], rows), BF16),
            jax.ShapeDtypeStruct((8, width), F32),
        ],
        scratch_shapes=[
            pltpu.VMEM(attn_out.shape, BF16),
            pltpu.VMEM(down.shape, BF16),
            pltpu.VMEM(gate_w.shape, BF16),
            pltpu.VMEM(up_w.shape, BF16),
            pltpu.VMEM((2, rows, width // 2), BF16),
            pltpu.VMEM((2, 2, rows, width // 2), BF16),
            pltpu.VMEM((2, rows, width // 2), BF16),
            pltpu.VMEM((hops - 1, 2, rows, width // 2), BF16),
            pltpu.VMEM((rows, units), BF16),
            pltpu.VMEM((CHUNK, width), BF16),
            pltpu.VMEM((3, rows, units), BF16),
            pltpu.VMEM((CHUNK, width), BF16),
            pltpu.VMEM((CHUNK, width), F32),
            pltpu.SemaphoreType.DMA((4,)),
            pltpu.SemaphoreType.DMA((6 * chunks + 2,)),
            pltpu.SemaphoreType.DMA((2, hops + 1, chunks)),
            pltpu.SemaphoreType.DMA((2, hops + 1, chunks)),
        ],
        compiler_params=pltpu.CompilerParams(
            collective_id=0, has_side_effects=True, vmem_limit_bytes=63 * 1024 * 1024
        ),
        cost_estimate=pl.CostEstimate(
            flops=2 * rows * width * units * 6, bytes_accessed=60 * 1024 * 1024, transcendentals=0
        ),
        name="feed_forward",
    )(joined_t, tokens, cotangent, gain, attn_out, down, gate_w, up_w)


def after(value, *others):
    return lax.optimization_barrier((value, others))[0]


def swap(value, axis, size, bit):
    return lax.ppermute(value, axis, [(i, i ^ bit) for i in range(size)])


def shift(value, axis, size, by):
    return lax.ppermute(value, axis, [(i, (i + by) % size) for i in range(size)])


def add_low(left, right):
    return (left.astype(F32) + right.astype(F32)).astype(BF16)


def pick(value, index):
    return lax.dynamic_index_in_dim(value, index, 0, keepdims=False)


def tensor_halves(value, size):
    low = value.astype(BF16)
    bit = lax.axis_index("tensor") % 2
    parts = low.reshape((2, low.shape[0] // 2) + low.shape[1:])
    return add_low(pick(parts, bit), swap(pick(parts, 1 - bit), "tensor", size, 1))


def tensor_pairs(mine, size):
    step = 2
    while step < size:
        mine = add_low(mine, swap(mine, "tensor", size, step))
        step *= 2
    return mine


def tensor_back(mine, size):
    bit = lax.axis_index("tensor") % 2
    other = swap(mine, "tensor", size, 1)
    return jnp.concatenate(
        [jnp.where(bit == 0, mine, other), jnp.where(bit == 0, other, mine)], axis=0
    ).astype(F32)


def tensor_sum(value, size):
    return tensor_back(tensor_pairs(tensor_halves(value, size), size), size)


def tensor_scatter(value, size):
    low = value.astype(BF16)
    t = lax.axis_index("tensor")
    step = 1
    while step < size:
        bit = (t // step) % 2
        parts = low.reshape((2, low.shape[0] // 2) + low.shape[1:])
        low = add_low(pick(parts, bit), swap(pick(parts, 1 - bit), "tensor", size, step))
        step *= 2
    return low


def tensor_unscatter(value, size):
    t = lax.axis_index("tensor")
    step = size // 2
    while step >= 1:
        bit = (t // step) % 2
        other = swap(value, "tensor", size, step)
        value = jnp.concatenate(
            [jnp.where(bit == 0, value, other), jnp.where(bit == 0, other, value)], axis=0
        )
        step //= 2
    return value


def line_send(pieces, size, step, arrived=None):
    z = lax.axis_index("context")
    last = size - 1
    up = pick(pieces, jnp.clip(size + z - step, 0, last))
    down = pick(pieces, jnp.clip(last - (size + (last - z) - step), 0, last))
    if arrived is not None:
        up = add_low(up, arrived[0])
        down = add_low(down, arrived[1])
    right = lax.ppermute(up, "context", [(i, i + 1) for i in range(step)])
    left = lax.ppermute(down, "context", [(last - i, last - i - 1) for i in range(step)])
    return (right, left)


def line_end(pieces, arrived):
    own = pick(pieces, lax.axis_index("context"))
    return own.astype(F32) + arrived[0].astype(F32) + arrived[1].astype(F32)


def line_spread(pair, size, step):
    right = lax.ppermute(pair[0], "context", [(i, i + 1) for i in range(step - 1, size - 1)])
    left = lax.ppermute(pair[1], "context", [(i, i - 1) for i in range(1, size - step + 1)])
    return (right, left)


def direct_scatter(pieces, size):
    z = lax.axis_index("context")
    total = pick(pieces, z).astype(F32)
    for by in range(1, size):
        total = total + shift(pick(pieces, (z + by) % size), "context", size, by).astype(F32)
    return total


def pair_scatter(value):
    d = lax.axis_index("dp")
    return add_low(pick(value, d), swap(pick(value, 1 - d), "dp", 2, 1))


def tensor_gather(value, size):
    t = lax.axis_index("tensor")
    out = jnp.zeros((size,) + value.shape, value.dtype)
    out = lax.dynamic_update_index_in_dim(out, value, t, 0)
    for by in range(1, size):
        got = shift(value, "tensor", size, by)
        out = lax.dynamic_update_index_in_dim(out, got, (t - by) % size, 0)
    return out


def per_device(
    sizes,
    tokens,
    cotangent,
    group_order,
    attn_gain,
    query_down,
    query_gain,
    latent_down,
    latent_gain,
    query_up,
    latent_up,
    attn_out,
    mlp_gain,
    gate_proj,
    up_proj,
    down_proj,
):
    contexts, tensors = sizes
    rows, width = tokens.shape[1:]
    blocks = group_order.shape[0]
    heads = query_up.shape[1] // (NOPE + ROPE)
    z = lax.axis_index("context")
    d = lax.axis_index("dp")
    t = lax.axis_index("tensor")
    half_width = width // 2
    share = half_width // contexts
    rank = query_down.shape[1]

    mine = lax.dynamic_slice_in_dim(group_order, 2 * z, 2)
    offsets = jnp.arange(HALF, dtype=jnp.int32)
    query_pos = (mine[:, None] * HALF + offsets[None, :]).reshape(rows)
    index = jnp.arange(blocks, dtype=jnp.int32)
    spot = ((z - index // 2) % contexts) * 2 * HALF + (index % 2) * HALF
    where = jnp.sum(
        jnp.where(group_order[None, :] == index[:, None], spot[None, :], 0), axis=1
    ).astype(jnp.int32)
    place = jnp.concatenate([mine, where])

    freq = 10000.0 ** (-2.0 * jnp.arange(ROPE // 2, dtype=F32) / ROPE)
    angle = query_pos.astype(F32)[:, None] * freq[None, :]
    cosine, sine = jnp.cos(angle), jnp.sin(angle)
    angle_t = freq[:, None] * query_pos.astype(F32)[None, :]
    cos_t, sin_t = jnp.cos(angle_t), jnp.sin(angle_t)

    inputs = tokens[0].astype(F32)
    upstream = cotangent[0].astype(F32)
    grad_feed = (RESIDUAL * upstream).astype(BF16)

    first_normed, first_inverse = scaled(inputs)
    hidden_one = (first_normed * attn_gain).astype(BF16)
    latent_raw = matmul(hidden_one, latent_down)
    cache_normed, cache_inverse = scaled(latent_raw[:, :KV_RANK])
    latent = (cache_normed * latent_gain).astype(BF16)
    key_rope = rotate(latent_raw[:, KV_RANK:], cosine, sine).astype(BF16)
    keys_own = jnp.concatenate([latent, key_rope], axis=1)
    bit = t % 2
    part = lax.dynamic_slice_in_dim(keys_own, bit * (rows // 2), rows // 2, 0)
    far = jnp.stack([shift(part, "context", contexts, by) for by in range(1, contexts)])
    far_other = swap(far, "tensor", tensors, 1)
    far_all = jnp.concatenate(
        [jnp.where(bit == 0, far, far_other), jnp.where(bit == 0, far_other, far)], axis=1
    )
    keys_all = jnp.concatenate([keys_own[None], far_all], axis=0).reshape(
        contexts * rows, KV_RANK + ROPE
    )
    latent_all = keys_all[:, :KV_RANK]
    rope_all = jnp.pad(keys_all[:, KV_RANK:], ((0, 0), (0, 128 - ROPE)))
    keys_all_t = keys_all.T
    latent_all_t = keys_all_t[:KV_RANK]
    rope_all_t = keys_all_t[KV_RANK:]
    latent_up_t = latent_up.T

    query_low = matmul(hidden_one, query_down)
    query_normed, query_inverse = scaled(query_low)
    query_latent = (query_normed * query_gain).astype(BF16)
    query_full_t = lax.dot_general(
        query_up, query_latent, (((0,), (1,)), ((), ())), preferred_element_type=F32
    ).reshape(heads, NOPE + ROPE, rows)
    first = query_full_t[:, 64:80]
    second = query_full_t[:, 80:96]
    q_t = jnp.concatenate(
        [
            query_full_t[:, :64],
            first * cos_t - second * sin_t,
            second * cos_t + first * sin_t,
        ],
        axis=1,
    ).astype(BF16)

    feed_t = grad_feed.T.reshape(2, contexts, share, rows)
    feed_t_sent = after(feed_t, far_all)
    feed_slots = [pick(jnp.swapaxes(feed_t, 0, 1), z)] + [
        shift(pick(jnp.swapaxes(feed_t_sent, 0, 1), (z + by) % contexts), "context", contexts, by)
        for by in range(1, contexts)
    ]

    joined_t, exact_t, lse = attention_forward(
        place, q_t, latent_all, latent_all_t, rope_all, latent_up, latent_up_t
    )

    (
        branch,
        hidden_two,
        hidden_mid,
        grad_gate,
        grad_upper,
        feed_part,
        grad_middle,
        dmix_t,
        grad_mlp_gain,
    ) = feed_forward(
        tensors,
        joined_t,
        tokens[0],
        cotangent[0],
        mlp_gain[None],
        attn_out,
        down_proj,
        gate_proj.T,
        up_proj.T,
    )
    grad_mlp_gain = jnp.sum(grad_mlp_gain, axis=0)
    middle = inputs + RESIDUAL * jnp.concatenate([branch[0], branch[1]], axis=1).astype(F32)
    hidden_two_t = hidden_two.T
    two_t_parts = hidden_two_t.reshape(2, half_width, rows)
    two_t_far = swap(pick(two_t_parts, 1 - d), "dp", 2, 1)

    spread_one = line_spread((hidden_mid, hidden_mid), contexts, 1)
    gate_far = swap(grad_gate, "dp", 2, 1)
    upper_far = swap(after(grad_upper, gate_far), "dp", 2, 1)

    spreads = [spread_one]
    spreads.append(line_spread(spreads[-1], contexts, 2))

    two_t_both = jnp.concatenate([pick(two_t_parts, d), two_t_far], axis=1)

    def weight_pieces(own, far):
        full = matmul(two_t_both, jnp.concatenate([own, far], axis=0)).astype(BF16)
        return full.reshape(contexts, share, own.shape[1])

    gate_pieces = weight_pieces(grad_gate, gate_far)
    gate_moved = line_send(gate_pieces, contexts, 1)

    grad_branch = (RESIDUAL * grad_middle).astype(BF16)
    grad_branch_t = grad_branch.T

    up_pieces = weight_pieces(grad_upper, upper_far)
    up_moved = line_send(up_pieces, contexts, 1)
    feed_half = tensor_halves(feed_part, tensors)

    halves = 2 if heads % (2 * GROUP) == 0 else 1
    count = heads // halves
    back = []
    ready = (up_pieces, gate_pieces, feed_half)
    steps = 2
    feed_mid = out_moved = None
    for half in range(halves):
        cut = slice(half * count, (half + 1) * count)
        back.append(
            attention_backward(
                after(place, ready),
                q_t[cut],
                latent_all,
                latent_all_t,
                rope_all,
                rope_all_t,
                latent_up[:, half * count * 128 : (half + 1) * count * 128],
                latent_up_t[half * count * 128 : (half + 1) * count * 128],
                exact_t[cut],
                lse[cut],
                dmix_t[half * count * V_DIM : (half + 1) * count * V_DIM],
                cos_t,
                sin_t,
            )
        )
        done = back[-1]
        if half == 0:
            feed_mid = tensor_pairs(after(feed_half, dmix_t), tensors)
            out_full = times_transposed(after(grad_branch_t, done), joined_t).astype(BF16)
            out_pieces = pair_scatter(out_full.reshape(2, contexts, share, joined_t.shape[0]))
        gate_moved = line_send(gate_pieces, contexts, steps, after(gate_moved, done))
        up_moved = line_send(up_pieces, contexts, steps, after(up_moved, done))
        spreads.append(line_spread(after(spreads[-1], done), contexts, steps + 1)) if (
            steps + 1 < contexts
        ) else None
        steps += 1
        ready = (done, out_full)
    dq_t = jnp.concatenate([b[0] for b in back], axis=0)
    grad_latent_up = jnp.concatenate([b[1] for b in back], axis=1)
    dlat_t = back[0][2]
    for b in back[1:]:
        dlat_t = dlat_t.astype(F32) + b[2].astype(F32)

    dlat_own = tensor_scatter(dlat_t, tensors)
    total = dlat_own[:, :rows].astype(F32)
    for by in range(1, contexts):
        moved = shift(dlat_own[:, by * rows : (by + 1) * rows], "context", contexts, -by)
        total = total + moved.astype(F32)
    grad_keys = tensor_unscatter(total.astype(BF16), tensors).astype(F32).T

    grad_query_full_t = dq_t.reshape(heads * (NOPE + ROPE), rows)
    grad_query_latent = tensor_sum(
        lax.dot_general(
            grad_query_full_t, query_up, (((0,), (1,)), ((), ())), preferred_element_type=F32
        ),
        tensors,
    )
    grad_query_up = lax.dot_general(
        query_latent, grad_query_full_t, (((0,), (1,)), ((), ())), preferred_element_type=F32
    ).astype(BF16)

    while steps < contexts:
        gate_moved = line_send(gate_pieces, contexts, steps, gate_moved)
        up_moved = line_send(up_pieces, contexts, steps, up_moved)
        if steps + 1 < contexts:
            spreads.append(line_spread(spreads[-1], contexts, steps + 1))
        steps += 1
    out_moved = None
    for step in range(1, contexts):
        out_moved = line_send(out_pieces, contexts, step, out_moved)

    feed = tensor_back(after(feed_mid, dq_t), tensors)
    layer_out = (middle + RESIDUAL * feed).astype(BF16)

    grad_query_low, grad_query_gain = norm_back(
        grad_query_latent, query_normed, query_inverse, query_gain
    )
    grad_cache, grad_latent_gain = norm_back(
        grad_keys[:, :KV_RANK], cache_normed, cache_inverse, latent_gain
    )
    grad_low = jnp.concatenate(
        [grad_query_low, grad_cache, unrotate(grad_keys[:, KV_RANK:], cosine, sine)], axis=1
    ).astype(BF16)
    grad_hidden_one = times_transposed(grad_low[:, :rank], query_down) + times_transposed(
        grad_low[:, rank:], latent_down
    )
    grad_norm_one, grad_attn_gain = norm_back(
        grad_hidden_one, first_normed, first_inverse, attn_gain
    )
    token_grad = grad_middle + grad_norm_one

    up_rows = grad_query_up.shape[0] // (2 * contexts)
    lat_rows = grad_latent_up.shape[0] // (2 * contexts)
    lanes = max(grad_query_up.shape[1], grad_latent_up.shape[1])

    def widen(value):
        value = jnp.pad(value, ((0, 0), (0, lanes - value.shape[1])))
        return value.reshape(2, contexts, -1, lanes)

    small = jnp.concatenate([widen(grad_query_up), widen(grad_latent_up)], axis=2)
    small = direct_scatter(pair_scatter(small), contexts)

    low = matmul(hidden_one.T, grad_low).astype(BF16)
    low = low.reshape(2, contexts, tensors, -1, grad_low.shape[1])
    low = lax.dynamic_index_in_dim(low, t, 2, keepdims=False)

    def spare(value):
        return value.reshape(2, contexts, -1)

    gains = jnp.concatenate(
        [spare(grad_attn_gain), spare(grad_query_gain), spare(grad_latent_gain), spare(grad_mlp_gain)],
        axis=2,
    ).astype(BF16)
    gains = jnp.pad(gains, ((0, 0), (0, 0), (0, grad_low.shape[1] - gains.shape[2])))
    low = jnp.concatenate([low, gains[:, :, None]], axis=2)
    low = direct_scatter(pair_scatter(low), contexts)
    gains = low[-1]
    low = tensor_gather(low[:-1].astype(BF16), tensors).reshape(-1, grad_low.shape[1]).astype(F32)
    edges = [0]
    for value in (attn_gain, query_gain, latent_gain, mlp_gain):
        edges.append(edges[-1] + value.shape[0] // (2 * contexts))
    gain_grads = [gains[a:b] for a, b in zip(edges[:-1], edges[1:])]

    slots = [hidden_mid]
    for s in range(1, contexts):
        slots.append(jnp.where(z >= s, spreads[s - 1][0], spreads[contexts - s - 1][1]))
    hidden_all = jnp.concatenate(slots, axis=0)
    feed_all = jnp.concatenate(feed_slots, axis=2).reshape(2 * share, contexts * rows)
    down_full = matmul(feed_all, hidden_all).reshape(2, share, -1)
    down_far = swap(pick(down_full, 1 - d).astype(BF16), "dp", 2, 1)
    grad_down = (pick(down_full, d) + down_far.astype(F32)).T

    return (
        layer_out[None],
        token_grad[None],
        gain_grads[0],
        low[:, :rank],
        gain_grads[1],
        low[:, rank:],
        gain_grads[2],
        small[:up_rows, : grad_query_up.shape[1]],
        small[up_rows:, : grad_latent_up.shape[1]],
        line_end(out_pieces, out_moved).T,
        gain_grads[3],
        line_end(gate_pieces, gate_moved),
        line_end(up_pieces, up_moved),
        grad_down,
    )


def solution(mesh):
    in_specs = (
        P("dp", "context", None),
        P("dp", "context", None),
        P(),
        P(),
        P(),
        P(),
        P(),
        P(),
        P(None, "tensor"),
        P(None, "tensor"),
        P("tensor", None),
        P(),
        P(None, "tensor"),
        P(None, "tensor"),
        P("tensor", None),
    )
    out_specs = (
        P("dp", "context", None),
        P("dp", "context", None),
        P(("dp", "context")),
        P(("dp", "context"), None),
        P(("dp", "context")),
        P(("dp", "context"), None),
        P(("dp", "context")),
        P(("dp", "context"), "tensor"),
        P(("dp", "context"), "tensor"),
        P("tensor", ("dp", "context")),
        P(("dp", "context")),
        P(("dp", "context"), "tensor"),
        P(("dp", "context"), "tensor"),
        P("tensor", ("dp", "context")),
    )
    sizes = (mesh.shape["context"], mesh.shape["tensor"])
    return jax.shard_map(
        functools.partial(per_device, sizes),
        mesh=mesh,
        in_specs=in_specs,
        out_specs=out_specs,
        check_vma=False,
    )
```

```python
import functools
import math

import jax
import jax.numpy as jnp
from jax import lax
from jax.experimental import pallas as pl
from jax.experimental.pallas import tpu as pltpu
from jax.sharding import PartitionSpec as P

NOPE = 64
ROPE = 32
V_DIM = 64
KV_RANK = 256
HALF = 256
GROUP = 5
CHUNK = 256

EPS = 1e-05
RESIDUAL = 1.4 / math.sqrt(62.0)
SCALE = 1.0 / math.sqrt(NOPE + ROPE)
LOG2E = 1.0 / math.log(2.0)
F32 = jnp.float32
BF16 = jnp.bfloat16


def matmul(left, right):
    return jnp.dot(left, right, preferred_element_type=F32)


def times_transposed(left, right):
    return lax.dot_general(left, right, (((1,), (1,)), ((), ())), preferred_element_type=F32)


def transposed_times(left, right):
    return lax.dot_general(left, right, (((0,), (0,)), ((), ())), preferred_element_type=F32)


MESH = pl.DeviceIdType.MESH


def greet(devices):
    barrier = pltpu.get_barrier_semaphore()
    for device in devices:
        pl.semaphore_signal(barrier, inc=1, device_id=device, device_id_type=MESH)
    pl.semaphore_wait(barrier, len(devices))


def line_of(z, contexts):
    return [{"context": lax.rem(z + by, contexts)} for by in range(1, contexts)]


def front_kernel(
    contexts,
    gains,
    tokens,
    cotangent,
    query_down,
    latent_down_t,
    query_up_t,
    cos_t,
    sin_t,
    q_t,
    latent,
    latent_t,
    rope_keys,
    rope_keys_t,
    one_inverse,
    query_normed,
    query_inverse,
    query_t,
    cache_t,
    cache_inverse_t,
    one_t,
    feed_t,
    one,
    low,
    keys,
    far,
    line_sem,
    line_got,
    pair_sem,
    pair_got,
):
    rows, width = tokens.shape
    rank = query_down.shape[1]
    kv = cache_t.shape[0]
    z = lax.axis_index("context")
    t = lax.axis_index("tensor")
    bit = lax.rem(t, 2)
    pair = t + 1 - 2 * bit
    gain_one = slice(0, width)
    gain_query = slice(2 * width, 2 * width + rank)
    gain_latent = slice(2 * width + rank, 2 * width + rank + kv)
    greet([{"tensor": pair}] + line_of(z, contexts))

    @pl.loop(0, rows // 32)
    def _(i):
        r = pl.ds(pl.multiple_of(i * 32, 32), 32)
        value = tokens[r, :].astype(F32)
        inverse = lax.rsqrt(jnp.mean(value * value, axis=-1, keepdims=True) + EPS)
        one_inverse[r, :] = inverse
        one[r, :] = (value * inverse * gains[:, gain_one]).astype(BF16)

    raw = times_transposed(latent_down_t[...], one[...])
    lat = raw[:kv]
    inverse = lax.rsqrt(jnp.mean(lat * lat, axis=0, keepdims=True) + EPS)
    cache_inverse_t[...] = inverse
    lat = lat * inverse
    cache_t[...] = lat.astype(BF16)
    column = jnp.broadcast_to(gains[:, gain_latent], (8, kv)).T[:, 0:1]
    keys[0:kv, :] = (lat * column).astype(BF16)
    first = raw[kv : kv + 16]
    second = raw[kv + 16 :]
    cosine = cos_t[...]
    sine = sin_t[...]
    keys[kv : kv + 16, :] = (first * cosine - second * sine).astype(BF16)
    keys[kv + 16 :, :] = (second * cosine + first * sine).astype(BF16)

    part = keys.shape[0] // 2
    mine = pl.ds(pl.multiple_of(bit * part, 16), part)
    sends = [
        pltpu.make_async_remote_copy(
            src_ref=keys.at[mine],
            dst_ref=far.at[bit, by - 1],
            send_sem=line_sem.at[by - 1],
            recv_sem=line_got.at[by - 1],
            device_id={"context": lax.rem(z + by, contexts)},
            device_id_type=MESH,
        )
        for by in range(1, contexts)
    ]
    for copy in sends:
        copy.start()

    low[...] = matmul(one[...], query_down[...])

    @pl.loop(0, rows // 32)
    def _(i):
        r = pl.ds(pl.multiple_of(i * 32, 32), 32)
        value = low[r, :]
        inverse = lax.rsqrt(jnp.mean(value * value, axis=-1, keepdims=True) + EPS)
        query_inverse[r, :] = inverse
        value = value * inverse
        query_normed[r, :] = value.astype(BF16)
        low[r, :] = value * gains[:, gain_query]

    query = low[...].astype(BF16)
    query_t[...] = query.T
    heads = q_t.shape[0]
    for h in range(heads):
        full = times_transposed(query_up_t[h * 96 : (h + 1) * 96, :], query)
        first = full[64:80]
        second = full[80:96]
        q_t[h, 0:64, :] = full[0:64].astype(BF16)
        q_t[h, 64:80, :] = (first * cosine - second * sine).astype(BF16)
        q_t[h, 80:96, :] = (second * cosine + first * sine).astype(BF16)

    for copy in sends:
        copy.wait_recv()
    share = pltpu.make_async_remote_copy(
        src_ref=far.at[bit],
        dst_ref=far.at[bit],
        send_sem=pair_sem,
        recv_sem=pair_got,
        device_id={"tensor": pair},
        device_id_type=MESH,
    )
    share.start()

    @pl.loop(0, width // 256)
    def _(i):
        lines = pl.ds(pl.multiple_of(i * 256, 256), 256)
        one_t[lines, :] = one[:, lines].T
        feed_t[lines, :] = (RESIDUAL * cotangent[:, lines].astype(F32)).astype(BF16).T

    share.wait_recv()
    latent_t[:, 0:rows] = keys[0:kv, :]
    rope_keys_t[:, 0:rows] = keys[kv:, :]
    for s in range(1, contexts):
        cols = slice(s * rows, (s + 1) * rows)
        latent_t[0:part, cols] = far[0, s - 1]
        latent_t[part:, cols] = far[1, s - 1, 0 : kv - part, :]
        rope_keys_t[:, cols] = far[1, s - 1, kv - part :, :]
    latent[...] = latent_t[...].T
    rope_keys[...] = jnp.concatenate(
        [rope_keys_t[...], jnp.zeros((128 - ROPE, rope_keys_t.shape[1]), BF16)], axis=0
    ).T
    for copy in sends:
        copy.wait_send()
    share.wait_send()


def front(contexts, gains, tokens, cotangent, query_down, latent_down_t, query_up_t, cos_t, sin_t):
    rows, width = tokens.shape
    rank = query_down.shape[1]
    span = latent_down_t.shape[0]
    heads = query_up_t.shape[0] // 96
    kv = span - ROPE
    keys = contexts * rows
    inside = pl.BlockSpec(memory_space=pltpu.VMEM)
    sds = jax.ShapeDtypeStruct
    dma = pltpu.SemaphoreType.DMA
    return pl.pallas_call(
        functools.partial(front_kernel, contexts),
        in_specs=[inside] * 8,
        out_specs=[inside] * 13,
        out_shape=[
            sds((heads, 96, rows), BF16),
            sds((keys, kv), BF16),
            sds((kv, keys), BF16),
            sds((keys, 128), BF16),
            sds((ROPE, keys), BF16),
            sds((rows, 1), F32),
            sds((rows, rank), BF16),
            sds((rows, 1), F32),
            sds((rank, rows), BF16),
            sds((kv, rows), BF16),
            sds((1, rows), F32),
            sds((width, rows), BF16),
            sds((width, rows), BF16),
        ],
        scratch_shapes=[
            pltpu.VMEM((rows, width), BF16),
            pltpu.VMEM((rows, rank), F32),
            pltpu.VMEM((span, rows), BF16),
            pltpu.VMEM((2, contexts - 1, span // 2, rows), BF16),
            dma((contexts - 1,)),
            dma((contexts - 1,)),
            dma,
            dma,
        ],
        compiler_params=pltpu.CompilerParams(
            collective_id=3, has_side_effects=True, vmem_limit_bytes=60 * 1024 * 1024
        ),
        cost_estimate=pl.CostEstimate(
            flops=2 * rows * width * 1200, bytes_accessed=30 * 1024 * 1024, transcendentals=0
        ),
        name="front",
    )(gains, tokens, cotangent, query_down, latent_down_t, query_up_t, cos_t, sin_t)


def load_heads(heads, latent, rope_keys, latent_up, q_t, kcat, q_wide):
    for h in range(heads):
        kcat[h, :, :128] = matmul(latent[...], latent_up[:, h * 128 : (h + 1) * 128]).astype(BF16)
        kcat[h, :, 128:] = rope_keys[...]
        q_wide[h, 0:64, :] = q_t[h, 0:64, :]
        q_wide[h, 64:128, :] = jnp.zeros((64, q_wide.shape[2]), BF16)
        q_wide[h, 128:160, :] = q_t[h, 64:96, :]
        q_wide[h, 160:256, :] = jnp.zeros((96, q_wide.shape[2]), BF16)


def causal():
    key_row = lax.broadcasted_iota(jnp.int32, (HALF, HALF), 0)
    query_col = lax.broadcasted_iota(jnp.int32, (HALF, HALF), 1)
    return key_row <= query_col


def fold(value, op):
    return op(value.reshape(HALF // 8, 8, value.shape[-1]), axis=0)


def forward_kernel(
    heads,
    contexts,
    order,
    q_t,
    latent,
    latent_t,
    rope_keys,
    latent_up,
    latent_up_t,
    joined_t,
    exact_t,
    lse,
    kcat,
    v_t,
    q_wide,
    scores,
    top,
    total,
    acc,
    lies,
):
    z = lax.axis_index("context")
    for i in range(2 * contexts):
        slot = lax.rem(z + contexts - i // 2, contexts)
        lies[order[i]] = slot * (2 * HALF) + (i % 2) * HALF
    load_heads(heads, latent, rope_keys, latent_up, q_t, kcat, q_wide)
    for h in range(heads):
        v_t[h] = matmul(latent_up_t[h * 128 + 64 : (h + 1) * 128, :], latent_t[...]).astype(BF16)
    factor = SCALE * LOG2E
    for block in range(2):
        cols = slice(block * HALF, (block + 1) * HALF)
        position = order[2 * z + block]

        def score(j, masked):
            rows = pl.ds(pl.multiple_of(lies[j], HALF), HALF)
            spot = pl.ds(pl.multiple_of(j * HALF, HALF), HALF)
            for h in range(heads):
                s = matmul(kcat[h, rows, :], q_wide[h, :, cols])
                if masked:
                    s = jnp.where(causal(), s, -1e30)
                scores[h, spot, :] = s
                peak = fold(s, jnp.max)
                top[h] = peak if masked else jnp.maximum(top[h], peak)

        score(position, True)

        @pl.loop(0, position)
        def _(j):
            score(j, False)

        for h in range(heads):
            peak = jnp.max(top[h], axis=0, keepdims=True) * factor
            top[h] = jnp.broadcast_to(peak, (8, HALF))
            total[h] = jnp.zeros((8, HALF), F32)
            acc[h] = jnp.zeros((V_DIM, HALF), F32)

        @pl.loop(0, position + 1)
        def _(j):
            rows = pl.ds(pl.multiple_of(lies[j], HALF), HALF)
            spot = pl.ds(pl.multiple_of(j * HALF, HALF), HALF)
            for h in range(heads):
                p = jnp.exp2(scores[h, spot, :] * factor - top[h, 0:1, :])
                total[h] += fold(p, jnp.sum)
                acc[h] += matmul(v_t[h, :, rows], p.astype(BF16))

        for h in range(heads):
            summed = jnp.sum(total[h], axis=0, keepdims=True)
            out = acc[h] / summed
            joined_t[h * V_DIM : (h + 1) * V_DIM, cols] = out.astype(BF16)
            exact_t[h, :, cols] = out
            lse[h, :, cols] = top[h, 0:1, :] + jnp.log2(summed)


def whole_spec(shape):
    return pl.BlockSpec(shape, lambda g: (0,) * len(shape))


def attention_forward(contexts, order, q_t, latent, latent_t, rope_keys, latent_up, latent_up_t):
    count, _, rows = q_t.shape
    keys = latent.shape[0]
    heads = GROUP
    flops = 2 * count * rows * keys * 384
    return pl.pallas_call(
        functools.partial(forward_kernel, heads, contexts),
        grid=(count // heads,),
        in_specs=[
            pl.BlockSpec(memory_space=pltpu.SMEM),
            pl.BlockSpec((heads, 96, rows), lambda g: (g, 0, 0)),
            whole_spec((keys, KV_RANK)),
            whole_spec((KV_RANK, keys)),
            whole_spec((keys, 128)),
            pl.BlockSpec((KV_RANK, heads * 128), lambda g: (0, g)),
            pl.BlockSpec((heads * 128, KV_RANK), lambda g: (g, 0)),
        ],
        out_specs=[
            pl.BlockSpec((heads * V_DIM, rows), lambda g: (g, 0)),
            pl.BlockSpec((heads, V_DIM, rows), lambda g: (g, 0, 0)),
            pl.BlockSpec((heads, 1, rows), lambda g: (g, 0, 0)),
        ],
        out_shape=[
            jax.ShapeDtypeStruct((count * V_DIM, rows), BF16),
            jax.ShapeDtypeStruct((count, V_DIM, rows), F32),
            jax.ShapeDtypeStruct((count, 1, rows), F32),
        ],
        scratch_shapes=[
            pltpu.VMEM((heads, keys, 256), BF16),
            pltpu.VMEM((heads, V_DIM, keys), BF16),
            pltpu.VMEM((heads, 256, rows), BF16),
            pltpu.VMEM((heads, keys, HALF), F32),
            pltpu.VMEM((heads, 8, HALF), F32),
            pltpu.VMEM((heads, 8, HALF), F32),
            pltpu.VMEM((heads, V_DIM, HALF), F32),
            pltpu.SMEM((keys // HALF,), jnp.int32),
        ],
        compiler_params=pltpu.CompilerParams(vmem_limit_bytes=56 * 1024 * 1024),
        cost_estimate=pl.CostEstimate(
            flops=flops, bytes_accessed=12 * 1024 * 1024, transcendentals=count * rows * keys
        ),
        name="attention_forward",
    )(order, q_t, latent, latent_t, rope_keys, latent_up, latent_up_t)


def cuts(size, step=512):
    count = max(1, size // step)
    edges = [i * step for i in range(count)] + [size]
    return list(zip(edges[:-1], edges[1:]))


def feed_forward_kernel(
    contexts,
    tensors,
    joined_t,
    tokens,
    cotangent,
    gain,
    attn_out_h,
    down_h,
    gate_h,
    up_h,
    feed_t_h,
    branch_o,
    two_o,
    hidden_o,
    dgate_o,
    dup_o,
    feed_o,
    dmiddle_o,
    dbranch_o,
    feed_all_o,
    far_two_o,
    far_dgate_o,
    near_o,
    dmix_t,
    gain_o,
    attn_out,
    down,
    gate_w,
    up_w,
    part,
    final,
    near,
    across,
    dhid,
    two,
    trio,
    feed,
    dmiddle,
    load_sem,
    save_sem,
    send_sem,
    recv_sem,
    pair_sem,
    pair_got,
    line_sem,
    line_got,
    turn_sem,
    turn_got,
    keep_sem,
):
    rows, width = tokens.shape
    half = width // 2
    t = lax.axis_index("tensor")
    bit = lax.rem(t, 2)
    pair = t + 1 - 2 * bit
    others = [pair]
    step = 2
    while step < tensors:
        others.append(t + step - 2 * step * lax.rem(t // step, 2))
        step *= 2

    loads = [
        pltpu.make_async_copy(src, dst, load_sem.at[i])
        for i, (src, dst) in enumerate(
            [(attn_out_h, attn_out), (down_h, down), (gate_h, gate_w), (up_h, up_w)]
        )
    ]
    for load in loads:
        load.start()

    d = lax.axis_index("dp")
    z = lax.axis_index("context")
    greet([{"tensor": i} for i in others] + line_of(z, contexts) + [{"dp": 1 - d}])

    share = half // contexts

    def turn(e, by):
        owner = lax.rem(z + by, contexts)
        src = feed_t_h.at[pl.ds(pl.multiple_of(e * half + owner * share, 16), share)]
        dst = feed_all_o.at[e * share : (e + 1) * share, by * rows : (by + 1) * rows]
        if by == 0:
            return pltpu.make_async_copy(src, dst, keep_sem.at[e])
        return pltpu.make_async_remote_copy(
            src_ref=src,
            dst_ref=dst,
            send_sem=turn_sem.at[e, by - 1],
            recv_sem=turn_got.at[e, by - 1],
            device_id={"context": owner},
            device_id_type=MESH,
        )

    turns = [turn(e, by) for e in range(2) for by in range(contexts)]
    for copy in turns:
        copy.start()

    def send(src, dst, job, kind, c, device):
        return pltpu.make_async_remote_copy(
            src_ref=src,
            dst_ref=dst,
            send_sem=send_sem.at[job, kind, c],
            recv_sem=recv_sem.at[job, kind, c],
            device_id={"tensor": device},
            device_id_type=MESH,
        )

    def span(c):
        return pl.ds(c * CHUNK, CHUNK)

    last = len(others)

    def hop(job, c, kind):
        if kind == 0:
            return send(
                part.at[1 - bit, span(c)], near.at[job, span(c)], job, 0, c, pair
            )
        if kind == last:
            here = final.at[job, bit, span(c)]
            return send(here, here, job, last, c, pair)
        src = near if kind == 1 else across.at[kind - 2]
        return send(
            src.at[job, span(c)], across.at[kind - 1, job, span(c)], job, kind, c, others[kind]
        )

    def reduce_pair(job, c):
        hop(job, c, 0).wait_recv()

        @pl.loop(0, CHUNK // 32)
        def _(i):
            r = pl.ds(pl.multiple_of(c * CHUNK + i * 32, 32), 32)
            near[job, r, :] = (
                near[job, r, :].astype(F32) + part[bit, r, :].astype(F32)
            ).astype(BF16)

        hop(job, c, 1).start()

    def reduce_across(job, c):
        for kind in range(1, last):
            hop(job, c, kind).wait_recv()
            src = near if kind == 1 else across.at[kind - 2]
            ending = kind == last - 1

            @pl.loop(0, CHUNK // 32)
            def _(i):
                r = pl.ds(pl.multiple_of(c * CHUNK + i * 32, 32), 32)
                value = (
                    src[job, r, :].astype(F32) + across[kind - 1, job, r, :].astype(F32)
                ).astype(BF16)
                if ending:
                    final[job, bit, r, :] = value
                else:
                    across[kind - 1, job, r, :] = value

            hop(job, c, kind + 1).start()
        hop(job, c, last).wait_recv()

    def middle_rows(r):
        parts = []
        for h in range(2):
            cols = slice(h * half, (h + 1) * half)
            parts.append(
                tokens[r, cols].astype(F32) + RESIDUAL * final[0, h, r, :].astype(F32)
            )
        square = sum(jnp.sum(p * p, axis=-1, keepdims=True) for p in parts)
        inverse = lax.rsqrt(square * (1.0 / width) + EPS)
        return parts, inverse

    def across_pair(c, kind):
        if kind == 0:
            src = two.at[:, pl.ds(pl.multiple_of((1 - d) * half, 128), half)]
            dst = far_two_o.at[span(c)]
        else:
            src, dst = trio.at[1, span(c)], far_dgate_o.at[span(c)]
        return pltpu.make_async_remote_copy(
            src_ref=src,
            dst_ref=dst,
            send_sem=pair_sem.at[kind, c],
            recv_sem=pair_got.at[kind, c],
            device_id={"dp": 1 - d},
            device_id_type=MESH,
        )

    def along_line(c, way):
        return pltpu.make_async_remote_copy(
            src_ref=trio.at[0, span(c)],
            dst_ref=near_o.at[way, span(c)],
            send_sem=line_sem.at[way, c],
            recv_sem=line_got.at[way, c],
            device_id={"context": z + 1 - 2 * way},
            device_id_type=MESH,
        )

    chunks = rows // CHUNK
    loads[0].wait()
    for c in range(chunks):
        left = joined_t[:, c * CHUNK : (c + 1) * CHUNK]

        @pl.loop(0, width // 256)
        def _(n):
            cols = pl.ds(pl.multiple_of(n * 256, 256), 256)
            side = n // (half // 256)
            place = pl.ds(pl.multiple_of(lax.rem(n, half // 256) * 256, 256), 256)
            part[side, span(c), place] = transposed_times(left, attn_out[:, cols]).astype(BF16)

        hop(0, c, 0).start()
    for c in range(chunks):
        reduce_pair(0, c)

    loads[1].wait()
    for c in range(chunks):

        @pl.loop(0, CHUNK // 32)
        def _(i):
            r = pl.ds(pl.multiple_of(c * CHUNK + i * 32, 32), 32)
            o = pl.ds(pl.multiple_of(i * 32, 32), 32)
            two[o, :] = (RESIDUAL * cotangent[r, :].astype(F32)).astype(BF16)

        for a, b in cuts(down.shape[0]):
            dhid[span(c), a:b] = times_transposed(two[...], down[a:b, :]).astype(BF16)

    loads[2].wait()
    loads[3].wait()
    saves = []

    def save(src, dst):
        copy = pltpu.make_async_copy(src, dst, save_sem.at[len(saves)])
        copy.start()
        saves.append(copy)
        return copy

    two_saved = None
    for c in range(chunks):
        reduce_across(0, c)
        if two_saved is not None:
            two_saved.wait()
            across_pair(c - 1, 0).wait_send()

        @pl.loop(0, CHUNK // 32)
        def _(i):
            r = pl.ds(pl.multiple_of(c * CHUNK + i * 32, 32), 32)
            o = pl.ds(pl.multiple_of(i * 32, 32), 32)
            parts, inverse = middle_rows(r)
            for h in range(2):
                cols = slice(h * half, (h + 1) * half)
                two[o, cols] = (parts[h] * inverse * gain[:, width + h * half : width + (h + 1) * half]).astype(BF16)

        two_saved = save(two, two_o.at[span(c)])
        across_pair(c, 0).start()
        for a, b in cuts(gate_w.shape[0]):
            gate = times_transposed(two[...], gate_w[a:b, :])
            upper = times_transposed(two[...], up_w[a:b, :])
            grad = dhid[span(c), a:b].astype(F32)
            sigma = 1.0 / (1.0 + jnp.exp(-gate))
            act = gate * sigma
            trio[0, span(c), a:b] = (act * upper).astype(BF16)
            trio[1, span(c), a:b] = (
                grad * upper * sigma * (1.0 + gate * (1.0 - sigma))
            ).astype(BF16)
            trio[2, span(c), a:b] = (grad * act).astype(BF16)
        for k, out in enumerate((hidden_o, dgate_o, dup_o)):
            save(trio.at[k, span(c)], out.at[span(c)])
        across_pair(c, 1).start()

        @pl.when(z < contexts - 1)
        def _():
            along_line(c, 0).start()

        @pl.when(z > 0)
        def _():
            along_line(c, 1).start()

        hop(0, c, 0).wait_send()

        @pl.loop(0, width // 256)
        def _(n):
            cols = pl.ds(pl.multiple_of(n * 256, 256), 256)
            side = n // (half // 256)
            place = pl.ds(pl.multiple_of(lax.rem(n, half // 256) * 256, 256), 256)
            value = matmul(trio[1, span(c), :], gate_w[:, cols])
            value += matmul(trio[2, span(c), :], up_w[:, cols])
            part[side, span(c), place] = value.astype(BF16)

        hop(1, c, 0).start()
        if c > 0:
            reduce_pair(1, c - 1)
    reduce_pair(1, chunks - 1)
    two_saved.wait()

    gain_o[...] = jnp.zeros_like(gain_o)
    feed_saved = dmiddle_saved = dbranch_saved = None
    for c in range(chunks):
        if feed_saved is not None:
            feed_saved.wait()

        @pl.loop(0, width // 256)
        def _(n):
            cols = pl.ds(pl.multiple_of(n * 256, 256), 256)
            feed[:, cols] = matmul(trio[0, span(c), :], down[:, cols]).astype(BF16)

        feed_saved = save(feed, feed_o.at[span(c)])
        reduce_across(1, c)
        if dmiddle_saved is not None:
            dmiddle_saved.wait()
            dbranch_saved.wait()
        else:
            across_pair(chunks - 1, 0).wait_send()

        @pl.loop(0, CHUNK // 32)
        def _(i):
            r = pl.ds(pl.multiple_of(c * CHUNK + i * 32, 32), 32)
            o = pl.ds(pl.multiple_of(i * 32, 32), 32)
            parts, inverse = middle_rows(r)
            dot = jnp.zeros((32, 1), F32)
            for h in range(2):
                cols = slice(h * half, (h + 1) * half)
                product = final[1, h, r, :].astype(F32) * (parts[h] * inverse)
                gain_o[:, cols] += jnp.sum(product.reshape(4, 8, half), axis=0)
                dot += jnp.sum(product * gain[:, width + h * half : width + (h + 1) * half], axis=-1, keepdims=True)
            dot = dot * (1.0 / width)
            for h in range(2):
                cols = slice(h * half, (h + 1) * half)
                weighted = final[1, h, r, :].astype(F32) * gain[:, width + h * half : width + (h + 1) * half]
                value = cotangent[r, cols].astype(F32) + inverse * (
                    weighted - parts[h] * inverse * dot
                )
                dmiddle[o, cols] = value
                two[o, cols] = (RESIDUAL * value).astype(BF16)

        dmiddle_saved = save(dmiddle, dmiddle_o.at[span(c)])
        dbranch_saved = save(two, dbranch_o.at[span(c)])
        dmix_t[:, c * CHUNK : (c + 1) * CHUNK] = times_transposed(attn_out[...], two[...]).astype(
            BF16
        )
    for h in range(2):
        save(final.at[0, h], branch_o.at[:, h * half : (h + 1) * half])
    for copy in saves[-2:] + [feed_saved, dmiddle_saved, dbranch_saved] + turns:
        copy.wait()
    for c in range(chunks):
        for k in range(3):
            saves[c * 4 + 1 + k].wait()
    for c in range(chunks):
        across_pair(c, 0).wait_recv()
        across_pair(c, 1).wait()

        @pl.when(z < contexts - 1)
        def _():
            along_line(c, 0).wait_send()
            along_line(c, 1).wait_recv()

        @pl.when(z > 0)
        def _():
            along_line(c, 1).wait_send()
            along_line(c, 0).wait_recv()

    for job in range(2):
        for c in range(chunks):
            for kind in range(1 - job, last + 1):
                hop(job, c, kind).wait_send()


def feed_forward(contexts, tensors, joined_t, tokens, cotangent, gain, attn_out, down, gate_w, up_w, feed_t):
    rows, width = tokens.shape
    units = down.shape[0]
    chunks = rows // CHUNK
    hops = tensors.bit_length() - 1
    anywhere = pl.BlockSpec(memory_space=pl.ANY)
    inside = pl.BlockSpec(memory_space=pltpu.VMEM)
    return pl.pallas_call(
        functools.partial(feed_forward_kernel, contexts, tensors),
        in_specs=[inside] * 4 + [anywhere] * 5,
        out_specs=[anywhere] * 12 + [inside] * 2,
        out_shape=[
            jax.ShapeDtypeStruct((rows, width), BF16),
            jax.ShapeDtypeStruct((rows, width), BF16),
            jax.ShapeDtypeStruct((rows, units), BF16),
            jax.ShapeDtypeStruct((rows, units), BF16),
            jax.ShapeDtypeStruct((rows, units), BF16),
            jax.ShapeDtypeStruct((rows, width), BF16),
            jax.ShapeDtypeStruct((rows, width), F32),
            jax.ShapeDtypeStruct((rows, width), BF16),
            jax.ShapeDtypeStruct((width // contexts, contexts * rows), BF16),
            jax.ShapeDtypeStruct((rows, width // 2), BF16),
            jax.ShapeDtypeStruct((rows, units), BF16),
            jax.ShapeDtypeStruct((2, rows, units), BF16),
            jax.ShapeDtypeStruct((joined_t.shape[0], rows), BF16),
            jax.ShapeDtypeStruct((8, width), F32),
        ],
        scratch_shapes=[
            pltpu.VMEM(attn_out.shape, BF16),
            pltpu.VMEM(down.shape, BF16),
            pltpu.VMEM(gate_w.shape, BF16),
            pltpu.VMEM(up_w.shape, BF16),
            pltpu.VMEM((2, rows, width // 2), BF16),
            pltpu.VMEM((2, 2, rows, width // 2), BF16),
            pltpu.VMEM((2, rows, width // 2), BF16),
            pltpu.VMEM((hops - 1, 2, rows, width // 2), BF16),
            pltpu.VMEM((rows, units), BF16),
            pltpu.VMEM((CHUNK, width), BF16),
            pltpu.VMEM((3, rows, units), BF16),
            pltpu.VMEM((CHUNK, width), BF16),
            pltpu.VMEM((CHUNK, width), F32),
            pltpu.SemaphoreType.DMA((4,)),
            pltpu.SemaphoreType.DMA((7 * chunks + 2,)),
            pltpu.SemaphoreType.DMA((2, hops + 1, chunks)),
            pltpu.SemaphoreType.DMA((2, hops + 1, chunks)),
        ]
        + [pltpu.SemaphoreType.DMA((2, chunks))] * 4
        + [pltpu.SemaphoreType.DMA((2, contexts - 1))] * 2
        + [pltpu.SemaphoreType.DMA((2,))],
        compiler_params=pltpu.CompilerParams(
            collective_id=0, has_side_effects=True, vmem_limit_bytes=63 * 1024 * 1024
        ),
        cost_estimate=pl.CostEstimate(
            flops=2 * rows * width * units * 6, bytes_accessed=60 * 1024 * 1024, transcendentals=0
        ),
        name="feed_forward",
    )(joined_t, tokens, cotangent, gain, attn_out, down, gate_w, up_w, feed_t)


def backward_kernel(
    contexts,
    group,
    order,
    q_t,
    latent,
    latent_t,
    rope_keys,
    rope_keys_t,
    latent_up,
    latent_up_t,
    exact_t,
    lse,
    dmix_t,
    cos_t,
    sin_t,
    two_h,
    far_two_h,
    dgate_h,
    far_dgate_h,
    dup_h,
    near_h,
    dq_t,
    grad_up,
    dlat_t,
    gate_o,
    up_o,
    up_got_o,
    far_dup_o,
    spread_o,
    kcat,
    k_t,
    q_wide,
    dmix_wide,
    q_nat,
    dmix_nat,
    delta,
    dq,
    pair,
    lat_acc,
    rope_acc,
    two,
    act,
    gate_w,
    up_w,
    arrived,
    load_sem,
    dup_sem,
    dup_got,
    gate_sem,
    gate_got,
    up_sem,
    up_got,
    spread_sem,
    spread_got,
):
    heads, _, rows = q_t.shape
    keys = latent.shape[0]
    tiles = keys // HALF
    last = contexts - 1
    half = two.shape[1]
    share = half // contexts
    d = lax.axis_index("dp")
    z = lax.axis_index("context")
    loads = [
        pltpu.make_async_copy(
            two_h.at[:, pl.ds(pl.multiple_of(d * half, 128), half)],
            two.at[0:rows],
            load_sem.at[0],
        ),
        pltpu.make_async_copy(far_two_h, two.at[rows : 2 * rows], load_sem.at[1]),
        pltpu.make_async_copy(dgate_h, act.at[0:rows], load_sem.at[2]),
        pltpu.make_async_copy(far_dgate_h, act.at[rows : 2 * rows], load_sem.at[3]),
    ]
    for load in loads:
        load.start()
    greet(line_of(z, contexts) + [{"dp": 1 - d}])

    swap_dup = pltpu.make_async_remote_copy(
        src_ref=dup_h,
        dst_ref=far_dup_o,
        send_sem=dup_sem,
        recv_sem=dup_got,
        device_id={"dp": 1 - d},
        device_id_type=MESH,
    )
    swap_dup.start()

    def line(src, dst, send_sem, recv_sem, way):
        return pltpu.make_async_remote_copy(
            src_ref=src,
            dst_ref=dst,
            send_sem=send_sem,
            recv_sem=recv_sem,
            device_id={"context": z + 1 - 2 * way},
            device_id_type=MESH,
        )

    along = [z, last - z]

    def spread(way, step):
        src = near_h.at[way] if step == 2 else spread_o.at[way, step - 3]
        i = (way, step - 2)
        return line(src, spread_o.at[i], spread_sem.at[i], spread_got.at[i], way)

    def spread_start(step):
        if step > last:
            return
        for way in range(2):
            if step > 2:

                @pl.when(along[way] >= step - 1)
                def _():
                    spread(way, step - 1).wait_recv()

            @pl.when((along[way] >= step - 1) & (along[way] < last))
            def _():
                spread(way, step).start()

    def spread_end():
        for way in range(2):
            for step in range(2, last + 1):
                if step == last:

                    @pl.when(along[way] >= step)
                    def _():
                        spread(way, step).wait_recv()

                @pl.when((along[way] >= step - 1) & (along[way] < last))
                def _():
                    spread(way, step).wait_send()

    def share_of(ref, index):
        return ref.at[pl.ds(pl.multiple_of(index * share, 16), share)]

    def farthest(way, step):
        right = z + 2 * contexts - step if way == 0 else contexts + step - 1 - along[1]
        return lax.rem(right, contexts)

    def reduce(ref, dst, send_sem, recv_sem, way, step):
        return line(
            share_of(ref, farthest(way, step)), dst, send_sem, recv_sem, way
        )

    def gate_step(way, step):
        i = (way, step - 1)
        return reduce(gate_w, arrived.at[i], gate_sem.at[i], gate_got.at[i], way, step)

    def up_step(way):
        return reduce(up_w, up_got_o.at[way], up_sem.at[way], up_got.at[way], way, 1)

    def add_rows(dst, src):
        @pl.loop(0, share // 16)
        def _(i):
            r = pl.ds(pl.multiple_of(i * 16, 16), 16)
            dst[r, :] = (dst[r, :].astype(F32) + src[r, :].astype(F32)).astype(BF16)

    def gate_start(step):
        if step > last:
            return
        for way in range(2):
            if step > 1:

                @pl.when((along[way] >= 1) & (along[way] < step))
                def _():
                    gate_step(way, step - 1).wait_recv()
                    add_rows(share_of(gate_w, farthest(way, step)), arrived.at[way, step - 2])

            @pl.when(along[way] < step)
            def _():
                gate_step(way, step).start()

    def gate_end():
        own = pl.multiple_of(z * share, 16)
        for way in range(2):

            @pl.when(along[way] >= 1)
            def _():
                gate_step(way, last).wait_recv()

        @pl.loop(0, share // 16)
        def _(i):
            r = pl.ds(pl.multiple_of(own + i * 16, 16), 16)
            q = pl.ds(pl.multiple_of(i * 16, 16), 16)
            value = gate_w[r, :].astype(F32)
            for way in range(2):
                value = jnp.where(
                    along[way] >= 1, value + arrived[way, last - 1, q, :].astype(F32), value
                )
            gate_o[q, :] = value

        for way in range(2):
            for step in range(1, last + 1):

                @pl.when(along[way] < step)
                def _():
                    gate_step(way, step).wait_send()

    def weight(ref):
        @pl.loop(0, half // 256)
        def _(n):
            cols = pl.ds(pl.multiple_of(n * 256, 256), 256)
            ref[cols, :] = transposed_times(two[:, cols], act[...]).astype(BF16)

    factor = SCALE * LOG2E
    row = lax.broadcasted_iota(jnp.int32, (HALF, rows), 0)
    spot = lax.broadcasted_iota(jnp.int32, (1, rows), 1)
    spot = jnp.where(
        spot < HALF, order[2 * z] * HALF + spot, order[2 * z + 1] * HALF + spot - HALF
    )

    def begin(g):
        for h in range(group):
            e = g * group + h
            span = slice(e * 128, (e + 1) * 128)
            kcat[h, :, :128] = matmul(latent[...], latent_up[:, span]).astype(BF16)
            kcat[h, :, 128:] = rope_keys[...]
            k_t[h, 0:64, :] = matmul(
                latent_up_t[e * 128 : e * 128 + 64, :], latent_t[...]
            ).astype(BF16)
            k_t[h, 64:96, :] = rope_keys_t[...]
            q_wide[h, 0:64, :] = q_t[e, 0:64, :]
            q_wide[h, 64:128, :] = jnp.zeros((64, rows), BF16)
            q_wide[h, 128:160, :] = q_t[e, 64:96, :]
            q_wide[h, 160:256, :] = jnp.zeros((96, rows), BF16)
            q_nat[h] = q_wide[h].T
            piece = dmix_t[e * V_DIM : (e + 1) * V_DIM, :]
            dmix_wide[h, 0:64, :] = jnp.zeros_like(piece)
            dmix_wide[h, 64:128, :] = piece
            dmix_nat[h] = dmix_wide[h].T
            delta[h] = jnp.sum(piece.astype(F32) * exact_t[e], axis=0, keepdims=True)
            dq[h] = jnp.zeros((96, rows), F32)

    def tiles_of(g, first, end):
        lane = lax.broadcasted_iota(jnp.int32, (1, 128), 1)
        scale = jnp.where(lane < NOPE, SCALE, 1.0).astype(F32)

        @pl.loop(first, end)
        def _(j):
            lines = pl.ds(pl.multiple_of(j * HALF, HALF), HALF)
            block = 2 * lax.rem(z + contexts - j // 2, contexts) + lax.rem(j, 2)
            allowed = row <= spot - order[block] * HALF
            turned = jnp.zeros((HALF, 128), F32)
            for h in range(group):
                e = g * group + h
                s = matmul(kcat[h, lines, :], q_wide[h])
                p = jnp.where(allowed, jnp.exp2(s * factor - lse[e]), 0.0)
                dp = matmul(kcat[h, lines, :128], dmix_wide[h])
                ds = (p * (dp - delta[h])).astype(BF16)
                dq[h] += matmul(k_t[h, :, lines], ds)
                dk = matmul(ds, q_nat[h])
                dv = matmul(p.astype(BF16), dmix_nat[h])
                pair[h, lines, :] = ((dk[:, :128] + dv) * scale).astype(BF16)
                turned += dk[:, 128:]
            rope_acc[lines, :] = turned if g == 0 else rope_acc[lines, :] + turned

    def finish(g):
        cosine = cos_t[...]
        sine = sin_t[...]
        for h in range(group):
            e = g * group + h
            span = slice(e * 128, (e + 1) * 128)
            value = dq[h] * SCALE
            first = value[64:80]
            second = value[80:96]
            dq_t[e, 0:64, :] = value[0:64].astype(BF16)
            dq_t[e, 64:80, :] = (first * cosine + second * sine).astype(BF16)
            dq_t[e, 80:96, :] = (second * cosine - first * sine).astype(BF16)
            grad_up[:, span] = matmul(latent_t[...], pair[h]).astype(BF16)
            change = times_transposed(latent_up[:, span], pair[h])
            lat_acc[...] = change if e == 0 else lat_acc[...] + change

    groups = heads // group
    total = groups * tiles
    stops = [total * (i + 1) // (last + 1) for i in range(last)]

    spread_start(2)
    for load in loads:
        load.wait()
    weight(gate_w)
    gate_start(1)
    done = 0
    for i, stop in enumerate(stops + [total]):
        while done < stop:
            g = done // tiles
            until = min(stop, (g + 1) * tiles)
            if done == g * tiles:
                begin(g)
            tiles_of(g, done - g * tiles, until - g * tiles)
            if until == (g + 1) * tiles:
                finish(g)
            done = until
        if i < last:
            gate_start(i + 2)
            spread_start(i + 3)
        if i == min(1, last - 1):
            swap_dup.wait_recv()
            again = [
                pltpu.make_async_copy(dup_h, act.at[0:rows], load_sem.at[2]),
                pltpu.make_async_copy(far_dup_o, act.at[rows : 2 * rows], load_sem.at[3]),
            ]
            for load in again:
                load.start()
            for load in again:
                load.wait()
            weight(up_w)
            keep = pltpu.make_async_copy(up_w, up_o, load_sem.at[0])
            keep.start()
            for way in range(2):

                @pl.when(along[way] == 0)
                def _():
                    up_step(way).start()

    dlat_t[0:KV_RANK, :] = lat_acc[...].astype(BF16)
    dlat_t[KV_RANK:, :] = (rope_acc[...] * SCALE).T[:ROPE].astype(BF16)
    gate_end()
    spread_end()
    keep.wait()
    swap_dup.wait_send()
    for way in range(2):

        @pl.when(along[way] == 0)
        def _():
            up_step(way).wait_send()

        @pl.when(along[way] == 1)
        def _():
            up_step(way).wait_recv()


def backward(
    contexts,
    order,
    q_t,
    latent,
    latent_t,
    rope_keys,
    rope_keys_t,
    latent_up,
    latent_up_t,
    exact_t,
    lse,
    dmix_t,
    cos_t,
    sin_t,
    two,
    far_two,
    dgate,
    far_dgate,
    dup,
    near,
):
    heads, _, rows = q_t.shape
    keys = latent.shape[0]
    group = GROUP
    units = dup.shape[1]
    half = far_two.shape[1]
    share = half // contexts
    last = contexts - 1
    anywhere = pl.BlockSpec(memory_space=pl.ANY)
    inside = pl.BlockSpec(memory_space=pltpu.VMEM)
    dma = pltpu.SemaphoreType.DMA
    return pl.pallas_call(
        functools.partial(backward_kernel, contexts, group),
        in_specs=[pl.BlockSpec(memory_space=pltpu.SMEM)] + [inside] * 12 + [anywhere] * 6,
        out_specs=[inside] * 4 + [anywhere] * 4,
        out_shape=[
            jax.ShapeDtypeStruct((heads, 96, rows), BF16),
            jax.ShapeDtypeStruct((KV_RANK, heads * 128), BF16),
            jax.ShapeDtypeStruct((KV_RANK + ROPE, keys), BF16),
            jax.ShapeDtypeStruct((share, units), F32),
            jax.ShapeDtypeStruct((half, units), BF16),
            jax.ShapeDtypeStruct((2, share, units), BF16),
            jax.ShapeDtypeStruct((rows, units), BF16),
            jax.ShapeDtypeStruct((2, last - 1, rows, units), BF16),
        ],
        scratch_shapes=[
            pltpu.VMEM((group, keys, 256), BF16),
            pltpu.VMEM((group, 96, keys), BF16),
            pltpu.VMEM((group, 256, rows), BF16),
            pltpu.VMEM((group, 128, rows), BF16),
            pltpu.VMEM((group, rows, 256), BF16),
            pltpu.VMEM((group, rows, 128), BF16),
            pltpu.VMEM((group, 1, rows), F32),
            pltpu.VMEM((group, 96, rows), F32),
            pltpu.VMEM((group, keys, 128), BF16),
            pltpu.VMEM((KV_RANK, keys), F32),
            pltpu.VMEM((keys, 128), F32),
            pltpu.VMEM((2 * rows, half), BF16),
            pltpu.VMEM((2 * rows, units), BF16),
            pltpu.VMEM((half, units), BF16),
            pltpu.VMEM((half, units), BF16),
            pltpu.VMEM((2, last, share, units), BF16),
            dma((4,)),
            dma,
            dma,
            dma((2, last)),
            dma((2, last)),
            dma((2,)),
            dma((2,)),
            dma((2, last - 1)),
            dma((2, last - 1)),
        ],
        compiler_params=pltpu.CompilerParams(
            collective_id=1, has_side_effects=True, vmem_limit_bytes=63 * 1024 * 1024
        ),
        cost_estimate=pl.CostEstimate(
            flops=2 * heads * rows * keys * 1000,
            bytes_accessed=40 * 1024 * 1024,
            transcendentals=heads * rows * keys,
        ),
        name="backward",
    )(
        order,
        q_t,
        latent,
        latent_t,
        rope_keys,
        rope_keys_t,
        latent_up,
        latent_up_t,
        exact_t,
        lse,
        dmix_t,
        cos_t,
        sin_t,
        two,
        far_two,
        dgate,
        far_dgate,
        dup,
        near,
    )


def tail_kernel(
    contexts,
    tensors,
    split,
    dq_t,
    query_up_t,
    query_t,
    query_normed,
    query_inverse,
    all_gains,
    dlat,
    cache_t,
    cache_inverse_t,
    cos_t,
    sin_t,
    lat_grad,
    joined_t,
    first_inverse,
    mlp_gain_grad,
    dbranch_h,
    hidden_h,
    near_h,
    spread_h,
    feed_t_h,
    up_h,
    up_got_h,
    one_t_h,
    query_down_h,
    latent_down_t_h,
    tokens_h,
    feed_h,
    norm_o,
    low_q_o,
    low_l_o,
    small_q_o,
    small_l_o,
    out_o,
    up_o,
    down_o,
    gain_o,
    feed_o,
    q_part,
    q_near,
    q_across,
    q_final,
    d_near,
    d_acc,
    d_across,
    d_got,
    d_all,
    d_final,
    u_w,
    u_far,
    u_got,
    l_far,
    l_got,
    wide,
    up_got,
    out_w,
    out_far,
    out_got,
    long,
    feed_t,
    down_w,
    down_far,
    f_part,
    f_near,
    f_across,
    dqa,
    dkva_t,
    one_t,
    low_q,
    low_l,
    low_q_far,
    low_l_far,
    low_q_got,
    low_l_got,
    low_q_all,
    low_l_all,
    query_down,
    latent_down_t,
    joined,
    dh1,
    stage,
    gains,
    gains_far,
    gains_got,
    send_sem,
    recv_sem,
    load_sem,
):
    rows = dlat.shape[1] // contexts
    width = wide.shape[1]
    half = width // 2
    share = half // contexts
    last = contexts - 1
    rank = query_normed.shape[1]
    kv = cache_t.shape[0]
    first_gain = slice(0, width)
    query_gain = slice(2 * width, 2 * width + rank)
    latent_gain = slice(2 * width + rank, 2 * width + rank + kv)
    d = lax.axis_index("dp")
    z = lax.axis_index("context")
    t = lax.axis_index("tensor")
    bit = lax.rem(t, 2)
    others = [t + 1 - 2 * bit]
    step = 2
    while step < tensors:
        others.append(t + step - 2 * step * lax.rem(t // step, 2))
        step *= 2
    spot = lax.rem(t, split)
    sharers = [t - spot + lax.rem(spot + k, split) for k in range(1, split)]

    used = [0]

    def remote(src, dst, **device):
        i = used[0]
        used[0] += 1
        return pltpu.make_async_remote_copy(
            src_ref=src,
            dst_ref=dst,
            send_sem=send_sem.at[i],
            recv_sem=recv_sem.at[i],
            device_id=device,
            device_id_type=MESH,
        )

    loaded = [0]

    def local(src, dst):
        i = loaded[0]
        loaded[0] += 1
        return pltpu.make_async_copy(src, dst, load_sem.at[i])

    def only(condition, copy, what):
        @pl.when(condition)
        def _():
            getattr(copy, what)()

    def add_rows(dst, left, right, count, chunk=16):
        @pl.loop(0, count // chunk)
        def _(i):
            r = pl.ds(pl.multiple_of(i * chunk, chunk), chunk)
            dst[r, :] = (left[r, :].astype(F32) + right[r, :].astype(F32)).astype(BF16)

    def piece(ref, index, size):
        return ref.at[pl.ds(pl.multiple_of(index * size, 16), size)]

    load_branch = local(dbranch_h, wide)
    load_hidden = [(None, local(hidden_h, long.at[0:rows]))]
    for s in range(1, contexts):
        back = contexts - s
        dst = long.at[s * rows : (s + 1) * rows]
        right = near_h.at[0] if s == 1 else spread_h.at[0, s - 2]
        left = near_h.at[1] if back == 1 else spread_h.at[1, back - 2]
        load_hidden.append((z >= s, local(right, dst)))
        load_hidden.append((z < s, local(left, dst)))
    load_feed_t = local(feed_t_h, feed_t)
    up_got0 = [long.at[half + way * share : half + (way + 1) * share] for way in range(2)]
    load_got = [local(up_got_h.at[way], up_got0[way]) for way in range(2)]
    load_one = local(one_t_h, one_t)
    load_down = [local(query_down_h, query_down), local(latent_down_t_h, latent_down_t)]

    def load_feed(c):
        return [
            local(
                feed_h.at[pl.ds(c * CHUNK, CHUNK), h * half : (h + 1) * half], f_part.at[h]
            )
            for h in range(2)
        ]

    feed_loads = [load_feed(c) for c in range(rows // CHUNK)]
    load_feed_t.start()
    for condition, copy in load_hidden:
        if condition is None:
            copy.start()
        else:
            only(condition, copy, "start")
    for copy in [load_branch, load_one] + load_down + feed_loads[0]:
        copy.start()

    peers = others if split == 2 else sharers
    greet([{"tensor": i} for i in peers] + line_of(z, contexts) + [{"dp": 1 - d}])

    d_rows = dlat.shape[0] // 2
    d_pair = remote(dlat.at[pl.ds(pl.multiple_of((1 - bit) * d_rows, 16), d_rows)], d_near, tensor=others[0])
    d_pair.start()

    q_rows = rows // 2
    for h in range(2):
        q_part[h] = transposed_times(
            dq_t[:, h * q_rows : (h + 1) * q_rows], query_up_t[...]
        ).astype(BF16)
    q_pair = remote(q_part.at[1 - bit], q_near, tensor=others[0])
    q_pair.start()

    u_w[...] = times_transposed(query_t[...], dq_t[...]).astype(BF16)
    u_half = u_w.shape[0] // 2
    l_half = lat_grad.shape[0] // 2
    u_pair = remote(
        u_w.at[pl.ds(pl.multiple_of((1 - d) * u_half, 16), u_half)], u_far, dp=1 - d
    )
    l_pair = remote(
        lat_grad.at[pl.ds(pl.multiple_of((1 - d) * l_half, 16), l_half)], l_far, dp=1 - d
    )
    u_pair.start()
    l_pair.start()

    q_pair.wait_recv()
    add_rows(q_near, q_near, q_part.at[bit], q_rows, 32)
    q_hops = []
    for k in range(1, len(others)):
        src = q_near if k == 1 else q_across.at[k - 2]
        q_hops.append(remote(src, q_across.at[k - 1], tensor=others[k]))
    q_hops[0].start()

    d_pair.wait_recv()
    mine = pl.multiple_of(bit * d_rows, 16)

    @pl.loop(0, d_rows // 16)
    def _(i):
        r = pl.ds(pl.multiple_of(i * 16, 16), 16)
        own = pl.ds(pl.multiple_of(mine + i * 16, 16), 16)
        value = (dlat[own, :].astype(F32) + d_near[r, :].astype(F32)).astype(BF16)
        for s in range(contexts):
            d_acc[s, r, :] = value[:, s * rows : (s + 1) * rows]

    d_hops = []
    lanes = rows
    start = 0
    for k in range(1, len(others)):
        lanes //= 2
        side = lax.rem(t // (2**k), 2)
        give = pl.ds(pl.multiple_of(start + (1 - side) * lanes, 128), lanes)
        start = pl.multiple_of(start + side * lanes, 128)
        d_hops.append(
            (remote(d_acc.at[:, :, give], d_across.at[k - 1, :, :, 0:lanes], tensor=others[k]),
             start, lanes)
        )

    d_hops[0][0].start()
    load_feed_t.wait()
    for condition, copy in load_hidden:
        if condition is None:
            copy.wait()
        else:
            only(condition, copy, "wait")
    chunk = 2 * share // 5 if (2 * share // 5) % 16 == 0 else share

    @pl.loop(0, 2 * share // chunk)
    def _(i):
        r = pl.ds(pl.multiple_of(i * chunk, 16), chunk)
        down_w[r, :] = matmul(feed_t[r, :], long[...]).astype(BF16)

    load_up = local(up_h, long.at[0:half])
    load_up.start()
    for copy in load_got:
        copy.start()
    down_pair = remote(piece(down_w, 1 - d, share), down_far, dp=1 - d)

    along = [z, last - z]

    def farthest(way, step):
        right = z + 2 * contexts - step if way == 0 else contexts + step - 1 - along[1]
        return lax.rem(right, contexts)

    def line_step(w, got, way, step, first):
        return remote(
            piece(w, farthest(way, step), share),
            got.at[way, step - first],
            context=z + 1 - 2 * way,
        )

    up_w = long
    up_steps = {
        (way, step): line_step(up_w, up_got, way, step, 2)
        for way in range(2)
        for step in range(2, last + 1)
    }
    out_steps = {
        (way, step): line_step(out_far, out_got, way, step, 1)
        for way in range(2)
        for step in range(1, last + 1)
    }

    def line_start(steps, w, got, first, step, before=None):
        for way in range(2):
            if step > 1:

                @pl.when((along[way] >= 1) & (along[way] < step))
                def _():
                    if step > first:
                        steps[way, step - 1].wait_recv()
                    source = before[way] if step == first else got.at[way, step - 1 - first]
                    target = piece(w, farthest(way, step), share)
                    add_rows(target, target, source, share)

            only(along[way] < step, steps[way, step], "start")

    def line_end(steps, w, got, first, result):
        for way in range(2):
            only(along[way] >= 1, steps[way, last], "wait_recv")

        @pl.loop(0, share // 16)
        def _(i):
            r = pl.ds(pl.multiple_of(z * share + i * 16, 16), 16)
            q = pl.ds(pl.multiple_of(i * 16, 16), 16)
            value = w[r, :].astype(F32)
            for way in range(2):
                value = jnp.where(
                    along[way] >= 1, value + got[way, last - first, q, :].astype(F32), value
                )
            result[q, :] = value

        for way in range(2):
            for step in range(first, last + 1):
                only(along[way] < step, steps[way, step], "wait_send")

    for copy in load_got:
        copy.wait()
    load_up.wait()
    line_start(up_steps, up_w, up_got, 2, 2, up_got0)

    f_pairs, f_hops, f_backs = [], [], []
    for c in range(rows // CHUNK):
        span = pl.ds(c * CHUNK, CHUNK)
        f_pairs.append(remote(f_part.at[1 - bit], f_near.at[c], tensor=others[0]))
        hops = []
        for k in range(1, len(others)):
            src = f_near.at[c] if k == 1 else f_across.at[k - 2, c]
            hops.append(remote(src, f_across.at[k - 1, c], tensor=others[k]))
        f_hops.append(hops)
        here = f_across.at[len(others) - 2, c]
        f_backs.append(
            (remote(here, feed_o.at[span, pl.ds(pl.multiple_of(bit * half, 128), half)], tensor=others[0]), local(here, feed_o.at[span, pl.ds(pl.multiple_of(bit * half, 128), half)]))
        )

    def feed_pair(c):
        for copy in feed_loads[c]:
            copy.wait()
        f_pairs[c].start()

    def feed_across(c):
        f_pairs[c].wait_recv()
        add_rows(f_near.at[c], f_near.at[c], f_part.at[bit], CHUNK, 32)
        f_hops[c][0].start()
        f_pairs[c].wait_send()
        if c + 1 < rows // CHUNK:
            for copy in feed_loads[c + 1]:
                copy.start()

    def feed_back(c):
        for k, hop in enumerate(f_hops[c]):
            hop.wait_recv()
            src = f_near.at[c] if k == 0 else f_across.at[k - 1, c]
            add_rows(f_across.at[k, c], src, f_across.at[k, c], CHUNK, 32)
            if k < len(f_hops[c]) - 1:
                f_hops[c][k + 1].start()
        for back in f_backs[c]:
            back.start()

    feed_pair(0)

    load_branch.wait()
    joined[...] = joined_t[...].T

    @pl.loop(0, width // 256)
    def _(n):
        cols = pl.ds(pl.multiple_of(n * 256, 256), 256)
        out_w[cols, :] = transposed_times(wide[:, cols], joined[...]).astype(BF16)

    out_pair = remote(
        out_w.at[pl.ds(pl.multiple_of((1 - d) * half, 16), half)], out_far, dp=1 - d
    )
    load_tokens = local(tokens_h, wide)
    load_tokens.start()

    final = len(q_hops) - 1
    for k, hop in enumerate(q_hops):
        hop.wait_recv()
        src = q_near if k == 0 else q_across.at[k - 1]
        dst = q_final.at[bit] if k == final else q_across.at[k]
        add_rows(dst, src, q_across.at[k], q_rows, 32)
        if k < final:
            q_hops[k + 1].start()
    q_back = remote(q_final.at[bit], q_final.at[bit], tensor=others[0])
    q_back.start()

    for k, (hop, begin, lane) in enumerate(d_hops):
        hop.wait_recv()
        keep = pl.ds(begin, lane)

        @pl.loop(0, contexts)
        def _(s):
            @pl.loop(0, d_rows // 16)
            def _(i):
                r = pl.ds(pl.multiple_of(i * 16, 16), 16)
                d_acc[s, r, keep] = (
                    d_acc[s, r, keep].astype(F32) + d_across[k, s, r, 0:lane].astype(F32)
                ).astype(BF16)

        if k + 1 < len(d_hops):
            d_hops[k + 1][0].start()
    keep = pl.ds(start, lanes)
    d_sends = [
        remote(
            d_acc.at[s, :, keep],
            d_got.at[s - 1],
            context=lax.rem(z + contexts - s, contexts),
        )
        for s in range(1, contexts)
    ]
    for copy in d_sends:
        copy.start()
    feed_across(0)
    u_pair.wait_recv()
    l_pair.wait_recv()
    out_pair.start()

    @pl.loop(0, u_half // 16)
    def _(i):
        r = pl.ds(pl.multiple_of(i * 16, 16), 16)
        own = pl.ds(pl.multiple_of(d * u_half + i * 16, 16), 16)
        u_far[r, :] = (u_far[r, :].astype(F32) + u_w[own, :].astype(F32)).astype(BF16)

    @pl.loop(0, l_half // 16)
    def _(i):
        r = pl.ds(pl.multiple_of(i * 16, 16), 16)
        own = pl.ds(pl.multiple_of(d * l_half + i * 16, 16), 16)
        l_far[r, :] = (l_far[r, :].astype(F32) + lat_grad[own, :].astype(F32)).astype(BF16)

    u_size = u_half // contexts
    l_size = l_half // contexts
    small_sends = []
    for by in range(1, contexts):
        owner = lax.rem(z + by, contexts)
        small_sends.append(remote(piece(u_far, owner, u_size), u_got.at[by - 1], context=owner))
        small_sends.append(remote(piece(l_far, owner, l_size), l_got.at[by - 1], context=owner))

    q_back.wait_recv()
    q_sum = jnp.zeros((8, rank), F32)

    def query_rows(i, acc):
        r = pl.ds(pl.multiple_of(i * 32, 32), 32)
        h = i // (q_rows // 32)
        o = pl.ds(pl.multiple_of(lax.rem(i, q_rows // 32) * 32, 32), 32)
        grad = q_final[h, o, :].astype(F32)
        normed = query_normed[r, :].astype(F32)
        weighted = grad * all_gains[:, query_gain]
        mean = jnp.mean(weighted * normed, axis=-1, keepdims=True)
        dqa[r, :] = (query_inverse[r, :] * (weighted - normed * mean)).astype(BF16)
        return acc + jnp.sum((grad * normed).reshape(4, 8, rank), axis=0)

    q_sum = lax.fori_loop(0, rows // 32, query_rows, q_sum)

    for copy in d_sends:
        copy.wait_recv()

    @pl.loop(0, d_rows // 16)
    def _(i):
        r = pl.ds(pl.multiple_of(i * 16, 16), 16)
        value = d_acc[0, r, keep].astype(F32)
        for s in range(1, contexts):
            value += d_got[s - 1, r, :].astype(F32)
        d_all[r, keep] = value.astype(BF16)

    d_gathers = []
    for k in range(len(others) - 1, 0, -1):
        here = d_all.at[:, pl.ds(start, lanes)]
        hop = remote(here, here, tensor=others[k])
        hop.start()
        hop.wait_recv()
        d_gathers.append(hop)
        side = lax.rem(t // (2**k), 2)
        start = pl.multiple_of(start - side * lanes, 128)
        lanes *= 2
    d_back = remote(d_all, d_final, tensor=others[0])
    d_back.start()
    for copy in small_sends:
        copy.start()
    if rows // CHUNK > 1:
        feed_pair(1)
    d_back.wait_recv()

    top = jnp.where(bit == 0, d_all[...], d_final[...]).astype(F32)
    bottom = jnp.where(bit == 0, d_final[...], d_all[...]).astype(F32)
    grad = jnp.concatenate([top, bottom], axis=0)
    lat = grad[:kv]
    normed = cache_t[...].astype(F32)
    column = jnp.broadcast_to(all_gains[:, latent_gain], (8, kv)).T[:, 0:1]
    weighted = lat * column
    mean = jnp.mean(weighted * normed, axis=0, keepdims=True)
    dkva_t[0:kv, :] = (cache_inverse_t[...] * (weighted - normed * mean)).astype(BF16)
    c_sum = jnp.sum((lat * normed).T, axis=0, keepdims=True)
    first = grad[kv : kv + 16]
    second = grad[kv + 16 :]
    cosine = cos_t[...]
    sine = sin_t[...]
    dkva_t[kv : kv + 16, :] = (first * cosine + second * sine).astype(BF16)
    dkva_t[kv + 16 :, :] = (second * cosine - first * sine).astype(BF16)

    load_one.wait()
    size = share // split

    @pl.loop(0, 2 * contexts)
    def _(i):
        r = pl.ds(pl.multiple_of((i * split + spot) * size, 16), size)
        o = pl.ds(pl.multiple_of(i * size, 16), size)
        low_q[o, :] = matmul(one_t[r, :], dqa[...]).astype(BF16)
        low_l[o, :] = times_transposed(one_t[r, :], dkva_t[...]).astype(BF16)

    low_half = contexts * size
    give = pl.ds(pl.multiple_of((1 - d) * low_half, 16), low_half)
    low_pairs = [
        remote(low_q.at[give], low_q_far, dp=1 - d),
        remote(low_l.at[give], low_l_far, dp=1 - d),
    ]
    for copy in low_pairs:
        copy.start()
    down_pair.start()
    line_start(up_steps, up_w, up_got, 2, 3) if last >= 3 else None
    if rows // CHUNK > 1:
        feed_across(1)

    for copy in load_down:
        copy.wait()
    load_tokens.wait()
    a_sum = jnp.zeros((8, width), F32)
    gains[...] = jnp.zeros_like(gains)
    block = dh1.shape[0]
    tall = 512

    def first_rows(c, acc):
        span = pl.ds(pl.multiple_of(c * block, block), block)
        for n in range(width // tall):
            lines = slice(n * tall, (n + 1) * tall)
            dh1[:, lines] = times_transposed(dqa[span, :], query_down[lines, :])
            dh1[:, lines] += transposed_times(dkva_t[:, span], latent_down_t[:, lines])

        def few(i, inner):
            o = pl.ds(pl.multiple_of(i * 16, 16), 16)
            r = pl.ds(pl.multiple_of(c * block + i * 16, 16), 16)
            grad = dh1[o, :]
            inverse = first_inverse[r, :]
            normed = wide[r, :].astype(F32) * inverse
            weighted = grad * all_gains[:, first_gain]
            mean = jnp.mean(weighted * normed, axis=-1, keepdims=True)
            wide[r, :] = (inverse * (weighted - normed * mean)).astype(BF16)
            return inner + jnp.sum((grad * normed).reshape(2, 8, width), axis=0)

        return lax.fori_loop(0, block // 16, few, acc)

    for c in range(rows // block):
        a_sum = first_rows(c, a_sum)
    save_norm = local(wide, norm_o)
    save_norm.start()

    parts = [
        jnp.sum(a_sum, axis=0, keepdims=True),
        jnp.sum(mlp_gain_grad[...], axis=0, keepdims=True),
        jnp.sum(q_sum, axis=0, keepdims=True),
        c_sum,
    ]
    line = jnp.concatenate(parts, axis=1)
    cut = gains.shape[1]
    for r in range(8):
        gains[r : r + 1, :] = line[:, r * cut : (r + 1) * cut]
    gains_pair = remote(gains, gains_far, dp=1 - d)
    gains_pair.start()

    feed_back(0)
    for step in range(1, last + 1):
        if step == 1:
            out_pair.wait_recv()

            @pl.loop(0, half // 16)
            def _(i):
                r = pl.ds(pl.multiple_of(i * 16, 16), 16)
                own = pl.ds(pl.multiple_of(d * half + i * 16, 16), 16)
                out_far[r, :] = (out_far[r, :].astype(F32) + out_w[own, :].astype(F32)).astype(
                    BF16
                )

        line_start(out_steps, out_far, out_got, 1, step)
        if step + 3 <= last:
            line_start(up_steps, up_w, up_got, 2, step + 3)
        if step == 1:
            gains_pair.wait_recv()
            gains_far[...] = gains_far[...] + gains[...]
            gains_sends = [
                remote(gains_far, gains_got.at[by - 1], context=lax.rem(z + by, contexts))
                for by in range(1, contexts)
            ]
            for copy in gains_sends:
                copy.start()
            for copy in low_pairs:
                copy.wait_recv()

            @pl.loop(0, low_half // 16)
            def _(i):
                r = pl.ds(pl.multiple_of(i * 16, 16), 16)
                own = pl.ds(pl.multiple_of(d * low_half + i * 16, 16), 16)
                low_q_far[r, :] = (
                    low_q_far[r, :].astype(F32) + low_q[own, :].astype(F32)
                ).astype(BF16)
                low_l_far[r, :] = (
                    low_l_far[r, :].astype(F32) + low_l[own, :].astype(F32)
                ).astype(BF16)

            low_sends = []
            for by in range(1, contexts):
                owner = lax.rem(z + by, contexts)
                low_sends.append(
                    remote(piece(low_q_far, owner, size), low_q_got.at[by - 1], context=owner)
                )
                low_sends.append(
                    remote(piece(low_l_far, owner, size), low_l_got.at[by - 1], context=owner)
                )
            for copy in low_sends:
                copy.start()
            for copy in small_sends:
                copy.wait_recv()
            for far, got, result, count in (
                (u_far, u_got, small_q_o, u_size),
                (l_far, l_got, small_l_o, l_size),
            ):

                @pl.loop(0, count // 16)
                def _(i):
                    r = pl.ds(pl.multiple_of(z * count + i * 16, 16), 16)
                    q = pl.ds(pl.multiple_of(i * 16, 16), 16)
                    value = far[r, :].astype(F32)
                    for by in range(1, contexts):
                        value += got[by - 1, q, :].astype(F32)
                    result[q, :] = value

    if rows // CHUNK > 1:
        feed_back(1)
    for copy in low_sends:
        copy.wait_recv()

    @pl.loop(0, size // 16)
    def _(i):
        r = pl.ds(pl.multiple_of(z * size + i * 16, 16), 16)
        q = pl.ds(pl.multiple_of(i * 16, 16), 16)
        for far, got, everyone in (
            (low_q_far, low_q_got, low_q_all),
            (low_l_far, low_l_got, low_l_all),
        ):
            value = far[r, :].astype(F32)
            for by in range(1, contexts):
                value += got[by - 1, q, :].astype(F32)
            everyone[spot, q, :] = value.astype(BF16)

    low_gathers = []
    for sharer in sharers:
        for everyone in (low_q_all, low_l_all):
            here = everyone.at[spot]
            copy = remote(here, here, tensor=sharer)
            copy.start()
            low_gathers.append(copy)
    down_pair.wait_recv()

    @pl.loop(0, share // 16)
    def _(i):
        r = pl.ds(pl.multiple_of(d * share + i * 16, 16), 16)
        q = pl.ds(pl.multiple_of(i * 16, 16), 16)
        stage[q, :] = down_w[r, :].astype(F32) + down_far[q, :].astype(F32)

    save_down = local(stage, down_o)
    save_down.start()
    save_down.wait()

    line_end(up_steps, up_w, up_got, 2, stage)
    save_up = local(stage, up_o)
    save_up.start()
    for copy in gains_sends:
        copy.wait_recv()
    value = gains_far[...]
    for by in range(1, contexts):
        value += gains_got[by - 1]
    gain_o[...] = value
    for copy in low_gathers:
        copy.wait_recv()
    save_low = [local(low_q_all, low_q_o), local(low_l_all, low_l_o)]
    for copy in save_low:
        copy.start()
    line_end(out_steps, out_far, out_got, 1, out_o)
    for copy in save_low + [save_norm, save_up]:
        copy.wait()
    for back, save in f_backs:
        back.wait_recv()
        save.wait()
    sent = [d_pair, q_pair, u_pair, l_pair, q_back, d_back, down_pair, out_pair, gains_pair]
    sent += q_hops + [hop[0] for hop in d_hops] + d_sends + d_gathers + small_sends
    sent += low_pairs + low_sends + low_gathers + gains_sends + [back[0] for back in f_backs]
    for hops in f_hops:
        sent += hops
    for copy in sent:
        copy.wait_send()


def tail(contexts, tensors, split, inside_args, outside_args):
    dq_t, query_t, dlat, lat_grad, joined = (inside_args[i] for i in (0, 2, 6, 11, 12))
    rows = query_t.shape[1]
    rank = query_t.shape[0]
    width = outside_args[0].shape[1]
    units = outside_args[1].shape[1]
    half = width // 2
    share = half // contexts
    size = share // split
    last = contexts - 1
    hops = tensors.bit_length() - 1
    kv = dlat.shape[0]
    d_rows = kv // 2
    lanes = rows >> (hops - 1)
    heads_q = dq_t.shape[0]
    lat_rows, lat_cols = lat_grad.shape
    count_gains = (2 * width + rank + lat_rows) // 8
    anywhere = pl.BlockSpec(memory_space=pl.ANY)
    inside = pl.BlockSpec(memory_space=pltpu.VMEM)
    vm = pltpu.VMEM
    sds = jax.ShapeDtypeStruct
    chunks = rows // CHUNK
    return pl.pallas_call(
        functools.partial(tail_kernel, contexts, tensors, split),
        in_specs=[inside] * len(inside_args) + [anywhere] * len(outside_args),
        out_specs=[anywhere] * 3 + [inside] * 3 + [anywhere] * 2 + [inside, anywhere],
        out_shape=[
            sds((rows, width), BF16),
            sds((split, size, rank), BF16),
            sds((split, size, kv), BF16),
            sds((rank // (2 * contexts), heads_q), F32),
            sds((lat_rows // (2 * contexts), lat_cols), F32),
            sds((share, joined.shape[0]), F32),
            sds((share, units), F32),
            sds((share, units), F32),
            sds((8, count_gains), F32),
            sds((rows, width), BF16),
        ],
        scratch_shapes=[
            vm((2, rows // 2, rank), BF16),
            vm((rows // 2, rank), BF16),
            vm((hops - 1, rows // 2, rank), BF16),
            vm((2, rows // 2, rank), BF16),
            vm((d_rows, contexts * rows), BF16),
            vm((contexts, d_rows, rows), BF16),
            vm((hops - 1, contexts, d_rows, rows // 2), BF16),
            vm((last, d_rows, lanes), BF16),
            vm((d_rows, rows), BF16),
            vm((d_rows, rows), BF16),
            vm((rank, heads_q), BF16),
            vm((rank // 2, heads_q), BF16),
            vm((last, rank // (2 * contexts), heads_q), BF16),
            vm((lat_rows // 2, lat_cols), BF16),
            vm((last, lat_rows // (2 * contexts), lat_cols), BF16),
            vm((rows, width), BF16),
            vm((2, last - 1, share, units), BF16),
            vm((width, joined.shape[0]), BF16),
            vm((half, joined.shape[0]), BF16),
            vm((2, last, share, joined.shape[0]), BF16),
            vm((contexts * rows, units), BF16),
            vm((2 * share, contexts * rows), BF16),
            vm((2 * share, units), BF16),
            vm((share, units), BF16),
            vm((2, CHUNK, half), BF16),
            vm((chunks, CHUNK, half), BF16),
            vm((hops - 1, chunks, CHUNK, half), BF16),
            vm((rows, rank), BF16),
            vm((kv, rows), BF16),
            vm((width, rows), BF16),
            vm((2 * contexts * size, rank), BF16),
            vm((2 * contexts * size, kv), BF16),
            vm((contexts * size, rank), BF16),
            vm((contexts * size, kv), BF16),
            vm((last, size, rank), BF16),
            vm((last, size, kv), BF16),
            vm((split, size, rank), BF16),
            vm((split, size, kv), BF16),
            vm((width, rank), BF16),
            vm((kv, width), BF16),
            vm((rows, joined.shape[0]), BF16),
            vm((128, width), F32),
            vm((share, units), F32),
            vm((8, count_gains), F32),
            vm((8, count_gains), F32),
            vm((last, 8, count_gains), F32),
            pltpu.SemaphoreType.DMA((128,)),
            pltpu.SemaphoreType.DMA((128,)),
            pltpu.SemaphoreType.DMA((48,)),
        ],
        compiler_params=pltpu.CompilerParams(
            collective_id=2, has_side_effects=True, vmem_limit_bytes=65000 * 1024
        ),
        cost_estimate=pl.CostEstimate(
            flops=2 * rows * width * units * 3, bytes_accessed=40 * 1024 * 1024, transcendentals=0
        ),
        name="tail",
    )(*inside_args, *outside_args)


def pick(value, index):
    return lax.dynamic_index_in_dim(value, index, 0, keepdims=False)


def per_device(
    sizes,
    tokens,
    cotangent,
    group_order,
    attn_gain,
    query_down,
    query_gain,
    latent_down,
    latent_gain,
    query_up,
    latent_up,
    attn_out,
    mlp_gain,
    gate_proj,
    up_proj,
    down_proj,
):
    contexts, tensors = sizes
    rows, width = tokens.shape[1:]
    heads = query_up.shape[1] // (NOPE + ROPE)
    z = lax.axis_index("context")
    d = lax.axis_index("dp")
    share = width // (2 * contexts)
    tokens = tokens[0]
    cotangent = cotangent[0]
    query_up_t = query_up.T
    latent_up_t = latent_up.T
    latent_down_t = latent_down.T
    gains = jnp.concatenate([attn_gain, mlp_gain, query_gain, latent_gain])[None]

    mine = lax.dynamic_slice_in_dim(group_order, 2 * z, 2)
    offsets = jnp.arange(HALF, dtype=jnp.int32)
    query_pos = (mine[:, None] * HALF + offsets[None, :]).reshape(rows)
    freq = 10000.0 ** (-2.0 * jnp.arange(ROPE // 2, dtype=F32) / ROPE)
    angle_t = freq[:, None] * query_pos.astype(F32)[None, :]
    cos_t, sin_t = jnp.cos(angle_t), jnp.sin(angle_t)

    (
        q_t,
        latent_all,
        latent_all_t,
        rope_all,
        rope_all_t,
        one_inverse,
        query_normed,
        query_inverse,
        query_t,
        cache_t,
        cache_inverse_t,
        one_t,
        feed_t,
    ) = front(
        contexts, gains, tokens, cotangent, query_down, latent_down_t, query_up_t, cos_t, sin_t
    )
    joined_t, exact_t, lse = attention_forward(
        contexts, group_order, q_t, latent_all, latent_all_t, rope_all, latent_up, latent_up_t
    )
    (
        branch,
        two,
        hidden,
        dgate,
        dup,
        feed_part,
        dmiddle,
        dbranch,
        feed_all,
        far_two,
        far_dgate,
        near,
        dmix_t,
        mlp_gain_grad,
    ) = feed_forward(
        contexts,
        tensors,
        joined_t,
        tokens,
        cotangent,
        gains,
        attn_out,
        down_proj,
        gate_proj.T,
        up_proj.T,
        feed_t,
    )
    dq_t, lat_grad, dlat_t, grad_gate_proj, up_pieces, up_got, _, spread = backward(
        contexts,
        group_order,
        q_t,
        latent_all,
        latent_all_t,
        rope_all,
        rope_all_t,
        latent_up,
        latent_up_t,
        exact_t,
        lse,
        dmix_t,
        cos_t,
        sin_t,
        two,
        far_two,
        dgate,
        far_dgate,
        dup,
        near,
    )
    split = tensors
    while (share // split) % 16 != 0 or share % split != 0:
        split //= 2
    (
        norm_one,
        low_q,
        low_l,
        small_q,
        small_l,
        grad_attn_out,
        grad_up_proj,
        grad_down,
        gain_sums,
        feed,
    ) = tail(
        contexts,
        tensors,
        split,
        [
            dq_t.reshape(heads * (NOPE + ROPE), rows),
            query_up_t,
            query_t,
            query_normed,
            query_inverse,
            gains,
            dlat_t,
            cache_t,
            cache_inverse_t,
            cos_t,
            sin_t,
            lat_grad,
            joined_t,
            one_inverse,
            mlp_gain_grad,
        ],
        [
            dbranch,
            hidden,
            near,
            spread,
            feed_all,
            up_pieces,
            up_got,
            one_t,
            query_down,
            latent_down_t,
            tokens,
            feed_part,
        ],
    )
    layer_out = (
        tokens.astype(F32) + RESIDUAL * branch.astype(F32) + RESIDUAL * feed.astype(F32)
    ).astype(BF16)
    token_grad = dmiddle + norm_one.astype(F32)

    gain_sums = gain_sums.reshape(-1)
    gain_grads = []
    edge = 0
    for value in (attn_gain, mlp_gain, query_gain, latent_gain):
        part = gain_sums[edge : edge + value.shape[0]].reshape(2 * contexts, -1)
        gain_grads.append(pick(part, d * contexts + z))
        edge += value.shape[0]

    return (
        layer_out[None],
        token_grad[None],
        gain_grads[0],
        low_q.reshape(share, -1).astype(F32),
        gain_grads[2],
        low_l.reshape(share, -1).astype(F32),
        gain_grads[3],
        small_q,
        small_l,
        grad_attn_out.T,
        gain_grads[1],
        grad_gate_proj,
        grad_up_proj,
        grad_down.T,
    )


def solution(mesh):
    in_specs = (
        P("dp", "context", None),
        P("dp", "context", None),
        P(),
        P(),
        P(),
        P(),
        P(),
        P(),
        P(None, "tensor"),
        P(None, "tensor"),
        P("tensor", None),
        P(),
        P(None, "tensor"),
        P(None, "tensor"),
        P("tensor", None),
    )
    out_specs = (
        P("dp", "context", None),
        P("dp", "context", None),
        P(("dp", "context")),
        P(("dp", "context"), None),
        P(("dp", "context")),
        P(("dp", "context"), None),
        P(("dp", "context")),
        P(("dp", "context"), "tensor"),
        P(("dp", "context"), "tensor"),
        P("tensor", ("dp", "context")),
        P(("dp", "context")),
        P(("dp", "context"), "tensor"),
        P(("dp", "context"), "tensor"),
        P("tensor", ("dp", "context")),
    )
    sizes = (mesh.shape["context"], mesh.shape["tensor"])
    return jax.shard_map(
        functools.partial(per_device, sizes),
        mesh=mesh,
        in_specs=in_specs,
        out_specs=out_specs,
        check_vma=False,
    )
```

```python
import functools
import math

import jax
import jax.numpy as jnp
from jax import lax
from jax.experimental import pallas as pl
from jax.experimental.pallas import tpu as pltpu
from jax.sharding import PartitionSpec as P

NOPE = 64
ROPE = 32
V_DIM = 64
KV_RANK = 256
HALF = 256
GROUP = 5
CHUNK = 256

EPS = 1e-05
RESIDUAL = 1.4 / math.sqrt(62.0)
SCALE = 1.0 / math.sqrt(NOPE + ROPE)
LOG2E = 1.0 / math.log(2.0)
F32 = jnp.float32
BF16 = jnp.bfloat16


def matmul(left, right):
    return jnp.dot(left, right, preferred_element_type=F32)


def times_transposed(left, right):
    return lax.dot_general(left, right, (((1,), (1,)), ((), ())), preferred_element_type=F32)


def transposed_times(left, right):
    return lax.dot_general(left, right, (((0,), (0,)), ((), ())), preferred_element_type=F32)


MESH = pl.DeviceIdType.MESH


def greet(devices):
    barrier = pltpu.get_barrier_semaphore()
    for device in devices:
        pl.semaphore_signal(barrier, inc=1, device_id=device, device_id_type=MESH)
    pl.semaphore_wait(barrier, len(devices))


def line_of(z, contexts):
    return [{"context": lax.rem(z + by, contexts)} for by in range(1, contexts)]


def front_kernel(
    contexts,
    gains,
    tokens,
    cotangent_h,
    query_down_h,
    latent_down_t,
    query_up_h,
    latent_up_h,
    cos_t,
    sin_t,
    q_t,
    latent,
    latent_t,
    rope_keys,
    rope_keys_t,
    one_inverse,
    query_normed,
    query_inverse,
    query_t,
    cache_t,
    cache_inverse_t,
    one_t,
    feed_t,
    latent_up_t,
    cotangent,
    query_down,
    query_up_t,
    latent_up,
    one,
    low,
    keys,
    far,
    line_sem,
    line_got,
    pair_sem,
    pair_got,
    load_sem,
):
    rows, width = tokens.shape
    loads = [
        pltpu.make_async_copy(src, dst, load_sem.at[i])
        for i, (src, dst) in enumerate(
            [
                (query_down_h, query_down),
                (query_up_h, query_up_t),
                (latent_up_h, latent_up),
                (cotangent_h, cotangent),
            ]
        )
    ]
    for load in loads:
        load.start()
    rank = query_down.shape[1]
    kv = cache_t.shape[0]
    z = lax.axis_index("context")
    t = lax.axis_index("tensor")
    bit = lax.rem(t, 2)
    pair = t + 1 - 2 * bit
    gain_one = slice(0, width)
    gain_query = slice(2 * width, 2 * width + rank)
    gain_latent = slice(2 * width + rank, 2 * width + rank + kv)
    greet([{"tensor": pair}] + line_of(z, contexts))

    @pl.loop(0, rows // 32)
    def _(i):
        r = pl.ds(pl.multiple_of(i * 32, 32), 32)
        value = tokens[r, :].astype(F32)
        inverse = lax.rsqrt(jnp.mean(value * value, axis=-1, keepdims=True) + EPS)
        one_inverse[r, :] = inverse
        one[r, :] = (value * inverse * gains[:, gain_one]).astype(BF16)

    raw = times_transposed(latent_down_t[...], one[...])
    lat = raw[:kv]
    inverse = lax.rsqrt(jnp.mean(lat * lat, axis=0, keepdims=True) + EPS)
    cache_inverse_t[...] = inverse
    lat = lat * inverse
    cache_t[...] = lat.astype(BF16)
    column = jnp.broadcast_to(gains[:, gain_latent], (8, kv)).T[:, 0:1]
    keys[0:kv, :] = (lat * column).astype(BF16)
    first = raw[kv : kv + 16]
    second = raw[kv + 16 :]
    cosine = cos_t[...]
    sine = sin_t[...]
    keys[kv : kv + 16, :] = (first * cosine - second * sine).astype(BF16)
    keys[kv + 16 :, :] = (second * cosine + first * sine).astype(BF16)

    part = keys.shape[0] // 2
    mine = pl.ds(pl.multiple_of(bit * part, 16), part)
    sends = [
        pltpu.make_async_remote_copy(
            src_ref=keys.at[mine],
            dst_ref=far.at[bit, by - 1],
            send_sem=line_sem.at[by - 1],
            recv_sem=line_got.at[by - 1],
            device_id={"context": lax.rem(z + by, contexts)},
            device_id_type=MESH,
        )
        for by in range(1, contexts)
    ]
    for copy in sends:
        copy.start()

    loads[0].wait()
    low[...] = matmul(one[...], query_down[...])

    @pl.loop(0, rows // 32)
    def _(i):
        r = pl.ds(pl.multiple_of(i * 32, 32), 32)
        value = low[r, :]
        inverse = lax.rsqrt(jnp.mean(value * value, axis=-1, keepdims=True) + EPS)
        query_inverse[r, :] = inverse
        value = value * inverse
        query_normed[r, :] = value.astype(BF16)
        low[r, :] = value * gains[:, gain_query]

    query = low[...].astype(BF16)
    query_t[...] = query.T
    heads = q_t.shape[0]
    loads[1].wait()
    for h in range(heads):
        full = times_transposed(query_up_t[h * 96 : (h + 1) * 96, :], query)
        first = full[64:80]
        second = full[80:96]
        q_t[h, 0:64, :] = full[0:64].astype(BF16)
        q_t[h, 64:80, :] = (first * cosine - second * sine).astype(BF16)
        q_t[h, 80:96, :] = (second * cosine + first * sine).astype(BF16)

    for copy in sends:
        copy.wait_recv()
    share = pltpu.make_async_remote_copy(
        src_ref=far.at[bit],
        dst_ref=far.at[bit],
        send_sem=pair_sem,
        recv_sem=pair_got,
        device_id={"tensor": pair},
        device_id_type=MESH,
    )
    share.start()

    loads[2].wait()
    latent_up_t[...] = latent_up[...].T
    loads[3].wait()

    @pl.loop(0, width // 256)
    def _(i):
        lines = pl.ds(pl.multiple_of(i * 256, 256), 256)
        one_t[lines, :] = one[:, lines].T
        feed_t[lines, :] = (RESIDUAL * cotangent[:, lines].astype(F32)).astype(BF16).T

    share.wait_recv()
    latent_t[:, 0:rows] = keys[0:kv, :]
    rope_keys_t[:, 0:rows] = keys[kv:, :]
    for s in range(1, contexts):
        cols = slice(s * rows, (s + 1) * rows)
        latent_t[0:part, cols] = far[0, s - 1]
        latent_t[part:, cols] = far[1, s - 1, 0 : kv - part, :]
        rope_keys_t[:, cols] = far[1, s - 1, kv - part :, :]
    latent[...] = latent_t[...].T
    rope_keys[...] = jnp.concatenate(
        [rope_keys_t[...], jnp.zeros((128 - ROPE, rope_keys_t.shape[1]), BF16)], axis=0
    ).T
    for copy in sends:
        copy.wait_send()
    share.wait_send()


def front(
    contexts,
    gains,
    tokens,
    cotangent,
    query_down,
    latent_down_t,
    query_up_t,
    latent_up,
    cos_t,
    sin_t,
):
    rows, width = tokens.shape
    rank = query_down.shape[1]
    span = latent_down_t.shape[0]
    heads = query_up_t.shape[0] // 96
    kv = span - ROPE
    keys = contexts * rows
    inside = pl.BlockSpec(memory_space=pltpu.VMEM)
    anywhere = pl.BlockSpec(memory_space=pl.ANY)
    sds = jax.ShapeDtypeStruct
    dma = pltpu.SemaphoreType.DMA
    return pl.pallas_call(
        functools.partial(front_kernel, contexts),
        in_specs=[inside] * 2
        + [anywhere] * 2
        + [inside]
        + [anywhere] * 2
        + [inside] * 2,
        out_specs=[inside] * 14,
        out_shape=[
            sds((heads, 96, rows), BF16),
            sds((keys, kv), BF16),
            sds((kv, keys), BF16),
            sds((keys, 128), BF16),
            sds((ROPE, keys), BF16),
            sds((rows, 1), F32),
            sds((rows, rank), BF16),
            sds((rows, 1), F32),
            sds((rank, rows), BF16),
            sds((kv, rows), BF16),
            sds((1, rows), F32),
            sds((width, rows), BF16),
            sds((width, rows), BF16),
            sds(latent_up.shape[::-1], BF16),
        ],
        scratch_shapes=[
            pltpu.VMEM(cotangent.shape, BF16),
            pltpu.VMEM(query_down.shape, BF16),
            pltpu.VMEM(query_up_t.shape, BF16),
            pltpu.VMEM(latent_up.shape, BF16),
            pltpu.VMEM((rows, width), BF16),
            pltpu.VMEM((rows, rank), F32),
            pltpu.VMEM((span, rows), BF16),
            pltpu.VMEM((2, contexts - 1, span // 2, rows), BF16),
            dma((contexts - 1,)),
            dma((contexts - 1,)),
            dma,
            dma,
            dma((4,)),
        ],
        compiler_params=pltpu.CompilerParams(
            collective_id=3, has_side_effects=True, vmem_limit_bytes=60 * 1024 * 1024
        ),
        cost_estimate=pl.CostEstimate(
            flops=2 * rows * width * 1200, bytes_accessed=30 * 1024 * 1024, transcendentals=0
        ),
        name="front",
    )(
        gains,
        tokens,
        cotangent,
        query_down,
        latent_down_t,
        query_up_t,
        latent_up,
        cos_t,
        sin_t,
    )


def load_heads(heads, latent, rope_keys, latent_up, q_t, kcat, q_wide):
    for h in range(heads):
        kcat[h, :, :128] = matmul(latent[...], latent_up[:, h * 128 : (h + 1) * 128]).astype(BF16)
        kcat[h, :, 128:] = rope_keys[...]
        q_wide[h, 0:64, :] = q_t[h, 0:64, :]
        q_wide[h, 64:128, :] = jnp.zeros((64, q_wide.shape[2]), BF16)
        q_wide[h, 128:160, :] = q_t[h, 64:96, :]
        q_wide[h, 160:256, :] = jnp.zeros((96, q_wide.shape[2]), BF16)


def causal():
    key_row = lax.broadcasted_iota(jnp.int32, (HALF, HALF), 0)
    query_col = lax.broadcasted_iota(jnp.int32, (HALF, HALF), 1)
    return key_row <= query_col


def fold(value, op):
    return op(value.reshape(HALF // 8, 8, value.shape[-1]), axis=0)


def forward_kernel(
    heads,
    contexts,
    order,
    q_t,
    latent,
    latent_t,
    rope_keys,
    latent_up,
    latent_up_t,
    joined_t,
    exact_t,
    lse,
    kcat,
    v_t,
    q_wide,
    scores,
    top,
    total,
    acc,
    lies,
):
    z = lax.axis_index("context")
    for i in range(2 * contexts):
        slot = lax.rem(z + contexts - i // 2, contexts)
        lies[order[i]] = slot * (2 * HALF) + (i % 2) * HALF
    load_heads(heads, latent, rope_keys, latent_up, q_t, kcat, q_wide)
    for h in range(heads):
        v_t[h] = matmul(latent_up_t[h * 128 + 64 : (h + 1) * 128, :], latent_t[...]).astype(BF16)
    factor = SCALE * LOG2E
    for block in range(2):
        cols = slice(block * HALF, (block + 1) * HALF)
        position = order[2 * z + block]

        def score(j, masked):
            rows = pl.ds(pl.multiple_of(lies[j], HALF), HALF)
            spot = pl.ds(pl.multiple_of(j * HALF, HALF), HALF)
            for h in range(heads):
                s = matmul(kcat[h, rows, :], q_wide[h, :, cols])
                if masked:
                    s = jnp.where(causal(), s, -1e30)
                scores[h, spot, :] = s
                peak = fold(s, jnp.max)
                top[h] = peak if masked else jnp.maximum(top[h], peak)

        score(position, True)

        @pl.loop(0, position)
        def _(j):
            score(j, False)

        for h in range(heads):
            peak = jnp.max(top[h], axis=0, keepdims=True) * factor
            top[h] = jnp.broadcast_to(peak, (8, HALF))
            total[h] = jnp.zeros((8, HALF), F32)
            acc[h] = jnp.zeros((V_DIM, HALF), F32)

        @pl.loop(0, position + 1)
        def _(j):
            rows = pl.ds(pl.multiple_of(lies[j], HALF), HALF)
            spot = pl.ds(pl.multiple_of(j * HALF, HALF), HALF)
            for h in range(heads):
                p = jnp.exp2(scores[h, spot, :] * factor - top[h, 0:1, :])
                total[h] += fold(p, jnp.sum)
                acc[h] += matmul(v_t[h, :, rows], p.astype(BF16))

        for h in range(heads):
            summed = jnp.sum(total[h], axis=0, keepdims=True)
            out = acc[h] / summed
            joined_t[h * V_DIM : (h + 1) * V_DIM, cols] = out.astype(BF16)
            exact_t[h, :, cols] = out
            lse[h, :, cols] = top[h, 0:1, :] + jnp.log2(summed)


def whole_spec(shape):
    return pl.BlockSpec(shape, lambda g: (0,) * len(shape))


def attention_forward(contexts, order, q_t, latent, latent_t, rope_keys, latent_up, latent_up_t):
    count, _, rows = q_t.shape
    keys = latent.shape[0]
    heads = GROUP
    flops = 2 * count * rows * keys * 384
    return pl.pallas_call(
        functools.partial(forward_kernel, heads, contexts),
        grid=(count // heads,),
        in_specs=[
            pl.BlockSpec(memory_space=pltpu.SMEM),
            pl.BlockSpec((heads, 96, rows), lambda g: (g, 0, 0)),
            whole_spec((keys, KV_RANK)),
            whole_spec((KV_RANK, keys)),
            whole_spec((keys, 128)),
            pl.BlockSpec((KV_RANK, heads * 128), lambda g: (0, g)),
            pl.BlockSpec((heads * 128, KV_RANK), lambda g: (g, 0)),
        ],
        out_specs=[
            pl.BlockSpec((heads * V_DIM, rows), lambda g: (g, 0)),
            pl.BlockSpec((heads, V_DIM, rows), lambda g: (g, 0, 0)),
            pl.BlockSpec((heads, 1, rows), lambda g: (g, 0, 0)),
        ],
        out_shape=[
            jax.ShapeDtypeStruct((count * V_DIM, rows), BF16),
            jax.ShapeDtypeStruct((count, V_DIM, rows), F32),
            jax.ShapeDtypeStruct((count, 1, rows), F32),
        ],
        scratch_shapes=[
            pltpu.VMEM((heads, keys, 256), BF16),
            pltpu.VMEM((heads, V_DIM, keys), BF16),
            pltpu.VMEM((heads, 256, rows), BF16),
            pltpu.VMEM((heads, keys, HALF), F32),
            pltpu.VMEM((heads, 8, HALF), F32),
            pltpu.VMEM((heads, 8, HALF), F32),
            pltpu.VMEM((heads, V_DIM, HALF), F32),
            pltpu.SMEM((keys // HALF,), jnp.int32),
        ],
        compiler_params=pltpu.CompilerParams(vmem_limit_bytes=56 * 1024 * 1024),
        cost_estimate=pl.CostEstimate(
            flops=flops, bytes_accessed=12 * 1024 * 1024, transcendentals=count * rows * keys
        ),
        name="attention_forward",
    )(order, q_t, latent, latent_t, rope_keys, latent_up, latent_up_t)


def cuts(size, step=512):
    count = max(1, size // step)
    edges = [i * step for i in range(count)] + [size]
    return list(zip(edges[:-1], edges[1:]))


def feed_forward_kernel(
    contexts,
    tensors,
    joined_t,
    tokens,
    cotangent,
    gain,
    attn_out_h,
    down_h,
    gate_h,
    up_h,
    feed_t_h,
    branch_o,
    two_o,
    hidden_o,
    dgate_o,
    dup_o,
    feed_o,
    dmiddle_o,
    dbranch_o,
    feed_all_o,
    far_two_o,
    far_dgate_o,
    near_o,
    dmix_t,
    gain_o,
    attn_out,
    down,
    gate_w,
    up_w,
    part,
    final,
    near,
    across,
    dhid,
    two,
    trio,
    feed,
    dmiddle,
    load_sem,
    save_sem,
    send_sem,
    recv_sem,
    pair_sem,
    pair_got,
    line_sem,
    line_got,
    turn_sem,
    turn_got,
    keep_sem,
    give_sem,
    give_got,
):
    rows, width = tokens.shape
    half = width // 2
    t = lax.axis_index("tensor")
    bit = lax.rem(t, 2)
    pair = t + 1 - 2 * bit
    others = [pair]
    step = 2
    while step < tensors:
        others.append(t + step - 2 * step * lax.rem(t // step, 2))
        step *= 2

    loads = [
        pltpu.make_async_copy(src, dst, load_sem.at[i])
        for i, (src, dst) in enumerate(
            [(attn_out_h, attn_out), (down_h, down), (gate_h, gate_w), (up_h, up_w)]
        )
    ]
    for load in loads:
        load.start()

    d = lax.axis_index("dp")
    z = lax.axis_index("context")
    greet([{"tensor": i} for i in others] + line_of(z, contexts) + [{"dp": 1 - d}])

    share = half // contexts

    part_share = share // 2

    def turn(e, by):
        owner = lax.rem(z + by, contexts)
        if by == 0:
            src = feed_t_h.at[pl.ds(pl.multiple_of(e * half + owner * share, 16), share)]
            dst = feed_all_o.at[e * share : (e + 1) * share, 0:rows]
            return pltpu.make_async_copy(src, dst, keep_sem.at[e])
        first = e * half + owner * share + bit * part_share
        src = feed_t_h.at[pl.ds(pl.multiple_of(first, 16), part_share)]
        lines = pl.ds(pl.multiple_of(e * share + bit * part_share, 16), part_share)
        dst = feed_all_o.at[lines, by * rows : (by + 1) * rows]
        return pltpu.make_async_remote_copy(
            src_ref=src,
            dst_ref=dst,
            send_sem=turn_sem.at[e, by - 1],
            recv_sem=turn_got.at[e, by - 1],
            device_id={"context": owner},
            device_id_type=MESH,
        )

    turns = [turn(e, by) for e in range(2) for by in range(contexts)]
    for copy in turns:
        copy.start()

    def to_pair(ref, i):
        return pltpu.make_async_remote_copy(
            src_ref=ref,
            dst_ref=ref,
            send_sem=give_sem.at[i],
            recv_sem=give_got.at[i],
            device_id={"tensor": pair},
            device_id_type=MESH,
        )

    def turn_pair(e):
        lines = pl.ds(pl.multiple_of(e * share + bit * part_share, 16), part_share)
        return to_pair(feed_all_o.at[lines, rows:], e)

    def two_pair(c):
        lines = pl.ds(pl.multiple_of(c * CHUNK + bit * (CHUNK // 2), 16), CHUNK // 2)
        return to_pair(far_two_o.at[lines], 2 + c)

    def send(src, dst, job, kind, c, device):
        return pltpu.make_async_remote_copy(
            src_ref=src,
            dst_ref=dst,
            send_sem=send_sem.at[job, kind, c],
            recv_sem=recv_sem.at[job, kind, c],
            device_id={"tensor": device},
            device_id_type=MESH,
        )

    def span(c):
        return pl.ds(c * CHUNK, CHUNK)

    last = len(others)

    def hop(job, c, kind):
        if kind == 0:
            return send(
                part.at[1 - bit, span(c)], near.at[job, span(c)], job, 0, c, pair
            )
        if kind == last:
            here = final.at[job, bit, span(c)]
            return send(here, here, job, last, c, pair)
        src = near if kind == 1 else across.at[kind - 2]
        return send(
            src.at[job, span(c)], across.at[kind - 1, job, span(c)], job, kind, c, others[kind]
        )

    def reduce_pair(job, c):
        hop(job, c, 0).wait_recv()

        @pl.loop(0, CHUNK // 32)
        def _(i):
            r = pl.ds(pl.multiple_of(c * CHUNK + i * 32, 32), 32)
            near[job, r, :] = (
                near[job, r, :].astype(F32) + part[bit, r, :].astype(F32)
            ).astype(BF16)

        hop(job, c, 1).start()

    def reduce_across(job, c):
        for kind in range(1, last):
            hop(job, c, kind).wait_recv()
            src = near if kind == 1 else across.at[kind - 2]
            ending = kind == last - 1

            @pl.loop(0, CHUNK // 32)
            def _(i):
                r = pl.ds(pl.multiple_of(c * CHUNK + i * 32, 32), 32)
                value = (
                    src[job, r, :].astype(F32) + across[kind - 1, job, r, :].astype(F32)
                ).astype(BF16)
                if ending:
                    final[job, bit, r, :] = value
                else:
                    across[kind - 1, job, r, :] = value

            hop(job, c, kind + 1).start()
        hop(job, c, last).wait_recv()

    def middle_rows(r):
        parts = []
        for h in range(2):
            cols = slice(h * half, (h + 1) * half)
            parts.append(
                tokens[r, cols].astype(F32) + RESIDUAL * final[0, h, r, :].astype(F32)
            )
        square = sum(jnp.sum(p * p, axis=-1, keepdims=True) for p in parts)
        inverse = lax.rsqrt(square * (1.0 / width) + EPS)
        return parts, inverse

    def across_pair(c, kind):
        if kind == 0:
            lines = pl.ds(pl.multiple_of(bit * (CHUNK // 2), 16), CHUNK // 2)
            src = two.at[lines, pl.ds(pl.multiple_of((1 - d) * half, 128), half)]
            lines = pl.ds(pl.multiple_of(c * CHUNK + bit * (CHUNK // 2), 16), CHUNK // 2)
            dst = far_two_o.at[lines]
        else:
            src, dst = trio.at[1, span(c)], far_dgate_o.at[span(c)]
        return pltpu.make_async_remote_copy(
            src_ref=src,
            dst_ref=dst,
            send_sem=pair_sem.at[kind, c],
            recv_sem=pair_got.at[kind, c],
            device_id={"dp": 1 - d},
            device_id_type=MESH,
        )

    def along_line(c, way):
        return pltpu.make_async_remote_copy(
            src_ref=trio.at[0, span(c)],
            dst_ref=near_o.at[way, span(c)],
            send_sem=line_sem.at[way, c],
            recv_sem=line_got.at[way, c],
            device_id={"context": z + 1 - 2 * way},
            device_id_type=MESH,
        )

    chunks = rows // CHUNK
    loads[0].wait()
    for c in range(chunks):
        left = joined_t[:, c * CHUNK : (c + 1) * CHUNK]

        for turn_of in range(2):
            side = 1 - bit if turn_of == 0 else bit

            @pl.loop(0, half // 256)
            def _(n):
                cols = pl.ds(pl.multiple_of(side * half + n * 256, 256), 256)
                place = pl.ds(pl.multiple_of(n * 256, 256), 256)
                part[side, span(c), place] = transposed_times(left, attn_out[:, cols]).astype(BF16)

            if turn_of == 0:
                hop(0, c, 0).start()
    for c in range(chunks):
        reduce_pair(0, c)

    loads[1].wait()
    for c in range(chunks):

        @pl.loop(0, CHUNK // 32)
        def _(i):
            r = pl.ds(pl.multiple_of(c * CHUNK + i * 32, 32), 32)
            o = pl.ds(pl.multiple_of(i * 32, 32), 32)
            two[o, :] = (RESIDUAL * cotangent[r, :].astype(F32)).astype(BF16)

        for a, b in cuts(down.shape[0]):
            dhid[span(c), a:b] = times_transposed(two[...], down[a:b, :]).astype(BF16)

    loads[2].wait()
    loads[3].wait()
    saves = []

    def save(src, dst):
        copy = pltpu.make_async_copy(src, dst, save_sem.at[len(saves)])
        copy.start()
        saves.append(copy)
        return copy

    two_saved = None
    for c in range(chunks):
        reduce_across(0, c)
        if c > 0:
            reduce_pair(1, c - 1)
        if two_saved is not None:
            two_saved.wait()
            across_pair(c - 1, 0).wait_send()

        @pl.loop(0, CHUNK // 32)
        def _(i):
            r = pl.ds(pl.multiple_of(c * CHUNK + i * 32, 32), 32)
            o = pl.ds(pl.multiple_of(i * 32, 32), 32)
            parts, inverse = middle_rows(r)
            for h in range(2):
                cols = slice(h * half, (h + 1) * half)
                two[o, cols] = (parts[h] * inverse * gain[:, width + h * half : width + (h + 1) * half]).astype(BF16)

        two_saved = save(two, two_o.at[span(c)])
        across_pair(c, 0).start()
        for a, b in cuts(gate_w.shape[0]):
            gate = times_transposed(two[...], gate_w[a:b, :])
            upper = times_transposed(two[...], up_w[a:b, :])
            grad = dhid[span(c), a:b].astype(F32)
            sigma = 1.0 / (1.0 + jnp.exp(-gate))
            act = gate * sigma
            trio[0, span(c), a:b] = (act * upper).astype(BF16)
            trio[1, span(c), a:b] = (
                grad * upper * sigma * (1.0 + gate * (1.0 - sigma))
            ).astype(BF16)
            trio[2, span(c), a:b] = (grad * act).astype(BF16)
        for k, out in enumerate((hidden_o, dgate_o, dup_o)):
            save(trio.at[k, span(c)], out.at[span(c)])
        across_pair(c, 1).start()

        @pl.when(z < contexts - 1)
        def _():
            along_line(c, 0).start()

        @pl.when(z > 0)
        def _():
            along_line(c, 1).start()

        hop(0, c, 0).wait_send()

        for turn_of in range(2):
            side = 1 - bit if turn_of == 0 else bit

            @pl.loop(0, half // 256)
            def _(n):
                cols = pl.ds(pl.multiple_of(side * half + n * 256, 256), 256)
                place = pl.ds(pl.multiple_of(n * 256, 256), 256)
                value = matmul(trio[1, span(c), :], gate_w[:, cols])
                value += matmul(trio[2, span(c), :], up_w[:, cols])
                part[side, span(c), place] = value.astype(BF16)

            if turn_of == 0:
                hop(1, c, 0).start()
    reduce_pair(1, chunks - 1)
    two_saved.wait()

    for e in range(2):
        for by in range(1, contexts):
            turns[e * contexts + by].wait_recv()
        turn_pair(e).start()
    for c in range(chunks):
        across_pair(c, 0).wait_recv()
        two_pair(c).start()

    gain_o[...] = jnp.zeros_like(gain_o)
    feed_saved = dmiddle_saved = dbranch_saved = None
    for c in range(chunks):
        if feed_saved is not None:
            feed_saved.wait()

        @pl.loop(0, width // 256)
        def _(n):
            cols = pl.ds(pl.multiple_of(n * 256, 256), 256)
            feed[:, cols] = matmul(trio[0, span(c), :], down[:, cols]).astype(BF16)

        feed_saved = save(feed, feed_o.at[span(c)])
        reduce_across(1, c)
        if dmiddle_saved is not None:
            dmiddle_saved.wait()
            dbranch_saved.wait()
        else:
            across_pair(chunks - 1, 0).wait_send()

        @pl.loop(0, CHUNK // 32)
        def _(i):
            r = pl.ds(pl.multiple_of(c * CHUNK + i * 32, 32), 32)
            o = pl.ds(pl.multiple_of(i * 32, 32), 32)
            parts, inverse = middle_rows(r)
            dot = jnp.zeros((32, 1), F32)
            for h in range(2):
                cols = slice(h * half, (h + 1) * half)
                product = final[1, h, r, :].astype(F32) * (parts[h] * inverse)
                gain_o[:, cols] += jnp.sum(product.reshape(4, 8, half), axis=0)
                dot += jnp.sum(product * gain[:, width + h * half : width + (h + 1) * half], axis=-1, keepdims=True)
            dot = dot * (1.0 / width)
            for h in range(2):
                cols = slice(h * half, (h + 1) * half)
                weighted = final[1, h, r, :].astype(F32) * gain[:, width + h * half : width + (h + 1) * half]
                value = cotangent[r, cols].astype(F32) + inverse * (
                    weighted - parts[h] * inverse * dot
                )
                dmiddle[o, cols] = value
                two[o, cols] = (RESIDUAL * value).astype(BF16)

        dmiddle_saved = save(dmiddle, dmiddle_o.at[span(c)])
        dbranch_saved = save(two, dbranch_o.at[span(c)])
        dmix_t[:, c * CHUNK : (c + 1) * CHUNK] = times_transposed(attn_out[...], two[...]).astype(
            BF16
        )
    for h in range(2):
        save(final.at[0, h], branch_o.at[:, h * half : (h + 1) * half])
    for copy in saves[-2:] + [feed_saved, dmiddle_saved, dbranch_saved]:
        copy.wait()
    for e in range(2):
        turns[e * contexts].wait()
        for by in range(1, contexts):
            turns[e * contexts + by].wait_send()
        turn_pair(e).wait()
    for c in range(chunks):
        for k in range(3):
            saves[c * 4 + 1 + k].wait()
    for c in range(chunks):
        two_pair(c).wait()
        across_pair(c, 1).wait()

        @pl.when(z < contexts - 1)
        def _():
            along_line(c, 0).wait_send()
            along_line(c, 1).wait_recv()

        @pl.when(z > 0)
        def _():
            along_line(c, 1).wait_send()
            along_line(c, 0).wait_recv()

    for job in range(2):
        for c in range(chunks):
            for kind in range(1 - job, last + 1):
                hop(job, c, kind).wait_send()


def feed_forward(contexts, tensors, joined_t, tokens, cotangent, gain, attn_out, down, gate_w, up_w, feed_t):
    rows, width = tokens.shape
    units = down.shape[0]
    chunks = rows // CHUNK
    hops = tensors.bit_length() - 1
    anywhere = pl.BlockSpec(memory_space=pl.ANY)
    inside = pl.BlockSpec(memory_space=pltpu.VMEM)
    return pl.pallas_call(
        functools.partial(feed_forward_kernel, contexts, tensors),
        in_specs=[inside] * 4 + [anywhere] * 5,
        out_specs=[anywhere] * 12 + [inside] * 2,
        out_shape=[
            jax.ShapeDtypeStruct((rows, width), BF16),
            jax.ShapeDtypeStruct((rows, width), BF16),
            jax.ShapeDtypeStruct((rows, units), BF16),
            jax.ShapeDtypeStruct((rows, units), BF16),
            jax.ShapeDtypeStruct((rows, units), BF16),
            jax.ShapeDtypeStruct((rows, width), BF16),
            jax.ShapeDtypeStruct((rows, width), F32),
            jax.ShapeDtypeStruct((rows, width), BF16),
            jax.ShapeDtypeStruct((width // contexts, contexts * rows), BF16),
            jax.ShapeDtypeStruct((rows, width // 2), BF16),
            jax.ShapeDtypeStruct((rows, units), BF16),
            jax.ShapeDtypeStruct((2, rows, units), BF16),
            jax.ShapeDtypeStruct((joined_t.shape[0], rows), BF16),
            jax.ShapeDtypeStruct((8, width), F32),
        ],
        scratch_shapes=[
            pltpu.VMEM(attn_out.shape, BF16),
            pltpu.VMEM(down.shape, BF16),
            pltpu.VMEM(gate_w.shape, BF16),
            pltpu.VMEM(up_w.shape, BF16),
            pltpu.VMEM((2, rows, width // 2), BF16),
            pltpu.VMEM((2, 2, rows, width // 2), BF16),
            pltpu.VMEM((2, rows, width // 2), BF16),
            pltpu.VMEM((hops - 1, 2, rows, width // 2), BF16),
            pltpu.VMEM((rows, units), BF16),
            pltpu.VMEM((CHUNK, width), BF16),
            pltpu.VMEM((3, rows, units), BF16),
            pltpu.VMEM((CHUNK, width), BF16),
            pltpu.VMEM((CHUNK, width), F32),
            pltpu.SemaphoreType.DMA((4,)),
            pltpu.SemaphoreType.DMA((7 * chunks + 2,)),
            pltpu.SemaphoreType.DMA((2, hops + 1, chunks)),
            pltpu.SemaphoreType.DMA((2, hops + 1, chunks)),
        ]
        + [pltpu.SemaphoreType.DMA((2, chunks))] * 4
        + [pltpu.SemaphoreType.DMA((2, contexts - 1))] * 2
        + [pltpu.SemaphoreType.DMA((2,))]
        + [pltpu.SemaphoreType.DMA((2 + chunks,))] * 2,
        compiler_params=pltpu.CompilerParams(
            collective_id=0, has_side_effects=True, vmem_limit_bytes=63 * 1024 * 1024
        ),
        cost_estimate=pl.CostEstimate(
            flops=2 * rows * width * units * 6, bytes_accessed=60 * 1024 * 1024, transcendentals=0
        ),
        name="feed_forward",
    )(joined_t, tokens, cotangent, gain, attn_out, down, gate_w, up_w, feed_t)


def backward_kernel(
    contexts,
    group,
    order,
    q_t,
    latent,
    latent_t,
    rope_keys,
    rope_keys_t,
    latent_up,
    latent_up_t,
    exact_t,
    lse,
    dmix_t,
    cos_t,
    sin_t,
    joined_t,
    two_h,
    far_two_h,
    dgate_h,
    far_dgate_h,
    dup_h,
    near_h,
    dbranch_h,
    dq_t,
    grad_up,
    dlat_t,
    gate_o,
    up_o,
    out_o,
    far_out_o,
    far_dup_o,
    spread_o,
    kcat,
    k_t,
    q_wide,
    dmix_wide,
    q_nat,
    dmix_nat,
    delta,
    dq,
    pair,
    lat_acc,
    rope_acc,
    two,
    act,
    gate_w,
    up_w,
    arrived,
    up_arrived,
    out_w,
    joined,
    load_sem,
    dup_sem,
    dup_got,
    out_sem,
    out_got,
    gate_sem,
    gate_got,
    up_sem,
    up_got,
    spread_sem,
    spread_got,
):
    heads, _, rows = q_t.shape
    keys = latent.shape[0]
    tiles = keys // HALF
    last = contexts - 1
    half = two.shape[1]
    share = half // contexts
    d = lax.axis_index("dp")
    z = lax.axis_index("context")
    loads = [
        pltpu.make_async_copy(
            two_h.at[:, pl.ds(pl.multiple_of(d * half, 128), half)],
            two.at[0:rows],
            load_sem.at[0],
        ),
        pltpu.make_async_copy(far_two_h, two.at[rows : 2 * rows], load_sem.at[1]),
        pltpu.make_async_copy(dgate_h, act.at[0:rows], load_sem.at[2]),
        pltpu.make_async_copy(far_dgate_h, act.at[rows : 2 * rows], load_sem.at[3]),
    ]
    for load in loads:
        load.start()
    greet(line_of(z, contexts) + [{"dp": 1 - d}])

    swap_dup = pltpu.make_async_remote_copy(
        src_ref=dup_h,
        dst_ref=far_dup_o,
        send_sem=dup_sem,
        recv_sem=dup_got,
        device_id={"dp": 1 - d},
        device_id_type=MESH,
    )
    swap_dup.start()

    def line(src, dst, send_sem, recv_sem, way):
        return pltpu.make_async_remote_copy(
            src_ref=src,
            dst_ref=dst,
            send_sem=send_sem,
            recv_sem=recv_sem,
            device_id={"context": z + 1 - 2 * way},
            device_id_type=MESH,
        )

    along = [z, last - z]

    def spread(way, step):
        src = near_h.at[way] if step == 2 else spread_o.at[way, step - 3]
        i = (way, step - 2)
        return line(src, spread_o.at[i], spread_sem.at[i], spread_got.at[i], way)

    def spread_start(step):
        if step > last:
            return
        for way in range(2):
            if step > 2:

                @pl.when(along[way] >= step - 1)
                def _():
                    spread(way, step - 1).wait_recv()

            @pl.when((along[way] >= step - 1) & (along[way] < last))
            def _():
                spread(way, step).start()

    def spread_end():
        for way in range(2):
            for step in range(2, last + 1):
                if step == last:

                    @pl.when(along[way] >= step)
                    def _():
                        spread(way, step).wait_recv()

                @pl.when((along[way] >= step - 1) & (along[way] < last))
                def _():
                    spread(way, step).wait_send()

    def share_of(ref, index):
        return ref.at[pl.ds(pl.multiple_of(index * share, 16), share)]

    def farthest(way, step):
        right = z + 2 * contexts - step if way == 0 else contexts + step - 1 - along[1]
        return lax.rem(right, contexts)

    def reduce(ref, dst, send_sem, recv_sem, way, step):
        return line(
            share_of(ref, farthest(way, step)), dst, send_sem, recv_sem, way
        )

    def gate_step(way, step):
        i = (way, step - 1)
        return reduce(gate_w, arrived.at[i], gate_sem.at[i], gate_got.at[i], way, step)

    def up_step(way):
        return reduce(up_w, up_arrived.at[way], up_sem.at[way], up_got.at[way], way, 1)

    def add_rows(dst, src):
        @pl.loop(0, share // 16)
        def _(i):
            r = pl.ds(pl.multiple_of(i * 16, 16), 16)
            dst[r, :] = (dst[r, :].astype(F32) + src[r, :].astype(F32)).astype(BF16)

    def gate_start(step):
        if step > last:
            return
        for way in range(2):
            if step > 1:

                @pl.when((along[way] >= 1) & (along[way] < step))
                def _():
                    gate_step(way, step - 1).wait_recv()
                    add_rows(share_of(gate_w, farthest(way, step)), arrived.at[way, step - 2])

            @pl.when(along[way] < step)
            def _():
                gate_step(way, step).start()

    def gate_end():
        own = pl.multiple_of(z * share, 16)
        for way in range(2):

            @pl.when(along[way] >= 1)
            def _():
                gate_step(way, last).wait_recv()

        @pl.loop(0, share // 16)
        def _(i):
            r = pl.ds(pl.multiple_of(own + i * 16, 16), 16)
            q = pl.ds(pl.multiple_of(i * 16, 16), 16)
            value = gate_w[r, :].astype(F32)
            for way in range(2):
                value = jnp.where(
                    along[way] >= 1, value + arrived[way, last - 1, q, :].astype(F32), value
                )
            gate_o[q, :] = value

        for way in range(2):
            for step in range(1, last + 1):

                @pl.when(along[way] < step)
                def _():
                    gate_step(way, step).wait_send()

    upper = 1 - z // ((contexts + 1) // 2)
    count = half // 256

    def weight(ref, start):
        def tile(i):
            n = i + upper * (count - 1 - 2 * i)
            cols = pl.ds(pl.multiple_of(n * 256, 256), 256)
            ref[cols, :] = transposed_times(two[:, cols], act[...]).astype(BF16)

        pl.loop(0, 2)(tile)
        start()
        pl.loop(2, count)(tile)

    factor = SCALE * LOG2E
    row = lax.broadcasted_iota(jnp.int32, (HALF, rows), 0)
    spot = lax.broadcasted_iota(jnp.int32, (1, rows), 1)
    spot = jnp.where(
        spot < HALF, order[2 * z] * HALF + spot, order[2 * z + 1] * HALF + spot - HALF
    )

    def begin(g):
        for h in range(group):
            e = g * group + h
            span = slice(e * 128, (e + 1) * 128)
            kcat[h, :, :128] = matmul(latent[...], latent_up[:, span]).astype(BF16)
            kcat[h, :, 128:] = rope_keys[...]
            k_t[h, 0:64, :] = matmul(
                latent_up_t[e * 128 : e * 128 + 64, :], latent_t[...]
            ).astype(BF16)
            k_t[h, 64:96, :] = rope_keys_t[...]
            q_wide[h, 0:64, :] = q_t[e, 0:64, :]
            q_wide[h, 64:128, :] = jnp.zeros((64, rows), BF16)
            q_wide[h, 128:160, :] = q_t[e, 64:96, :]
            q_wide[h, 160:256, :] = jnp.zeros((96, rows), BF16)
            q_nat[h] = q_wide[h].T
            piece = dmix_t[e * V_DIM : (e + 1) * V_DIM, :]
            dmix_wide[h, 0:64, :] = jnp.zeros_like(piece)
            dmix_wide[h, 64:128, :] = piece
            dmix_nat[h] = dmix_wide[h].T
            delta[h] = jnp.sum(piece.astype(F32) * exact_t[e], axis=0, keepdims=True)
            dq[h] = jnp.zeros((96, rows), F32)

    def tiles_of(g, first, end):
        lane = lax.broadcasted_iota(jnp.int32, (1, 128), 1)
        scale = jnp.where(lane < NOPE, SCALE, 1.0).astype(F32)

        @pl.loop(first, end)
        def _(j):
            lines = pl.ds(pl.multiple_of(j * HALF, HALF), HALF)
            block = 2 * lax.rem(z + contexts - j // 2, contexts) + lax.rem(j, 2)
            allowed = row <= spot - order[block] * HALF
            turned = jnp.zeros((HALF, 128), F32)
            for h in range(group):
                e = g * group + h
                s = matmul(kcat[h, lines, :], q_wide[h])
                p = jnp.where(allowed, jnp.exp2(s * factor - lse[e]), 0.0)
                dp = matmul(kcat[h, lines, :128], dmix_wide[h])
                ds = (p * (dp - delta[h])).astype(BF16)
                dq[h] += matmul(k_t[h, :, lines], ds)
                dk = matmul(ds, q_nat[h])
                dv = matmul(p.astype(BF16), dmix_nat[h])
                pair[h, lines, :] = ((dk[:, :128] + dv) * scale).astype(BF16)
                turned += dk[:, 128:]
            rope_acc[lines, :] = turned if g == 0 else rope_acc[lines, :] + turned

    def finish(g):
        cosine = cos_t[...]
        sine = sin_t[...]
        for h in range(group):
            e = g * group + h
            span = slice(e * 128, (e + 1) * 128)
            value = dq[h] * SCALE
            first = value[64:80]
            second = value[80:96]
            dq_t[e, 0:64, :] = value[0:64].astype(BF16)
            dq_t[e, 64:80, :] = (first * cosine + second * sine).astype(BF16)
            dq_t[e, 80:96, :] = (second * cosine - first * sine).astype(BF16)
            grad_up[:, span] = matmul(latent_t[...], pair[h]).astype(BF16)
            change = times_transposed(latent_up[:, span], pair[h])
            lat_acc[...] = change if e == 0 else lat_acc[...] + change

    groups = heads // group
    total = groups * tiles
    stops = [total * (i + 1) // (last + 1) for i in range(last)]

    spread_start(2)
    for load in loads:
        load.wait()
    weight(gate_w, lambda: gate_start(1))
    done = 0
    for i, stop in enumerate(stops + [total]):
        while done < stop:
            g = done // tiles
            until = min(stop, (g + 1) * tiles)
            if done == g * tiles:
                begin(g)
            tiles_of(g, done - g * tiles, until - g * tiles)
            if until == (g + 1) * tiles:
                finish(g)
            done = until
        if i < last:
            gate_start(i + 2)
            spread_start(i + 3)
        if i == min(1, last - 1):
            swap_dup.wait_recv()
            again = [
                pltpu.make_async_copy(dup_h, act.at[0:rows], load_sem.at[2]),
                pltpu.make_async_copy(far_dup_o, act.at[rows : 2 * rows], load_sem.at[3]),
            ]
            for load in again:
                load.start()
            for load in again:
                load.wait()

            def up_start():
                for way in range(2):

                    @pl.when(along[way] == 0)
                    def _():
                        up_step(way).start()

            weight(up_w, up_start)
            parts = [
                pltpu.make_async_copy(
                    dbranch_h.at[:, e * half : (e + 1) * half],
                    two.at[e * rows : (e + 1) * rows],
                    load_sem.at[2 + e],
                )
                for e in range(2)
            ]
            for load in parts:
                load.start()
            keep = pltpu.make_async_copy(up_w, up_o, load_sem.at[0])
            keep.start()
            joined[...] = joined_t[...].T
            for load in parts:
                load.wait()
            for e in range(2):

                @pl.loop(0, half // 256)
                def _(n):
                    cols = pl.ds(pl.multiple_of(n * 256, 256), 256)
                    lines = pl.ds(pl.multiple_of(e * half + n * 256, 256), 256)
                    out_w[lines, :] = transposed_times(
                        two[e * rows : (e + 1) * rows, cols], joined[...]
                    ).astype(BF16)

            swap_out = pltpu.make_async_remote_copy(
                src_ref=out_w.at[pl.ds(pl.multiple_of((1 - d) * half, 16), half)],
                dst_ref=far_out_o,
                send_sem=out_sem,
                recv_sem=out_got,
                device_id={"dp": 1 - d},
                device_id_type=MESH,
            )
            swap_out.start()
            keep_out = pltpu.make_async_copy(
                out_w.at[pl.ds(pl.multiple_of(d * half, 16), half)], out_o, load_sem.at[1]
            )
            keep_out.start()

    dlat_t[0:KV_RANK, :] = lat_acc[...].astype(BF16)
    dlat_t[KV_RANK:, :] = (rope_acc[...] * SCALE).T[:ROPE].astype(BF16)
    gate_end()
    spread_end()
    keep.wait()
    keep_out.wait()
    swap_dup.wait_send()
    for way in range(2):

        @pl.when(along[way] == 0)
        def _():
            up_step(way).wait_send()

        @pl.when(along[way] == 1)
        def _():
            up_step(way).wait_recv()
            piece = share_of(up_w, farthest(way, 2))
            add_rows(piece, up_arrived.at[way])
            again = pltpu.make_async_copy(
                piece, share_of(up_o, farthest(way, 2)), load_sem.at[2]
            )
            again.start()
            again.wait()

    swap_out.wait()


def backward(
    contexts,
    order,
    q_t,
    latent,
    latent_t,
    rope_keys,
    rope_keys_t,
    latent_up,
    latent_up_t,
    exact_t,
    lse,
    dmix_t,
    cos_t,
    sin_t,
    joined_t,
    two,
    far_two,
    dgate,
    far_dgate,
    dup,
    near,
    dbranch,
):
    heads, _, rows = q_t.shape
    keys = latent.shape[0]
    group = GROUP
    units = dup.shape[1]
    half = far_two.shape[1]
    share = half // contexts
    last = contexts - 1
    anywhere = pl.BlockSpec(memory_space=pl.ANY)
    inside = pl.BlockSpec(memory_space=pltpu.VMEM)
    dma = pltpu.SemaphoreType.DMA
    return pl.pallas_call(
        functools.partial(backward_kernel, contexts, group),
        in_specs=[pl.BlockSpec(memory_space=pltpu.SMEM)] + [inside] * 13 + [anywhere] * 7,
        out_specs=[inside] * 4 + [anywhere] * 5,
        out_shape=[
            jax.ShapeDtypeStruct((heads, 96, rows), BF16),
            jax.ShapeDtypeStruct((KV_RANK, heads * 128), BF16),
            jax.ShapeDtypeStruct((KV_RANK + ROPE, keys), BF16),
            jax.ShapeDtypeStruct((share, units), F32),
            jax.ShapeDtypeStruct((half, units), BF16),
            jax.ShapeDtypeStruct((half, joined_t.shape[0]), BF16),
            jax.ShapeDtypeStruct((half, joined_t.shape[0]), BF16),
            jax.ShapeDtypeStruct((rows, units), BF16),
            jax.ShapeDtypeStruct((2, last - 1, rows, units), BF16),
        ],
        scratch_shapes=[
            pltpu.VMEM((group, keys, 256), BF16),
            pltpu.VMEM((group, 96, keys), BF16),
            pltpu.VMEM((group, 256, rows), BF16),
            pltpu.VMEM((group, 128, rows), BF16),
            pltpu.VMEM((group, rows, 256), BF16),
            pltpu.VMEM((group, rows, 128), BF16),
            pltpu.VMEM((group, 1, rows), F32),
            pltpu.VMEM((group, 96, rows), F32),
            pltpu.VMEM((group, keys, 128), BF16),
            pltpu.VMEM((KV_RANK, keys), F32),
            pltpu.VMEM((keys, 128), F32),
            pltpu.VMEM((2 * rows, half), BF16),
            pltpu.VMEM((2 * rows, units), BF16),
            pltpu.VMEM((half, units), BF16),
            pltpu.VMEM((half, units), BF16),
            pltpu.VMEM((2, last, share, units), BF16),
            pltpu.VMEM((2, share, units), BF16),
            pltpu.VMEM((2 * half, joined_t.shape[0]), BF16),
            pltpu.VMEM((rows, joined_t.shape[0]), BF16),
            dma((4,)),
            dma,
            dma,
            dma,
            dma,
            dma((2, last)),
            dma((2, last)),
            dma((2,)),
            dma((2,)),
            dma((2, last - 1)),
            dma((2, last - 1)),
        ],
        compiler_params=pltpu.CompilerParams(
            collective_id=1, has_side_effects=True, vmem_limit_bytes=65000 * 1024
        ),
        cost_estimate=pl.CostEstimate(
            flops=2 * heads * rows * keys * 1000,
            bytes_accessed=40 * 1024 * 1024,
            transcendentals=heads * rows * keys,
        ),
        name="backward",
    )(
        order,
        q_t,
        latent,
        latent_t,
        rope_keys,
        rope_keys_t,
        latent_up,
        latent_up_t,
        exact_t,
        lse,
        dmix_t,
        cos_t,
        sin_t,
        joined_t,
        two,
        far_two,
        dgate,
        far_dgate,
        dup,
        near,
        dbranch,
    )


def tail_kernel(
    contexts,
    tensors,
    split,
    dq_t,
    query_up_t,
    query_t,
    query_normed,
    query_inverse,
    all_gains,
    dlat,
    cache_t,
    cache_inverse_t,
    cos_t,
    sin_t,
    lat_grad,
    first_inverse,
    mlp_gain_grad,
    out_h,
    far_out_h,
    hidden_h,
    near_h,
    spread_h,
    feed_t_h,
    up_h,
    one_t_h,
    query_down_h,
    latent_down_t_h,
    tokens_h,
    feed_h,
    norm_o,
    low_q_o,
    low_l_o,
    small_q_o,
    small_l_o,
    out_o,
    up_o,
    down_o,
    gain_o,
    feed_o,
    q_part,
    q_near,
    q_across,
    q_final,
    d_near,
    d_acc,
    d_across,
    d_got,
    d_all,
    d_final,
    u_w,
    u_far,
    u_got,
    l_far,
    l_got,
    wide,
    up_got,
    out_w,
    out_far,
    out_got,
    long,
    feed_t,
    down_w,
    down_far,
    f_part,
    f_near,
    f_across,
    dqa,
    dkva_t,
    one_t,
    low_q,
    low_l,
    low_q_far,
    low_l_far,
    low_q_got,
    low_l_got,
    low_q_all,
    low_l_all,
    query_down,
    latent_down_t,
    dh1,
    stage,
    gains,
    gains_far,
    gains_got,
    send_sem,
    recv_sem,
    load_sem,
):
    rows = dlat.shape[1] // contexts
    width = wide.shape[1]
    half = width // 2
    share = half // contexts
    last = contexts - 1
    rank = query_normed.shape[1]
    kv = cache_t.shape[0]
    first_gain = slice(0, width)
    query_gain = slice(2 * width, 2 * width + rank)
    latent_gain = slice(2 * width + rank, 2 * width + rank + kv)
    d = lax.axis_index("dp")
    z = lax.axis_index("context")
    t = lax.axis_index("tensor")
    bit = lax.rem(t, 2)
    others = [t + 1 - 2 * bit]
    step = 2
    while step < tensors:
        others.append(t + step - 2 * step * lax.rem(t // step, 2))
        step *= 2
    spot = lax.rem(t, split)
    sharers = [t - spot + lax.rem(spot + k, split) for k in range(1, split)]

    used = [0]

    def remote(src, dst, **device):
        i = used[0]
        used[0] += 1
        return pltpu.make_async_remote_copy(
            src_ref=src,
            dst_ref=dst,
            send_sem=send_sem.at[i],
            recv_sem=recv_sem.at[i],
            device_id=device,
            device_id_type=MESH,
        )

    loaded = [0]

    def local(src, dst):
        i = loaded[0]
        loaded[0] += 1
        return pltpu.make_async_copy(src, dst, load_sem.at[i])

    def only(condition, copy, what):
        @pl.when(condition)
        def _():
            getattr(copy, what)()

    def add_rows(dst, left, right, count, chunk=16):
        @pl.loop(0, count // chunk)
        def _(i):
            r = pl.ds(pl.multiple_of(i * chunk, chunk), chunk)
            dst[r, :] = (left[r, :].astype(F32) + right[r, :].astype(F32)).astype(BF16)

    def piece(ref, index, size):
        return ref.at[pl.ds(pl.multiple_of(index * size, 16), size)]

    load_out = [local(out_h, out_w), local(far_out_h, out_far)]
    load_tokens = local(tokens_h, wide)
    load_hidden = [(None, local(hidden_h, long.at[0:rows]))]
    for s in range(1, contexts):
        back = contexts - s
        dst = long.at[s * rows : (s + 1) * rows]
        right = near_h.at[0] if s == 1 else spread_h.at[0, s - 2]
        left = near_h.at[1] if back == 1 else spread_h.at[1, back - 2]
        load_hidden.append((z >= s, local(right, dst)))
        load_hidden.append((z < s, local(left, dst)))
    load_feed_t = local(feed_t_h, feed_t)
    load_one = local(one_t_h, one_t)
    load_down = [local(query_down_h, query_down), local(latent_down_t_h, latent_down_t)]

    def load_feed(c):
        return [
            local(
                feed_h.at[pl.ds(c * CHUNK, CHUNK), h * half : (h + 1) * half], f_part.at[h]
            )
            for h in range(2)
        ]

    feed_loads = [load_feed(c) for c in range(rows // CHUNK)]
    for copy in load_out:
        copy.start()
    load_feed_t.start()
    for condition, copy in load_hidden:
        if condition is None:
            copy.start()
        else:
            only(condition, copy, "start")
    for copy in [load_one, load_tokens] + load_down + feed_loads[0]:
        copy.start()

    peers = others if split == 2 else sharers
    greet([{"tensor": i} for i in peers] + line_of(z, contexts) + [{"dp": 1 - d}])

    along = [z, last - z]

    def farthest(way, step):
        right = z + 2 * contexts - step if way == 0 else contexts + step - 1 - along[1]
        return lax.rem(right, contexts)

    def line_step(w, got, way, step, first):
        return remote(
            piece(w, farthest(way, step), share),
            got.at[way, step - first],
            context=z + 1 - 2 * way,
        )

    up_w = long
    up_steps = {
        (way, step): line_step(up_h if step == 2 else up_w, up_got, way, step, 2)
        for way in range(2)
        for step in range(2, last + 1)
    }
    out_steps = {
        (way, step): line_step(out_far, out_got, way, step, 1)
        for way in range(2)
        for step in range(1, last + 1)
    }

    def line_start(steps, w, got, first, step):
        for way in range(2):
            if step > first:

                @pl.when((along[way] >= 1) & (along[way] < step))
                def _():
                    steps[way, step - 1].wait_recv()
                    target = piece(w, farthest(way, step), share)
                    add_rows(target, target, got.at[way, step - 1 - first], share)

            only(along[way] < step, steps[way, step], "start")

    def line_end(steps, w, got, first, result):
        for way in range(2):
            only(along[way] >= 1, steps[way, last], "wait_recv")

        @pl.loop(0, share // 16)
        def _(i):
            r = pl.ds(pl.multiple_of(z * share + i * 16, 16), 16)
            q = pl.ds(pl.multiple_of(i * 16, 16), 16)
            value = w[r, :].astype(F32)
            for way in range(2):
                value = jnp.where(
                    along[way] >= 1, value + got[way, last - first, q, :].astype(F32), value
                )
            result[q, :] = value

        for way in range(2):
            for step in range(first, last + 1):
                only(along[way] < step, steps[way, step], "wait_send")

    line_start(up_steps, up_w, up_got, 2, 2)

    d_rows = dlat.shape[0] // 2
    d_pair = remote(dlat.at[pl.ds(pl.multiple_of((1 - bit) * d_rows, 16), d_rows)], d_near, tensor=others[0])
    d_pair.start()

    q_rows = rows // 2
    for h in range(2):
        q_part[h] = transposed_times(
            dq_t[:, h * q_rows : (h + 1) * q_rows], query_up_t[...]
        ).astype(BF16)
    q_pair = remote(q_part.at[1 - bit], q_near, tensor=others[0])
    q_pair.start()

    for copy in load_out:
        copy.wait()
    add_rows(out_far, out_far, out_w, half, 32)
    line_start(out_steps, out_far, out_got, 1, 1)

    u_w[...] = times_transposed(query_t[...], dq_t[...]).astype(BF16)
    u_half = u_w.shape[0] // 2
    l_half = lat_grad.shape[0] // 2
    u_pair = remote(
        u_w.at[pl.ds(pl.multiple_of((1 - d) * u_half, 16), u_half)], u_far, dp=1 - d
    )
    l_pair = remote(
        lat_grad.at[pl.ds(pl.multiple_of((1 - d) * l_half, 16), l_half)], l_far, dp=1 - d
    )
    u_pair.start()
    l_pair.start()

    d_pair.wait_recv()
    mine = pl.multiple_of(bit * d_rows, 16)

    @pl.loop(0, d_rows // 16)
    def _(i):
        r = pl.ds(pl.multiple_of(i * 16, 16), 16)
        own = pl.ds(pl.multiple_of(mine + i * 16, 16), 16)
        value = (dlat[own, :].astype(F32) + d_near[r, :].astype(F32)).astype(BF16)
        for s in range(contexts):
            d_acc[s, r, :] = value[:, s * rows : (s + 1) * rows]

    d_hops = []
    lanes = rows
    start = 0
    for k in range(1, len(others)):
        lanes //= 2
        side = lax.rem(t // (2**k), 2)
        give = pl.ds(pl.multiple_of(start + (1 - side) * lanes, 128), lanes)
        start = pl.multiple_of(start + side * lanes, 128)
        d_hops.append(
            (remote(d_acc.at[:, :, give], d_across.at[k - 1, :, :, 0:lanes], tensor=others[k]),
             start, lanes)
        )

    d_hops[0][0].start()
    q_pair.wait_recv()
    add_rows(q_near, q_near, q_part.at[bit], q_rows, 32)
    q_hops = []
    for k in range(1, len(others)):
        src = q_near if k == 1 else q_across.at[k - 2]
        q_hops.append(remote(src, q_across.at[k - 1], tensor=others[k]))
    q_hops[0].start()

    load_feed_t.wait()
    for condition, copy in load_hidden:
        if condition is None:
            copy.wait()
        else:
            only(condition, copy, "wait")
    chunk = 2 * share // 5 if (2 * share // 5) % 16 == 0 else share

    @pl.loop(0, 2 * share // chunk)
    def _(i):
        r = pl.ds(pl.multiple_of(i * chunk, 16), chunk)
        down_w[r, :] = matmul(feed_t[r, :], long[...]).astype(BF16)

    load_up = local(up_h, long.at[0:half])
    load_up.start()
    down_pair = remote(piece(down_w, 1 - d, share), down_far, dp=1 - d)

    f_pairs, f_hops, f_backs = [], [], []
    for c in range(rows // CHUNK):
        span = pl.ds(c * CHUNK, CHUNK)
        f_pairs.append(remote(f_part.at[1 - bit], f_near.at[c], tensor=others[0]))
        hops = []
        for k in range(1, len(others)):
            src = f_near.at[c] if k == 1 else f_across.at[k - 2, c]
            hops.append(remote(src, f_across.at[k - 1, c], tensor=others[k]))
        f_hops.append(hops)
        here = f_across.at[len(others) - 2, c]
        f_backs.append(
            (remote(here, feed_o.at[span, pl.ds(pl.multiple_of(bit * half, 128), half)], tensor=others[0]), local(here, feed_o.at[span, pl.ds(pl.multiple_of(bit * half, 128), half)]))
        )

    def feed_pair(c):
        for copy in feed_loads[c]:
            copy.wait()
        f_pairs[c].start()

    def feed_across(c):
        f_pairs[c].wait_recv()
        add_rows(f_near.at[c], f_near.at[c], f_part.at[bit], CHUNK, 32)
        f_hops[c][0].start()
        f_pairs[c].wait_send()
        if c + 1 < rows // CHUNK:
            for copy in feed_loads[c + 1]:
                copy.start()

    def feed_back(c):
        for k, hop in enumerate(f_hops[c]):
            hop.wait_recv()
            src = f_near.at[c] if k == 0 else f_across.at[k - 1, c]
            add_rows(f_across.at[k, c], src, f_across.at[k, c], CHUNK, 32)
            if k < len(f_hops[c]) - 1:
                f_hops[c][k + 1].start()
        for back in f_backs[c]:
            back.start()


    for k, (hop, begin, lane) in enumerate(d_hops):
        hop.wait_recv()
        keep = pl.ds(begin, lane)

        @pl.loop(0, contexts)
        def _(s):
            @pl.loop(0, d_rows // 16)
            def _(i):
                r = pl.ds(pl.multiple_of(i * 16, 16), 16)
                d_acc[s, r, keep] = (
                    d_acc[s, r, keep].astype(F32) + d_across[k, s, r, 0:lane].astype(F32)
                ).astype(BF16)

        if k + 1 < len(d_hops):
            d_hops[k + 1][0].start()
    keep = pl.ds(start, lanes)
    d_sends = [
        remote(
            d_acc.at[s, :, keep],
            d_got.at[s - 1],
            context=lax.rem(z + contexts - s, contexts),
        )
        for s in range(1, contexts)
    ]
    for copy in d_sends:
        copy.start()
    final = len(q_hops) - 1
    for k, hop in enumerate(q_hops):
        hop.wait_recv()
        src = q_near if k == 0 else q_across.at[k - 1]
        dst = q_final.at[bit] if k == final else q_across.at[k]
        add_rows(dst, src, q_across.at[k], q_rows, 32)
        if k < final:
            q_hops[k + 1].start()
    q_back = remote(q_final.at[bit], q_final.at[bit], tensor=others[0])
    q_back.start()

    feed_pair(0)
    line_start(out_steps, out_far, out_got, 1, 2) if last >= 2 else None
    load_up.wait()
    line_start(up_steps, up_w, up_got, 2, 3) if last >= 3 else None
    u_pair.wait_recv()
    l_pair.wait_recv()

    @pl.loop(0, u_half // 16)
    def _(i):
        r = pl.ds(pl.multiple_of(i * 16, 16), 16)
        own = pl.ds(pl.multiple_of(d * u_half + i * 16, 16), 16)
        u_far[r, :] = (u_far[r, :].astype(F32) + u_w[own, :].astype(F32)).astype(BF16)

    @pl.loop(0, l_half // 16)
    def _(i):
        r = pl.ds(pl.multiple_of(i * 16, 16), 16)
        own = pl.ds(pl.multiple_of(d * l_half + i * 16, 16), 16)
        l_far[r, :] = (l_far[r, :].astype(F32) + lat_grad[own, :].astype(F32)).astype(BF16)

    u_size = u_half // contexts
    l_size = l_half // contexts
    small_sends = []
    for by in range(1, contexts):
        owner = lax.rem(z + by, contexts)
        small_sends.append(remote(piece(u_far, owner, u_size), u_got.at[by - 1], context=owner))
        small_sends.append(remote(piece(l_far, owner, l_size), l_got.at[by - 1], context=owner))
    for copy in small_sends:
        copy.start()
    feed_across(0)

    q_back.wait_recv()
    q_sum = jnp.zeros((8, rank), F32)

    def query_rows(i, acc):
        r = pl.ds(pl.multiple_of(i * 32, 32), 32)
        h = i // (q_rows // 32)
        o = pl.ds(pl.multiple_of(lax.rem(i, q_rows // 32) * 32, 32), 32)
        grad = q_final[h, o, :].astype(F32)
        normed = query_normed[r, :].astype(F32)
        weighted = grad * all_gains[:, query_gain]
        mean = jnp.mean(weighted * normed, axis=-1, keepdims=True)
        dqa[r, :] = (query_inverse[r, :] * (weighted - normed * mean)).astype(BF16)
        return acc + jnp.sum((grad * normed).reshape(4, 8, rank), axis=0)

    q_sum = lax.fori_loop(0, rows // 32, query_rows, q_sum)

    for copy in d_sends:
        copy.wait_recv()

    @pl.loop(0, d_rows // 16)
    def _(i):
        r = pl.ds(pl.multiple_of(i * 16, 16), 16)
        value = d_acc[0, r, keep].astype(F32)
        for s in range(1, contexts):
            value += d_got[s - 1, r, :].astype(F32)
        d_all[r, keep] = value.astype(BF16)

    d_gathers = []
    for k in range(len(others) - 1, 0, -1):
        here = d_all.at[:, pl.ds(start, lanes)]
        hop = remote(here, here, tensor=others[k])
        hop.start()
        hop.wait_recv()
        d_gathers.append(hop)
        side = lax.rem(t // (2**k), 2)
        start = pl.multiple_of(start - side * lanes, 128)
        lanes *= 2
    d_back = remote(d_all, d_final, tensor=others[0])
    d_back.start()
    if rows // CHUNK > 1:
        feed_pair(1)
    d_back.wait_recv()

    top = jnp.where(bit == 0, d_all[...], d_final[...]).astype(F32)
    bottom = jnp.where(bit == 0, d_final[...], d_all[...]).astype(F32)
    grad = jnp.concatenate([top, bottom], axis=0)
    lat = grad[:kv]
    normed = cache_t[...].astype(F32)
    column = jnp.broadcast_to(all_gains[:, latent_gain], (8, kv)).T[:, 0:1]
    weighted = lat * column
    mean = jnp.mean(weighted * normed, axis=0, keepdims=True)
    dkva_t[0:kv, :] = (cache_inverse_t[...] * (weighted - normed * mean)).astype(BF16)
    c_sum = jnp.sum((lat * normed).T, axis=0, keepdims=True)
    first = grad[kv : kv + 16]
    second = grad[kv + 16 :]
    cosine = cos_t[...]
    sine = sin_t[...]
    dkva_t[kv : kv + 16, :] = (first * cosine + second * sine).astype(BF16)
    dkva_t[kv + 16 :, :] = (second * cosine - first * sine).astype(BF16)

    load_one.wait()
    size = share // split

    @pl.loop(0, 2 * contexts)
    def _(i):
        r = pl.ds(pl.multiple_of((i * split + spot) * size, 16), size)
        o = pl.ds(pl.multiple_of(i * size, 16), size)
        low_q[o, :] = matmul(one_t[r, :], dqa[...]).astype(BF16)
        low_l[o, :] = times_transposed(one_t[r, :], dkva_t[...]).astype(BF16)

    low_half = contexts * size
    give = pl.ds(pl.multiple_of((1 - d) * low_half, 16), low_half)
    low_pairs = [
        remote(low_q.at[give], low_q_far, dp=1 - d),
        remote(low_l.at[give], low_l_far, dp=1 - d),
    ]
    for copy in low_pairs:
        copy.start()
    down_pair.start()
    line_start(out_steps, out_far, out_got, 1, 3) if last >= 3 else None
    if rows // CHUNK > 1:
        feed_across(1)

    for copy in load_down:
        copy.wait()
    load_tokens.wait()
    a_sum = jnp.zeros((8, width), F32)
    gains[...] = jnp.zeros_like(gains)
    block = dh1.shape[0]
    tall = 512

    def first_rows(c, acc):
        span = pl.ds(pl.multiple_of(c * block, block), block)
        for n in range(width // tall):
            lines = slice(n * tall, (n + 1) * tall)
            dh1[:, lines] = times_transposed(dqa[span, :], query_down[lines, :])
            dh1[:, lines] += transposed_times(dkva_t[:, span], latent_down_t[:, lines])

        def few(i, inner):
            o = pl.ds(pl.multiple_of(i * 16, 16), 16)
            r = pl.ds(pl.multiple_of(c * block + i * 16, 16), 16)
            grad = dh1[o, :]
            inverse = first_inverse[r, :]
            normed = wide[r, :].astype(F32) * inverse
            weighted = grad * all_gains[:, first_gain]
            mean = jnp.mean(weighted * normed, axis=-1, keepdims=True)
            wide[r, :] = (inverse * (weighted - normed * mean)).astype(BF16)
            return inner + jnp.sum((grad * normed).reshape(2, 8, width), axis=0)

        return lax.fori_loop(0, block // 16, few, acc)

    for c in range(rows // block):
        a_sum = first_rows(c, a_sum)
    save_norm = local(wide, norm_o)
    save_norm.start()

    parts = [
        jnp.sum(a_sum, axis=0, keepdims=True),
        jnp.sum(mlp_gain_grad[...], axis=0, keepdims=True),
        jnp.sum(q_sum, axis=0, keepdims=True),
        c_sum,
    ]
    line = jnp.concatenate(parts, axis=1)
    cut = gains.shape[1]
    for r in range(8):
        gains[r : r + 1, :] = line[:, r * cut : (r + 1) * cut]
    gains_pair = remote(gains, gains_far, dp=1 - d)
    gains_pair.start()

    feed_back(0)
    gains_pair.wait_recv()
    gains_far[...] = gains_far[...] + gains[...]
    gains_sends = [
        remote(gains_far, gains_got.at[by - 1], context=lax.rem(z + by, contexts))
        for by in range(1, contexts)
    ]
    for copy in gains_sends:
        copy.start()
    for copy in low_pairs:
        copy.wait_recv()

    @pl.loop(0, low_half // 16)
    def _(i):
        r = pl.ds(pl.multiple_of(i * 16, 16), 16)
        own = pl.ds(pl.multiple_of(d * low_half + i * 16, 16), 16)
        low_q_far[r, :] = (
            low_q_far[r, :].astype(F32) + low_q[own, :].astype(F32)
        ).astype(BF16)
        low_l_far[r, :] = (
            low_l_far[r, :].astype(F32) + low_l[own, :].astype(F32)
        ).astype(BF16)

    low_sends = []
    for by in range(1, contexts):
        owner = lax.rem(z + by, contexts)
        low_sends.append(
            remote(piece(low_q_far, owner, size), low_q_got.at[by - 1], context=owner)
        )
        low_sends.append(
            remote(piece(low_l_far, owner, size), low_l_got.at[by - 1], context=owner)
        )
    for copy in low_sends:
        copy.start()
    for copy in small_sends:
        copy.wait_recv()
    for far, got, result, count in (
        (u_far, u_got, small_q_o, u_size),
        (l_far, l_got, small_l_o, l_size),
    ):

        @pl.loop(0, count // 16)
        def _(i):
            r = pl.ds(pl.multiple_of(z * count + i * 16, 16), 16)
            q = pl.ds(pl.multiple_of(i * 16, 16), 16)
            value = far[r, :].astype(F32)
            for by in range(1, contexts):
                value += got[by - 1, q, :].astype(F32)
            result[q, :] = value

    for step in range(4, last + 1):
        line_start(out_steps, out_far, out_got, 1, step)
        line_start(up_steps, up_w, up_got, 2, step)
    if rows // CHUNK > 1:
        feed_back(1)
    for copy in low_sends:
        copy.wait_recv()

    @pl.loop(0, size // 16)
    def _(i):
        r = pl.ds(pl.multiple_of(z * size + i * 16, 16), 16)
        q = pl.ds(pl.multiple_of(i * 16, 16), 16)
        for far, got, everyone in (
            (low_q_far, low_q_got, low_q_all),
            (low_l_far, low_l_got, low_l_all),
        ):
            value = far[r, :].astype(F32)
            for by in range(1, contexts):
                value += got[by - 1, q, :].astype(F32)
            everyone[spot, q, :] = value.astype(BF16)

    low_gathers = []
    for sharer in sharers:
        for everyone in (low_q_all, low_l_all):
            here = everyone.at[spot]
            copy = remote(here, here, tensor=sharer)
            copy.start()
            low_gathers.append(copy)
    down_pair.wait_recv()

    @pl.loop(0, share // 16)
    def _(i):
        r = pl.ds(pl.multiple_of(d * share + i * 16, 16), 16)
        q = pl.ds(pl.multiple_of(i * 16, 16), 16)
        stage[q, :] = down_w[r, :].astype(F32) + down_far[q, :].astype(F32)

    save_down = local(stage, down_o)
    save_down.start()
    save_down.wait()

    line_end(up_steps, up_w, up_got, 2, stage)
    save_up = local(stage, up_o)
    save_up.start()
    for copy in gains_sends:
        copy.wait_recv()
    value = gains_far[...]
    for by in range(1, contexts):
        value += gains_got[by - 1]
    gain_o[...] = value
    for copy in low_gathers:
        copy.wait_recv()
    save_low = [local(low_q_all, low_q_o), local(low_l_all, low_l_o)]
    for copy in save_low:
        copy.start()
    line_end(out_steps, out_far, out_got, 1, out_o)
    for copy in save_low + [save_norm, save_up]:
        copy.wait()
    for back, save in f_backs:
        back.wait_recv()
        save.wait()
    sent = [d_pair, q_pair, u_pair, l_pair, q_back, d_back, down_pair, gains_pair]
    sent += q_hops + [hop[0] for hop in d_hops] + d_sends + d_gathers + small_sends
    sent += low_pairs + low_sends + low_gathers + gains_sends + [back[0] for back in f_backs]
    for hops in f_hops:
        sent += hops
    for copy in sent:
        copy.wait_send()


def tail(contexts, tensors, split, inside_args, outside_args):
    dq_t, query_t, dlat, lat_grad = (inside_args[i] for i in (0, 2, 6, 11))
    out_cols = outside_args[0].shape[1]
    rows = query_t.shape[1]
    rank = query_t.shape[0]
    width = outside_args[9].shape[1]
    units = outside_args[2].shape[1]
    half = width // 2
    share = half // contexts
    size = share // split
    last = contexts - 1
    hops = tensors.bit_length() - 1
    kv = dlat.shape[0]
    d_rows = kv // 2
    lanes = rows >> (hops - 1)
    heads_q = dq_t.shape[0]
    lat_rows, lat_cols = lat_grad.shape
    count_gains = (2 * width + rank + lat_rows) // 8
    anywhere = pl.BlockSpec(memory_space=pl.ANY)
    inside = pl.BlockSpec(memory_space=pltpu.VMEM)
    vm = pltpu.VMEM
    sds = jax.ShapeDtypeStruct
    chunks = rows // CHUNK
    return pl.pallas_call(
        functools.partial(tail_kernel, contexts, tensors, split),
        in_specs=[inside] * len(inside_args) + [anywhere] * len(outside_args),
        out_specs=[anywhere] * 3 + [inside] * 3 + [anywhere] * 2 + [inside, anywhere],
        out_shape=[
            sds((rows, width), BF16),
            sds((split, size, rank), BF16),
            sds((split, size, kv), BF16),
            sds((rank // (2 * contexts), heads_q), F32),
            sds((lat_rows // (2 * contexts), lat_cols), F32),
            sds((share, out_cols), F32),
            sds((share, units), F32),
            sds((share, units), F32),
            sds((8, count_gains), F32),
            sds((rows, width), BF16),
        ],
        scratch_shapes=[
            vm((2, rows // 2, rank), BF16),
            vm((rows // 2, rank), BF16),
            vm((hops - 1, rows // 2, rank), BF16),
            vm((2, rows // 2, rank), BF16),
            vm((d_rows, contexts * rows), BF16),
            vm((contexts, d_rows, rows), BF16),
            vm((hops - 1, contexts, d_rows, rows // 2), BF16),
            vm((last, d_rows, lanes), BF16),
            vm((d_rows, rows), BF16),
            vm((d_rows, rows), BF16),
            vm((rank, heads_q), BF16),
            vm((rank // 2, heads_q), BF16),
            vm((last, rank // (2 * contexts), heads_q), BF16),
            vm((lat_rows // 2, lat_cols), BF16),
            vm((last, lat_rows // (2 * contexts), lat_cols), BF16),
            vm((rows, width), BF16),
            vm((2, last - 1, share, units), BF16),
            vm((half, out_cols), BF16),
            vm((half, out_cols), BF16),
            vm((2, last, share, out_cols), BF16),
            vm((contexts * rows, units), BF16),
            vm((2 * share, contexts * rows), BF16),
            vm((2 * share, units), BF16),
            vm((share, units), BF16),
            vm((2, CHUNK, half), BF16),
            vm((chunks, CHUNK, half), BF16),
            vm((hops - 1, chunks, CHUNK, half), BF16),
            vm((rows, rank), BF16),
            vm((kv, rows), BF16),
            vm((width, rows), BF16),
            vm((2 * contexts * size, rank), BF16),
            vm((2 * contexts * size, kv), BF16),
            vm((contexts * size, rank), BF16),
            vm((contexts * size, kv), BF16),
            vm((last, size, rank), BF16),
            vm((last, size, kv), BF16),
            vm((split, size, rank), BF16),
            vm((split, size, kv), BF16),
            vm((width, rank), BF16),
            vm((kv, width), BF16),
            vm((128, width), F32),
            vm((share, units), F32),
            vm((8, count_gains), F32),
            vm((8, count_gains), F32),
            vm((last, 8, count_gains), F32),
            pltpu.SemaphoreType.DMA((128,)),
            pltpu.SemaphoreType.DMA((128,)),
            pltpu.SemaphoreType.DMA((48,)),
        ],
        compiler_params=pltpu.CompilerParams(
            collective_id=2, has_side_effects=True, vmem_limit_bytes=65000 * 1024
        ),
        cost_estimate=pl.CostEstimate(
            flops=2 * rows * width * units * 3, bytes_accessed=40 * 1024 * 1024, transcendentals=0
        ),
        name="tail",
    )(*inside_args, *outside_args)


def finish_kernel(
    count,
    tokens,
    branch,
    feed,
    dmiddle,
    norm_one,
    low_q,
    low_l,
    *rest,
):
    given = rest[:count]
    layer_out, token_grad, low_q_o, low_l_o = rest[count : count + 4]
    taken = rest[count + 4 :]
    for src, dst in zip(given, taken):
        dst[...] = src[...]

    @pl.when(pl.program_id(0) == 0)
    def _():
        low_q_o[...] = low_q[...].astype(F32)
        low_l_o[...] = low_l[...].astype(F32).T

    added = branch[...].astype(F32) + feed[...].astype(F32)
    layer_out[...] = (tokens[...].astype(F32) + RESIDUAL * added).astype(BF16)
    token_grad[...] = dmiddle[...] + norm_one[...].astype(F32)


def finish(tokens, branch, feed, dmiddle, norm_one, low_q, low_l, given):
    rows, width = tokens.shape
    steps = 4
    tiled = pl.BlockSpec((rows // steps, width), lambda i: (i, 0))
    passed = [
        pl.BlockSpec((g.shape[0] // steps, g.shape[1]), lambda i: (i, 0))
        if g.shape[0] % (8 * steps) == 0
        else whole_spec(g.shape)
        for g in given
    ]
    sds = jax.ShapeDtypeStruct
    return pl.pallas_call(
        functools.partial(finish_kernel, len(given)),
        grid=(steps,),
        in_specs=[tiled] * 5
        + [whole_spec(low_q.shape), whole_spec(low_l.shape)]
        + passed,
        out_specs=[tiled] * 2
        + [whole_spec(low_q.shape), whole_spec(low_l.shape[::-1])]
        + passed,
        out_shape=[
            sds((rows, width), BF16),
            sds((rows, width), F32),
            sds(low_q.shape, F32),
            sds(low_l.shape[::-1], F32),
        ]
        + [sds(g.shape, g.dtype) for g in given],
        compiler_params=pltpu.CompilerParams(vmem_limit_bytes=65000 * 1024),
        name="finish",
    )(tokens, branch, feed, dmiddle, norm_one, low_q, low_l, *given)


def pick(value, index):
    return lax.dynamic_index_in_dim(value, index, 0, keepdims=False)


def per_device(
    sizes,
    tokens,
    cotangent,
    group_order,
    attn_gain,
    query_down,
    query_gain,
    latent_down,
    latent_gain,
    query_up,
    latent_up,
    attn_out,
    mlp_gain,
    gate_proj,
    up_proj,
    down_proj,
):
    contexts, tensors = sizes
    rows, width = tokens.shape[1:]
    heads = query_up.shape[1] // (NOPE + ROPE)
    z = lax.axis_index("context")
    d = lax.axis_index("dp")
    share = width // (2 * contexts)
    tokens = tokens[0]
    cotangent = cotangent[0]
    query_up_t = query_up.T
    latent_down_t = latent_down.T
    gains = jnp.concatenate([attn_gain, mlp_gain, query_gain, latent_gain])[None]

    mine = lax.dynamic_slice_in_dim(group_order, 2 * z, 2)
    offsets = jnp.arange(HALF, dtype=jnp.int32)
    query_pos = (mine[:, None] * HALF + offsets[None, :]).reshape(rows)
    freq = 10000.0 ** (-2.0 * jnp.arange(ROPE // 2, dtype=F32) / ROPE)
    angle_t = freq[:, None] * query_pos.astype(F32)[None, :]
    cos_t, sin_t = jnp.cos(angle_t), jnp.sin(angle_t)

    (
        q_t,
        latent_all,
        latent_all_t,
        rope_all,
        rope_all_t,
        one_inverse,
        query_normed,
        query_inverse,
        query_t,
        cache_t,
        cache_inverse_t,
        one_t,
        feed_t,
        latent_up_t,
    ) = front(
        contexts,
        gains,
        tokens,
        cotangent,
        query_down,
        latent_down_t,
        query_up_t,
        latent_up,
        cos_t,
        sin_t,
    )
    joined_t, exact_t, lse = attention_forward(
        contexts, group_order, q_t, latent_all, latent_all_t, rope_all, latent_up, latent_up_t
    )
    (
        branch,
        two,
        hidden,
        dgate,
        dup,
        feed_part,
        dmiddle,
        dbranch,
        feed_all,
        far_two,
        far_dgate,
        near,
        dmix_t,
        mlp_gain_grad,
    ) = feed_forward(
        contexts,
        tensors,
        joined_t,
        tokens,
        cotangent,
        gains,
        attn_out,
        down_proj,
        gate_proj.T,
        up_proj.T,
        feed_t,
    )
    dq_t, lat_grad, dlat_t, grad_gate_proj, up_pieces, out_part, far_out, _, spread = backward(
        contexts,
        group_order,
        q_t,
        latent_all,
        latent_all_t,
        rope_all,
        rope_all_t,
        latent_up,
        latent_up_t,
        exact_t,
        lse,
        dmix_t,
        cos_t,
        sin_t,
        joined_t,
        two,
        far_two,
        dgate,
        far_dgate,
        dup,
        near,
        dbranch,
    )
    split = tensors
    while (share // split) % 16 != 0 or share % split != 0:
        split //= 2
    (
        norm_one,
        low_q,
        low_l,
        small_q,
        small_l,
        grad_attn_out,
        grad_up_proj,
        grad_down,
        gain_sums,
        feed,
    ) = tail(
        contexts,
        tensors,
        split,
        [
            dq_t.reshape(heads * (NOPE + ROPE), rows),
            query_up_t,
            query_t,
            query_normed,
            query_inverse,
            gains,
            dlat_t,
            cache_t,
            cache_inverse_t,
            cos_t,
            sin_t,
            lat_grad,
            one_inverse,
            mlp_gain_grad,
        ],
        [
            out_part,
            far_out,
            hidden,
            near,
            spread,
            feed_all,
            up_pieces,
            one_t,
            query_down,
            latent_down_t,
            tokens,
            feed_part,
        ],
    )
    (
        layer_out,
        token_grad,
        low_q,
        low_l,
        grad_gate_proj,
        grad_up_proj,
        grad_down,
        grad_attn_out,
        small_q,
        small_l,
    ) = finish(
        tokens,
        branch,
        feed,
        dmiddle,
        norm_one,
        low_q.reshape(share, -1),
        low_l.reshape(share, -1),
        [grad_gate_proj, grad_up_proj, grad_down, grad_attn_out, small_q, small_l],
    )

    gain_sums = gain_sums.reshape(-1)
    gain_grads = []
    edge = 0
    for value in (attn_gain, mlp_gain, query_gain, latent_gain):
        part = gain_sums[edge : edge + value.shape[0]].reshape(2 * contexts, -1)
        gain_grads.append(pick(part, d * contexts + z))
        edge += value.shape[0]

    return (
        layer_out[None],
        token_grad[None],
        gain_grads[0],
        low_q,
        gain_grads[2],
        low_l.T,
        gain_grads[3],
        small_q,
        small_l,
        grad_attn_out.T,
        gain_grads[1],
        grad_gate_proj,
        grad_up_proj,
        grad_down.T,
    )


def solution(mesh):
    in_specs = (
        P("dp", "context", None),
        P("dp", "context", None),
        P(),
        P(),
        P(),
        P(),
        P(),
        P(),
        P(None, "tensor"),
        P(None, "tensor"),
        P("tensor", None),
        P(),
        P(None, "tensor"),
        P(None, "tensor"),
        P("tensor", None),
    )
    out_specs = (
        P("dp", "context", None),
        P("dp", "context", None),
        P(("dp", "context")),
        P(("dp", "context"), None),
        P(("dp", "context")),
        P(("dp", "context"), None),
        P(("dp", "context")),
        P(("dp", "context"), "tensor"),
        P(("dp", "context"), "tensor"),
        P("tensor", ("dp", "context")),
        P(("dp", "context")),
        P(("dp", "context"), "tensor"),
        P(("dp", "context"), "tensor"),
        P("tensor", ("dp", "context")),
    )
    sizes = (mesh.shape["context"], mesh.shape["tensor"])
    return jax.shard_map(
        functools.partial(per_device, sizes),
        mesh=mesh,
        in_specs=in_specs,
        out_specs=out_specs,
        check_vma=False,
    )
```

```python
import functools
import math

import jax
import jax.numpy as jnp
from jax import lax
from jax.experimental import pallas as pl
from jax.experimental.pallas import tpu as pltpu
from jax.sharding import PartitionSpec as P

NOPE = 64
ROPE = 32
V_DIM = 64
KV_RANK = 256
HALF = 256
GROUP = 5
CHUNK = 256

EPS = 1e-05
RESIDUAL = 1.4 / math.sqrt(62.0)
SCALE = 1.0 / math.sqrt(NOPE + ROPE)
LOG2E = 1.0 / math.log(2.0)
F32 = jnp.float32
BF16 = jnp.bfloat16


def matmul(left, right):
    return jnp.dot(left, right, preferred_element_type=F32)


def times_transposed(left, right):
    return lax.dot_general(left, right, (((1,), (1,)), ((), ())), preferred_element_type=F32)


def transposed_times(left, right):
    return lax.dot_general(left, right, (((0,), (0,)), ((), ())), preferred_element_type=F32)


MESH = pl.DeviceIdType.MESH


def greet(devices):
    barrier = pltpu.get_barrier_semaphore()
    for device in devices:
        pl.semaphore_signal(barrier, inc=1, device_id=device, device_id_type=MESH)
    pl.semaphore_wait(barrier, len(devices))


def line_of(z, contexts):
    return [{"context": lax.rem(z + by, contexts)} for by in range(1, contexts)]


def front_kernel(
    contexts,
    gains,
    tokens,
    cotangent_h,
    query_down_h,
    latent_down_t,
    query_up_h,
    latent_up_h,
    cos_t,
    sin_t,
    q_t,
    latent,
    latent_t,
    rope_keys,
    rope_keys_t,
    one_inverse,
    query_normed,
    query_inverse,
    query_t,
    cache_t,
    cache_inverse_t,
    one_t,
    feed_t,
    latent_up_t,
    cotangent,
    query_down,
    query_up_t,
    latent_up,
    one,
    low,
    keys,
    far,
    line_sem,
    line_got,
    pair_sem,
    pair_got,
    load_sem,
):
    rows, width = tokens.shape
    loads = [
        pltpu.make_async_copy(src, dst, load_sem.at[i])
        for i, (src, dst) in enumerate(
            [
                (query_down_h, query_down),
                (query_up_h, query_up_t),
                (latent_up_h, latent_up),
                (cotangent_h, cotangent),
            ]
        )
    ]
    for load in loads:
        load.start()
    rank = query_down.shape[1]
    kv = cache_t.shape[0]
    z = lax.axis_index("context")
    t = lax.axis_index("tensor")
    bit = lax.rem(t, 2)
    pair = t + 1 - 2 * bit
    gain_one = slice(0, width)
    gain_query = slice(2 * width, 2 * width + rank)
    gain_latent = slice(2 * width + rank, 2 * width + rank + kv)
    greet([{"tensor": pair}] + line_of(z, contexts))

    @pl.loop(0, rows // 32)
    def _(i):
        r = pl.ds(pl.multiple_of(i * 32, 32), 32)
        value = tokens[r, :].astype(F32)
        inverse = lax.rsqrt(jnp.mean(value * value, axis=-1, keepdims=True) + EPS)
        one_inverse[r, :] = inverse
        one[r, :] = (value * inverse * gains[:, gain_one]).astype(BF16)

    raw = times_transposed(latent_down_t[...], one[...])
    lat = raw[:kv]
    inverse = lax.rsqrt(jnp.mean(lat * lat, axis=0, keepdims=True) + EPS)
    cache_inverse_t[...] = inverse
    lat = lat * inverse
    cache_t[...] = lat.astype(BF16)
    column = jnp.broadcast_to(gains[:, gain_latent], (8, kv)).T[:, 0:1]
    keys[0:kv, :] = (lat * column).astype(BF16)
    first = raw[kv : kv + 16]
    second = raw[kv + 16 :]
    cosine = cos_t[...]
    sine = sin_t[...]
    keys[kv : kv + 16, :] = (first * cosine - second * sine).astype(BF16)
    keys[kv + 16 :, :] = (second * cosine + first * sine).astype(BF16)

    part = keys.shape[0] // 2
    mine = pl.ds(pl.multiple_of(bit * part, 16), part)
    sends = [
        pltpu.make_async_remote_copy(
            src_ref=keys.at[mine],
            dst_ref=far.at[bit, by - 1],
            send_sem=line_sem.at[by - 1],
            recv_sem=line_got.at[by - 1],
            device_id={"context": lax.rem(z + by, contexts)},
            device_id_type=MESH,
        )
        for by in range(1, contexts)
    ]
    for copy in sends:
        copy.start()

    loads[0].wait()
    low[...] = matmul(one[...], query_down[...])

    @pl.loop(0, rows // 32)
    def _(i):
        r = pl.ds(pl.multiple_of(i * 32, 32), 32)
        value = low[r, :]
        inverse = lax.rsqrt(jnp.mean(value * value, axis=-1, keepdims=True) + EPS)
        query_inverse[r, :] = inverse
        value = value * inverse
        query_normed[r, :] = value.astype(BF16)
        low[r, :] = value * gains[:, gain_query]

    query = low[...].astype(BF16)
    query_t[...] = query.T
    heads = q_t.shape[0]
    loads[1].wait()
    for h in range(heads):
        full = times_transposed(query_up_t[h * 96 : (h + 1) * 96, :], query)
        first = full[64:80]
        second = full[80:96]
        q_t[h, 0:64, :] = full[0:64].astype(BF16)
        q_t[h, 64:80, :] = (first * cosine - second * sine).astype(BF16)
        q_t[h, 80:96, :] = (second * cosine + first * sine).astype(BF16)

    for copy in sends:
        copy.wait_recv()
    share = pltpu.make_async_remote_copy(
        src_ref=far.at[bit],
        dst_ref=far.at[bit],
        send_sem=pair_sem,
        recv_sem=pair_got,
        device_id={"tensor": pair},
        device_id_type=MESH,
    )
    share.start()

    loads[2].wait()
    latent_up_t[...] = latent_up[...].T
    loads[3].wait()

    @pl.loop(0, width // 256)
    def _(i):
        lines = pl.ds(pl.multiple_of(i * 256, 256), 256)
        one_t[lines, :] = one[:, lines].T
        feed_t[lines, :] = (RESIDUAL * cotangent[:, lines].astype(F32)).astype(BF16).T

    share.wait_recv()
    latent_t[:, 0:rows] = keys[0:kv, :]
    rope_keys_t[:, 0:rows] = keys[kv:, :]
    for s in range(1, contexts):
        cols = slice(s * rows, (s + 1) * rows)
        latent_t[0:part, cols] = far[0, s - 1]
        latent_t[part:, cols] = far[1, s - 1, 0 : kv - part, :]
        rope_keys_t[:, cols] = far[1, s - 1, kv - part :, :]
    latent[...] = latent_t[...].T
    rope_keys[...] = jnp.concatenate(
        [rope_keys_t[...], jnp.zeros((128 - ROPE, rope_keys_t.shape[1]), BF16)], axis=0
    ).T
    for copy in sends:
        copy.wait_send()
    share.wait_send()


def front(
    contexts,
    gains,
    tokens,
    cotangent,
    query_down,
    latent_down_t,
    query_up_t,
    latent_up,
    cos_t,
    sin_t,
):
    rows, width = tokens.shape
    rank = query_down.shape[1]
    span = latent_down_t.shape[0]
    heads = query_up_t.shape[0] // 96
    kv = span - ROPE
    keys = contexts * rows
    inside = pl.BlockSpec(memory_space=pltpu.VMEM)
    anywhere = pl.BlockSpec(memory_space=pl.ANY)
    sds = jax.ShapeDtypeStruct
    dma = pltpu.SemaphoreType.DMA
    return pl.pallas_call(
        functools.partial(front_kernel, contexts),
        in_specs=[inside] * 2
        + [anywhere] * 2
        + [inside]
        + [anywhere] * 2
        + [inside] * 2,
        out_specs=[inside] * 14,
        out_shape=[
            sds((heads, 96, rows), BF16),
            sds((keys, kv), BF16),
            sds((kv, keys), BF16),
            sds((keys, 128), BF16),
            sds((ROPE, keys), BF16),
            sds((rows, 1), F32),
            sds((rows, rank), BF16),
            sds((rows, 1), F32),
            sds((rank, rows), BF16),
            sds((kv, rows), BF16),
            sds((1, rows), F32),
            sds((width, rows), BF16),
            sds((width, rows), BF16),
            sds(latent_up.shape[::-1], BF16),
        ],
        scratch_shapes=[
            pltpu.VMEM(cotangent.shape, BF16),
            pltpu.VMEM(query_down.shape, BF16),
            pltpu.VMEM(query_up_t.shape, BF16),
            pltpu.VMEM(latent_up.shape, BF16),
            pltpu.VMEM((rows, width), BF16),
            pltpu.VMEM((rows, rank), F32),
            pltpu.VMEM((span, rows), BF16),
            pltpu.VMEM((2, contexts - 1, span // 2, rows), BF16),
            dma((contexts - 1,)),
            dma((contexts - 1,)),
            dma,
            dma,
            dma((4,)),
        ],
        compiler_params=pltpu.CompilerParams(
            collective_id=3, has_side_effects=True, vmem_limit_bytes=60 * 1024 * 1024
        ),
        cost_estimate=pl.CostEstimate(
            flops=2 * rows * width * 1200, bytes_accessed=30 * 1024 * 1024, transcendentals=0
        ),
        name="front",
    )(
        gains,
        tokens,
        cotangent,
        query_down,
        latent_down_t,
        query_up_t,
        latent_up,
        cos_t,
        sin_t,
    )


def load_heads(heads, latent, rope_keys, latent_up, q_t, kcat, q_wide):
    for h in range(heads):
        kcat[h, :, :128] = matmul(latent[...], latent_up[:, h * 128 : (h + 1) * 128]).astype(BF16)
        kcat[h, :, 128:] = rope_keys[...]
        q_wide[h, 0:64, :] = q_t[h, 0:64, :]
        q_wide[h, 64:128, :] = jnp.zeros((64, q_wide.shape[2]), BF16)
        q_wide[h, 128:160, :] = q_t[h, 64:96, :]
        q_wide[h, 160:256, :] = jnp.zeros((96, q_wide.shape[2]), BF16)


def causal():
    key_row = lax.broadcasted_iota(jnp.int32, (HALF, HALF), 0)
    query_col = lax.broadcasted_iota(jnp.int32, (HALF, HALF), 1)
    return key_row <= query_col


def fold(value, op):
    return op(value.reshape(HALF // 8, 8, value.shape[-1]), axis=0)


def forward_kernel(
    heads,
    contexts,
    order,
    q_t,
    latent,
    latent_t,
    rope_keys,
    latent_up,
    latent_up_t,
    joined_t,
    exact_t,
    lse,
    kcat,
    v_t,
    q_wide,
    scores,
    top,
    total,
    acc,
    lies,
):
    z = lax.axis_index("context")
    for i in range(2 * contexts):
        slot = lax.rem(z + contexts - i // 2, contexts)
        lies[order[i]] = slot * (2 * HALF) + (i % 2) * HALF
    load_heads(heads, latent, rope_keys, latent_up, q_t, kcat, q_wide)
    for h in range(heads):
        v_t[h] = matmul(latent_up_t[h * 128 + 64 : (h + 1) * 128, :], latent_t[...]).astype(BF16)
    factor = SCALE * LOG2E
    for block in range(2):
        cols = slice(block * HALF, (block + 1) * HALF)
        position = order[2 * z + block]

        def score(j, masked):
            rows = pl.ds(pl.multiple_of(lies[j], HALF), HALF)
            spot = pl.ds(pl.multiple_of(j * HALF, HALF), HALF)
            for h in range(heads):
                s = matmul(kcat[h, rows, :], q_wide[h, :, cols])
                if masked:
                    s = jnp.where(causal(), s, -1e30)
                scores[h, spot, :] = s
                peak = fold(s, jnp.max)
                top[h] = peak if masked else jnp.maximum(top[h], peak)

        score(position, True)

        @pl.loop(0, position)
        def _(j):
            score(j, False)

        for h in range(heads):
            peak = jnp.max(top[h], axis=0, keepdims=True) * factor
            top[h] = jnp.broadcast_to(peak, (8, HALF))
            total[h] = jnp.zeros((8, HALF), F32)
            acc[h] = jnp.zeros((V_DIM, HALF), F32)

        @pl.loop(0, position + 1)
        def _(j):
            rows = pl.ds(pl.multiple_of(lies[j], HALF), HALF)
            spot = pl.ds(pl.multiple_of(j * HALF, HALF), HALF)
            for h in range(heads):
                p = jnp.exp2(scores[h, spot, :] * factor - top[h, 0:1, :])
                total[h] += fold(p, jnp.sum)
                acc[h] += matmul(v_t[h, :, rows], p.astype(BF16))

        for h in range(heads):
            summed = jnp.sum(total[h], axis=0, keepdims=True)
            out = acc[h] / summed
            joined_t[h * V_DIM : (h + 1) * V_DIM, cols] = out.astype(BF16)
            exact_t[h, :, cols] = out
            lse[h, :, cols] = top[h, 0:1, :] + jnp.log2(summed)


def whole_spec(shape):
    return pl.BlockSpec(shape, lambda g: (0,) * len(shape))


def attention_forward(contexts, order, q_t, latent, latent_t, rope_keys, latent_up, latent_up_t):
    count, _, rows = q_t.shape
    keys = latent.shape[0]
    heads = GROUP
    flops = 2 * count * rows * keys * 384
    return pl.pallas_call(
        functools.partial(forward_kernel, heads, contexts),
        grid=(count // heads,),
        in_specs=[
            pl.BlockSpec(memory_space=pltpu.SMEM),
            pl.BlockSpec((heads, 96, rows), lambda g: (g, 0, 0)),
            whole_spec((keys, KV_RANK)),
            whole_spec((KV_RANK, keys)),
            whole_spec((keys, 128)),
            pl.BlockSpec((KV_RANK, heads * 128), lambda g: (0, g)),
            pl.BlockSpec((heads * 128, KV_RANK), lambda g: (g, 0)),
        ],
        out_specs=[
            pl.BlockSpec((heads * V_DIM, rows), lambda g: (g, 0)),
            pl.BlockSpec((heads, V_DIM, rows), lambda g: (g, 0, 0)),
            pl.BlockSpec((heads, 1, rows), lambda g: (g, 0, 0)),
        ],
        out_shape=[
            jax.ShapeDtypeStruct((count * V_DIM, rows), BF16),
            jax.ShapeDtypeStruct((count, V_DIM, rows), F32),
            jax.ShapeDtypeStruct((count, 1, rows), F32),
        ],
        scratch_shapes=[
            pltpu.VMEM((heads, keys, 256), BF16),
            pltpu.VMEM((heads, V_DIM, keys), BF16),
            pltpu.VMEM((heads, 256, rows), BF16),
            pltpu.VMEM((heads, keys, HALF), F32),
            pltpu.VMEM((heads, 8, HALF), F32),
            pltpu.VMEM((heads, 8, HALF), F32),
            pltpu.VMEM((heads, V_DIM, HALF), F32),
            pltpu.SMEM((keys // HALF,), jnp.int32),
        ],
        compiler_params=pltpu.CompilerParams(vmem_limit_bytes=56 * 1024 * 1024),
        cost_estimate=pl.CostEstimate(
            flops=flops, bytes_accessed=12 * 1024 * 1024, transcendentals=count * rows * keys
        ),
        name="attention_forward",
    )(order, q_t, latent, latent_t, rope_keys, latent_up, latent_up_t)


def cuts(size, step=512):
    count = max(1, size // step)
    edges = [i * step for i in range(count)] + [size]
    return list(zip(edges[:-1], edges[1:]))


def feed_forward_kernel(
    contexts,
    tensors,
    joined_t,
    tokens,
    cotangent,
    gain,
    attn_out_h,
    down_h,
    gate_h,
    up_h,
    feed_t_h,
    branch_o,
    two_o,
    hidden_o,
    dgate_o,
    dup_o,
    feed_o,
    dmiddle_o,
    dbranch_o,
    feed_all_o,
    far_two_o,
    far_dgate_o,
    near_o,
    dmix_t,
    gain_o,
    attn_out,
    down,
    gate_w,
    up_w,
    part,
    final,
    near,
    across,
    dhid,
    two,
    trio,
    feed,
    dmiddle,
    load_sem,
    save_sem,
    send_sem,
    recv_sem,
    pair_sem,
    pair_got,
    line_sem,
    line_got,
    turn_sem,
    turn_got,
    keep_sem,
    give_sem,
    give_got,
):
    rows, width = tokens.shape
    half = width // 2
    t = lax.axis_index("tensor")
    bit = lax.rem(t, 2)
    pair = t + 1 - 2 * bit
    others = [pair]
    step = 2
    while step < tensors:
        others.append(t + step - 2 * step * lax.rem(t // step, 2))
        step *= 2

    loads = [
        pltpu.make_async_copy(src, dst, load_sem.at[i])
        for i, (src, dst) in enumerate(
            [(attn_out_h, attn_out), (down_h, down), (gate_h, gate_w), (up_h, up_w)]
        )
    ]
    for load in loads:
        load.start()

    d = lax.axis_index("dp")
    z = lax.axis_index("context")
    greet([{"tensor": i} for i in others] + line_of(z, contexts) + [{"dp": 1 - d}])

    share = half // contexts

    part_share = share // 2

    def turn(e, by):
        owner = lax.rem(z + by, contexts)
        if by == 0:
            src = feed_t_h.at[pl.ds(pl.multiple_of(e * half + owner * share, 16), share)]
            dst = feed_all_o.at[e * share : (e + 1) * share, 0:rows]
            return pltpu.make_async_copy(src, dst, keep_sem.at[e])
        first = e * half + owner * share + bit * part_share
        src = feed_t_h.at[pl.ds(pl.multiple_of(first, 16), part_share)]
        lines = pl.ds(pl.multiple_of(e * share + bit * part_share, 16), part_share)
        dst = feed_all_o.at[lines, by * rows : (by + 1) * rows]
        return pltpu.make_async_remote_copy(
            src_ref=src,
            dst_ref=dst,
            send_sem=turn_sem.at[e, by - 1],
            recv_sem=turn_got.at[e, by - 1],
            device_id={"context": owner},
            device_id_type=MESH,
        )

    turns = [turn(e, by) for e in range(2) for by in range(contexts)]
    for copy in turns:
        copy.start()

    def to_pair(ref, i):
        return pltpu.make_async_remote_copy(
            src_ref=ref,
            dst_ref=ref,
            send_sem=give_sem.at[i],
            recv_sem=give_got.at[i],
            device_id={"tensor": pair},
            device_id_type=MESH,
        )

    def turn_pair(e):
        lines = pl.ds(pl.multiple_of(e * share + bit * part_share, 16), part_share)
        return to_pair(feed_all_o.at[lines, rows:], e)

    def two_pair(c):
        lines = pl.ds(pl.multiple_of(c * CHUNK + bit * (CHUNK // 2), 16), CHUNK // 2)
        return to_pair(far_two_o.at[lines], 2 + c)

    def send(src, dst, job, kind, c, device):
        return pltpu.make_async_remote_copy(
            src_ref=src,
            dst_ref=dst,
            send_sem=send_sem.at[job, kind, c],
            recv_sem=recv_sem.at[job, kind, c],
            device_id={"tensor": device},
            device_id_type=MESH,
        )

    def span(c):
        return pl.ds(c * CHUNK, CHUNK)

    last = len(others)

    def hop(job, c, kind):
        if kind == 0:
            return send(
                part.at[1 - bit, span(c)], near.at[job, span(c)], job, 0, c, pair
            )
        if kind == last:
            here = final.at[job, bit, span(c)]
            return send(here, here, job, last, c, pair)
        src = near if kind == 1 else across.at[kind - 2]
        return send(
            src.at[job, span(c)], across.at[kind - 1, job, span(c)], job, kind, c, others[kind]
        )

    def reduce_pair(job, c):
        hop(job, c, 0).wait_recv()

        @pl.loop(0, CHUNK // 32)
        def _(i):
            r = pl.ds(pl.multiple_of(c * CHUNK + i * 32, 32), 32)
            near[job, r, :] = (
                near[job, r, :].astype(F32) + part[bit, r, :].astype(F32)
            ).astype(BF16)

        hop(job, c, 1).start()

    def reduce_across(job, c):
        for kind in range(1, last):
            hop(job, c, kind).wait_recv()
            src = near if kind == 1 else across.at[kind - 2]
            ending = kind == last - 1

            @pl.loop(0, CHUNK // 32)
            def _(i):
                r = pl.ds(pl.multiple_of(c * CHUNK + i * 32, 32), 32)
                value = (
                    src[job, r, :].astype(F32) + across[kind - 1, job, r, :].astype(F32)
                ).astype(BF16)
                if ending:
                    final[job, bit, r, :] = value
                else:
                    across[kind - 1, job, r, :] = value

            hop(job, c, kind + 1).start()
        hop(job, c, last).wait_recv()

    def middle_rows(r):
        parts = []
        for h in range(2):
            cols = slice(h * half, (h + 1) * half)
            parts.append(
                tokens[r, cols].astype(F32) + RESIDUAL * final[0, h, r, :].astype(F32)
            )
        square = sum(jnp.sum(p * p, axis=-1, keepdims=True) for p in parts)
        inverse = lax.rsqrt(square * (1.0 / width) + EPS)
        return parts, inverse

    def across_pair(c, kind):
        if kind == 0:
            lines = pl.ds(pl.multiple_of(bit * (CHUNK // 2), 16), CHUNK // 2)
            src = two.at[lines, pl.ds(pl.multiple_of((1 - d) * half, 128), half)]
            lines = pl.ds(pl.multiple_of(c * CHUNK + bit * (CHUNK // 2), 16), CHUNK // 2)
            dst = far_two_o.at[lines]
        else:
            src, dst = trio.at[1, span(c)], far_dgate_o.at[span(c)]
        return pltpu.make_async_remote_copy(
            src_ref=src,
            dst_ref=dst,
            send_sem=pair_sem.at[kind, c],
            recv_sem=pair_got.at[kind, c],
            device_id={"dp": 1 - d},
            device_id_type=MESH,
        )

    def along_line(c, way):
        return pltpu.make_async_remote_copy(
            src_ref=trio.at[0, span(c)],
            dst_ref=near_o.at[way, span(c)],
            send_sem=line_sem.at[way, c],
            recv_sem=line_got.at[way, c],
            device_id={"context": z + 1 - 2 * way},
            device_id_type=MESH,
        )

    chunks = rows // CHUNK
    loads[0].wait()
    for c in range(chunks):
        left = joined_t[:, c * CHUNK : (c + 1) * CHUNK]

        for turn_of in range(2):
            side = 1 - bit if turn_of == 0 else bit

            @pl.loop(0, half // 256)
            def _(n):
                cols = pl.ds(pl.multiple_of(side * half + n * 256, 256), 256)
                place = pl.ds(pl.multiple_of(n * 256, 256), 256)
                part[side, span(c), place] = transposed_times(left, attn_out[:, cols]).astype(BF16)

            if turn_of == 0:
                hop(0, c, 0).start()
    for c in range(chunks):
        reduce_pair(0, c)

    loads[1].wait()
    for c in range(chunks):

        @pl.loop(0, CHUNK // 32)
        def _(i):
            r = pl.ds(pl.multiple_of(c * CHUNK + i * 32, 32), 32)
            o = pl.ds(pl.multiple_of(i * 32, 32), 32)
            two[o, :] = (RESIDUAL * cotangent[r, :].astype(F32)).astype(BF16)

        for a, b in cuts(down.shape[0]):
            dhid[span(c), a:b] = times_transposed(two[...], down[a:b, :]).astype(BF16)

    loads[2].wait()
    loads[3].wait()
    saves = []

    def save(src, dst):
        copy = pltpu.make_async_copy(src, dst, save_sem.at[len(saves)])
        copy.start()
        saves.append(copy)
        return copy

    two_saved = None
    for c in range(chunks):
        reduce_across(0, c)
        if c > 0:
            reduce_pair(1, c - 1)
        if two_saved is not None:
            two_saved.wait()
            across_pair(c - 1, 0).wait_send()

        @pl.loop(0, CHUNK // 32)
        def _(i):
            r = pl.ds(pl.multiple_of(c * CHUNK + i * 32, 32), 32)
            o = pl.ds(pl.multiple_of(i * 32, 32), 32)
            parts, inverse = middle_rows(r)
            for h in range(2):
                cols = slice(h * half, (h + 1) * half)
                two[o, cols] = (parts[h] * inverse * gain[:, width + h * half : width + (h + 1) * half]).astype(BF16)

        two_saved = save(two, two_o.at[span(c)])
        across_pair(c, 0).start()
        for a, b in cuts(gate_w.shape[0]):
            gate = times_transposed(two[...], gate_w[a:b, :])
            upper = times_transposed(two[...], up_w[a:b, :])
            grad = dhid[span(c), a:b].astype(F32)
            sigma = 1.0 / (1.0 + jnp.exp(-gate))
            act = gate * sigma
            trio[0, span(c), a:b] = (act * upper).astype(BF16)
            trio[1, span(c), a:b] = (
                grad * upper * sigma * (1.0 + gate * (1.0 - sigma))
            ).astype(BF16)
            trio[2, span(c), a:b] = (grad * act).astype(BF16)
        for k, out in enumerate((hidden_o, dgate_o, dup_o)):
            save(trio.at[k, span(c)], out.at[span(c)])
        across_pair(c, 1).start()

        @pl.when(z < contexts - 1)
        def _():
            along_line(c, 0).start()

        @pl.when(z > 0)
        def _():
            along_line(c, 1).start()

        hop(0, c, 0).wait_send()

        for turn_of in range(2):
            side = 1 - bit if turn_of == 0 else bit

            @pl.loop(0, half // 256)
            def _(n):
                cols = pl.ds(pl.multiple_of(side * half + n * 256, 256), 256)
                place = pl.ds(pl.multiple_of(n * 256, 256), 256)
                value = matmul(trio[1, span(c), :], gate_w[:, cols])
                value += matmul(trio[2, span(c), :], up_w[:, cols])
                part[side, span(c), place] = value.astype(BF16)

            if turn_of == 0:
                hop(1, c, 0).start()
    reduce_pair(1, chunks - 1)
    two_saved.wait()

    for e in range(2):
        for by in range(1, contexts):
            turns[e * contexts + by].wait_recv()
        turn_pair(e).start()
    for c in range(chunks):
        across_pair(c, 0).wait_recv()
        two_pair(c).start()

    gain_o[...] = jnp.zeros_like(gain_o)
    feed_saved = dmiddle_saved = dbranch_saved = None
    for c in range(chunks):
        if feed_saved is not None:
            feed_saved.wait()

        @pl.loop(0, width // 256)
        def _(n):
            cols = pl.ds(pl.multiple_of(n * 256, 256), 256)
            feed[:, cols] = matmul(trio[0, span(c), :], down[:, cols]).astype(BF16)

        feed_saved = save(feed, feed_o.at[span(c)])
        reduce_across(1, c)
        if dmiddle_saved is not None:
            dmiddle_saved.wait()
            dbranch_saved.wait()
        else:
            across_pair(chunks - 1, 0).wait_send()

        @pl.loop(0, CHUNK // 32)
        def _(i):
            r = pl.ds(pl.multiple_of(c * CHUNK + i * 32, 32), 32)
            o = pl.ds(pl.multiple_of(i * 32, 32), 32)
            parts, inverse = middle_rows(r)
            dot = jnp.zeros((32, 1), F32)
            for h in range(2):
                cols = slice(h * half, (h + 1) * half)
                product = final[1, h, r, :].astype(F32) * (parts[h] * inverse)
                gain_o[:, cols] += jnp.sum(product.reshape(4, 8, half), axis=0)
                dot += jnp.sum(product * gain[:, width + h * half : width + (h + 1) * half], axis=-1, keepdims=True)
            dot = dot * (1.0 / width)
            for h in range(2):
                cols = slice(h * half, (h + 1) * half)
                weighted = final[1, h, r, :].astype(F32) * gain[:, width + h * half : width + (h + 1) * half]
                value = cotangent[r, cols].astype(F32) + inverse * (
                    weighted - parts[h] * inverse * dot
                )
                dmiddle[o, cols] = value
                two[o, cols] = (RESIDUAL * value).astype(BF16)

        dmiddle_saved = save(dmiddle, dmiddle_o.at[span(c)])
        dbranch_saved = save(two, dbranch_o.at[span(c)])
        dmix_t[:, c * CHUNK : (c + 1) * CHUNK] = times_transposed(attn_out[...], two[...]).astype(
            BF16
        )
    for h in range(2):
        save(final.at[0, h], branch_o.at[:, h * half : (h + 1) * half])
    for copy in saves[-2:] + [feed_saved, dmiddle_saved, dbranch_saved]:
        copy.wait()
    for e in range(2):
        turns[e * contexts].wait()
        for by in range(1, contexts):
            turns[e * contexts + by].wait_send()
        turn_pair(e).wait()
    for c in range(chunks):
        for k in range(3):
            saves[c * 4 + 1 + k].wait()
    for c in range(chunks):
        two_pair(c).wait()
        across_pair(c, 1).wait()

        @pl.when(z < contexts - 1)
        def _():
            along_line(c, 0).wait_send()
            along_line(c, 1).wait_recv()

        @pl.when(z > 0)
        def _():
            along_line(c, 1).wait_send()
            along_line(c, 0).wait_recv()

    for job in range(2):
        for c in range(chunks):
            for kind in range(1 - job, last + 1):
                hop(job, c, kind).wait_send()


def feed_forward(contexts, tensors, joined_t, tokens, cotangent, gain, attn_out, down, gate_w, up_w, feed_t):
    rows, width = tokens.shape
    units = down.shape[0]
    chunks = rows // CHUNK
    hops = tensors.bit_length() - 1
    anywhere = pl.BlockSpec(memory_space=pl.ANY)
    inside = pl.BlockSpec(memory_space=pltpu.VMEM)
    return pl.pallas_call(
        functools.partial(feed_forward_kernel, contexts, tensors),
        in_specs=[inside] * 4 + [anywhere] * 5,
        out_specs=[anywhere] * 12 + [inside] * 2,
        out_shape=[
            jax.ShapeDtypeStruct((rows, width), BF16),
            jax.ShapeDtypeStruct((rows, width), BF16),
            jax.ShapeDtypeStruct((rows, units), BF16),
            jax.ShapeDtypeStruct((rows, units), BF16),
            jax.ShapeDtypeStruct((rows, units), BF16),
            jax.ShapeDtypeStruct((rows, width), BF16),
            jax.ShapeDtypeStruct((rows, width), F32),
            jax.ShapeDtypeStruct((rows, width), BF16),
            jax.ShapeDtypeStruct((width // contexts, contexts * rows), BF16),
            jax.ShapeDtypeStruct((rows, width // 2), BF16),
            jax.ShapeDtypeStruct((rows, units), BF16),
            jax.ShapeDtypeStruct((2, rows, units), BF16),
            jax.ShapeDtypeStruct((joined_t.shape[0], rows), BF16),
            jax.ShapeDtypeStruct((8, width), F32),
        ],
        scratch_shapes=[
            pltpu.VMEM(attn_out.shape, BF16),
            pltpu.VMEM(down.shape, BF16),
            pltpu.VMEM(gate_w.shape, BF16),
            pltpu.VMEM(up_w.shape, BF16),
            pltpu.VMEM((2, rows, width // 2), BF16),
            pltpu.VMEM((2, 2, rows, width // 2), BF16),
            pltpu.VMEM((2, rows, width // 2), BF16),
            pltpu.VMEM((hops - 1, 2, rows, width // 2), BF16),
            pltpu.VMEM((rows, units), BF16),
            pltpu.VMEM((CHUNK, width), BF16),
            pltpu.VMEM((3, rows, units), BF16),
            pltpu.VMEM((CHUNK, width), BF16),
            pltpu.VMEM((CHUNK, width), F32),
            pltpu.SemaphoreType.DMA((4,)),
            pltpu.SemaphoreType.DMA((7 * chunks + 2,)),
            pltpu.SemaphoreType.DMA((2, hops + 1, chunks)),
            pltpu.SemaphoreType.DMA((2, hops + 1, chunks)),
        ]
        + [pltpu.SemaphoreType.DMA((2, chunks))] * 4
        + [pltpu.SemaphoreType.DMA((2, contexts - 1))] * 2
        + [pltpu.SemaphoreType.DMA((2,))]
        + [pltpu.SemaphoreType.DMA((2 + chunks,))] * 2,
        compiler_params=pltpu.CompilerParams(
            collective_id=0, has_side_effects=True, vmem_limit_bytes=63 * 1024 * 1024
        ),
        cost_estimate=pl.CostEstimate(
            flops=2 * rows * width * units * 6, bytes_accessed=60 * 1024 * 1024, transcendentals=0
        ),
        name="feed_forward",
    )(joined_t, tokens, cotangent, gain, attn_out, down, gate_w, up_w, feed_t)


def backward_kernel(
    contexts,
    group,
    order,
    q_t,
    latent,
    latent_t,
    rope_keys,
    rope_keys_t,
    latent_up,
    latent_up_t,
    exact_t,
    lse,
    dmix_t,
    cos_t,
    sin_t,
    joined_t,
    two_h,
    far_two_h,
    dgate_h,
    far_dgate_h,
    dup_h,
    near_h,
    dbranch_h,
    dq_t,
    grad_up,
    dlat_t,
    gate_o,
    up_o,
    out_o,
    far_out_o,
    far_dup_o,
    spread_o,
    kcat,
    k_t,
    q_wide,
    dmix_wide,
    q_nat,
    dmix_nat,
    delta,
    dq,
    pair,
    lat_acc,
    rope_acc,
    two,
    act,
    gate_w,
    up_w,
    arrived,
    up_arrived,
    out_w,
    joined,
    load_sem,
    dup_sem,
    dup_got,
    out_sem,
    out_got,
    gate_sem,
    gate_got,
    up_sem,
    up_got,
    spread_sem,
    spread_got,
):
    heads, _, rows = q_t.shape
    keys = latent.shape[0]
    tiles = keys // HALF
    last = contexts - 1
    half = two.shape[1]
    share = half // contexts
    d = lax.axis_index("dp")
    z = lax.axis_index("context")
    loads = [
        pltpu.make_async_copy(
            two_h.at[:, pl.ds(pl.multiple_of(d * half, 128), half)],
            two.at[0:rows],
            load_sem.at[0],
        ),
        pltpu.make_async_copy(far_two_h, two.at[rows : 2 * rows], load_sem.at[1]),
        pltpu.make_async_copy(dgate_h, act.at[0:rows], load_sem.at[2]),
        pltpu.make_async_copy(far_dgate_h, act.at[rows : 2 * rows], load_sem.at[3]),
    ]
    for load in loads:
        load.start()
    greet(line_of(z, contexts) + [{"dp": 1 - d}])

    swap_dup = pltpu.make_async_remote_copy(
        src_ref=dup_h,
        dst_ref=far_dup_o,
        send_sem=dup_sem,
        recv_sem=dup_got,
        device_id={"dp": 1 - d},
        device_id_type=MESH,
    )
    swap_dup.start()

    def line(src, dst, send_sem, recv_sem, way):
        return pltpu.make_async_remote_copy(
            src_ref=src,
            dst_ref=dst,
            send_sem=send_sem,
            recv_sem=recv_sem,
            device_id={"context": z + 1 - 2 * way},
            device_id_type=MESH,
        )

    along = [z, last - z]

    def spread(way, step):
        src = near_h.at[way] if step == 2 else spread_o.at[way, step - 3]
        i = (way, step - 2)
        return line(src, spread_o.at[i], spread_sem.at[i], spread_got.at[i], way)

    def spread_start(step):
        if step > last:
            return
        for way in range(2):
            if step > 2:

                @pl.when(along[way] >= step - 1)
                def _():
                    spread(way, step - 1).wait_recv()

            @pl.when((along[way] >= step - 1) & (along[way] < last))
            def _():
                spread(way, step).start()

    def spread_end():
        for way in range(2):
            for step in range(2, last + 1):
                if step == last:

                    @pl.when(along[way] >= step)
                    def _():
                        spread(way, step).wait_recv()

                @pl.when((along[way] >= step - 1) & (along[way] < last))
                def _():
                    spread(way, step).wait_send()

    def share_of(ref, index):
        return ref.at[pl.ds(pl.multiple_of(index * share, 16), share)]

    def farthest(way, step):
        right = z + 2 * contexts - step if way == 0 else contexts + step - 1 - along[1]
        return lax.rem(right, contexts)

    def reduce(ref, dst, send_sem, recv_sem, way, step):
        return line(
            share_of(ref, farthest(way, step)), dst, send_sem, recv_sem, way
        )

    def gate_step(way, step):
        i = (way, step - 1)
        return reduce(gate_w, arrived.at[i], gate_sem.at[i], gate_got.at[i], way, step)

    def up_step(way):
        return reduce(up_w, up_arrived.at[way], up_sem.at[way], up_got.at[way], way, 1)

    def add_rows(dst, src):
        @pl.loop(0, share // 16)
        def _(i):
            r = pl.ds(pl.multiple_of(i * 16, 16), 16)
            dst[r, :] = (dst[r, :].astype(F32) + src[r, :].astype(F32)).astype(BF16)

    def gate_start(step):
        if step > last:
            return
        for way in range(2):
            if step > 1:

                @pl.when((along[way] >= 1) & (along[way] < step))
                def _():
                    gate_step(way, step - 1).wait_recv()
                    add_rows(share_of(gate_w, farthest(way, step)), arrived.at[way, step - 2])

            @pl.when(along[way] < step)
            def _():
                gate_step(way, step).start()

    def gate_end():
        own = pl.multiple_of(z * share, 16)
        for way in range(2):

            @pl.when(along[way] >= 1)
            def _():
                gate_step(way, last).wait_recv()

        @pl.loop(0, share // 16)
        def _(i):
            r = pl.ds(pl.multiple_of(own + i * 16, 16), 16)
            q = pl.ds(pl.multiple_of(i * 16, 16), 16)
            value = gate_w[r, :].astype(F32)
            for way in range(2):
                value = jnp.where(
                    along[way] >= 1, value + arrived[way, last - 1, q, :].astype(F32), value
                )
            gate_o[q, :] = value

        for way in range(2):
            for step in range(1, last + 1):

                @pl.when(along[way] < step)
                def _():
                    gate_step(way, step).wait_send()

    upper = 1 - z // ((contexts + 1) // 2)
    count = half // 256

    def weight(ref, start):
        def tile(i):
            n = i + upper * (count - 1 - 2 * i)
            cols = pl.ds(pl.multiple_of(n * 256, 256), 256)
            ref[cols, :] = transposed_times(two[:, cols], act[...]).astype(BF16)

        pl.loop(0, 2)(tile)
        start()
        pl.loop(2, count)(tile)

    factor = SCALE * LOG2E
    row = lax.broadcasted_iota(jnp.int32, (HALF, rows), 0)
    spot = lax.broadcasted_iota(jnp.int32, (1, rows), 1)
    spot = jnp.where(
        spot < HALF, order[2 * z] * HALF + spot, order[2 * z + 1] * HALF + spot - HALF
    )

    def begin(g):
        for h in range(group):
            e = g * group + h
            span = slice(e * 128, (e + 1) * 128)
            kcat[h, :, :128] = matmul(latent[...], latent_up[:, span]).astype(BF16)
            kcat[h, :, 128:] = rope_keys[...]
            k_t[h, 0:64, :] = matmul(
                latent_up_t[e * 128 : e * 128 + 64, :], latent_t[...]
            ).astype(BF16)
            k_t[h, 64:96, :] = rope_keys_t[...]
            q_wide[h, 0:64, :] = q_t[e, 0:64, :]
            q_wide[h, 64:128, :] = jnp.zeros((64, rows), BF16)
            q_wide[h, 128:160, :] = q_t[e, 64:96, :]
            q_wide[h, 160:256, :] = jnp.zeros((96, rows), BF16)
            q_nat[h] = q_wide[h].T
            piece = dmix_t[e * V_DIM : (e + 1) * V_DIM, :]
            dmix_wide[h, 0:64, :] = jnp.zeros_like(piece)
            dmix_wide[h, 64:128, :] = piece
            dmix_nat[h] = dmix_wide[h].T
            delta[h] = jnp.sum(piece.astype(F32) * exact_t[e], axis=0, keepdims=True)
            dq[h] = jnp.zeros((96, rows), F32)

    def tiles_of(g, first, end):
        lane = lax.broadcasted_iota(jnp.int32, (1, 128), 1)
        scale = jnp.where(lane < NOPE, SCALE, 1.0).astype(F32)

        @pl.loop(first, end)
        def _(j):
            lines = pl.ds(pl.multiple_of(j * HALF, HALF), HALF)
            block = 2 * lax.rem(z + contexts - j // 2, contexts) + lax.rem(j, 2)
            allowed = row <= spot - order[block] * HALF
            turned = jnp.zeros((HALF, 128), F32)
            for h in range(group):
                e = g * group + h
                s = matmul(kcat[h, lines, :], q_wide[h])
                p = jnp.where(allowed, jnp.exp2(s * factor - lse[e]), 0.0)
                dp = matmul(kcat[h, lines, :128], dmix_wide[h])
                ds = (p * (dp - delta[h])).astype(BF16)
                dq[h] += matmul(k_t[h, :, lines], ds)
                dk = matmul(ds, q_nat[h])
                dv = matmul(p.astype(BF16), dmix_nat[h])
                pair[h, lines, :] = ((dk[:, :128] + dv) * scale).astype(BF16)
                turned += dk[:, 128:]
            rope_acc[lines, :] = turned if g == 0 else rope_acc[lines, :] + turned

    def finish(g):
        cosine = cos_t[...]
        sine = sin_t[...]
        for h in range(group):
            e = g * group + h
            span = slice(e * 128, (e + 1) * 128)
            value = dq[h] * SCALE
            first = value[64:80]
            second = value[80:96]
            dq_t[e, 0:64, :] = value[0:64].astype(BF16)
            dq_t[e, 64:80, :] = (first * cosine + second * sine).astype(BF16)
            dq_t[e, 80:96, :] = (second * cosine - first * sine).astype(BF16)
            grad_up[:, span] = matmul(latent_t[...], pair[h]).astype(BF16)
            change = times_transposed(latent_up[:, span], pair[h])
            lat_acc[...] = change if e == 0 else lat_acc[...] + change

    groups = heads // group
    total = groups * tiles
    stops = [total * (i + 1) // (last + 1) for i in range(last)]

    spread_start(2)
    for load in loads:
        load.wait()
    weight(gate_w, lambda: gate_start(1))
    done = 0
    for i, stop in enumerate(stops + [total]):
        while done < stop:
            g = done // tiles
            until = min(stop, (g + 1) * tiles)
            if done == g * tiles:
                begin(g)
            tiles_of(g, done - g * tiles, until - g * tiles)
            if until == (g + 1) * tiles:
                finish(g)
            done = until
        if i < last:
            gate_start(i + 2)
            spread_start(i + 3)
        if i == min(1, last - 1):
            swap_dup.wait_recv()
            again = [
                pltpu.make_async_copy(dup_h, act.at[0:rows], load_sem.at[2]),
                pltpu.make_async_copy(far_dup_o, act.at[rows : 2 * rows], load_sem.at[3]),
            ]
            for load in again:
                load.start()
            for load in again:
                load.wait()

            def up_start():
                for way in range(2):

                    @pl.when(along[way] == 0)
                    def _():
                        up_step(way).start()

            weight(up_w, up_start)
            parts = [
                pltpu.make_async_copy(
                    dbranch_h.at[:, e * half : (e + 1) * half],
                    two.at[e * rows : (e + 1) * rows],
                    load_sem.at[2 + e],
                )
                for e in range(2)
            ]
            for load in parts:
                load.start()
            keep = pltpu.make_async_copy(up_w, up_o, load_sem.at[0])
            keep.start()
            joined[...] = joined_t[...].T
            for load in parts:
                load.wait()
            for e in range(2):

                @pl.loop(0, half // 256)
                def _(n):
                    cols = pl.ds(pl.multiple_of(n * 256, 256), 256)
                    lines = pl.ds(pl.multiple_of(e * half + n * 256, 256), 256)
                    out_w[lines, :] = transposed_times(
                        two[e * rows : (e + 1) * rows, cols], joined[...]
                    ).astype(BF16)

            swap_out = pltpu.make_async_remote_copy(
                src_ref=out_w.at[pl.ds(pl.multiple_of((1 - d) * half, 16), half)],
                dst_ref=far_out_o,
                send_sem=out_sem,
                recv_sem=out_got,
                device_id={"dp": 1 - d},
                device_id_type=MESH,
            )
            swap_out.start()
            keep_out = pltpu.make_async_copy(
                out_w.at[pl.ds(pl.multiple_of(d * half, 16), half)], out_o, load_sem.at[1]
            )
            keep_out.start()

    dlat_t[0:KV_RANK, :] = lat_acc[...].astype(BF16)
    dlat_t[KV_RANK:, :] = (rope_acc[...] * SCALE).T[:ROPE].astype(BF16)
    gate_end()
    spread_end()
    keep.wait()
    keep_out.wait()
    swap_dup.wait_send()
    for way in range(2):

        @pl.when(along[way] == 0)
        def _():
            up_step(way).wait_send()

        @pl.when(along[way] == 1)
        def _():
            up_step(way).wait_recv()
            piece = share_of(up_w, farthest(way, 2))
            add_rows(piece, up_arrived.at[way])
            again = pltpu.make_async_copy(
                piece, share_of(up_o, farthest(way, 2)), load_sem.at[2]
            )
            again.start()
            again.wait()

    swap_out.wait()


def backward(
    contexts,
    order,
    q_t,
    latent,
    latent_t,
    rope_keys,
    rope_keys_t,
    latent_up,
    latent_up_t,
    exact_t,
    lse,
    dmix_t,
    cos_t,
    sin_t,
    joined_t,
    two,
    far_two,
    dgate,
    far_dgate,
    dup,
    near,
    dbranch,
):
    heads, _, rows = q_t.shape
    keys = latent.shape[0]
    group = GROUP
    units = dup.shape[1]
    half = far_two.shape[1]
    share = half // contexts
    last = contexts - 1
    anywhere = pl.BlockSpec(memory_space=pl.ANY)
    inside = pl.BlockSpec(memory_space=pltpu.VMEM)
    dma = pltpu.SemaphoreType.DMA
    return pl.pallas_call(
        functools.partial(backward_kernel, contexts, group),
        in_specs=[pl.BlockSpec(memory_space=pltpu.SMEM)] + [inside] * 13 + [anywhere] * 7,
        out_specs=[inside] * 4 + [anywhere] * 5,
        out_shape=[
            jax.ShapeDtypeStruct((heads, 96, rows), BF16),
            jax.ShapeDtypeStruct((KV_RANK, heads * 128), BF16),
            jax.ShapeDtypeStruct((KV_RANK + ROPE, keys), BF16),
            jax.ShapeDtypeStruct((share, units), F32),
            jax.ShapeDtypeStruct((half, units), BF16),
            jax.ShapeDtypeStruct((half, joined_t.shape[0]), BF16),
            jax.ShapeDtypeStruct((half, joined_t.shape[0]), BF16),
            jax.ShapeDtypeStruct((rows, units), BF16),
            jax.ShapeDtypeStruct((2, last - 1, rows, units), BF16),
        ],
        scratch_shapes=[
            pltpu.VMEM((group, keys, 256), BF16),
            pltpu.VMEM((group, 96, keys), BF16),
            pltpu.VMEM((group, 256, rows), BF16),
            pltpu.VMEM((group, 128, rows), BF16),
            pltpu.VMEM((group, rows, 256), BF16),
            pltpu.VMEM((group, rows, 128), BF16),
            pltpu.VMEM((group, 1, rows), F32),
            pltpu.VMEM((group, 96, rows), F32),
            pltpu.VMEM((group, keys, 128), BF16),
            pltpu.VMEM((KV_RANK, keys), F32),
            pltpu.VMEM((keys, 128), F32),
            pltpu.VMEM((2 * rows, half), BF16),
            pltpu.VMEM((2 * rows, units), BF16),
            pltpu.VMEM((half, units), BF16),
            pltpu.VMEM((half, units), BF16),
            pltpu.VMEM((2, last, share, units), BF16),
            pltpu.VMEM((2, share, units), BF16),
            pltpu.VMEM((2 * half, joined_t.shape[0]), BF16),
            pltpu.VMEM((rows, joined_t.shape[0]), BF16),
            dma((4,)),
            dma,
            dma,
            dma,
            dma,
            dma((2, last)),
            dma((2, last)),
            dma((2,)),
            dma((2,)),
            dma((2, last - 1)),
            dma((2, last - 1)),
        ],
        compiler_params=pltpu.CompilerParams(
            collective_id=1, has_side_effects=True, vmem_limit_bytes=65000 * 1024
        ),
        cost_estimate=pl.CostEstimate(
            flops=2 * heads * rows * keys * 1000,
            bytes_accessed=40 * 1024 * 1024,
            transcendentals=heads * rows * keys,
        ),
        name="backward",
    )(
        order,
        q_t,
        latent,
        latent_t,
        rope_keys,
        rope_keys_t,
        latent_up,
        latent_up_t,
        exact_t,
        lse,
        dmix_t,
        cos_t,
        sin_t,
        joined_t,
        two,
        far_two,
        dgate,
        far_dgate,
        dup,
        near,
        dbranch,
    )


def tail_kernel(
    contexts,
    tensors,
    split,
    dq_t,
    query_up_t,
    query_t,
    query_normed,
    query_inverse,
    all_gains,
    dlat,
    cache_t,
    cache_inverse_t,
    cos_t,
    sin_t,
    lat_grad,
    first_inverse,
    mlp_gain_grad,
    out_h,
    far_out_h,
    hidden_h,
    near_h,
    spread_h,
    feed_t_h,
    up_h,
    one_t_h,
    query_down_h,
    latent_down_t_h,
    tokens_h,
    feed_h,
    norm_o,
    low_q_o,
    low_l_o,
    small_q_o,
    small_l_o,
    out_o,
    up_o,
    down_o,
    gain_o,
    feed_o,
    q_part,
    q_near,
    q_across,
    q_final,
    d_near,
    d_acc,
    d_across,
    d_got,
    d_all,
    d_final,
    u_w,
    u_far,
    u_got,
    l_far,
    l_got,
    wide,
    up_got,
    out_w,
    out_far,
    out_got,
    long,
    feed_t,
    down_w,
    down_far,
    f_part,
    f_near,
    f_across,
    dqa,
    dkva_t,
    one_t,
    low_q,
    low_l,
    low_q_far,
    low_l_far,
    low_q_got,
    low_l_got,
    low_q_all,
    low_l_all,
    query_down,
    latent_down_t,
    dh1,
    stage,
    gains,
    gains_far,
    gains_got,
    send_sem,
    recv_sem,
    load_sem,
):
    rows = dlat.shape[1] // contexts
    width = wide.shape[1]
    half = width // 2
    share = half // contexts
    last = contexts - 1
    rank = query_normed.shape[1]
    kv = cache_t.shape[0]
    first_gain = slice(0, width)
    query_gain = slice(2 * width, 2 * width + rank)
    latent_gain = slice(2 * width + rank, 2 * width + rank + kv)
    d = lax.axis_index("dp")
    z = lax.axis_index("context")
    t = lax.axis_index("tensor")
    bit = lax.rem(t, 2)
    others = [t + 1 - 2 * bit]
    step = 2
    while step < tensors:
        others.append(t + step - 2 * step * lax.rem(t // step, 2))
        step *= 2
    spot = lax.rem(t, split)
    sharers = [t - spot + lax.rem(spot + k, split) for k in range(1, split)]

    used = [0]

    def remote(src, dst, **device):
        i = used[0]
        used[0] += 1
        return pltpu.make_async_remote_copy(
            src_ref=src,
            dst_ref=dst,
            send_sem=send_sem.at[i],
            recv_sem=recv_sem.at[i],
            device_id=device,
            device_id_type=MESH,
        )

    loaded = [0]

    def local(src, dst):
        i = loaded[0]
        loaded[0] += 1
        return pltpu.make_async_copy(src, dst, load_sem.at[i])

    def only(condition, copy, what):
        @pl.when(condition)
        def _():
            getattr(copy, what)()

    def add_rows(dst, left, right, count, chunk=16):
        @pl.loop(0, count // chunk)
        def _(i):
            r = pl.ds(pl.multiple_of(i * chunk, chunk), chunk)
            dst[r, :] = (left[r, :].astype(F32) + right[r, :].astype(F32)).astype(BF16)

    def piece(ref, index, size):
        return ref.at[pl.ds(pl.multiple_of(index * size, 16), size)]

    load_out = [local(out_h, out_w), local(far_out_h, out_far)]
    load_tokens = local(tokens_h, wide)
    load_hidden = [(None, local(hidden_h, long.at[0:rows]))]
    for s in range(1, contexts):
        back = contexts - s
        dst = long.at[s * rows : (s + 1) * rows]
        right = near_h.at[0] if s == 1 else spread_h.at[0, s - 2]
        left = near_h.at[1] if back == 1 else spread_h.at[1, back - 2]
        load_hidden.append((z >= s, local(right, dst)))
        load_hidden.append((z < s, local(left, dst)))
    load_feed_t = local(feed_t_h, feed_t)
    load_one = local(one_t_h, one_t)
    load_down = [local(query_down_h, query_down), local(latent_down_t_h, latent_down_t)]

    def load_feed(c):
        return [
            local(
                feed_h.at[pl.ds(c * CHUNK, CHUNK), h * half : (h + 1) * half], f_part.at[h]
            )
            for h in range(2)
        ]

    feed_loads = [load_feed(c) for c in range(rows // CHUNK)]
    for copy in load_out:
        copy.start()
    load_feed_t.start()
    for condition, copy in load_hidden:
        if condition is None:
            copy.start()
        else:
            only(condition, copy, "start")
    for copy in [load_one, load_tokens] + load_down + feed_loads[0]:
        copy.start()

    peers = others if split == 2 else sharers
    greet([{"tensor": i} for i in peers] + line_of(z, contexts) + [{"dp": 1 - d}])

    along = [z, last - z]

    def farthest(way, step):
        right = z + 2 * contexts - step if way == 0 else contexts + step - 1 - along[1]
        return lax.rem(right, contexts)

    def line_step(w, got, way, step, first):
        return remote(
            piece(w, farthest(way, step), share),
            got.at[way, step - first],
            context=z + 1 - 2 * way,
        )

    up_w = long
    up_steps = {
        (way, step): line_step(up_h if step == 2 else up_w, up_got, way, step, 2)
        for way in range(2)
        for step in range(2, last + 1)
    }
    out_steps = {
        (way, step): line_step(out_far, out_got, way, step, 1)
        for way in range(2)
        for step in range(1, last + 1)
    }

    def line_start(steps, w, got, first, step):
        for way in range(2):
            if step > first:

                @pl.when((along[way] >= 1) & (along[way] < step))
                def _():
                    steps[way, step - 1].wait_recv()
                    target = piece(w, farthest(way, step), share)
                    add_rows(target, target, got.at[way, step - 1 - first], share)

            only(along[way] < step, steps[way, step], "start")

    def line_end(steps, w, got, first, result):
        for way in range(2):
            only(along[way] >= 1, steps[way, last], "wait_recv")

        @pl.loop(0, share // 16)
        def _(i):
            r = pl.ds(pl.multiple_of(z * share + i * 16, 16), 16)
            q = pl.ds(pl.multiple_of(i * 16, 16), 16)
            value = w[r, :].astype(F32)
            for way in range(2):
                value = jnp.where(
                    along[way] >= 1, value + got[way, last - first, q, :].astype(F32), value
                )
            result[q, :] = value

        for way in range(2):
            for step in range(first, last + 1):
                only(along[way] < step, steps[way, step], "wait_send")

    line_start(up_steps, up_w, up_got, 2, 2)

    d_rows = dlat.shape[0] // 2
    d_pair = remote(dlat.at[pl.ds(pl.multiple_of((1 - bit) * d_rows, 16), d_rows)], d_near, tensor=others[0])
    d_pair.start()

    q_rows = rows // 2
    for h in range(2):
        q_part[h] = transposed_times(
            dq_t[:, h * q_rows : (h + 1) * q_rows], query_up_t[...]
        ).astype(BF16)
    q_pair = remote(q_part.at[1 - bit], q_near, tensor=others[0])
    q_pair.start()

    for copy in load_out:
        copy.wait()
    add_rows(out_far, out_far, out_w, half, 32)
    line_start(out_steps, out_far, out_got, 1, 1)

    u_w[...] = times_transposed(query_t[...], dq_t[...]).astype(BF16)
    u_half = u_w.shape[0] // 2
    l_half = lat_grad.shape[0] // 2
    u_pair = remote(
        u_w.at[pl.ds(pl.multiple_of((1 - d) * u_half, 16), u_half)], u_far, dp=1 - d
    )
    l_pair = remote(
        lat_grad.at[pl.ds(pl.multiple_of((1 - d) * l_half, 16), l_half)], l_far, dp=1 - d
    )
    u_pair.start()
    l_pair.start()

    d_pair.wait_recv()
    mine = pl.multiple_of(bit * d_rows, 16)

    @pl.loop(0, d_rows // 16)
    def _(i):
        r = pl.ds(pl.multiple_of(i * 16, 16), 16)
        own = pl.ds(pl.multiple_of(mine + i * 16, 16), 16)
        value = (dlat[own, :].astype(F32) + d_near[r, :].astype(F32)).astype(BF16)
        for s in range(contexts):
            d_acc[s, r, :] = value[:, s * rows : (s + 1) * rows]

    d_hops = []
    lanes = rows
    start = 0
    for k in range(1, len(others)):
        lanes //= 2
        side = lax.rem(t // (2**k), 2)
        give = pl.ds(pl.multiple_of(start + (1 - side) * lanes, 128), lanes)
        start = pl.multiple_of(start + side * lanes, 128)
        d_hops.append(
            (remote(d_acc.at[:, :, give], d_across.at[k - 1, :, :, 0:lanes], tensor=others[k]),
             start, lanes)
        )

    d_hops[0][0].start()
    q_pair.wait_recv()
    add_rows(q_near, q_near, q_part.at[bit], q_rows, 32)
    q_hops = []
    for k in range(1, len(others)):
        src = q_near if k == 1 else q_across.at[k - 2]
        q_hops.append(remote(src, q_across.at[k - 1], tensor=others[k]))
    q_hops[0].start()

    load_feed_t.wait()
    for condition, copy in load_hidden:
        if condition is None:
            copy.wait()
        else:
            only(condition, copy, "wait")
    chunk = 2 * share // 5 if (2 * share // 5) % 16 == 0 else share

    @pl.loop(0, 2 * share // chunk)
    def _(i):
        r = pl.ds(pl.multiple_of(i * chunk, 16), chunk)
        down_w[r, :] = matmul(feed_t[r, :], long[...]).astype(BF16)

    load_up = local(up_h, long.at[0:half])
    load_up.start()
    down_pair = remote(piece(down_w, 1 - d, share), down_far, dp=1 - d)

    f_pairs, f_hops, f_backs = [], [], []
    for c in range(rows // CHUNK):
        span = pl.ds(c * CHUNK, CHUNK)
        f_pairs.append(remote(f_part.at[1 - bit], f_near.at[c], tensor=others[0]))
        hops = []
        for k in range(1, len(others)):
            src = f_near.at[c] if k == 1 else f_across.at[k - 2, c]
            hops.append(remote(src, f_across.at[k - 1, c], tensor=others[k]))
        f_hops.append(hops)
        here = f_across.at[len(others) - 2, c]
        f_backs.append(
            (remote(here, feed_o.at[span, pl.ds(pl.multiple_of(bit * half, 128), half)], tensor=others[0]), local(here, feed_o.at[span, pl.ds(pl.multiple_of(bit * half, 128), half)]))
        )

    def feed_pair(c):
        for copy in feed_loads[c]:
            copy.wait()
        f_pairs[c].start()

    def feed_across(c):
        f_pairs[c].wait_recv()
        add_rows(f_near.at[c], f_near.at[c], f_part.at[bit], CHUNK, 32)
        f_hops[c][0].start()
        f_pairs[c].wait_send()
        if c + 1 < rows // CHUNK:
            for copy in feed_loads[c + 1]:
                copy.start()

    def feed_back(c):
        for k, hop in enumerate(f_hops[c]):
            hop.wait_recv()
            src = f_near.at[c] if k == 0 else f_across.at[k - 1, c]
            add_rows(f_across.at[k, c], src, f_across.at[k, c], CHUNK, 32)
            if k < len(f_hops[c]) - 1:
                f_hops[c][k + 1].start()
        for back in f_backs[c]:
            back.start()


    for k, (hop, begin, lane) in enumerate(d_hops):
        hop.wait_recv()
        keep = pl.ds(begin, lane)

        @pl.loop(0, contexts)
        def _(s):
            @pl.loop(0, d_rows // 16)
            def _(i):
                r = pl.ds(pl.multiple_of(i * 16, 16), 16)
                d_acc[s, r, keep] = (
                    d_acc[s, r, keep].astype(F32) + d_across[k, s, r, 0:lane].astype(F32)
                ).astype(BF16)

        if k + 1 < len(d_hops):
            d_hops[k + 1][0].start()
    keep = pl.ds(start, lanes)
    d_sends = [
        remote(
            d_acc.at[s, :, keep],
            d_got.at[s - 1],
            context=lax.rem(z + contexts - s, contexts),
        )
        for s in range(1, contexts)
    ]
    for copy in d_sends:
        copy.start()
    final = len(q_hops) - 1
    for k, hop in enumerate(q_hops):
        hop.wait_recv()
        src = q_near if k == 0 else q_across.at[k - 1]
        dst = q_final.at[bit] if k == final else q_across.at[k]
        add_rows(dst, src, q_across.at[k], q_rows, 32)
        if k < final:
            q_hops[k + 1].start()
    q_back = remote(q_final.at[bit], q_final.at[bit], tensor=others[0])
    q_back.start()

    feed_pair(0)
    load_up.wait()
    line_start(up_steps, up_w, up_got, 2, 3) if last >= 3 else None
    line_start(out_steps, out_far, out_got, 1, 2) if last >= 2 else None
    u_pair.wait_recv()
    l_pair.wait_recv()

    @pl.loop(0, u_half // 16)
    def _(i):
        r = pl.ds(pl.multiple_of(i * 16, 16), 16)
        own = pl.ds(pl.multiple_of(d * u_half + i * 16, 16), 16)
        u_far[r, :] = (u_far[r, :].astype(F32) + u_w[own, :].astype(F32)).astype(BF16)

    @pl.loop(0, l_half // 16)
    def _(i):
        r = pl.ds(pl.multiple_of(i * 16, 16), 16)
        own = pl.ds(pl.multiple_of(d * l_half + i * 16, 16), 16)
        l_far[r, :] = (l_far[r, :].astype(F32) + lat_grad[own, :].astype(F32)).astype(BF16)

    u_size = u_half // contexts
    l_size = l_half // contexts
    small_sends = []
    for by in range(1, contexts):
        owner = lax.rem(z + by, contexts)
        small_sends.append(remote(piece(u_far, owner, u_size), u_got.at[by - 1], context=owner))
        small_sends.append(remote(piece(l_far, owner, l_size), l_got.at[by - 1], context=owner))
    for copy in small_sends:
        copy.start()
    feed_across(0)

    q_back.wait_recv()
    q_sum = jnp.zeros((8, rank), F32)

    def query_rows(i, acc):
        r = pl.ds(pl.multiple_of(i * 32, 32), 32)
        h = i // (q_rows // 32)
        o = pl.ds(pl.multiple_of(lax.rem(i, q_rows // 32) * 32, 32), 32)
        grad = q_final[h, o, :].astype(F32)
        normed = query_normed[r, :].astype(F32)
        weighted = grad * all_gains[:, query_gain]
        mean = jnp.mean(weighted * normed, axis=-1, keepdims=True)
        dqa[r, :] = (query_inverse[r, :] * (weighted - normed * mean)).astype(BF16)
        return acc + jnp.sum((grad * normed).reshape(4, 8, rank), axis=0)

    q_sum = lax.fori_loop(0, rows // 32, query_rows, q_sum)

    for copy in d_sends:
        copy.wait_recv()

    @pl.loop(0, d_rows // 16)
    def _(i):
        r = pl.ds(pl.multiple_of(i * 16, 16), 16)
        value = d_acc[0, r, keep].astype(F32)
        for s in range(1, contexts):
            value += d_got[s - 1, r, :].astype(F32)
        d_all[r, keep] = value.astype(BF16)

    d_gathers = []
    for k in range(len(others) - 1, 0, -1):
        here = d_all.at[:, pl.ds(start, lanes)]
        hop = remote(here, here, tensor=others[k])
        hop.start()
        hop.wait_recv()
        d_gathers.append(hop)
        side = lax.rem(t // (2**k), 2)
        start = pl.multiple_of(start - side * lanes, 128)
        lanes *= 2
    d_back = remote(d_all, d_final, tensor=others[0])
    d_back.start()
    if rows // CHUNK > 1:
        feed_pair(1)
    d_back.wait_recv()

    top = jnp.where(bit == 0, d_all[...], d_final[...]).astype(F32)
    bottom = jnp.where(bit == 0, d_final[...], d_all[...]).astype(F32)
    grad = jnp.concatenate([top, bottom], axis=0)
    lat = grad[:kv]
    normed = cache_t[...].astype(F32)
    column = jnp.broadcast_to(all_gains[:, latent_gain], (8, kv)).T[:, 0:1]
    weighted = lat * column
    mean = jnp.mean(weighted * normed, axis=0, keepdims=True)
    dkva_t[0:kv, :] = (cache_inverse_t[...] * (weighted - normed * mean)).astype(BF16)
    c_sum = jnp.sum((lat * normed).T, axis=0, keepdims=True)
    first = grad[kv : kv + 16]
    second = grad[kv + 16 :]
    cosine = cos_t[...]
    sine = sin_t[...]
    dkva_t[kv : kv + 16, :] = (first * cosine + second * sine).astype(BF16)
    dkva_t[kv + 16 :, :] = (second * cosine - first * sine).astype(BF16)

    load_one.wait()
    size = share // split

    @pl.loop(0, 2 * contexts)
    def _(i):
        r = pl.ds(pl.multiple_of((i * split + spot) * size, 16), size)
        o = pl.ds(pl.multiple_of(i * size, 16), size)
        low_q[o, :] = matmul(one_t[r, :], dqa[...]).astype(BF16)
        low_l[o, :] = times_transposed(one_t[r, :], dkva_t[...]).astype(BF16)

    low_half = contexts * size
    give = pl.ds(pl.multiple_of((1 - d) * low_half, 16), low_half)
    low_pairs = [
        remote(low_q.at[give], low_q_far, dp=1 - d),
        remote(low_l.at[give], low_l_far, dp=1 - d),
    ]
    for copy in low_pairs:
        copy.start()
    down_pair.start()
    line_start(out_steps, out_far, out_got, 1, 3) if last >= 3 else None
    if rows // CHUNK > 1:
        feed_across(1)

    for copy in load_down:
        copy.wait()
    load_tokens.wait()
    a_sum = jnp.zeros((8, width), F32)
    gains[...] = jnp.zeros_like(gains)
    block = dh1.shape[0]
    tall = 512

    def first_rows(c, acc):
        span = pl.ds(pl.multiple_of(c * block, block), block)
        for n in range(width // tall):
            lines = slice(n * tall, (n + 1) * tall)
            dh1[:, lines] = times_transposed(dqa[span, :], query_down[lines, :])
            dh1[:, lines] += transposed_times(dkva_t[:, span], latent_down_t[:, lines])

        def few(i, inner):
            o = pl.ds(pl.multiple_of(i * 16, 16), 16)
            r = pl.ds(pl.multiple_of(c * block + i * 16, 16), 16)
            grad = dh1[o, :]
            inverse = first_inverse[r, :]
            normed = wide[r, :].astype(F32) * inverse
            weighted = grad * all_gains[:, first_gain]
            mean = jnp.mean(weighted * normed, axis=-1, keepdims=True)
            wide[r, :] = (inverse * (weighted - normed * mean)).astype(BF16)
            return inner + jnp.sum((grad * normed).reshape(2, 8, width), axis=0)

        return lax.fori_loop(0, block // 16, few, acc)

    for c in range(rows // block):
        a_sum = first_rows(c, a_sum)
    save_norm = local(wide, norm_o)
    save_norm.start()

    parts = [
        jnp.sum(a_sum, axis=0, keepdims=True),
        jnp.sum(mlp_gain_grad[...], axis=0, keepdims=True),
        jnp.sum(q_sum, axis=0, keepdims=True),
        c_sum,
    ]
    line = jnp.concatenate(parts, axis=1)
    cut = gains.shape[1]
    for r in range(8):
        gains[r : r + 1, :] = line[:, r * cut : (r + 1) * cut]
    gains_pair = remote(gains, gains_far, dp=1 - d)
    gains_pair.start()

    feed_back(0)
    gains_pair.wait_recv()
    gains_far[...] = gains_far[...] + gains[...]
    gains_sends = [
        remote(gains_far, gains_got.at[by - 1], context=lax.rem(z + by, contexts))
        for by in range(1, contexts)
    ]
    for copy in gains_sends:
        copy.start()
    for copy in low_pairs:
        copy.wait_recv()

    @pl.loop(0, low_half // 16)
    def _(i):
        r = pl.ds(pl.multiple_of(i * 16, 16), 16)
        own = pl.ds(pl.multiple_of(d * low_half + i * 16, 16), 16)
        low_q_far[r, :] = (
            low_q_far[r, :].astype(F32) + low_q[own, :].astype(F32)
        ).astype(BF16)
        low_l_far[r, :] = (
            low_l_far[r, :].astype(F32) + low_l[own, :].astype(F32)
        ).astype(BF16)

    low_sends = []
    for by in range(1, contexts):
        owner = lax.rem(z + by, contexts)
        low_sends.append(
            remote(piece(low_q_far, owner, size), low_q_got.at[by - 1], context=owner)
        )
        low_sends.append(
            remote(piece(low_l_far, owner, size), low_l_got.at[by - 1], context=owner)
        )
    for copy in low_sends:
        copy.start()
    for copy in small_sends:
        copy.wait_recv()
    for far, got, result, count in (
        (u_far, u_got, small_q_o, u_size),
        (l_far, l_got, small_l_o, l_size),
    ):

        @pl.loop(0, count // 16)
        def _(i):
            r = pl.ds(pl.multiple_of(z * count + i * 16, 16), 16)
            q = pl.ds(pl.multiple_of(i * 16, 16), 16)
            value = far[r, :].astype(F32)
            for by in range(1, contexts):
                value += got[by - 1, q, :].astype(F32)
            result[q, :] = value

    for step in range(4, last + 1):
        line_start(out_steps, out_far, out_got, 1, step)
        line_start(up_steps, up_w, up_got, 2, step)
    if rows // CHUNK > 1:
        feed_back(1)
    for copy in low_sends:
        copy.wait_recv()

    @pl.loop(0, size // 16)
    def _(i):
        r = pl.ds(pl.multiple_of(z * size + i * 16, 16), 16)
        q = pl.ds(pl.multiple_of(i * 16, 16), 16)
        for far, got, everyone in (
            (low_q_far, low_q_got, low_q_all),
            (low_l_far, low_l_got, low_l_all),
        ):
            value = far[r, :].astype(F32)
            for by in range(1, contexts):
                value += got[by - 1, q, :].astype(F32)
            everyone[spot, q, :] = value.astype(BF16)

    low_gathers = []
    for sharer in sharers:
        for everyone in (low_q_all, low_l_all):
            here = everyone.at[spot]
            copy = remote(here, here, tensor=sharer)
            copy.start()
            low_gathers.append(copy)
    down_pair.wait_recv()

    @pl.loop(0, share // 16)
    def _(i):
        r = pl.ds(pl.multiple_of(d * share + i * 16, 16), 16)
        q = pl.ds(pl.multiple_of(i * 16, 16), 16)
        stage[q, :] = down_w[r, :].astype(F32) + down_far[q, :].astype(F32)

    save_down = local(stage, down_o)
    save_down.start()
    save_down.wait()

    line_end(up_steps, up_w, up_got, 2, stage)
    save_up = local(stage, up_o)
    save_up.start()
    for copy in gains_sends:
        copy.wait_recv()
    value = gains_far[...]
    for by in range(1, contexts):
        value += gains_got[by - 1]
    gain_o[...] = value
    for copy in low_gathers:
        copy.wait_recv()
    save_low = [local(low_q_all, low_q_o), local(low_l_all, low_l_o)]
    for copy in save_low:
        copy.start()
    line_end(out_steps, out_far, out_got, 1, out_o)
    for copy in save_low + [save_norm, save_up]:
        copy.wait()
    for back, save in f_backs:
        back.wait_recv()
        save.wait()
    sent = [d_pair, q_pair, u_pair, l_pair, q_back, d_back, down_pair, gains_pair]
    sent += q_hops + [hop[0] for hop in d_hops] + d_sends + d_gathers + small_sends
    sent += low_pairs + low_sends + low_gathers + gains_sends + [back[0] for back in f_backs]
    for hops in f_hops:
        sent += hops
    for copy in sent:
        copy.wait_send()


def tail(contexts, tensors, split, inside_args, outside_args):
    dq_t, query_t, dlat, lat_grad = (inside_args[i] for i in (0, 2, 6, 11))
    out_cols = outside_args[0].shape[1]
    rows = query_t.shape[1]
    rank = query_t.shape[0]
    width = outside_args[9].shape[1]
    units = outside_args[2].shape[1]
    half = width // 2
    share = half // contexts
    size = share // split
    last = contexts - 1
    hops = tensors.bit_length() - 1
    kv = dlat.shape[0]
    d_rows = kv // 2
    lanes = rows >> (hops - 1)
    heads_q = dq_t.shape[0]
    lat_rows, lat_cols = lat_grad.shape
    count_gains = (2 * width + rank + lat_rows) // 8
    anywhere = pl.BlockSpec(memory_space=pl.ANY)
    inside = pl.BlockSpec(memory_space=pltpu.VMEM)
    vm = pltpu.VMEM
    sds = jax.ShapeDtypeStruct
    chunks = rows // CHUNK
    return pl.pallas_call(
        functools.partial(tail_kernel, contexts, tensors, split),
        in_specs=[inside] * len(inside_args) + [anywhere] * len(outside_args),
        out_specs=[anywhere] * 3 + [inside] * 3 + [anywhere] * 2 + [inside, anywhere],
        out_shape=[
            sds((rows, width), BF16),
            sds((split, size, rank), BF16),
            sds((split, size, kv), BF16),
            sds((rank // (2 * contexts), heads_q), F32),
            sds((lat_rows // (2 * contexts), lat_cols), F32),
            sds((share, out_cols), F32),
            sds((share, units), F32),
            sds((share, units), F32),
            sds((8, count_gains), F32),
            sds((rows, width), BF16),
        ],
        scratch_shapes=[
            vm((2, rows // 2, rank), BF16),
            vm((rows // 2, rank), BF16),
            vm((hops - 1, rows // 2, rank), BF16),
            vm((2, rows // 2, rank), BF16),
            vm((d_rows, contexts * rows), BF16),
            vm((contexts, d_rows, rows), BF16),
            vm((hops - 1, contexts, d_rows, rows // 2), BF16),
            vm((last, d_rows, lanes), BF16),
            vm((d_rows, rows), BF16),
            vm((d_rows, rows), BF16),
            vm((rank, heads_q), BF16),
            vm((rank // 2, heads_q), BF16),
            vm((last, rank // (2 * contexts), heads_q), BF16),
            vm((lat_rows // 2, lat_cols), BF16),
            vm((last, lat_rows // (2 * contexts), lat_cols), BF16),
            vm((rows, width), BF16),
            vm((2, last - 1, share, units), BF16),
            vm((half, out_cols), BF16),
            vm((half, out_cols), BF16),
            vm((2, last, share, out_cols), BF16),
            vm((contexts * rows, units), BF16),
            vm((2 * share, contexts * rows), BF16),
            vm((2 * share, units), BF16),
            vm((share, units), BF16),
            vm((2, CHUNK, half), BF16),
            vm((chunks, CHUNK, half), BF16),
            vm((hops - 1, chunks, CHUNK, half), BF16),
            vm((rows, rank), BF16),
            vm((kv, rows), BF16),
            vm((width, rows), BF16),
            vm((2 * contexts * size, rank), BF16),
            vm((2 * contexts * size, kv), BF16),
            vm((contexts * size, rank), BF16),
            vm((contexts * size, kv), BF16),
            vm((last, size, rank), BF16),
            vm((last, size, kv), BF16),
            vm((split, size, rank), BF16),
            vm((split, size, kv), BF16),
            vm((width, rank), BF16),
            vm((kv, width), BF16),
            vm((128, width), F32),
            vm((share, units), F32),
            vm((8, count_gains), F32),
            vm((8, count_gains), F32),
            vm((last, 8, count_gains), F32),
            pltpu.SemaphoreType.DMA((128,)),
            pltpu.SemaphoreType.DMA((128,)),
            pltpu.SemaphoreType.DMA((48,)),
        ],
        compiler_params=pltpu.CompilerParams(
            collective_id=2, has_side_effects=True, vmem_limit_bytes=65000 * 1024
        ),
        cost_estimate=pl.CostEstimate(
            flops=2 * rows * width * units * 3, bytes_accessed=40 * 1024 * 1024, transcendentals=0
        ),
        name="tail",
    )(*inside_args, *outside_args)


def finish_kernel(
    count,
    tokens,
    branch,
    feed,
    dmiddle,
    norm_one,
    low_q,
    low_l,
    *rest,
):
    given = rest[:count]
    layer_out, token_grad, low_q_o, low_l_o = rest[count : count + 4]
    taken = rest[count + 4 :]
    for src, dst in zip(given, taken):
        dst[...] = src[...]

    @pl.when(pl.program_id(0) == 0)
    def _():
        low_q_o[...] = low_q[...].astype(F32)
        low_l_o[...] = low_l[...].astype(F32).T

    added = branch[...].astype(F32) + feed[...].astype(F32)
    layer_out[...] = (tokens[...].astype(F32) + RESIDUAL * added).astype(BF16)
    token_grad[...] = dmiddle[...] + norm_one[...].astype(F32)


def finish(tokens, branch, feed, dmiddle, norm_one, low_q, low_l, given):
    rows, width = tokens.shape
    steps = 4
    tiled = pl.BlockSpec((rows // steps, width), lambda i: (i, 0))
    passed = [
        pl.BlockSpec((g.shape[0] // steps, g.shape[1]), lambda i: (i, 0))
        if g.shape[0] % (8 * steps) == 0
        else whole_spec(g.shape)
        for g in given
    ]
    sds = jax.ShapeDtypeStruct
    return pl.pallas_call(
        functools.partial(finish_kernel, len(given)),
        grid=(steps,),
        in_specs=[tiled] * 5
        + [whole_spec(low_q.shape), whole_spec(low_l.shape)]
        + passed,
        out_specs=[tiled] * 2
        + [whole_spec(low_q.shape), whole_spec(low_l.shape[::-1])]
        + passed,
        out_shape=[
            sds((rows, width), BF16),
            sds((rows, width), F32),
            sds(low_q.shape, F32),
            sds(low_l.shape[::-1], F32),
        ]
        + [sds(g.shape, g.dtype) for g in given],
        compiler_params=pltpu.CompilerParams(vmem_limit_bytes=65000 * 1024),
        name="finish",
    )(tokens, branch, feed, dmiddle, norm_one, low_q, low_l, *given)


def pick(value, index):
    return lax.dynamic_index_in_dim(value, index, 0, keepdims=False)


def per_device(
    sizes,
    tokens,
    cotangent,
    group_order,
    attn_gain,
    query_down,
    query_gain,
    latent_down,
    latent_gain,
    query_up,
    latent_up,
    attn_out,
    mlp_gain,
    gate_proj,
    up_proj,
    down_proj,
):
    contexts, tensors = sizes
    rows, width = tokens.shape[1:]
    heads = query_up.shape[1] // (NOPE + ROPE)
    z = lax.axis_index("context")
    d = lax.axis_index("dp")
    share = width // (2 * contexts)
    tokens = tokens[0]
    cotangent = cotangent[0]
    query_up_t = query_up.T
    latent_down_t = latent_down.T
    gains = jnp.concatenate([attn_gain, mlp_gain, query_gain, latent_gain])[None]

    mine = lax.dynamic_slice_in_dim(group_order, 2 * z, 2)
    offsets = jnp.arange(HALF, dtype=jnp.int32)
    query_pos = (mine[:, None] * HALF + offsets[None, :]).reshape(rows)
    freq = 10000.0 ** (-2.0 * jnp.arange(ROPE // 2, dtype=F32) / ROPE)
    angle_t = freq[:, None] * query_pos.astype(F32)[None, :]
    cos_t, sin_t = jnp.cos(angle_t), jnp.sin(angle_t)

    (
        q_t,
        latent_all,
        latent_all_t,
        rope_all,
        rope_all_t,
        one_inverse,
        query_normed,
        query_inverse,
        query_t,
        cache_t,
        cache_inverse_t,
        one_t,
        feed_t,
        latent_up_t,
    ) = front(
        contexts,
        gains,
        tokens,
        cotangent,
        query_down,
        latent_down_t,
        query_up_t,
        latent_up,
        cos_t,
        sin_t,
    )
    joined_t, exact_t, lse = attention_forward(
        contexts, group_order, q_t, latent_all, latent_all_t, rope_all, latent_up, latent_up_t
    )
    (
        branch,
        two,
        hidden,
        dgate,
        dup,
        feed_part,
        dmiddle,
        dbranch,
        feed_all,
        far_two,
        far_dgate,
        near,
        dmix_t,
        mlp_gain_grad,
    ) = feed_forward(
        contexts,
        tensors,
        joined_t,
        tokens,
        cotangent,
        gains,
        attn_out,
        down_proj,
        gate_proj.T,
        up_proj.T,
        feed_t,
    )
    dq_t, lat_grad, dlat_t, grad_gate_proj, up_pieces, out_part, far_out, _, spread = backward(
        contexts,
        group_order,
        q_t,
        latent_all,
        latent_all_t,
        rope_all,
        rope_all_t,
        latent_up,
        latent_up_t,
        exact_t,
        lse,
        dmix_t,
        cos_t,
        sin_t,
        joined_t,
        two,
        far_two,
        dgate,
        far_dgate,
        dup,
        near,
        dbranch,
    )
    split = tensors
    while (share // split) % 16 != 0 or share % split != 0:
        split //= 2
    (
        norm_one,
        low_q,
        low_l,
        small_q,
        small_l,
        grad_attn_out,
        grad_up_proj,
        grad_down,
        gain_sums,
        feed,
    ) = tail(
        contexts,
        tensors,
        split,
        [
            dq_t.reshape(heads * (NOPE + ROPE), rows),
            query_up_t,
            query_t,
            query_normed,
            query_inverse,
            gains,
            dlat_t,
            cache_t,
            cache_inverse_t,
            cos_t,
            sin_t,
            lat_grad,
            one_inverse,
            mlp_gain_grad,
        ],
        [
            out_part,
            far_out,
            hidden,
            near,
            spread,
            feed_all,
            up_pieces,
            one_t,
            query_down,
            latent_down_t,
            tokens,
            feed_part,
        ],
    )
    (
        layer_out,
        token_grad,
        low_q,
        low_l,
        grad_gate_proj,
        grad_up_proj,
        grad_down,
        grad_attn_out,
        small_q,
        small_l,
    ) = finish(
        tokens,
        branch,
        feed,
        dmiddle,
        norm_one,
        low_q.reshape(share, -1),
        low_l.reshape(share, -1),
        [grad_gate_proj, grad_up_proj, grad_down, grad_attn_out, small_q, small_l],
    )

    gain_sums = gain_sums.reshape(-1)
    gain_grads = []
    edge = 0
    for value in (attn_gain, mlp_gain, query_gain, latent_gain):
        part = gain_sums[edge : edge + value.shape[0]].reshape(2 * contexts, -1)
        gain_grads.append(pick(part, d * contexts + z))
        edge += value.shape[0]

    return (
        layer_out[None],
        token_grad[None],
        gain_grads[0],
        low_q,
        gain_grads[2],
        low_l.T,
        gain_grads[3],
        small_q,
        small_l,
        grad_attn_out.T,
        gain_grads[1],
        grad_gate_proj,
        grad_up_proj,
        grad_down.T,
    )


def solution(mesh):
    in_specs = (
        P("dp", "context", None),
        P("dp", "context", None),
        P(),
        P(),
        P(),
        P(),
        P(),
        P(),
        P(None, "tensor"),
        P(None, "tensor"),
        P("tensor", None),
        P(),
        P(None, "tensor"),
        P(None, "tensor"),
        P("tensor", None),
    )
    out_specs = (
        P("dp", "context", None),
        P("dp", "context", None),
        P(("dp", "context")),
        P(("dp", "context"), None),
        P(("dp", "context")),
        P(("dp", "context"), None),
        P(("dp", "context")),
        P(("dp", "context"), "tensor"),
        P(("dp", "context"), "tensor"),
        P("tensor", ("dp", "context")),
        P(("dp", "context")),
        P(("dp", "context"), "tensor"),
        P(("dp", "context"), "tensor"),
        P("tensor", ("dp", "context")),
    )
    sizes = (mesh.shape["context"], mesh.shape["tensor"])
    return jax.shard_map(
        functools.partial(per_device, sizes),
        mesh=mesh,
        in_specs=in_specs,
        out_specs=out_specs,
        check_vma=False,
    )
```

```python
import functools
import math

import jax
import jax.numpy as jnp
from jax import lax
from jax.experimental import pallas as pl
from jax.experimental.pallas import tpu as pltpu
from jax.sharding import PartitionSpec as P

NOPE = 64
ROPE = 32
V_DIM = 64
KV_RANK = 256
HALF = 256
GROUP = 5
CHUNK = 256

EPS = 1e-05
RESIDUAL = 1.4 / math.sqrt(62.0)
SCALE = 1.0 / math.sqrt(NOPE + ROPE)
LOG2E = 1.0 / math.log(2.0)
F32 = jnp.float32
BF16 = jnp.bfloat16


def matmul(left, right):
    return jnp.dot(left, right, preferred_element_type=F32)


def times_transposed(left, right):
    return lax.dot_general(left, right, (((1,), (1,)), ((), ())), preferred_element_type=F32)


def transposed_times(left, right):
    return lax.dot_general(left, right, (((0,), (0,)), ((), ())), preferred_element_type=F32)


MESH = pl.DeviceIdType.MESH


def greet(devices):
    barrier = pltpu.get_barrier_semaphore()
    for device in devices:
        pl.semaphore_signal(barrier, inc=1, device_id=device, device_id_type=MESH)
    pl.semaphore_wait(barrier, len(devices))


def line_of(z, contexts):
    return [{"context": lax.rem(z + by, contexts)} for by in range(1, contexts)]


def front_kernel(
    contexts,
    gains,
    tokens,
    cotangent_h,
    query_down_h,
    latent_down_t,
    query_up_h,
    latent_up_h,
    cos_t,
    sin_t,
    q_t,
    latent,
    latent_t,
    rope_keys,
    rope_keys_t,
    one_inverse,
    query_normed,
    query_inverse,
    query_t,
    cache_t,
    cache_inverse_t,
    one_t,
    feed_t,
    latent_up_t,
    cotangent,
    query_down,
    query_up_t,
    latent_up,
    one,
    low,
    keys,
    far,
    line_sem,
    line_got,
    pair_sem,
    pair_got,
    load_sem,
):
    rows, width = tokens.shape
    loads = [
        pltpu.make_async_copy(src, dst, load_sem.at[i])
        for i, (src, dst) in enumerate(
            [
                (query_down_h, query_down),
                (query_up_h, query_up_t),
                (latent_up_h, latent_up),
                (cotangent_h, cotangent),
            ]
        )
    ]
    for load in loads:
        load.start()
    rank = query_down.shape[1]
    kv = cache_t.shape[0]
    z = lax.axis_index("context")
    t = lax.axis_index("tensor")
    bit = lax.rem(t, 2)
    pair = t + 1 - 2 * bit
    gain_one = slice(0, width)
    gain_query = slice(2 * width, 2 * width + rank)
    gain_latent = slice(2 * width + rank, 2 * width + rank + kv)
    greet([{"tensor": pair}] + line_of(z, contexts))

    @pl.loop(0, rows // 32)
    def _(i):
        r = pl.ds(pl.multiple_of(i * 32, 32), 32)
        value = tokens[r, :].astype(F32)
        inverse = lax.rsqrt(jnp.mean(value * value, axis=-1, keepdims=True) + EPS)
        one_inverse[r, :] = inverse
        one[r, :] = (value * inverse * gains[:, gain_one]).astype(BF16)

    raw = times_transposed(latent_down_t[...], one[...])
    lat = raw[:kv]
    inverse = lax.rsqrt(jnp.mean(lat * lat, axis=0, keepdims=True) + EPS)
    cache_inverse_t[...] = inverse
    lat = lat * inverse
    cache_t[...] = lat.astype(BF16)
    column = jnp.broadcast_to(gains[:, gain_latent], (8, kv)).T[:, 0:1]
    keys[0:kv, :] = (lat * column).astype(BF16)
    first = raw[kv : kv + 16]
    second = raw[kv + 16 :]
    cosine = cos_t[...]
    sine = sin_t[...]
    keys[kv : kv + 16, :] = (first * cosine - second * sine).astype(BF16)
    keys[kv + 16 :, :] = (second * cosine + first * sine).astype(BF16)

    part = keys.shape[0] // 2
    mine = pl.ds(pl.multiple_of(bit * part, 16), part)
    sends = [
        pltpu.make_async_remote_copy(
            src_ref=keys.at[mine],
            dst_ref=far.at[bit, by - 1],
            send_sem=line_sem.at[by - 1],
            recv_sem=line_got.at[by - 1],
            device_id={"context": lax.rem(z + by, contexts)},
            device_id_type=MESH,
        )
        for by in range(1, contexts)
    ]
    for copy in sends:
        copy.start()

    loads[0].wait()
    low[...] = matmul(one[...], query_down[...])

    @pl.loop(0, rows // 32)
    def _(i):
        r = pl.ds(pl.multiple_of(i * 32, 32), 32)
        value = low[r, :]
        inverse = lax.rsqrt(jnp.mean(value * value, axis=-1, keepdims=True) + EPS)
        query_inverse[r, :] = inverse
        value = value * inverse
        query_normed[r, :] = value.astype(BF16)
        low[r, :] = value * gains[:, gain_query]

    query = low[...].astype(BF16)
    query_t[...] = query.T
    heads = q_t.shape[0]
    loads[1].wait()
    for h in range(heads):
        full = times_transposed(query_up_t[h * 96 : (h + 1) * 96, :], query)
        first = full[64:80]
        second = full[80:96]
        q_t[h, 0:64, :] = full[0:64].astype(BF16)
        q_t[h, 64:80, :] = (first * cosine - second * sine).astype(BF16)
        q_t[h, 80:96, :] = (second * cosine + first * sine).astype(BF16)

    for copy in sends:
        copy.wait_recv()
    share = pltpu.make_async_remote_copy(
        src_ref=far.at[bit],
        dst_ref=far.at[bit],
        send_sem=pair_sem,
        recv_sem=pair_got,
        device_id={"tensor": pair},
        device_id_type=MESH,
    )
    share.start()

    loads[2].wait()
    latent_up_t[...] = latent_up[...].T
    loads[3].wait()

    @pl.loop(0, width // 256)
    def _(i):
        lines = pl.ds(pl.multiple_of(i * 256, 256), 256)
        one_t[lines, :] = one[:, lines].T
        feed_t[lines, :] = (RESIDUAL * cotangent[:, lines].astype(F32)).astype(BF16).T

    share.wait_recv()
    latent_t[:, 0:rows] = keys[0:kv, :]
    rope_keys_t[:, 0:rows] = keys[kv:, :]
    for s in range(1, contexts):
        cols = slice(s * rows, (s + 1) * rows)
        latent_t[0:part, cols] = far[0, s - 1]
        latent_t[part:, cols] = far[1, s - 1, 0 : kv - part, :]
        rope_keys_t[:, cols] = far[1, s - 1, kv - part :, :]
    latent[...] = latent_t[...].T
    rope_keys[...] = jnp.concatenate(
        [rope_keys_t[...], jnp.zeros((128 - ROPE, rope_keys_t.shape[1]), BF16)], axis=0
    ).T
    for copy in sends:
        copy.wait_send()
    share.wait_send()


def front(
    contexts,
    gains,
    tokens,
    cotangent,
    query_down,
    latent_down_t,
    query_up_t,
    latent_up,
    cos_t,
    sin_t,
):
    rows, width = tokens.shape
    rank = query_down.shape[1]
    span = latent_down_t.shape[0]
    heads = query_up_t.shape[0] // 96
    kv = span - ROPE
    keys = contexts * rows
    inside = pl.BlockSpec(memory_space=pltpu.VMEM)
    anywhere = pl.BlockSpec(memory_space=pl.ANY)
    sds = jax.ShapeDtypeStruct
    dma = pltpu.SemaphoreType.DMA
    return pl.pallas_call(
        functools.partial(front_kernel, contexts),
        in_specs=[inside] * 2
        + [anywhere] * 2
        + [inside]
        + [anywhere] * 2
        + [inside] * 2,
        out_specs=[inside] * 14,
        out_shape=[
            sds((heads, 96, rows), BF16),
            sds((keys, kv), BF16),
            sds((kv, keys), BF16),
            sds((keys, 128), BF16),
            sds((ROPE, keys), BF16),
            sds((rows, 1), F32),
            sds((rows, rank), BF16),
            sds((rows, 1), F32),
            sds((rank, rows), BF16),
            sds((kv, rows), BF16),
            sds((1, rows), F32),
            sds((width, rows), BF16),
            sds((width, rows), BF16),
            sds(latent_up.shape[::-1], BF16),
        ],
        scratch_shapes=[
            pltpu.VMEM(cotangent.shape, BF16),
            pltpu.VMEM(query_down.shape, BF16),
            pltpu.VMEM(query_up_t.shape, BF16),
            pltpu.VMEM(latent_up.shape, BF16),
            pltpu.VMEM((rows, width), BF16),
            pltpu.VMEM((rows, rank), F32),
            pltpu.VMEM((span, rows), BF16),
            pltpu.VMEM((2, contexts - 1, span // 2, rows), BF16),
            dma((contexts - 1,)),
            dma((contexts - 1,)),
            dma,
            dma,
            dma((4,)),
        ],
        compiler_params=pltpu.CompilerParams(
            collective_id=3, has_side_effects=True, vmem_limit_bytes=60 * 1024 * 1024
        ),
        cost_estimate=pl.CostEstimate(
            flops=2 * rows * width * 1200, bytes_accessed=30 * 1024 * 1024, transcendentals=0
        ),
        name="front",
    )(
        gains,
        tokens,
        cotangent,
        query_down,
        latent_down_t,
        query_up_t,
        latent_up,
        cos_t,
        sin_t,
    )


def load_heads(heads, latent, rope_keys, latent_up, q_t, kcat, q_wide):
    for h in range(heads):
        kcat[h, :, :128] = matmul(latent[...], latent_up[:, h * 128 : (h + 1) * 128]).astype(BF16)
        kcat[h, :, 128:] = rope_keys[...]
        q_wide[h, 0:64, :] = q_t[h, 0:64, :]
        q_wide[h, 64:128, :] = jnp.zeros((64, q_wide.shape[2]), BF16)
        q_wide[h, 128:160, :] = q_t[h, 64:96, :]
        q_wide[h, 160:256, :] = jnp.zeros((96, q_wide.shape[2]), BF16)


def causal():
    key_row = lax.broadcasted_iota(jnp.int32, (HALF, HALF), 0)
    query_col = lax.broadcasted_iota(jnp.int32, (HALF, HALF), 1)
    return key_row <= query_col


def fold(value, op):
    return op(value.reshape(HALF // 8, 8, value.shape[-1]), axis=0)


def forward_kernel(
    heads,
    contexts,
    order,
    q_t,
    latent,
    latent_t,
    rope_keys,
    latent_up,
    latent_up_t,
    joined_t,
    exact_t,
    lse,
    kcat,
    v_t,
    q_wide,
    scores,
    top,
    total,
    acc,
    lies,
):
    z = lax.axis_index("context")
    for i in range(2 * contexts):
        slot = lax.rem(z + contexts - i // 2, contexts)
        lies[order[i]] = slot * (2 * HALF) + (i % 2) * HALF
    load_heads(heads, latent, rope_keys, latent_up, q_t, kcat, q_wide)
    for h in range(heads):
        v_t[h] = matmul(latent_up_t[h * 128 + 64 : (h + 1) * 128, :], latent_t[...]).astype(BF16)
    factor = SCALE * LOG2E
    for block in range(2):
        cols = slice(block * HALF, (block + 1) * HALF)
        position = order[2 * z + block]

        def score(j, masked):
            rows = pl.ds(pl.multiple_of(lies[j], HALF), HALF)
            spot = pl.ds(pl.multiple_of(j * HALF, HALF), HALF)
            for h in range(heads):
                s = matmul(kcat[h, rows, :], q_wide[h, :, cols])
                if masked:
                    s = jnp.where(causal(), s, -1e30)
                scores[h, spot, :] = s
                peak = fold(s, jnp.max)
                top[h] = peak if masked else jnp.maximum(top[h], peak)

        score(position, True)

        @pl.loop(0, position)
        def _(j):
            score(j, False)

        for h in range(heads):
            peak = jnp.max(top[h], axis=0, keepdims=True) * factor
            top[h] = jnp.broadcast_to(peak, (8, HALF))
            total[h] = jnp.zeros((8, HALF), F32)
            acc[h] = jnp.zeros((V_DIM, HALF), F32)

        @pl.loop(0, position + 1)
        def _(j):
            rows = pl.ds(pl.multiple_of(lies[j], HALF), HALF)
            spot = pl.ds(pl.multiple_of(j * HALF, HALF), HALF)
            for h in range(heads):
                p = jnp.exp2(scores[h, spot, :] * factor - top[h, 0:1, :])
                total[h] += fold(p, jnp.sum)
                acc[h] += matmul(v_t[h, :, rows], p.astype(BF16))

        for h in range(heads):
            summed = jnp.sum(total[h], axis=0, keepdims=True)
            out = acc[h] / summed
            joined_t[h * V_DIM : (h + 1) * V_DIM, cols] = out.astype(BF16)
            exact_t[h, :, cols] = out
            lse[h, :, cols] = top[h, 0:1, :] + jnp.log2(summed)


def whole_spec(shape):
    return pl.BlockSpec(shape, lambda g: (0,) * len(shape))


def attention_forward(contexts, order, q_t, latent, latent_t, rope_keys, latent_up, latent_up_t):
    count, _, rows = q_t.shape
    keys = latent.shape[0]
    heads = GROUP
    flops = 2 * count * rows * keys * 384
    return pl.pallas_call(
        functools.partial(forward_kernel, heads, contexts),
        grid=(count // heads,),
        in_specs=[
            pl.BlockSpec(memory_space=pltpu.SMEM),
            pl.BlockSpec((heads, 96, rows), lambda g: (g, 0, 0)),
            whole_spec((keys, KV_RANK)),
            whole_spec((KV_RANK, keys)),
            whole_spec((keys, 128)),
            pl.BlockSpec((KV_RANK, heads * 128), lambda g: (0, g)),
            pl.BlockSpec((heads * 128, KV_RANK), lambda g: (g, 0)),
        ],
        out_specs=[
            pl.BlockSpec((heads * V_DIM, rows), lambda g: (g, 0)),
            pl.BlockSpec((heads, V_DIM, rows), lambda g: (g, 0, 0)),
            pl.BlockSpec((heads, 1, rows), lambda g: (g, 0, 0)),
        ],
        out_shape=[
            jax.ShapeDtypeStruct((count * V_DIM, rows), BF16),
            jax.ShapeDtypeStruct((count, V_DIM, rows), F32),
            jax.ShapeDtypeStruct((count, 1, rows), F32),
        ],
        scratch_shapes=[
            pltpu.VMEM((heads, keys, 256), BF16),
            pltpu.VMEM((heads, V_DIM, keys), BF16),
            pltpu.VMEM((heads, 256, rows), BF16),
            pltpu.VMEM((heads, keys, HALF), F32),
            pltpu.VMEM((heads, 8, HALF), F32),
            pltpu.VMEM((heads, 8, HALF), F32),
            pltpu.VMEM((heads, V_DIM, HALF), F32),
            pltpu.SMEM((keys // HALF,), jnp.int32),
        ],
        compiler_params=pltpu.CompilerParams(vmem_limit_bytes=56 * 1024 * 1024),
        cost_estimate=pl.CostEstimate(
            flops=flops, bytes_accessed=12 * 1024 * 1024, transcendentals=count * rows * keys
        ),
        name="attention_forward",
    )(order, q_t, latent, latent_t, rope_keys, latent_up, latent_up_t)


def cuts(size, step=512):
    count = max(1, size // step)
    edges = [i * step for i in range(count)] + [size]
    return list(zip(edges[:-1], edges[1:]))


def feed_forward_kernel(
    contexts,
    tensors,
    joined_t,
    tokens,
    cotangent,
    gain,
    attn_out_h,
    down_h,
    gate_h,
    up_h,
    feed_t_h,
    branch_o,
    two_o,
    hidden_o,
    dgate_o,
    dup_o,
    feed_o,
    dmiddle_o,
    dbranch_o,
    feed_all_o,
    far_two_o,
    far_dgate_o,
    near_o,
    dmix_t,
    gain_o,
    attn_out,
    down,
    gate_w,
    up_w,
    part,
    final,
    near,
    across,
    dhid,
    two,
    trio,
    feed,
    dmiddle,
    load_sem,
    save_sem,
    send_sem,
    recv_sem,
    pair_sem,
    pair_got,
    line_sem,
    line_got,
    turn_sem,
    turn_got,
    keep_sem,
    give_sem,
    give_got,
):
    rows, width = tokens.shape
    half = width // 2
    t = lax.axis_index("tensor")
    bit = lax.rem(t, 2)
    pair = t + 1 - 2 * bit
    others = [pair]
    step = 2
    while step < tensors:
        others.append(t + step - 2 * step * lax.rem(t // step, 2))
        step *= 2

    loads = [
        pltpu.make_async_copy(src, dst, load_sem.at[i])
        for i, (src, dst) in enumerate(
            [(attn_out_h, attn_out), (down_h, down), (gate_h, gate_w), (up_h, up_w)]
        )
    ]
    for load in loads:
        load.start()

    d = lax.axis_index("dp")
    z = lax.axis_index("context")
    greet([{"tensor": i} for i in others] + line_of(z, contexts) + [{"dp": 1 - d}])

    share = half // contexts

    part_share = share // 2

    def turn(e, by):
        owner = lax.rem(z + by, contexts)
        if by == 0:
            src = feed_t_h.at[pl.ds(pl.multiple_of(e * half + owner * share, 16), share)]
            dst = feed_all_o.at[e * share : (e + 1) * share, 0:rows]
            return pltpu.make_async_copy(src, dst, keep_sem.at[e])
        first = e * half + owner * share + bit * part_share
        src = feed_t_h.at[pl.ds(pl.multiple_of(first, 16), part_share)]
        lines = pl.ds(pl.multiple_of(e * share + bit * part_share, 16), part_share)
        dst = feed_all_o.at[lines, by * rows : (by + 1) * rows]
        return pltpu.make_async_remote_copy(
            src_ref=src,
            dst_ref=dst,
            send_sem=turn_sem.at[e, by - 1],
            recv_sem=turn_got.at[e, by - 1],
            device_id={"context": owner},
            device_id_type=MESH,
        )

    turns = [turn(e, by) for e in range(2) for by in range(contexts)]
    for copy in turns:
        copy.start()

    def to_pair(ref, i):
        return pltpu.make_async_remote_copy(
            src_ref=ref,
            dst_ref=ref,
            send_sem=give_sem.at[i],
            recv_sem=give_got.at[i],
            device_id={"tensor": pair},
            device_id_type=MESH,
        )

    def turn_pair(e):
        lines = pl.ds(pl.multiple_of(e * share + bit * part_share, 16), part_share)
        return to_pair(feed_all_o.at[lines, rows:], e)

    def two_pair(c):
        lines = pl.ds(pl.multiple_of(c * CHUNK + bit * (CHUNK // 2), 16), CHUNK // 2)
        return to_pair(far_two_o.at[lines], 2 + c)

    def send(src, dst, job, kind, c, device):
        return pltpu.make_async_remote_copy(
            src_ref=src,
            dst_ref=dst,
            send_sem=send_sem.at[job, kind, c],
            recv_sem=recv_sem.at[job, kind, c],
            device_id={"tensor": device},
            device_id_type=MESH,
        )

    def span(c):
        return pl.ds(c * CHUNK, CHUNK)

    last = len(others)

    def hop(job, c, kind):
        if kind == 0:
            return send(
                part.at[1 - bit, span(c)], near.at[job, span(c)], job, 0, c, pair
            )
        if kind == last:
            here = final.at[job, bit, span(c)]
            return send(here, here, job, last, c, pair)
        src = near if kind == 1 else across.at[kind - 2]
        return send(
            src.at[job, span(c)], across.at[kind - 1, job, span(c)], job, kind, c, others[kind]
        )

    def reduce_pair(job, c):
        hop(job, c, 0).wait_recv()

        @pl.loop(0, CHUNK // 32)
        def _(i):
            r = pl.ds(pl.multiple_of(c * CHUNK + i * 32, 32), 32)
            near[job, r, :] = (
                near[job, r, :].astype(F32) + part[bit, r, :].astype(F32)
            ).astype(BF16)

        hop(job, c, 1).start()

    def reduce_across(job, c):
        for kind in range(1, last):
            hop(job, c, kind).wait_recv()
            src = near if kind == 1 else across.at[kind - 2]
            ending = kind == last - 1

            @pl.loop(0, CHUNK // 32)
            def _(i):
                r = pl.ds(pl.multiple_of(c * CHUNK + i * 32, 32), 32)
                value = (
                    src[job, r, :].astype(F32) + across[kind - 1, job, r, :].astype(F32)
                ).astype(BF16)
                if ending:
                    final[job, bit, r, :] = value
                else:
                    across[kind - 1, job, r, :] = value

            hop(job, c, kind + 1).start()
        hop(job, c, last).wait_recv()

    def middle_rows(r):
        parts = []
        for h in range(2):
            cols = slice(h * half, (h + 1) * half)
            parts.append(
                tokens[r, cols].astype(F32) + RESIDUAL * final[0, h, r, :].astype(F32)
            )
        square = sum(jnp.sum(p * p, axis=-1, keepdims=True) for p in parts)
        inverse = lax.rsqrt(square * (1.0 / width) + EPS)
        return parts, inverse

    def across_pair(c, kind):
        if kind == 0:
            lines = pl.ds(pl.multiple_of(bit * (CHUNK // 2), 16), CHUNK // 2)
            src = two.at[lines, pl.ds(pl.multiple_of((1 - d) * half, 128), half)]
            lines = pl.ds(pl.multiple_of(c * CHUNK + bit * (CHUNK // 2), 16), CHUNK // 2)
            dst = far_two_o.at[lines]
        else:
            src, dst = trio.at[1, span(c)], far_dgate_o.at[span(c)]
        return pltpu.make_async_remote_copy(
            src_ref=src,
            dst_ref=dst,
            send_sem=pair_sem.at[kind, c],
            recv_sem=pair_got.at[kind, c],
            device_id={"dp": 1 - d},
            device_id_type=MESH,
        )

    def along_line(c, way):
        return pltpu.make_async_remote_copy(
            src_ref=trio.at[0, span(c)],
            dst_ref=near_o.at[way, span(c)],
            send_sem=line_sem.at[way, c],
            recv_sem=line_got.at[way, c],
            device_id={"context": z + 1 - 2 * way},
            device_id_type=MESH,
        )

    chunks = rows // CHUNK
    loads[0].wait()
    for c in range(chunks):
        left = joined_t[:, c * CHUNK : (c + 1) * CHUNK]

        for turn_of in range(2):
            side = 1 - bit if turn_of == 0 else bit

            @pl.loop(0, half // 256)
            def _(n):
                cols = pl.ds(pl.multiple_of(side * half + n * 256, 256), 256)
                place = pl.ds(pl.multiple_of(n * 256, 256), 256)
                part[side, span(c), place] = transposed_times(left, attn_out[:, cols]).astype(BF16)

            if turn_of == 0:
                hop(0, c, 0).start()
    for c in range(chunks):
        reduce_pair(0, c)

    loads[1].wait()
    for c in range(chunks):

        @pl.loop(0, CHUNK // 32)
        def _(i):
            r = pl.ds(pl.multiple_of(c * CHUNK + i * 32, 32), 32)
            o = pl.ds(pl.multiple_of(i * 32, 32), 32)
            two[o, :] = (RESIDUAL * cotangent[r, :].astype(F32)).astype(BF16)

        for a, b in cuts(down.shape[0]):
            dhid[span(c), a:b] = times_transposed(two[...], down[a:b, :]).astype(BF16)

    loads[2].wait()
    loads[3].wait()
    saves = []

    def save(src, dst):
        copy = pltpu.make_async_copy(src, dst, save_sem.at[len(saves)])
        copy.start()
        saves.append(copy)
        return copy

    two_saved = None
    for c in range(chunks):
        reduce_across(0, c)
        if c > 0:
            reduce_pair(1, c - 1)
        if two_saved is not None:
            two_saved.wait()
            across_pair(c - 1, 0).wait_send()

        @pl.loop(0, CHUNK // 32)
        def _(i):
            r = pl.ds(pl.multiple_of(c * CHUNK + i * 32, 32), 32)
            o = pl.ds(pl.multiple_of(i * 32, 32), 32)
            parts, inverse = middle_rows(r)
            for h in range(2):
                cols = slice(h * half, (h + 1) * half)
                two[o, cols] = (parts[h] * inverse * gain[:, width + h * half : width + (h + 1) * half]).astype(BF16)

        two_saved = save(two, two_o.at[span(c)])
        across_pair(c, 0).start()
        for a, b in cuts(gate_w.shape[0]):
            gate = times_transposed(two[...], gate_w[a:b, :])
            upper = times_transposed(two[...], up_w[a:b, :])
            grad = dhid[span(c), a:b].astype(F32)
            sigma = 1.0 / (1.0 + jnp.exp(-gate))
            act = gate * sigma
            trio[0, span(c), a:b] = (act * upper).astype(BF16)
            trio[1, span(c), a:b] = (
                grad * upper * sigma * (1.0 + gate * (1.0 - sigma))
            ).astype(BF16)
            trio[2, span(c), a:b] = (grad * act).astype(BF16)
        for k, out in enumerate((hidden_o, dgate_o, dup_o)):
            save(trio.at[k, span(c)], out.at[span(c)])
        across_pair(c, 1).start()

        @pl.when(z < contexts - 1)
        def _():
            along_line(c, 0).start()

        @pl.when(z > 0)
        def _():
            along_line(c, 1).start()

        hop(0, c, 0).wait_send()

        for turn_of in range(2):
            side = 1 - bit if turn_of == 0 else bit

            @pl.loop(0, half // 256)
            def _(n):
                cols = pl.ds(pl.multiple_of(side * half + n * 256, 256), 256)
                place = pl.ds(pl.multiple_of(n * 256, 256), 256)
                value = matmul(trio[1, span(c), :], gate_w[:, cols])
                value += matmul(trio[2, span(c), :], up_w[:, cols])
                part[side, span(c), place] = value.astype(BF16)

            if turn_of == 0:
                hop(1, c, 0).start()
    reduce_pair(1, chunks - 1)
    two_saved.wait()

    for e in range(2):
        for by in range(1, contexts):
            turns[e * contexts + by].wait_recv()
        turn_pair(e).start()
    for c in range(chunks):
        across_pair(c, 0).wait_recv()
        two_pair(c).start()

    gain_o[...] = jnp.zeros_like(gain_o)
    feed_saved = dmiddle_saved = dbranch_saved = None
    for c in range(chunks):
        if feed_saved is not None:
            feed_saved.wait()

        @pl.loop(0, width // 256)
        def _(n):
            cols = pl.ds(pl.multiple_of(n * 256, 256), 256)
            feed[:, cols] = matmul(trio[0, span(c), :], down[:, cols]).astype(BF16)

        feed_saved = save(feed, feed_o.at[span(c)])
        reduce_across(1, c)
        if dmiddle_saved is not None:
            dmiddle_saved.wait()
            dbranch_saved.wait()
        else:
            across_pair(chunks - 1, 0).wait_send()

        @pl.loop(0, CHUNK // 32)
        def _(i):
            r = pl.ds(pl.multiple_of(c * CHUNK + i * 32, 32), 32)
            o = pl.ds(pl.multiple_of(i * 32, 32), 32)
            parts, inverse = middle_rows(r)
            dot = jnp.zeros((32, 1), F32)
            for h in range(2):
                cols = slice(h * half, (h + 1) * half)
                product = final[1, h, r, :].astype(F32) * (parts[h] * inverse)
                gain_o[:, cols] += jnp.sum(product.reshape(4, 8, half), axis=0)
                dot += jnp.sum(product * gain[:, width + h * half : width + (h + 1) * half], axis=-1, keepdims=True)
            dot = dot * (1.0 / width)
            for h in range(2):
                cols = slice(h * half, (h + 1) * half)
                weighted = final[1, h, r, :].astype(F32) * gain[:, width + h * half : width + (h + 1) * half]
                value = cotangent[r, cols].astype(F32) + inverse * (
                    weighted - parts[h] * inverse * dot
                )
                dmiddle[o, cols] = value
                two[o, cols] = (RESIDUAL * value).astype(BF16)

        dmiddle_saved = save(dmiddle, dmiddle_o.at[span(c)])
        dbranch_saved = save(two, dbranch_o.at[span(c)])
        dmix_t[:, c * CHUNK : (c + 1) * CHUNK] = times_transposed(attn_out[...], two[...]).astype(
            BF16
        )
    for h in range(2):
        save(final.at[0, h], branch_o.at[:, h * half : (h + 1) * half])
    for copy in saves[-2:] + [feed_saved, dmiddle_saved, dbranch_saved]:
        copy.wait()
    for e in range(2):
        turns[e * contexts].wait()
        for by in range(1, contexts):
            turns[e * contexts + by].wait_send()
        turn_pair(e).wait()
    for c in range(chunks):
        for k in range(3):
            saves[c * 4 + 1 + k].wait()
    for c in range(chunks):
        two_pair(c).wait()
        across_pair(c, 1).wait()

        @pl.when(z < contexts - 1)
        def _():
            along_line(c, 0).wait_send()
            along_line(c, 1).wait_recv()

        @pl.when(z > 0)
        def _():
            along_line(c, 1).wait_send()
            along_line(c, 0).wait_recv()

    for job in range(2):
        for c in range(chunks):
            for kind in range(1 - job, last + 1):
                hop(job, c, kind).wait_send()


def feed_forward(contexts, tensors, joined_t, tokens, cotangent, gain, attn_out, down, gate_w, up_w, feed_t):
    rows, width = tokens.shape
    units = down.shape[0]
    chunks = rows // CHUNK
    hops = tensors.bit_length() - 1
    anywhere = pl.BlockSpec(memory_space=pl.ANY)
    inside = pl.BlockSpec(memory_space=pltpu.VMEM)
    return pl.pallas_call(
        functools.partial(feed_forward_kernel, contexts, tensors),
        in_specs=[inside] * 4 + [anywhere] * 5,
        out_specs=[anywhere] * 12 + [inside] * 2,
        out_shape=[
            jax.ShapeDtypeStruct((rows, width), BF16),
            jax.ShapeDtypeStruct((rows, width), BF16),
            jax.ShapeDtypeStruct((rows, units), BF16),
            jax.ShapeDtypeStruct((rows, units), BF16),
            jax.ShapeDtypeStruct((rows, units), BF16),
            jax.ShapeDtypeStruct((rows, width), BF16),
            jax.ShapeDtypeStruct((rows, width), F32),
            jax.ShapeDtypeStruct((rows, width), BF16),
            jax.ShapeDtypeStruct((width // contexts, contexts * rows), BF16),
            jax.ShapeDtypeStruct((rows, width // 2), BF16),
            jax.ShapeDtypeStruct((rows, units), BF16),
            jax.ShapeDtypeStruct((2, rows, units), BF16),
            jax.ShapeDtypeStruct((joined_t.shape[0], rows), BF16),
            jax.ShapeDtypeStruct((8, width), F32),
        ],
        scratch_shapes=[
            pltpu.VMEM(attn_out.shape, BF16),
            pltpu.VMEM(down.shape, BF16),
            pltpu.VMEM(gate_w.shape, BF16),
            pltpu.VMEM(up_w.shape, BF16),
            pltpu.VMEM((2, rows, width // 2), BF16),
            pltpu.VMEM((2, 2, rows, width // 2), BF16),
            pltpu.VMEM((2, rows, width // 2), BF16),
            pltpu.VMEM((hops - 1, 2, rows, width // 2), BF16),
            pltpu.VMEM((rows, units), BF16),
            pltpu.VMEM((CHUNK, width), BF16),
            pltpu.VMEM((3, rows, units), BF16),
            pltpu.VMEM((CHUNK, width), BF16),
            pltpu.VMEM((CHUNK, width), F32),
            pltpu.SemaphoreType.DMA((4,)),
            pltpu.SemaphoreType.DMA((7 * chunks + 2,)),
            pltpu.SemaphoreType.DMA((2, hops + 1, chunks)),
            pltpu.SemaphoreType.DMA((2, hops + 1, chunks)),
        ]
        + [pltpu.SemaphoreType.DMA((2, chunks))] * 4
        + [pltpu.SemaphoreType.DMA((2, contexts - 1))] * 2
        + [pltpu.SemaphoreType.DMA((2,))]
        + [pltpu.SemaphoreType.DMA((2 + chunks,))] * 2,
        compiler_params=pltpu.CompilerParams(
            collective_id=0, has_side_effects=True, vmem_limit_bytes=63 * 1024 * 1024
        ),
        cost_estimate=pl.CostEstimate(
            flops=2 * rows * width * units * 6, bytes_accessed=60 * 1024 * 1024, transcendentals=0
        ),
        name="feed_forward",
    )(joined_t, tokens, cotangent, gain, attn_out, down, gate_w, up_w, feed_t)


def backward_kernel(
    contexts,
    group,
    order,
    q_t,
    latent,
    latent_t,
    rope_keys,
    rope_keys_t,
    latent_up,
    latent_up_t,
    exact_t,
    lse,
    dmix_t,
    cos_t,
    sin_t,
    joined_t,
    two_h,
    far_two_h,
    dgate_h,
    far_dgate_h,
    dup_h,
    near_h,
    dbranch_h,
    dq_t,
    grad_up,
    dlat_t,
    gate_o,
    up_o,
    out_o,
    far_out_o,
    far_dup_o,
    spread_o,
    kcat,
    k_t,
    q_wide,
    dmix_wide,
    q_nat,
    dmix_nat,
    delta,
    dq,
    pair,
    lat_acc,
    rope_acc,
    two,
    act,
    gate_w,
    up_w,
    arrived,
    up_arrived,
    out_w,
    joined,
    load_sem,
    dup_sem,
    dup_got,
    out_sem,
    out_got,
    gate_sem,
    gate_got,
    up_sem,
    up_got,
    spread_sem,
    spread_got,
):
    heads, _, rows = q_t.shape
    keys = latent.shape[0]
    tiles = keys // HALF
    last = contexts - 1
    half = two.shape[1]
    share = half // contexts
    d = lax.axis_index("dp")
    z = lax.axis_index("context")
    loads = [
        pltpu.make_async_copy(
            two_h.at[:, pl.ds(pl.multiple_of(d * half, 128), half)],
            two.at[0:rows],
            load_sem.at[0],
        ),
        pltpu.make_async_copy(far_two_h, two.at[rows : 2 * rows], load_sem.at[1]),
        pltpu.make_async_copy(dgate_h, act.at[0:rows], load_sem.at[2]),
        pltpu.make_async_copy(far_dgate_h, act.at[rows : 2 * rows], load_sem.at[3]),
    ]
    for load in loads:
        load.start()
    greet(line_of(z, contexts) + [{"dp": 1 - d}])

    swap_dup = pltpu.make_async_remote_copy(
        src_ref=dup_h,
        dst_ref=far_dup_o,
        send_sem=dup_sem,
        recv_sem=dup_got,
        device_id={"dp": 1 - d},
        device_id_type=MESH,
    )
    swap_dup.start()

    def line(src, dst, send_sem, recv_sem, way):
        return pltpu.make_async_remote_copy(
            src_ref=src,
            dst_ref=dst,
            send_sem=send_sem,
            recv_sem=recv_sem,
            device_id={"context": z + 1 - 2 * way},
            device_id_type=MESH,
        )

    along = [z, last - z]

    def spread(way, step):
        src = near_h.at[way] if step == 2 else spread_o.at[way, step - 3]
        i = (way, step - 2)
        return line(src, spread_o.at[i], spread_sem.at[i], spread_got.at[i], way)

    def spread_start(step):
        if step > last:
            return
        for way in range(2):
            if step > 2:

                @pl.when(along[way] >= step - 1)
                def _():
                    spread(way, step - 1).wait_recv()

            @pl.when((along[way] >= step - 1) & (along[way] < last))
            def _():
                spread(way, step).start()

    def spread_end():
        for way in range(2):
            for step in range(2, last + 1):
                if step == last:

                    @pl.when(along[way] >= step)
                    def _():
                        spread(way, step).wait_recv()

                @pl.when((along[way] >= step - 1) & (along[way] < last))
                def _():
                    spread(way, step).wait_send()

    def share_of(ref, index):
        return ref.at[pl.ds(pl.multiple_of(index * share, 16), share)]

    def farthest(way, step):
        right = z + 2 * contexts - step if way == 0 else contexts + step - 1 - along[1]
        return lax.rem(right, contexts)

    def reduce(ref, dst, send_sem, recv_sem, way, step):
        return line(
            share_of(ref, farthest(way, step)), dst, send_sem, recv_sem, way
        )

    def gate_step(way, step):
        i = (way, step - 1)
        return reduce(gate_w, arrived.at[i], gate_sem.at[i], gate_got.at[i], way, step)

    def up_step(way):
        return reduce(up_w, up_arrived.at[way], up_sem.at[way], up_got.at[way], way, 1)

    def add_rows(dst, src):
        @pl.loop(0, share // 16)
        def _(i):
            r = pl.ds(pl.multiple_of(i * 16, 16), 16)
            dst[r, :] = (dst[r, :].astype(F32) + src[r, :].astype(F32)).astype(BF16)

    def gate_start(step):
        if step > last:
            return
        for way in range(2):
            if step > 1:

                @pl.when((along[way] >= 1) & (along[way] < step))
                def _():
                    gate_step(way, step - 1).wait_recv()
                    add_rows(share_of(gate_w, farthest(way, step)), arrived.at[way, step - 2])

            @pl.when(along[way] < step)
            def _():
                gate_step(way, step).start()

    def gate_end():
        own = pl.multiple_of(z * share, 16)
        for way in range(2):

            @pl.when(along[way] >= 1)
            def _():
                gate_step(way, last).wait_recv()

        @pl.loop(0, share // 16)
        def _(i):
            r = pl.ds(pl.multiple_of(own + i * 16, 16), 16)
            q = pl.ds(pl.multiple_of(i * 16, 16), 16)
            value = gate_w[r, :].astype(F32)
            for way in range(2):
                value = jnp.where(
                    along[way] >= 1, value + arrived[way, last - 1, q, :].astype(F32), value
                )
            gate_o[q, :] = value

        for way in range(2):
            for step in range(1, last + 1):

                @pl.when(along[way] < step)
                def _():
                    gate_step(way, step).wait_send()

    upper = 1 - z // ((contexts + 1) // 2)
    count = half // 256

    def weight(ref, start):
        def tile(i):
            n = i + upper * (count - 1 - 2 * i)
            cols = pl.ds(pl.multiple_of(n * 256, 256), 256)
            ref[cols, :] = transposed_times(two[:, cols], act[...]).astype(BF16)

        pl.loop(0, 2)(tile)
        start()
        pl.loop(2, count)(tile)

    factor = SCALE * LOG2E
    row = lax.broadcasted_iota(jnp.int32, (HALF, rows), 0)
    spot = lax.broadcasted_iota(jnp.int32, (1, rows), 1)
    spot = jnp.where(
        spot < HALF, order[2 * z] * HALF + spot, order[2 * z + 1] * HALF + spot - HALF
    )

    def begin(g):
        for h in range(group):
            e = g * group + h
            span = slice(e * 128, (e + 1) * 128)
            kcat[h, :, :128] = matmul(latent[...], latent_up[:, span]).astype(BF16)
            kcat[h, :, 128:] = rope_keys[...]
            k_t[h, 0:64, :] = matmul(
                latent_up_t[e * 128 : e * 128 + 64, :], latent_t[...]
            ).astype(BF16)
            k_t[h, 64:96, :] = rope_keys_t[...]
            q_wide[h, 0:64, :] = q_t[e, 0:64, :]
            q_wide[h, 64:128, :] = jnp.zeros((64, rows), BF16)
            q_wide[h, 128:160, :] = q_t[e, 64:96, :]
            q_wide[h, 160:256, :] = jnp.zeros((96, rows), BF16)
            q_nat[h] = q_wide[h].T
            piece = dmix_t[e * V_DIM : (e + 1) * V_DIM, :]
            dmix_wide[h, 0:64, :] = jnp.zeros_like(piece)
            dmix_wide[h, 64:128, :] = piece
            dmix_nat[h] = dmix_wide[h].T
            delta[h] = jnp.sum(piece.astype(F32) * exact_t[e], axis=0, keepdims=True)
            dq[h] = jnp.zeros((96, rows), F32)

    def tiles_of(g, first, end):
        lane = lax.broadcasted_iota(jnp.int32, (1, 128), 1)
        scale = jnp.where(lane < NOPE, SCALE, 1.0).astype(F32)

        @pl.loop(first, end)
        def _(j):
            lines = pl.ds(pl.multiple_of(j * HALF, HALF), HALF)
            block = 2 * lax.rem(z + contexts - j // 2, contexts) + lax.rem(j, 2)
            allowed = row <= spot - order[block] * HALF
            turned = jnp.zeros((HALF, 128), F32)
            for h in range(group):
                e = g * group + h
                s = matmul(kcat[h, lines, :], q_wide[h])
                p = jnp.where(allowed, jnp.exp2(s * factor - lse[e]), 0.0)
                dp = matmul(kcat[h, lines, :128], dmix_wide[h])
                ds = (p * (dp - delta[h])).astype(BF16)
                dq[h] += matmul(k_t[h, :, lines], ds)
                dk = matmul(ds, q_nat[h])
                dv = matmul(p.astype(BF16), dmix_nat[h])
                pair[h, lines, :] = ((dk[:, :128] + dv) * scale).astype(BF16)
                turned += dk[:, 128:]
            rope_acc[lines, :] = turned if g == 0 else rope_acc[lines, :] + turned

    def finish(g):
        cosine = cos_t[...]
        sine = sin_t[...]
        for h in range(group):
            e = g * group + h
            span = slice(e * 128, (e + 1) * 128)
            value = dq[h] * SCALE
            first = value[64:80]
            second = value[80:96]
            dq_t[e, 0:64, :] = value[0:64].astype(BF16)
            dq_t[e, 64:80, :] = (first * cosine + second * sine).astype(BF16)
            dq_t[e, 80:96, :] = (second * cosine - first * sine).astype(BF16)
            grad_up[:, span] = matmul(latent_t[...], pair[h]).astype(BF16)
            change = times_transposed(latent_up[:, span], pair[h])
            lat_acc[...] = change if e == 0 else lat_acc[...] + change

    groups = heads // group
    total = groups * tiles
    stops = [min(total, total * 5 * (i + 1) // (4 * (last + 1))) for i in range(last)]

    spread_start(2)
    for load in loads:
        load.wait()
    weight(gate_w, lambda: gate_start(1))
    done = 0
    for i, stop in enumerate(stops + [total]):
        while done < stop:
            g = done // tiles
            until = min(stop, (g + 1) * tiles)
            if done == g * tiles:
                begin(g)
            tiles_of(g, done - g * tiles, until - g * tiles)
            if until == (g + 1) * tiles:
                finish(g)
            done = until
        if i < last:
            gate_start(i + 2)
            spread_start(i + 3)
        if i == min(1, last - 1):
            swap_dup.wait_recv()
            again = [
                pltpu.make_async_copy(dup_h, act.at[0:rows], load_sem.at[2]),
                pltpu.make_async_copy(far_dup_o, act.at[rows : 2 * rows], load_sem.at[3]),
            ]
            for load in again:
                load.start()
            for load in again:
                load.wait()

            def up_start():
                for way in range(2):

                    @pl.when(along[way] == 0)
                    def _():
                        up_step(way).start()

            weight(up_w, up_start)
            parts = [
                pltpu.make_async_copy(
                    dbranch_h.at[:, e * half : (e + 1) * half],
                    two.at[e * rows : (e + 1) * rows],
                    load_sem.at[2 + e],
                )
                for e in range(2)
            ]
            for load in parts:
                load.start()
            keep = pltpu.make_async_copy(up_w, up_o, load_sem.at[0])
            keep.start()
            joined[...] = joined_t[...].T
            for load in parts:
                load.wait()
            for e in range(2):

                @pl.loop(0, half // 256)
                def _(n):
                    cols = pl.ds(pl.multiple_of(n * 256, 256), 256)
                    lines = pl.ds(pl.multiple_of(e * half + n * 256, 256), 256)
                    out_w[lines, :] = transposed_times(
                        two[e * rows : (e + 1) * rows, cols], joined[...]
                    ).astype(BF16)

            swap_out = pltpu.make_async_remote_copy(
                src_ref=out_w.at[pl.ds(pl.multiple_of((1 - d) * half, 16), half)],
                dst_ref=far_out_o,
                send_sem=out_sem,
                recv_sem=out_got,
                device_id={"dp": 1 - d},
                device_id_type=MESH,
            )
            swap_out.start()
            keep_out = pltpu.make_async_copy(
                out_w.at[pl.ds(pl.multiple_of(d * half, 16), half)], out_o, load_sem.at[1]
            )
            keep_out.start()

    dlat_t[0:KV_RANK, :] = lat_acc[...].astype(BF16)
    dlat_t[KV_RANK:, :] = (rope_acc[...] * SCALE).T[:ROPE].astype(BF16)
    gate_end()
    spread_end()
    keep.wait()
    keep_out.wait()
    swap_dup.wait_send()
    for way in range(2):

        @pl.when(along[way] == 0)
        def _():
            up_step(way).wait_send()

        @pl.when(along[way] == 1)
        def _():
            up_step(way).wait_recv()
            piece = share_of(up_w, farthest(way, 2))
            add_rows(piece, up_arrived.at[way])
            again = pltpu.make_async_copy(
                piece, share_of(up_o, farthest(way, 2)), load_sem.at[2]
            )
            again.start()
            again.wait()

    swap_out.wait()


def backward(
    contexts,
    order,
    q_t,
    latent,
    latent_t,
    rope_keys,
    rope_keys_t,
    latent_up,
    latent_up_t,
    exact_t,
    lse,
    dmix_t,
    cos_t,
    sin_t,
    joined_t,
    two,
    far_two,
    dgate,
    far_dgate,
    dup,
    near,
    dbranch,
):
    heads, _, rows = q_t.shape
    keys = latent.shape[0]
    group = GROUP
    units = dup.shape[1]
    half = far_two.shape[1]
    share = half // contexts
    last = contexts - 1
    anywhere = pl.BlockSpec(memory_space=pl.ANY)
    inside = pl.BlockSpec(memory_space=pltpu.VMEM)
    dma = pltpu.SemaphoreType.DMA
    return pl.pallas_call(
        functools.partial(backward_kernel, contexts, group),
        in_specs=[pl.BlockSpec(memory_space=pltpu.SMEM)] + [inside] * 13 + [anywhere] * 7,
        out_specs=[inside] * 4 + [anywhere] * 5,
        out_shape=[
            jax.ShapeDtypeStruct((heads, 96, rows), BF16),
            jax.ShapeDtypeStruct((KV_RANK, heads * 128), BF16),
            jax.ShapeDtypeStruct((KV_RANK + ROPE, keys), BF16),
            jax.ShapeDtypeStruct((share, units), F32),
            jax.ShapeDtypeStruct((half, units), BF16),
            jax.ShapeDtypeStruct((half, joined_t.shape[0]), BF16),
            jax.ShapeDtypeStruct((half, joined_t.shape[0]), BF16),
            jax.ShapeDtypeStruct((rows, units), BF16),
            jax.ShapeDtypeStruct((2, last - 1, rows, units), BF16),
        ],
        scratch_shapes=[
            pltpu.VMEM((group, keys, 256), BF16),
            pltpu.VMEM((group, 96, keys), BF16),
            pltpu.VMEM((group, 256, rows), BF16),
            pltpu.VMEM((group, 128, rows), BF16),
            pltpu.VMEM((group, rows, 256), BF16),
            pltpu.VMEM((group, rows, 128), BF16),
            pltpu.VMEM((group, 1, rows), F32),
            pltpu.VMEM((group, 96, rows), F32),
            pltpu.VMEM((group, keys, 128), BF16),
            pltpu.VMEM((KV_RANK, keys), F32),
            pltpu.VMEM((keys, 128), F32),
            pltpu.VMEM((2 * rows, half), BF16),
            pltpu.VMEM((2 * rows, units), BF16),
            pltpu.VMEM((half, units), BF16),
            pltpu.VMEM((half, units), BF16),
            pltpu.VMEM((2, last, share, units), BF16),
            pltpu.VMEM((2, share, units), BF16),
            pltpu.VMEM((2 * half, joined_t.shape[0]), BF16),
            pltpu.VMEM((rows, joined_t.shape[0]), BF16),
            dma((4,)),
            dma,
            dma,
            dma,
            dma,
            dma((2, last)),
            dma((2, last)),
            dma((2,)),
            dma((2,)),
            dma((2, last - 1)),
            dma((2, last - 1)),
        ],
        compiler_params=pltpu.CompilerParams(
            collective_id=1, has_side_effects=True, vmem_limit_bytes=65000 * 1024
        ),
        cost_estimate=pl.CostEstimate(
            flops=2 * heads * rows * keys * 1000,
            bytes_accessed=40 * 1024 * 1024,
            transcendentals=heads * rows * keys,
        ),
        name="backward",
    )(
        order,
        q_t,
        latent,
        latent_t,
        rope_keys,
        rope_keys_t,
        latent_up,
        latent_up_t,
        exact_t,
        lse,
        dmix_t,
        cos_t,
        sin_t,
        joined_t,
        two,
        far_two,
        dgate,
        far_dgate,
        dup,
        near,
        dbranch,
    )


def tail_kernel(
    contexts,
    tensors,
    split,
    dq_t,
    query_up_t,
    query_t,
    query_normed,
    query_inverse,
    all_gains,
    dlat,
    cache_t,
    cache_inverse_t,
    cos_t,
    sin_t,
    lat_grad,
    first_inverse,
    mlp_gain_grad,
    out_h,
    far_out_h,
    hidden_h,
    near_h,
    spread_h,
    feed_t_h,
    up_h,
    one_t_h,
    query_down_h,
    latent_down_t_h,
    tokens_h,
    feed_h,
    norm_o,
    low_q_o,
    low_l_o,
    small_q_o,
    small_l_o,
    out_o,
    up_o,
    down_o,
    gain_o,
    feed_o,
    q_part,
    q_near,
    q_across,
    q_final,
    d_near,
    d_acc,
    d_across,
    d_got,
    d_all,
    d_final,
    u_w,
    u_far,
    u_got,
    l_far,
    l_got,
    wide,
    up_got,
    out_w,
    out_far,
    out_got,
    long,
    feed_t,
    down_w,
    down_far,
    f_part,
    f_near,
    f_across,
    dqa,
    dkva_t,
    one_t,
    low_q,
    low_l,
    low_q_far,
    low_l_far,
    low_q_got,
    low_l_got,
    low_q_all,
    low_l_all,
    query_down,
    latent_down_t,
    dh1,
    stage,
    gains,
    gains_far,
    gains_got,
    send_sem,
    recv_sem,
    load_sem,
):
    rows = dlat.shape[1] // contexts
    width = wide.shape[1]
    half = width // 2
    share = half // contexts
    last = contexts - 1
    rank = query_normed.shape[1]
    kv = cache_t.shape[0]
    first_gain = slice(0, width)
    query_gain = slice(2 * width, 2 * width + rank)
    latent_gain = slice(2 * width + rank, 2 * width + rank + kv)
    d = lax.axis_index("dp")
    z = lax.axis_index("context")
    t = lax.axis_index("tensor")
    bit = lax.rem(t, 2)
    others = [t + 1 - 2 * bit]
    step = 2
    while step < tensors:
        others.append(t + step - 2 * step * lax.rem(t // step, 2))
        step *= 2
    spot = lax.rem(t, split)
    sharers = [t - spot + lax.rem(spot + k, split) for k in range(1, split)]

    used = [0]

    def remote(src, dst, **device):
        i = used[0]
        used[0] += 1
        return pltpu.make_async_remote_copy(
            src_ref=src,
            dst_ref=dst,
            send_sem=send_sem.at[i],
            recv_sem=recv_sem.at[i],
            device_id=device,
            device_id_type=MESH,
        )

    loaded = [0]

    def local(src, dst):
        i = loaded[0]
        loaded[0] += 1
        return pltpu.make_async_copy(src, dst, load_sem.at[i])

    def only(condition, copy, what):
        @pl.when(condition)
        def _():
            getattr(copy, what)()

    def add_rows(dst, left, right, count, chunk=16):
        @pl.loop(0, count // chunk)
        def _(i):
            r = pl.ds(pl.multiple_of(i * chunk, chunk), chunk)
            dst[r, :] = (left[r, :].astype(F32) + right[r, :].astype(F32)).astype(BF16)

    def piece(ref, index, size):
        return ref.at[pl.ds(pl.multiple_of(index * size, 16), size)]

    load_out = [local(out_h, out_w), local(far_out_h, out_far)]
    load_tokens = local(tokens_h, wide)
    load_hidden = [(None, local(hidden_h, long.at[0:rows]))]
    for s in range(1, contexts):
        back = contexts - s
        dst = long.at[s * rows : (s + 1) * rows]
        right = near_h.at[0] if s == 1 else spread_h.at[0, s - 2]
        left = near_h.at[1] if back == 1 else spread_h.at[1, back - 2]
        load_hidden.append((z >= s, local(right, dst)))
        load_hidden.append((z < s, local(left, dst)))
    load_feed_t = local(feed_t_h, feed_t)
    load_one = local(one_t_h, one_t)
    load_down = [local(query_down_h, query_down), local(latent_down_t_h, latent_down_t)]

    def load_feed(c):
        return [
            local(
                feed_h.at[pl.ds(c * CHUNK, CHUNK), h * half : (h + 1) * half], f_part.at[h]
            )
            for h in range(2)
        ]

    feed_loads = [load_feed(c) for c in range(rows // CHUNK)]
    for copy in load_out:
        copy.start()
    load_feed_t.start()
    for condition, copy in load_hidden:
        if condition is None:
            copy.start()
        else:
            only(condition, copy, "start")
    for copy in [load_one, load_tokens] + load_down + feed_loads[0]:
        copy.start()

    peers = others if split == 2 else sharers
    greet([{"tensor": i} for i in peers] + line_of(z, contexts) + [{"dp": 1 - d}])

    along = [z, last - z]

    def farthest(way, step):
        right = z + 2 * contexts - step if way == 0 else contexts + step - 1 - along[1]
        return lax.rem(right, contexts)

    def line_step(w, got, way, step, first):
        return remote(
            piece(w, farthest(way, step), share),
            got.at[way, step - first],
            context=z + 1 - 2 * way,
        )

    up_w = long
    up_steps = {
        (way, step): line_step(up_h if step == 2 else up_w, up_got, way, step, 2)
        for way in range(2)
        for step in range(2, last + 1)
    }
    out_steps = {
        (way, step): line_step(out_far, out_got, way, step, 1)
        for way in range(2)
        for step in range(1, last + 1)
    }

    def line_start(steps, w, got, first, step):
        for way in range(2):
            if step > first:

                @pl.when((along[way] >= 1) & (along[way] < step))
                def _():
                    steps[way, step - 1].wait_recv()
                    target = piece(w, farthest(way, step), share)
                    add_rows(target, target, got.at[way, step - 1 - first], share)

            only(along[way] < step, steps[way, step], "start")

    def line_end(steps, w, got, first, result):
        for way in range(2):
            only(along[way] >= 1, steps[way, last], "wait_recv")

        @pl.loop(0, share // 16)
        def _(i):
            r = pl.ds(pl.multiple_of(z * share + i * 16, 16), 16)
            q = pl.ds(pl.multiple_of(i * 16, 16), 16)
            value = w[r, :].astype(F32)
            for way in range(2):
                value = jnp.where(
                    along[way] >= 1, value + got[way, last - first, q, :].astype(F32), value
                )
            result[q, :] = value

        for way in range(2):
            for step in range(first, last + 1):
                only(along[way] < step, steps[way, step], "wait_send")

    line_start(up_steps, up_w, up_got, 2, 2)

    d_rows = dlat.shape[0] // 2
    d_pair = remote(dlat.at[pl.ds(pl.multiple_of((1 - bit) * d_rows, 16), d_rows)], d_near, tensor=others[0])
    d_pair.start()

    q_rows = rows // 2
    for h in range(2):
        q_part[h] = transposed_times(
            dq_t[:, h * q_rows : (h + 1) * q_rows], query_up_t[...]
        ).astype(BF16)
    q_pair = remote(q_part.at[1 - bit], q_near, tensor=others[0])
    q_pair.start()

    for copy in load_out:
        copy.wait()
    add_rows(out_far, out_far, out_w, half, 32)
    line_start(out_steps, out_far, out_got, 1, 1)

    u_w[...] = times_transposed(query_t[...], dq_t[...]).astype(BF16)
    u_half = u_w.shape[0] // 2
    l_half = lat_grad.shape[0] // 2
    u_pair = remote(
        u_w.at[pl.ds(pl.multiple_of((1 - d) * u_half, 16), u_half)], u_far, dp=1 - d
    )
    l_pair = remote(
        lat_grad.at[pl.ds(pl.multiple_of((1 - d) * l_half, 16), l_half)], l_far, dp=1 - d
    )
    u_pair.start()
    l_pair.start()

    d_pair.wait_recv()
    mine = pl.multiple_of(bit * d_rows, 16)

    @pl.loop(0, d_rows // 16)
    def _(i):
        r = pl.ds(pl.multiple_of(i * 16, 16), 16)
        own = pl.ds(pl.multiple_of(mine + i * 16, 16), 16)
        value = (dlat[own, :].astype(F32) + d_near[r, :].astype(F32)).astype(BF16)
        for s in range(contexts):
            d_acc[s, r, :] = value[:, s * rows : (s + 1) * rows]

    d_hops = []
    lanes = rows
    start = 0
    for k in range(1, len(others)):
        lanes //= 2
        side = lax.rem(t // (2**k), 2)
        give = pl.ds(pl.multiple_of(start + (1 - side) * lanes, 128), lanes)
        start = pl.multiple_of(start + side * lanes, 128)
        d_hops.append(
            (remote(d_acc.at[:, :, give], d_across.at[k - 1, :, :, 0:lanes], tensor=others[k]),
             start, lanes)
        )

    d_hops[0][0].start()
    q_pair.wait_recv()
    add_rows(q_near, q_near, q_part.at[bit], q_rows, 32)
    q_hops = []
    for k in range(1, len(others)):
        src = q_near if k == 1 else q_across.at[k - 2]
        q_hops.append(remote(src, q_across.at[k - 1], tensor=others[k]))
    q_hops[0].start()

    load_feed_t.wait()
    for condition, copy in load_hidden:
        if condition is None:
            copy.wait()
        else:
            only(condition, copy, "wait")
    chunk = 2 * share // 5 if (2 * share // 5) % 16 == 0 else share

    @pl.loop(0, 2 * share // chunk)
    def _(i):
        r = pl.ds(pl.multiple_of(i * chunk, 16), chunk)
        down_w[r, :] = matmul(feed_t[r, :], long[...]).astype(BF16)

    load_up = local(up_h, long.at[0:half])
    load_up.start()
    down_pair = remote(piece(down_w, 1 - d, share), down_far, dp=1 - d)

    f_pairs, f_hops, f_backs = [], [], []
    for c in range(rows // CHUNK):
        span = pl.ds(c * CHUNK, CHUNK)
        f_pairs.append(remote(f_part.at[1 - bit], f_near.at[c], tensor=others[0]))
        hops = []
        for k in range(1, len(others)):
            src = f_near.at[c] if k == 1 else f_across.at[k - 2, c]
            hops.append(remote(src, f_across.at[k - 1, c], tensor=others[k]))
        f_hops.append(hops)
        here = f_across.at[len(others) - 2, c]
        f_backs.append(
            (remote(here, feed_o.at[span, pl.ds(pl.multiple_of(bit * half, 128), half)], tensor=others[0]), local(here, feed_o.at[span, pl.ds(pl.multiple_of(bit * half, 128), half)]))
        )

    def feed_pair(c):
        for copy in feed_loads[c]:
            copy.wait()
        f_pairs[c].start()

    def feed_across(c):
        f_pairs[c].wait_recv()
        add_rows(f_near.at[c], f_near.at[c], f_part.at[bit], CHUNK, 32)
        f_hops[c][0].start()
        f_pairs[c].wait_send()
        if c + 1 < rows // CHUNK:
            for copy in feed_loads[c + 1]:
                copy.start()

    def feed_back(c):
        for k, hop in enumerate(f_hops[c]):
            hop.wait_recv()
            src = f_near.at[c] if k == 0 else f_across.at[k - 1, c]
            add_rows(f_across.at[k, c], src, f_across.at[k, c], CHUNK, 32)
            if k < len(f_hops[c]) - 1:
                f_hops[c][k + 1].start()
        for back in f_backs[c]:
            back.start()


    for k, (hop, begin, lane) in enumerate(d_hops):
        hop.wait_recv()
        keep = pl.ds(begin, lane)

        @pl.loop(0, contexts)
        def _(s):
            @pl.loop(0, d_rows // 16)
            def _(i):
                r = pl.ds(pl.multiple_of(i * 16, 16), 16)
                d_acc[s, r, keep] = (
                    d_acc[s, r, keep].astype(F32) + d_across[k, s, r, 0:lane].astype(F32)
                ).astype(BF16)

        if k + 1 < len(d_hops):
            d_hops[k + 1][0].start()
    keep = pl.ds(start, lanes)
    d_sends = [
        remote(
            d_acc.at[s, :, keep],
            d_got.at[s - 1],
            context=lax.rem(z + contexts - s, contexts),
        )
        for s in range(1, contexts)
    ]
    for copy in d_sends:
        copy.start()
    final = len(q_hops) - 1
    for k, hop in enumerate(q_hops):
        hop.wait_recv()
        src = q_near if k == 0 else q_across.at[k - 1]
        dst = q_final.at[bit] if k == final else q_across.at[k]
        add_rows(dst, src, q_across.at[k], q_rows, 32)
        if k < final:
            q_hops[k + 1].start()
    q_back = remote(q_final.at[bit], q_final.at[bit], tensor=others[0])
    q_back.start()

    feed_pair(0)
    load_up.wait()
    line_start(up_steps, up_w, up_got, 2, 3) if last >= 3 else None
    line_start(out_steps, out_far, out_got, 1, 2) if last >= 2 else None
    u_pair.wait_recv()
    l_pair.wait_recv()

    @pl.loop(0, u_half // 16)
    def _(i):
        r = pl.ds(pl.multiple_of(i * 16, 16), 16)
        own = pl.ds(pl.multiple_of(d * u_half + i * 16, 16), 16)
        u_far[r, :] = (u_far[r, :].astype(F32) + u_w[own, :].astype(F32)).astype(BF16)

    @pl.loop(0, l_half // 16)
    def _(i):
        r = pl.ds(pl.multiple_of(i * 16, 16), 16)
        own = pl.ds(pl.multiple_of(d * l_half + i * 16, 16), 16)
        l_far[r, :] = (l_far[r, :].astype(F32) + lat_grad[own, :].astype(F32)).astype(BF16)

    u_size = u_half // contexts
    l_size = l_half // contexts
    small_sends = []
    for by in range(1, contexts):
        owner = lax.rem(z + by, contexts)
        small_sends.append(remote(piece(u_far, owner, u_size), u_got.at[by - 1], context=owner))
        small_sends.append(remote(piece(l_far, owner, l_size), l_got.at[by - 1], context=owner))
    for copy in small_sends:
        copy.start()
    feed_across(0)

    q_back.wait_recv()
    q_sum = jnp.zeros((8, rank), F32)

    def query_rows(i, acc):
        r = pl.ds(pl.multiple_of(i * 32, 32), 32)
        h = i // (q_rows // 32)
        o = pl.ds(pl.multiple_of(lax.rem(i, q_rows // 32) * 32, 32), 32)
        grad = q_final[h, o, :].astype(F32)
        normed = query_normed[r, :].astype(F32)
        weighted = grad * all_gains[:, query_gain]
        mean = jnp.mean(weighted * normed, axis=-1, keepdims=True)
        dqa[r, :] = (query_inverse[r, :] * (weighted - normed * mean)).astype(BF16)
        return acc + jnp.sum((grad * normed).reshape(4, 8, rank), axis=0)

    q_sum = lax.fori_loop(0, rows // 32, query_rows, q_sum)

    for copy in d_sends:
        copy.wait_recv()

    @pl.loop(0, d_rows // 16)
    def _(i):
        r = pl.ds(pl.multiple_of(i * 16, 16), 16)
        value = d_acc[0, r, keep].astype(F32)
        for s in range(1, contexts):
            value += d_got[s - 1, r, :].astype(F32)
        d_all[r, keep] = value.astype(BF16)

    d_gathers = []
    for k in range(len(others) - 1, 0, -1):
        here = d_all.at[:, pl.ds(start, lanes)]
        hop = remote(here, here, tensor=others[k])
        hop.start()
        hop.wait_recv()
        d_gathers.append(hop)
        side = lax.rem(t // (2**k), 2)
        start = pl.multiple_of(start - side * lanes, 128)
        lanes *= 2
    d_back = remote(d_all, d_final, tensor=others[0])
    d_back.start()
    if rows // CHUNK > 1:
        feed_pair(1)
    d_back.wait_recv()

    top = jnp.where(bit == 0, d_all[...], d_final[...]).astype(F32)
    bottom = jnp.where(bit == 0, d_final[...], d_all[...]).astype(F32)
    grad = jnp.concatenate([top, bottom], axis=0)
    lat = grad[:kv]
    normed = cache_t[...].astype(F32)
    column = jnp.broadcast_to(all_gains[:, latent_gain], (8, kv)).T[:, 0:1]
    weighted = lat * column
    mean = jnp.mean(weighted * normed, axis=0, keepdims=True)
    dkva_t[0:kv, :] = (cache_inverse_t[...] * (weighted - normed * mean)).astype(BF16)
    c_sum = jnp.sum((lat * normed).T, axis=0, keepdims=True)
    first = grad[kv : kv + 16]
    second = grad[kv + 16 :]
    cosine = cos_t[...]
    sine = sin_t[...]
    dkva_t[kv : kv + 16, :] = (first * cosine + second * sine).astype(BF16)
    dkva_t[kv + 16 :, :] = (second * cosine - first * sine).astype(BF16)

    load_one.wait()
    size = share // split

    @pl.loop(0, 2 * contexts)
    def _(i):
        r = pl.ds(pl.multiple_of((i * split + spot) * size, 16), size)
        o = pl.ds(pl.multiple_of(i * size, 16), size)
        low_q[o, :] = matmul(one_t[r, :], dqa[...]).astype(BF16)
        low_l[o, :] = times_transposed(one_t[r, :], dkva_t[...]).astype(BF16)

    low_half = contexts * size
    give = pl.ds(pl.multiple_of((1 - d) * low_half, 16), low_half)
    low_pairs = [
        remote(low_q.at[give], low_q_far, dp=1 - d),
        remote(low_l.at[give], low_l_far, dp=1 - d),
    ]
    for copy in low_pairs:
        copy.start()
    down_pair.start()
    line_start(out_steps, out_far, out_got, 1, 3) if last >= 3 else None
    if rows // CHUNK > 1:
        feed_across(1)

    for copy in load_down:
        copy.wait()
    load_tokens.wait()
    a_sum = jnp.zeros((8, width), F32)
    gains[...] = jnp.zeros_like(gains)
    block = dh1.shape[0]
    tall = 512

    def first_rows(c, acc):
        span = pl.ds(pl.multiple_of(c * block, block), block)
        for n in range(width // tall):
            lines = slice(n * tall, (n + 1) * tall)
            dh1[:, lines] = times_transposed(dqa[span, :], query_down[lines, :])
            dh1[:, lines] += transposed_times(dkva_t[:, span], latent_down_t[:, lines])

        def few(i, inner):
            o = pl.ds(pl.multiple_of(i * 16, 16), 16)
            r = pl.ds(pl.multiple_of(c * block + i * 16, 16), 16)
            grad = dh1[o, :]
            inverse = first_inverse[r, :]
            normed = wide[r, :].astype(F32) * inverse
            weighted = grad * all_gains[:, first_gain]
            mean = jnp.mean(weighted * normed, axis=-1, keepdims=True)
            wide[r, :] = (inverse * (weighted - normed * mean)).astype(BF16)
            return inner + jnp.sum((grad * normed).reshape(2, 8, width), axis=0)

        return lax.fori_loop(0, block // 16, few, acc)

    for c in range(rows // block):
        a_sum = first_rows(c, a_sum)
    save_norm = local(wide, norm_o)
    save_norm.start()

    parts = [
        jnp.sum(a_sum, axis=0, keepdims=True),
        jnp.sum(mlp_gain_grad[...], axis=0, keepdims=True),
        jnp.sum(q_sum, axis=0, keepdims=True),
        c_sum,
    ]
    line = jnp.concatenate(parts, axis=1)
    cut = gains.shape[1]
    for r in range(8):
        gains[r : r + 1, :] = line[:, r * cut : (r + 1) * cut]
    gains_pair = remote(gains, gains_far, dp=1 - d)
    gains_pair.start()

    feed_back(0)
    gains_pair.wait_recv()
    gains_far[...] = gains_far[...] + gains[...]
    gains_sends = [
        remote(gains_far, gains_got.at[by - 1], context=lax.rem(z + by, contexts))
        for by in range(1, contexts)
    ]
    for copy in gains_sends:
        copy.start()
    for copy in low_pairs:
        copy.wait_recv()

    @pl.loop(0, low_half // 16)
    def _(i):
        r = pl.ds(pl.multiple_of(i * 16, 16), 16)
        own = pl.ds(pl.multiple_of(d * low_half + i * 16, 16), 16)
        low_q_far[r, :] = (
            low_q_far[r, :].astype(F32) + low_q[own, :].astype(F32)
        ).astype(BF16)
        low_l_far[r, :] = (
            low_l_far[r, :].astype(F32) + low_l[own, :].astype(F32)
        ).astype(BF16)

    low_sends = []
    for by in range(1, contexts):
        owner = lax.rem(z + by, contexts)
        low_sends.append(
            remote(piece(low_q_far, owner, size), low_q_got.at[by - 1], context=owner)
        )
        low_sends.append(
            remote(piece(low_l_far, owner, size), low_l_got.at[by - 1], context=owner)
        )
    for copy in low_sends:
        copy.start()
    for copy in small_sends:
        copy.wait_recv()
    for far, got, result, count in (
        (u_far, u_got, small_q_o, u_size),
        (l_far, l_got, small_l_o, l_size),
    ):

        @pl.loop(0, count // 16)
        def _(i):
            r = pl.ds(pl.multiple_of(z * count + i * 16, 16), 16)
            q = pl.ds(pl.multiple_of(i * 16, 16), 16)
            value = far[r, :].astype(F32)
            for by in range(1, contexts):
                value += got[by - 1, q, :].astype(F32)
            result[q, :] = value

    for step in range(4, last + 1):
        line_start(out_steps, out_far, out_got, 1, step)
        line_start(up_steps, up_w, up_got, 2, step)
    if rows // CHUNK > 1:
        feed_back(1)
    for copy in low_sends:
        copy.wait_recv()

    @pl.loop(0, size // 16)
    def _(i):
        r = pl.ds(pl.multiple_of(z * size + i * 16, 16), 16)
        q = pl.ds(pl.multiple_of(i * 16, 16), 16)
        for far, got, everyone in (
            (low_q_far, low_q_got, low_q_all),
            (low_l_far, low_l_got, low_l_all),
        ):
            value = far[r, :].astype(F32)
            for by in range(1, contexts):
                value += got[by - 1, q, :].astype(F32)
            everyone[spot, q, :] = value.astype(BF16)

    low_gathers = []
    for sharer in sharers:
        for everyone in (low_q_all, low_l_all):
            here = everyone.at[spot]
            copy = remote(here, here, tensor=sharer)
            copy.start()
            low_gathers.append(copy)
    down_pair.wait_recv()

    @pl.loop(0, share // 16)
    def _(i):
        r = pl.ds(pl.multiple_of(d * share + i * 16, 16), 16)
        q = pl.ds(pl.multiple_of(i * 16, 16), 16)
        stage[q, :] = down_w[r, :].astype(F32) + down_far[q, :].astype(F32)

    save_down = local(stage, down_o)
    save_down.start()
    save_down.wait()

    line_end(up_steps, up_w, up_got, 2, stage)
    save_up = local(stage, up_o)
    save_up.start()
    for copy in gains_sends:
        copy.wait_recv()
    value = gains_far[...]
    for by in range(1, contexts):
        value += gains_got[by - 1]
    gain_o[...] = value
    for copy in low_gathers:
        copy.wait_recv()
    save_low = [local(low_q_all, low_q_o), local(low_l_all, low_l_o)]
    for copy in save_low:
        copy.start()
    line_end(out_steps, out_far, out_got, 1, out_o)
    for copy in save_low + [save_norm, save_up]:
        copy.wait()
    for back, save in f_backs:
        back.wait_recv()
        save.wait()
    sent = [d_pair, q_pair, u_pair, l_pair, q_back, d_back, down_pair, gains_pair]
    sent += q_hops + [hop[0] for hop in d_hops] + d_sends + d_gathers + small_sends
    sent += low_pairs + low_sends + low_gathers + gains_sends + [back[0] for back in f_backs]
    for hops in f_hops:
        sent += hops
    for copy in sent:
        copy.wait_send()


def tail(contexts, tensors, split, inside_args, outside_args):
    dq_t, query_t, dlat, lat_grad = (inside_args[i] for i in (0, 2, 6, 11))
    out_cols = outside_args[0].shape[1]
    rows = query_t.shape[1]
    rank = query_t.shape[0]
    width = outside_args[9].shape[1]
    units = outside_args[2].shape[1]
    half = width // 2
    share = half // contexts
    size = share // split
    last = contexts - 1
    hops = tensors.bit_length() - 1
    kv = dlat.shape[0]
    d_rows = kv // 2
    lanes = rows >> (hops - 1)
    heads_q = dq_t.shape[0]
    lat_rows, lat_cols = lat_grad.shape
    count_gains = (2 * width + rank + lat_rows) // 8
    anywhere = pl.BlockSpec(memory_space=pl.ANY)
    inside = pl.BlockSpec(memory_space=pltpu.VMEM)
    vm = pltpu.VMEM
    sds = jax.ShapeDtypeStruct
    chunks = rows // CHUNK
    return pl.pallas_call(
        functools.partial(tail_kernel, contexts, tensors, split),
        in_specs=[inside] * len(inside_args) + [anywhere] * len(outside_args),
        out_specs=[anywhere] * 3 + [inside] * 3 + [anywhere] * 2 + [inside, anywhere],
        out_shape=[
            sds((rows, width), BF16),
            sds((split, size, rank), BF16),
            sds((split, size, kv), BF16),
            sds((rank // (2 * contexts), heads_q), F32),
            sds((lat_rows // (2 * contexts), lat_cols), F32),
            sds((share, out_cols), F32),
            sds((share, units), F32),
            sds((share, units), F32),
            sds((8, count_gains), F32),
            sds((rows, width), BF16),
        ],
        scratch_shapes=[
            vm((2, rows // 2, rank), BF16),
            vm((rows // 2, rank), BF16),
            vm((hops - 1, rows // 2, rank), BF16),
            vm((2, rows // 2, rank), BF16),
            vm((d_rows, contexts * rows), BF16),
            vm((contexts, d_rows, rows), BF16),
            vm((hops - 1, contexts, d_rows, rows // 2), BF16),
            vm((last, d_rows, lanes), BF16),
            vm((d_rows, rows), BF16),
            vm((d_rows, rows), BF16),
            vm((rank, heads_q), BF16),
            vm((rank // 2, heads_q), BF16),
            vm((last, rank // (2 * contexts), heads_q), BF16),
            vm((lat_rows // 2, lat_cols), BF16),
            vm((last, lat_rows // (2 * contexts), lat_cols), BF16),
            vm((rows, width), BF16),
            vm((2, last - 1, share, units), BF16),
            vm((half, out_cols), BF16),
            vm((half, out_cols), BF16),
            vm((2, last, share, out_cols), BF16),
            vm((contexts * rows, units), BF16),
            vm((2 * share, contexts * rows), BF16),
            vm((2 * share, units), BF16),
            vm((share, units), BF16),
            vm((2, CHUNK, half), BF16),
            vm((chunks, CHUNK, half), BF16),
            vm((hops - 1, chunks, CHUNK, half), BF16),
            vm((rows, rank), BF16),
            vm((kv, rows), BF16),
            vm((width, rows), BF16),
            vm((2 * contexts * size, rank), BF16),
            vm((2 * contexts * size, kv), BF16),
            vm((contexts * size, rank), BF16),
            vm((contexts * size, kv), BF16),
            vm((last, size, rank), BF16),
            vm((last, size, kv), BF16),
            vm((split, size, rank), BF16),
            vm((split, size, kv), BF16),
            vm((width, rank), BF16),
            vm((kv, width), BF16),
            vm((128, width), F32),
            vm((share, units), F32),
            vm((8, count_gains), F32),
            vm((8, count_gains), F32),
            vm((last, 8, count_gains), F32),
            pltpu.SemaphoreType.DMA((128,)),
            pltpu.SemaphoreType.DMA((128,)),
            pltpu.SemaphoreType.DMA((48,)),
        ],
        compiler_params=pltpu.CompilerParams(
            collective_id=2, has_side_effects=True, vmem_limit_bytes=65000 * 1024
        ),
        cost_estimate=pl.CostEstimate(
            flops=2 * rows * width * units * 3, bytes_accessed=40 * 1024 * 1024, transcendentals=0
        ),
        name="tail",
    )(*inside_args, *outside_args)


def finish_kernel(
    count,
    tokens,
    branch,
    feed,
    dmiddle,
    norm_one,
    low_q,
    low_l,
    *rest,
):
    given = rest[:count]
    layer_out, token_grad, low_q_o, low_l_o = rest[count : count + 4]
    taken = rest[count + 4 :]
    for src, dst in zip(given, taken):
        dst[...] = src[...]

    @pl.when(pl.program_id(0) == 0)
    def _():
        low_q_o[...] = low_q[...].astype(F32)
        low_l_o[...] = low_l[...].astype(F32).T

    added = branch[...].astype(F32) + feed[...].astype(F32)
    layer_out[...] = (tokens[...].astype(F32) + RESIDUAL * added).astype(BF16)
    token_grad[...] = dmiddle[...] + norm_one[...].astype(F32)


def finish(tokens, branch, feed, dmiddle, norm_one, low_q, low_l, given):
    rows, width = tokens.shape
    steps = 4
    tiled = pl.BlockSpec((rows // steps, width), lambda i: (i, 0))
    passed = [
        pl.BlockSpec((g.shape[0] // steps, g.shape[1]), lambda i: (i, 0))
        if g.shape[0] % (8 * steps) == 0
        else whole_spec(g.shape)
        for g in given
    ]
    sds = jax.ShapeDtypeStruct
    return pl.pallas_call(
        functools.partial(finish_kernel, len(given)),
        grid=(steps,),
        in_specs=[tiled] * 5
        + [whole_spec(low_q.shape), whole_spec(low_l.shape)]
        + passed,
        out_specs=[tiled] * 2
        + [whole_spec(low_q.shape), whole_spec(low_l.shape[::-1])]
        + passed,
        out_shape=[
            sds((rows, width), BF16),
            sds((rows, width), F32),
            sds(low_q.shape, F32),
            sds(low_l.shape[::-1], F32),
        ]
        + [sds(g.shape, g.dtype) for g in given],
        compiler_params=pltpu.CompilerParams(vmem_limit_bytes=65000 * 1024),
        name="finish",
    )(tokens, branch, feed, dmiddle, norm_one, low_q, low_l, *given)


def pick(value, index):
    return lax.dynamic_index_in_dim(value, index, 0, keepdims=False)


def per_device(
    sizes,
    tokens,
    cotangent,
    group_order,
    attn_gain,
    query_down,
    query_gain,
    latent_down,
    latent_gain,
    query_up,
    latent_up,
    attn_out,
    mlp_gain,
    gate_proj,
    up_proj,
    down_proj,
):
    contexts, tensors = sizes
    rows, width = tokens.shape[1:]
    heads = query_up.shape[1] // (NOPE + ROPE)
    z = lax.axis_index("context")
    d = lax.axis_index("dp")
    share = width // (2 * contexts)
    tokens = tokens[0]
    cotangent = cotangent[0]
    query_up_t = query_up.T
    latent_down_t = latent_down.T
    gains = jnp.concatenate([attn_gain, mlp_gain, query_gain, latent_gain])[None]

    mine = lax.dynamic_slice_in_dim(group_order, 2 * z, 2)
    offsets = jnp.arange(HALF, dtype=jnp.int32)
    query_pos = (mine[:, None] * HALF + offsets[None, :]).reshape(rows)
    freq = 10000.0 ** (-2.0 * jnp.arange(ROPE // 2, dtype=F32) / ROPE)
    angle_t = freq[:, None] * query_pos.astype(F32)[None, :]
    cos_t, sin_t = jnp.cos(angle_t), jnp.sin(angle_t)

    (
        q_t,
        latent_all,
        latent_all_t,
        rope_all,
        rope_all_t,
        one_inverse,
        query_normed,
        query_inverse,
        query_t,
        cache_t,
        cache_inverse_t,
        one_t,
        feed_t,
        latent_up_t,
    ) = front(
        contexts,
        gains,
        tokens,
        cotangent,
        query_down,
        latent_down_t,
        query_up_t,
        latent_up,
        cos_t,
        sin_t,
    )
    joined_t, exact_t, lse = attention_forward(
        contexts, group_order, q_t, latent_all, latent_all_t, rope_all, latent_up, latent_up_t
    )
    (
        branch,
        two,
        hidden,
        dgate,
        dup,
        feed_part,
        dmiddle,
        dbranch,
        feed_all,
        far_two,
        far_dgate,
        near,
        dmix_t,
        mlp_gain_grad,
    ) = feed_forward(
        contexts,
        tensors,
        joined_t,
        tokens,
        cotangent,
        gains,
        attn_out,
        down_proj,
        gate_proj.T,
        up_proj.T,
        feed_t,
    )
    dq_t, lat_grad, dlat_t, grad_gate_proj, up_pieces, out_part, far_out, _, spread = backward(
        contexts,
        group_order,
        q_t,
        latent_all,
        latent_all_t,
        rope_all,
        rope_all_t,
        latent_up,
        latent_up_t,
        exact_t,
        lse,
        dmix_t,
        cos_t,
        sin_t,
        joined_t,
        two,
        far_two,
        dgate,
        far_dgate,
        dup,
        near,
        dbranch,
    )
    split = tensors
    while (share // split) % 16 != 0 or share % split != 0:
        split //= 2
    (
        norm_one,
        low_q,
        low_l,
        small_q,
        small_l,
        grad_attn_out,
        grad_up_proj,
        grad_down,
        gain_sums,
        feed,
    ) = tail(
        contexts,
        tensors,
        split,
        [
            dq_t.reshape(heads * (NOPE + ROPE), rows),
            query_up_t,
            query_t,
            query_normed,
            query_inverse,
            gains,
            dlat_t,
            cache_t,
            cache_inverse_t,
            cos_t,
            sin_t,
            lat_grad,
            one_inverse,
            mlp_gain_grad,
        ],
        [
            out_part,
            far_out,
            hidden,
            near,
            spread,
            feed_all,
            up_pieces,
            one_t,
            query_down,
            latent_down_t,
            tokens,
            feed_part,
        ],
    )
    (
        layer_out,
        token_grad,
        low_q,
        low_l,
        grad_gate_proj,
        grad_up_proj,
        grad_down,
        grad_attn_out,
        small_q,
        small_l,
    ) = finish(
        tokens,
        branch,
        feed,
        dmiddle,
        norm_one,
        low_q.reshape(share, -1),
        low_l.reshape(share, -1),
        [grad_gate_proj, grad_up_proj, grad_down, grad_attn_out, small_q, small_l],
    )

    gain_sums = gain_sums.reshape(-1)
    gain_grads = []
    edge = 0
    for value in (attn_gain, mlp_gain, query_gain, latent_gain):
        part = gain_sums[edge : edge + value.shape[0]].reshape(2 * contexts, -1)
        gain_grads.append(pick(part, d * contexts + z))
        edge += value.shape[0]

    return (
        layer_out[None],
        token_grad[None],
        gain_grads[0],
        low_q,
        gain_grads[2],
        low_l.T,
        gain_grads[3],
        small_q,
        small_l,
        grad_attn_out.T,
        gain_grads[1],
        grad_gate_proj,
        grad_up_proj,
        grad_down.T,
    )


def solution(mesh):
    in_specs = (
        P("dp", "context", None),
        P("dp", "context", None),
        P(),
        P(),
        P(),
        P(),
        P(),
        P(),
        P(None, "tensor"),
        P(None, "tensor"),
        P("tensor", None),
        P(),
        P(None, "tensor"),
        P(None, "tensor"),
        P("tensor", None),
    )
    out_specs = (
        P("dp", "context", None),
        P("dp", "context", None),
        P(("dp", "context")),
        P(("dp", "context"), None),
        P(("dp", "context")),
        P(("dp", "context"), None),
        P(("dp", "context")),
        P(("dp", "context"), "tensor"),
        P(("dp", "context"), "tensor"),
        P("tensor", ("dp", "context")),
        P(("dp", "context")),
        P(("dp", "context"), "tensor"),
        P(("dp", "context"), "tensor"),
        P("tensor", ("dp", "context")),
    )
    sizes = (mesh.shape["context"], mesh.shape["tensor"])
    return jax.shard_map(
        functools.partial(per_device, sizes),
        mesh=mesh,
        in_specs=in_specs,
        out_specs=out_specs,
        check_vma=False,
    )
```
